128 devices in a mesh: dp: 32 (over x, z, y_lo), expert: 4 (over y_hi, core).
Axes of the slice: x: 4, y: 4 (y_hi: 2, y_lo: 2; y = y_hi * 2 + y_lo), z: 4, core: 2. Of those that a mesh axis runs over, the one named last changes fastest.
Arguments:
- tokens: bfloat16 [16384, 1024], P(('dp', 'expert')), may hold values from -24 to 24
- segments: int32 [16384], P(('dp', 'expert')), may hold values from 0 to 6, as said below
- routes: int32 [16384, 8], P(('dp', 'expert')), may hold values from 0 to 31, all different within a row
- drop_order: int32 [128, 1024], P(('dp', 'expert')), may hold values from 0 to 1023, each once within a row
- gain_attn: bfloat16 [1024], replicated, may hold values from 0.5 to 1.5
- w_query: bfloat16 [1024, 1024], replicated, may hold values from -0.1875 to 0.1875
- w_key: bfloat16 [1024, 512], replicated, may hold values from -0.1875 to 0.1875
- w_value: bfloat16 [1024, 512], replicated, may hold values from -0.1875 to 0.1875
- w_out: bfloat16 [1024, 1024], replicated, may hold values from -1 to 1
- gain_mlp: bfloat16 [1024], replicated, may hold values from 0.5 to 1.5
- w_router: bfloat16 [1024, 32], replicated, may hold values from -0.09375 to 0.09375
- w_gate: bfloat16 [32, 1024, 512], P('expert'), may hold values from -0.1875 to 0.1875
- w_up: bfloat16 [32, 1024, 512], P('expert'), may hold values from -0.1875 to 0.1875
- w_down: bfloat16 [32, 512, 1024], P('expert'), may hold values from -1 to 1
- cotangent: bfloat16 [16384, 1024], P(('dp', 'expert')), may hold values from -6 to 6
Outputs:
- block_out: bfloat16 [16384, 1024], P(('dp', 'expert'))
- d_tokens: bfloat16 [16384, 1024], P(('dp', 'expert'))
- d_gain_attn: float32 [1024], P(('dp', 'expert'))
- d_w_query: float32 [1024, 1024], P(('dp', 'expert'))
- d_w_key: float32 [1024, 512], P(('dp', 'expert'))
- d_w_value: float32 [1024, 512], P(('dp', 'expert'))
- d_w_out: float32 [1024, 1024], P(('dp', 'expert'))
- d_gain_mlp: float32 [1024], P(('dp', 'expert'))
- d_w_router: float32 [1024, 32], P(('dp', 'expert'))
- d_w_gate: float32 [32, 1024, 512], P('expert', 'dp')
- d_w_up: float32 [32, 1024, 512], P('expert', 'dp')
- d_w_down: float32 [32, 512, 1024], P('expert', 'dp')
The draws below stay inside these ranges and needn't reach their ends.
Inputs may be any that keep to these rules, and one draw needn't show every extreme that they name: `segments`: within each sequence of 1024 tokens the numbers start at 0, never fall and rise by at most one from a token to the next; one document runs from the sequence's first 128 tokens into its last 128. `routes`: each token names 8 different experts. `drop_order`: each row is an order of the pairs t * 8 + k of one device's 128 tokens, t counted within that device; pairs earlier in it claim slots first.
All inputs are finite; a program needn't handle non-finite values.
Results may differ from the reference program's by a relative error of at most 0.025.
Values may be sent and summed in bfloat16 or wider, within the bound.
No kernel may reach another device: no remote copies, remote signals or barrier semaphores. Data moves between devices by JAX's collectives and lax.ppermute only.
A program may use at most 192 MiB of HBM per device.

```python
import jax
import jax.numpy as jnp
from jax import lax

D = 1024
H = 16
KVH = 8
HD = 64
FE = 512
TOPK = 8
TOK_DEV = 128
EXPERTS = 32
WIN = 512
LEN = 1024
TOKENS = 16384
CAP = 36


def draw_segments(key, part):
    key = jax.random.fold_in(key, 7)
    seq_count = TOKENS // LEN
    stride_len = (TOK_DEV - 1) // 3
    head_key, tail_key = jax.random.split(key)
    bases = 1 + jnp.arange(3, dtype=jnp.int32) * stride_len
    head_cuts = bases[None, :] + jax.random.randint(head_key, (seq_count, 3), 0, stride_len)
    tail_cuts = LEN - TOK_DEV + bases[None, :] + jax.random.randint(tail_key, (seq_count, 3), 0, stride_len)
    cuts = jnp.concatenate([head_cuts, tail_cuts], axis=1).astype(jnp.int32)
    seq_rows = jnp.broadcast_to(jnp.arange(seq_count, dtype=jnp.int32)[:, None], cuts.shape)
    marks = jnp.zeros((seq_count, LEN), jnp.int32).at[seq_rows, cuts].add(1)
    return jnp.cumsum(marks, axis=1).astype(jnp.int32).reshape(-1)


def spiked(values, own_key, source, target, shards_of, factor):
    owner, partner = [(jnp.arange(values.shape[dim]) // (values.shape[dim] // shards_of)).reshape([-1 if axis == dim else 1 for axis in range(values.ndim)]) for dim in (source, target)]
    chosen = jax.random.permutation(own_key, shards_of)[partner]
    strong = (owner == chosen) | (owner == (partner + shards_of // 2) % shards_of)
    return jnp.where(strong, factor * values, values)


def block_scale(rng, shape, shards, smallest, largest):
    factor_of = 1.0
    for axis_at, blocks in shards:
        draws = jax.random.uniform(jax.random.fold_in(jax.random.fold_in(rng, 6), axis_at), (blocks,), jnp.float32, smallest / len(shards), largest / len(shards))
        factor_of = factor_of * jnp.repeat(jnp.exp(draws), shape[axis_at] // blocks).reshape((-1,) + (1,) * (len(shape) - 1 - axis_at))
    return factor_of


def distinct(stream_key, rows, number_of, top, lift):
    ranking = jax.random.permutation(jax.random.fold_in(stream_key, 1), number_of)
    boost = ranking
    for power in range(3):
        boost = boost * boost // number_of
    boost = boost * lift // number_of
    lots = jax.random.randint(jax.random.fold_in(stream_key, 2), (rows, number_of), 0, 4096) + boost
    holders = jax.random.permutation(jax.random.fold_in(stream_key, 3), rows)[jnp.arange(number_of) % rows]
    lots = jnp.where(jnp.arange(rows)[:, None] == holders[None, :], 1 << 14, lots)
    priority = lots * number_of + jnp.arange(number_of)
    return lax.top_k(priority.astype(jnp.int32), top)[1].astype(jnp.int32)


def centred(rng, extent, width, reach, shards=(), kind=jnp.bfloat16):
    array = jax.random.normal(rng, extent, jnp.float32) * width
    if len(shards) > 0:
        array = block_scale(rng, extent, shards, -0.22, 0.18) * array
    return jnp.clip(array, min=-reach, max=reach).astype(kind)


def bell_draw_with(rng, dims, scale, reach, shards, heavy, held_as=jnp.bfloat16):
    drawn = scale * jax.random.normal(rng, dims, jnp.float32)
    if shards:
        drawn = drawn * block_scale(rng, dims, shards, -0.22, 0.18)
    return jnp.clip(spiked(drawn, jax.random.fold_in(rng, 3), *heavy), -reach, reach).astype(held_as)


def setup_inputs(seed: int = 0) -> dict:
    seeds = jax.random.split(jax.random.key(seed), 16)
    return {
        "tokens": bell_draw_with(seeds[0], (TOKENS, D), 1.0, 24.0, ((0, 128),), (0, 1, 128, 5.5)),
        "segments": draw_segments(jax.random.fold_in(seeds[15], 71), 0),
        "routes": distinct(seeds[2], TOKENS, EXPERTS, TOPK, 2048),
        "drop_order": jax.vmap(lambda own: jax.random.permutation(own, TOK_DEV * TOPK))(jax.random.split(seeds[3], (TOKENS // TOK_DEV))).reshape((TOKENS // TOK_DEV, TOK_DEV * TOPK)).astype(jnp.int32),
        "gain_attn": jnp.clip(1.0 + 0.1 * jax.random.normal(seeds[4], (D,), jnp.float32), 0.5, 1.5).astype(jnp.bfloat16),
        "w_query": centred(seeds[5], (D, H * HD), D ** -0.5, 0.1875),
        "w_key": centred(seeds[6], (D, KVH * HD), D ** -0.5, 0.1875),
        "w_value": centred(seeds[7], (D, KVH * HD), D ** -0.5, 0.1875),
        "w_out": centred(seeds[8], (H * HD, D), (H * HD // 32) ** -0.5, 1.0),
        "gain_mlp": jnp.clip(1.0 + 0.1 * jax.random.normal(seeds[9], (D,), jnp.float32), 0.5, 1.5).astype(jnp.bfloat16),
        "w_router": centred(seeds[10], (D, EXPERTS), (4 * D) ** -0.5, 0.09375),
        "w_gate": centred(seeds[11], (EXPERTS, D, FE), D ** -0.5, 0.1875, ((0, 4),)),
        "w_up": centred(seeds[12], (EXPERTS, D, FE), D ** -0.5, 0.1875, ((0, 4),)),
        "w_down": centred(seeds[13], (EXPERTS, FE, D), (FE // 16) ** -0.5, 1.0, ((0, 4),)),
        "cotangent": centred(seeds[14], (TOKENS, D), 1.0, 6.0, ((0, 128),)),
    }


EPS = 1e-06
THETA = 10000.0
NEG = -1e+30
HIGH = lax.Precision.HIGHEST

@jax.custom_vjp
def low(v):
    return lax.optimization_barrier(v.astype(jnp.bfloat16)).astype(jnp.float32)

@jax.custom_vjp
def low_back(v):
    return v

def low_keep(v):
    return (low(v), None)

def low_pass(kept, grad):
    return (grad,)

def back_keep(v):
    return (v, None)

def back_low(kept, grad):
    return (low(grad),)
low.defvjp(low_keep, low_pass)
low_back.defvjp(back_keep, back_low)

def rms_scale(array_in):
    return lax.rsqrt(lax.optimization_barrier(jnp.mean(array_in * array_in, axis=-1, keepdims=True)) + EPS)

def rotate(array_in, positions):
    half_dim = array_in.shape[-1] // 2
    frequency = THETA ** (-jnp.arange(half_dim, dtype=jnp.float32) * 2.0 / array_in.shape[-1])
    angles = positions.astype(jnp.float32)[:, None] * frequency[None, :]
    cosine = jnp.cos(angles)[:, None, :]
    sine_tab = jnp.sin(angles)[:, None, :]
    lead_half = array_in[..., :half_dim]
    tail_half = array_in[..., half_dim:]
    return jnp.concatenate([lead_half * cosine - tail_half * sine_tab, tail_half * cosine + lead_half * sine_tab], axis=-1)

def softmax_rows(scores):
    row_top = lax.optimization_barrier(jnp.max(scores, axis=-1, keepdims=True))
    expo_rows = jnp.exp(scores - row_top)
    return expo_rows / lax.optimization_barrier(jnp.sum(expo_rows, axis=-1, keepdims=True))

def slot_table(route_rows, order_row):
    ranked = route_rows.reshape(-1)[order_row]
    onehot = (ranked[:, None] == jnp.arange(EXPERTS, dtype=jnp.int32)[None, :]).astype(jnp.int32)
    before = (jnp.cumsum(onehot, axis=0) - onehot).astype(jnp.int32)
    rank_in = lax.optimization_barrier(jnp.sum(before * onehot, axis=1)).astype(jnp.int32)
    target = jnp.where(rank_in < CAP, ranked * CAP + rank_in, EXPERTS * CAP).astype(jnp.int32)
    empty = jnp.full((EXPERTS * CAP,), TOK_DEV * TOPK, jnp.int32)
    return empty.at[target].set(order_row.astype(jnp.int32), mode='drop')

def attend_sequence(items):
    q_seq, k_seq, v_seq, seg_seq = items
    block_rows = min(512, LEN)
    block_count = LEN // block_rows
    key_pos = jnp.arange(LEN, dtype=jnp.int32)
    score_scale = HD ** (-0.5)

    def one_block(block_item):
        q_block, seg_block, pos_block = block_item
        scores = jnp.einsum('tgjd,sgd->gjts', q_block, k_seq, precision=HIGH) * score_scale
        scores = low_back(scores)
        allowed = (key_pos[None, :] <= pos_block[:, None]) & (key_pos[None, :] > pos_block[:, None] - WIN)
        allowed = allowed & (seg_seq[None, :] == seg_block[:, None])
        scores = jnp.where(allowed[None, None], scores, NEG)
        prob_rows = softmax_rows(scores)
        return jnp.einsum('gjts,sgd->tgjd', low(prob_rows), v_seq, precision=HIGH)
    attended = lax.map(jax.checkpoint(one_block), (q_seq.reshape((block_count, block_rows) + q_seq.shape[1:]), seg_seq.reshape(block_count, block_rows), key_pos.reshape(block_count, block_rows)))
    return attended.reshape(q_seq.shape)

def expert_block(rows_in, gate_rows, pairs, w_gate, w_up, w_down):
    slot_token = pairs // TOPK
    rows_pad = jnp.concatenate([rows_in, jnp.zeros((1, D), rows_in.dtype)], axis=0)
    gate_pad = jnp.concatenate([gate_rows, jnp.zeros((1,), gate_rows.dtype)], axis=0)
    slot_rows = low_back(rows_pad[slot_token]).reshape(EXPERTS, CAP, D)
    gate_h = low_back(jnp.einsum('ecd,edf->ecf', slot_rows, w_gate, precision=HIGH))
    up_h = low_back(jnp.einsum('ecd,edf->ecf', slot_rows, w_up, precision=HIGH))
    act = low(gate_h * jax.nn.sigmoid(gate_h) * up_h)
    expert_out = low_back(low(jnp.einsum('ecf,efd->ecd', act, w_down, precision=HIGH))).reshape(EXPERTS * CAP, D)
    slot_gate = low(gate_pad[pairs])
    mixed = jnp.zeros((TOK_DEV + 1, D), expert_out.dtype).at[slot_token].add(slot_gate[:, None] * expert_out)
    return mixed[:TOK_DEV]

def reference(tokens, segments, routes, drop_order, gain_attn, w_query, w_key, w_value, w_out, gain_mlp, w_router, w_gate, w_up, w_down, cotangent):
    block_total = TOKENS // TOK_DEV
    seq_count = TOKENS // LEN
    slot_pairs = jax.vmap(slot_table)(routes.reshape(block_total, TOK_DEV, TOPK), drop_order)
    positions = (jnp.arange(TOKENS, dtype=jnp.int32) % LEN).astype(jnp.int32)
    group_size = H // KVH

    def forward(x_in, gain_one, wq_in, wk_in, wv_in, wo_in, gain_two, wr_in, wg_in, wu_in, wd_in):
        attn_in = low(x_in * rms_scale(x_in) * gain_one)
        q_lin = low_back(jnp.dot(attn_in, wq_in, precision=HIGH)).reshape(TOKENS, H, HD)
        k_lin = low_back(jnp.dot(attn_in, wk_in, precision=HIGH)).reshape(TOKENS, KVH, HD)
        queries = low_back(low(rotate(q_lin, positions)))
        keys = low_back(low(rotate(k_lin, positions)))
        values = low_back(low(jnp.dot(attn_in, wv_in, precision=HIGH))).reshape(TOKENS, KVH, HD)
        attended = lax.map(attend_sequence, (queries.reshape(seq_count, LEN, KVH, group_size, HD), keys.reshape(seq_count, LEN, KVH, HD), values.reshape(seq_count, LEN, KVH, HD), segments.reshape(seq_count, LEN)))
        attn_out = low_back(low(attended.reshape(TOKENS, H * HD)))
        h_mid = x_in + low_back(jnp.dot(attn_out, wo_in, precision=HIGH))
        mlp_in = low(h_mid * rms_scale(h_mid) * gain_two)
        logits = low_back(jnp.dot(mlp_in, wr_in, precision=HIGH))
        chosen = jnp.take_along_axis(logits, routes, axis=1)
        gate_probs = softmax_rows(chosen)

        def run_block(block_item):
            return expert_block(block_item[0], block_item[1], block_item[2], wg_in, wu_in, wd_in)
        mixed = lax.map(jax.checkpoint(run_block), (mlp_in.reshape(block_total, TOK_DEV, D), gate_probs.reshape(block_total, TOK_DEV * TOPK), slot_pairs))
        return h_mid + low_back(mixed.reshape(TOKENS, D))
    inputs = tuple((item.astype(jnp.float32) for item in (tokens, gain_attn, w_query, w_key, w_value, w_out, gain_mlp, w_router, w_gate, w_up, w_down)))
    result, pull = jax.vjp(forward, *inputs)
    grads = pull(cotangent.astype(jnp.float32))
    return (result.astype(jnp.bfloat16), grads[0].astype(jnp.bfloat16), grads[1], grads[2], grads[3], grads[4], grads[5], grads[6], grads[7], grads[8], grads[9], grads[10])
```

```python
import functools

import jax
import jax.numpy as jnp
import numpy as np
from jax import lax
from jax.experimental import pallas as pl
from jax.experimental.pallas import tpu as pltpu
from jax.sharding import Mesh, PartitionSpec as P

H = 16
KVH = 8
HD = 64
D = 1024
FE = 512
TOPK = 8
EXPERTS = 32
CAP = 36
ROWS = 128
LEN = 1024
BLOCKS = LEN // ROWS
WIN = 512
LOCAL = 4
PAIRS = BLOCKS // 2
SLOTS = 80
EROWS = PAIRS * SLOTS
AUG = D + 128
SEG_LANE = 32
GAIN_LANE = 32
EPS = 1e-06
THETA = 10000.0
NEG = -1e30
BF = jnp.bfloat16
F32 = jnp.float32
GROUP = ("yl", "yh", "c")
VMEM_LIMIT = 56 * 1024 * 1024


def mm(left, right):
    return jnp.dot(left, right, preferred_element_type=F32)


def mm_nt(left, right):
    return lax.dot_general(left, right, (((1,), (1,)), ((), ())), preferred_element_type=F32)


def mm_tn(left, right):
    return lax.dot_general(left, right, (((0,), (0,)), ((), ())), preferred_element_type=F32)


def rotary_tables():
    half = HD // 2
    frequency = THETA ** (-np.arange(half, dtype=np.float64) * 2.0 / HD)
    angles = np.arange(LEN, dtype=np.float64)[:, None] * frequency[None, :]
    cosine = np.cos(angles)
    sine = np.sin(angles)
    cos_full = np.concatenate([cosine] * 4, axis=1).astype(np.float32)
    sin_full = np.concatenate([-sine, sine, -sine, sine], axis=1).astype(np.float32)
    return cos_full, sin_full


def swap_halves(array_in):
    half = HD // 2
    lane = lax.broadcasted_iota(jnp.int32, array_in.shape, 1)
    ahead = pltpu.roll(array_in, array_in.shape[1] - half, 1)
    behind = pltpu.roll(array_in, half, 1)
    return jnp.where(lane % HD < half, ahead, behind)


def vmem():
    return pl.BlockSpec(memory_space=pltpu.VMEM)


def params():
    return pltpu.CompilerParams(vmem_limit_bytes=VMEM_LIMIT)


def cost(flops, nbytes):
    return pl.CostEstimate(flops=int(flops), bytes_accessed=int(nbytes), transcendentals=0)


def full(shape):
    return pl.BlockSpec(shape, lambda *_: (0,) * len(shape))


def slots_kernel(routes_ref, order_ref, seg_ref, meta_ref, place_ref):
    order = order_ref[...]
    index = lax.broadcasted_iota(jnp.int32, (1, ROWS * TOPK), 1)
    token_of = order // TOPK
    choice_of = order - token_of * TOPK
    at_token = (token_of == lax.broadcasted_iota(jnp.int32, (ROWS, ROWS * TOPK), 0)).astype(F32)
    choice = lax.broadcasted_iota(jnp.int32, (2 * TOPK, ROWS * TOPK), 0)
    high = index // 32
    low = index - high * 32
    part = jnp.where(choice < TOPK, high, low).astype(F32)
    choice_mod = jnp.where(choice < TOPK, choice, choice - TOPK)
    table = jnp.where(choice_mod == choice_of, part, 0.0)
    found = mm_nt(at_token.astype(BF), table.astype(BF))
    place = found[:, :TOPK] * 32.0 + found[:, TOPK:]
    lane = lax.broadcasted_iota(jnp.int32, (ROWS, 128), 1)
    wide = jnp.concatenate(
        [
            routes_ref[...].astype(F32),
            jnp.broadcast_to(seg_ref[...], (TOPK, ROWS)).astype(F32),
            jnp.zeros((ROWS - 2 * TOPK, ROWS), F32),
        ],
        axis=0,
    )
    turned = jnp.transpose(wide)
    lane_f = lane.astype(F32)
    placed = jnp.full((ROWS, 128), 4096.0, F32)
    for k in range(TOPK):
        placed = jnp.where(turned[:, k : k + 1] == lane_f, place[:, k : k + 1], placed)
    place_ref[...] = placed

    def count(step, total):
        for inner in range(8):
            row = place_ref[pl.ds(step * 8 + inner, 1), :]
            total = total + jnp.where(row < placed, 1.0, 0.0)
        return total

    rank = lax.fori_loop(0, ROWS // 8, count, jnp.zeros((ROWS, 128), F32))
    slot = jnp.where(placed < 4000.0, jnp.where(rank < CAP, rank, -1.0), -2.0)
    meta_ref[...] = jnp.where(lane == SEG_LANE, turned[:, TOPK : TOPK + 1], slot).astype(BF)


def slots(routes_t, drop_order, segments):
    return pl.pallas_call(
        slots_kernel,
        out_shape=jax.ShapeDtypeStruct((ROWS, 128), BF),
        in_specs=[vmem()] * 3,
        out_specs=vmem(),
        scratch_shapes=[pltpu.VMEM((ROWS, 128), F32)],
        compiler_params=params(),
        cost_estimate=cost(2e9, 1e5),
        name="slots",
    )(routes_t, drop_order, segments)


def attend_kernel(idx, *refs):
    xs = refs[:8]
    meta_ref, gain, wq, wk, wv, cos_ref, sin_ref = refs[8:15]
    attn_in, q_ref, k_ref, v_ref, p_ref, out_ref = refs[15:21]
    seg_row, seg_col = refs[21:23]
    gain_full = gain[...].astype(F32)
    for r in range(BLOCKS):
        rows = pl.ds(pl.multiple_of(idx[r] * ROWS, ROWS), ROWS)
        x = xs[r][...].astype(F32)
        scale = lax.rsqrt(jnp.mean(x * x, axis=1, keepdims=True) + EPS)
        attn_in[rows, :] = (x * scale * gain_full).astype(BF)
    for r in range(BLOCKS):
        rows = slice(r * ROWS, (r + 1) * ROWS)
        meta = meta_ref[rows, :].astype(F32)
        seg_col[rows, :] = meta
        seg_row[:, rows] = jnp.transpose(meta)[SEG_LANE : SEG_LANE + 8, :]
    own = idx[8]
    odd = (own % 2) == 1
    half = LEN // 2
    for part in range(2):
        rows = slice(part * half, (part + 1) * half)
        block = attn_in[rows, :]
        cosine = cos_ref[rows, :]
        sine = sin_ref[rows, :]
        q = mm(block, wq[...])
        q = q * cosine + swap_halves(q) * sine
        q_ref[rows, :] = (q.astype(BF).astype(F32) * HD**-0.5).astype(BF)
        k = mm(block, wk[...])
        k = jnp.where(odd, pltpu.roll(k, HD, 1), k)
        k = k * cosine + swap_halves(k) * sine
        k_ref[rows, :] = k[:, :HD].astype(BF)
        v = mm(block, wv[...])
        v = jnp.where(odd, pltpu.roll(v, HD, 1), v)
        v_ref[rows, :] = v[:, :HD].astype(BF)
    for i in range(BLOCKS):
        lo = max(0, i - WIN // ROWS) * ROWS
        hi = (i + 1) * ROWS
        span = hi - lo
        rows = slice(i * ROWS, hi)
        q2 = jnp.concatenate([q_ref[rows, :HD], q_ref[rows, HD:]], axis=0)
        scores = mm_nt(q2, k_ref[lo:hi, :])
        q_pos = i * ROWS + lax.broadcasted_iota(jnp.int32, (ROWS, span), 0)
        k_pos = lo + lax.broadcasted_iota(jnp.int32, (ROWS, span), 1)
        allowed = (k_pos <= q_pos) & (k_pos > q_pos - WIN)
        allowed = allowed & (
            seg_row[0:1, lo:hi] == seg_col[rows, SEG_LANE : SEG_LANE + 1]
        )
        bias = jnp.where(allowed, 0.0, NEG)
        scores = scores + jnp.concatenate([bias, bias], axis=0)
        top = jnp.max(scores, axis=1, keepdims=True)
        expo = jnp.exp(scores - top)
        total = jnp.sum(expo, axis=1, keepdims=True)
        probs = (expo / total).astype(BF)
        p_ref[i, :, :span] = probs
        out = mm(probs, v_ref[lo:hi, :])
        out_ref[rows, :] = jnp.concatenate([out[:ROWS], out[ROWS:]], axis=1).astype(BF)


def attend(idx, xs, meta, gain, w_query, w_key, w_value, cos_tab, sin_tab):
    span = WIN + ROWS
    shapes = [
        jax.ShapeDtypeStruct((LEN, D), BF),
        jax.ShapeDtypeStruct((LEN, 2 * HD), BF),
        jax.ShapeDtypeStruct((LEN, HD), BF),
        jax.ShapeDtypeStruct((LEN, HD), BF),
        jax.ShapeDtypeStruct((BLOCKS, 2 * ROWS, span), BF),
        jax.ShapeDtypeStruct((LEN, 2 * HD), BF),
    ]
    grid_spec = pltpu.PrefetchScalarGridSpec(
        num_scalar_prefetch=1,
        grid=(1,),
        in_specs=[full((ROWS, D))] * 8
        + [
            full((LEN, 128)),
            full((1, D)),
            pl.BlockSpec((D, 128), lambda i, s: (0, s[8])),
            pl.BlockSpec((D, 128), lambda i, s: (0, s[8] // 2)),
            pl.BlockSpec((D, 128), lambda i, s: (0, s[8] // 2)),
            full((LEN, 128)),
            full((LEN, 128)),
        ],
        out_specs=[full(s.shape) for s in shapes],
        scratch_shapes=[pltpu.VMEM((8, LEN), F32), pltpu.VMEM((LEN, 128), F32)],
    )
    return pl.pallas_call(
        attend_kernel,
        grid_spec=grid_spec,
        out_shape=shapes,
        compiler_params=params(),
        cost_estimate=cost(1.1e10, 1.5e7),
        name="attend",
    )(idx, *xs, meta, gain, w_query, w_key, w_value, cos_tab, sin_tab)


def project_kernel(idx, *refs):
    xs = refs[:8]
    aos = refs[8:16]
    meta_ref, w_out, gain, w_router = refs[16:20]
    mlp_in, slot_t, gate_t, h_own, gate_own, ao_all = refs[20:26]
    x_all, h_all, gates = refs[26:29]
    for r in range(BLOCKS):
        rows = pl.ds(pl.multiple_of(idx[r] * ROWS, ROWS), ROWS)
        x_all[rows, :] = xs[r][...]
        ao_all[:, rows] = aos[r][...]
    gain_full = gain[...].astype(F32)
    chunk = 256
    for part in range(LEN // chunk):
        rows = slice(part * chunk, (part + 1) * chunk)
        h = x_all[rows, :].astype(F32) + mm(ao_all[rows, :], w_out[...])
        h_all[rows, :] = h
        scale = lax.rsqrt(jnp.mean(h * h, axis=1, keepdims=True) + EPS)
        normed = (h * scale * gain_full).astype(BF)
        mlp_in[rows, :] = normed
        logits = mm(normed, w_router[...])
        slot = meta_ref[rows, :].astype(F32)
        lane = lax.broadcasted_iota(jnp.int32, slot.shape, 1)
        routed = (slot > -1.5) & (lane < EXPERTS)
        logits = jnp.where(routed, logits, NEG)
        top = jnp.max(logits, axis=1, keepdims=True)
        expo = jnp.where(routed, jnp.exp(logits - top), 0.0)
        gate = expo / jnp.sum(expo, axis=1, keepdims=True)
        gates[rows, :] = gate
        slot_t[:, rows] = jnp.transpose(slot)[:EXPERTS, :]
        gate_t[:, rows] = jnp.transpose(gate)[:EXPERTS, :]
    own = pl.ds(pl.multiple_of(idx[8] * ROWS, ROWS), ROWS)
    h_own[...] = h_all[own, :]
    gate_own[...] = gates[own, :]


def project(idx, xs, aos, meta, w_out, gain, w_router):
    shapes = [
        jax.ShapeDtypeStruct((LEN, D), BF),
        jax.ShapeDtypeStruct((EXPERTS, LEN), F32),
        jax.ShapeDtypeStruct((EXPERTS, LEN), F32),
        jax.ShapeDtypeStruct((ROWS, D), F32),
        jax.ShapeDtypeStruct((ROWS, 128), F32),
        jax.ShapeDtypeStruct((LEN, D), BF),
    ]
    grid_spec = pltpu.PrefetchScalarGridSpec(
        num_scalar_prefetch=1,
        grid=(1,),
        in_specs=[full((ROWS, D))] * 8
        + [full((LEN, 128))] * 9
        + [full((D, D)), full((1, D)), full((D, 128))],
        out_specs=[full(s.shape) for s in shapes],
        scratch_shapes=[
            pltpu.VMEM((LEN, D), BF),
            pltpu.VMEM((LEN, D), F32),
            pltpu.VMEM((LEN, 128), F32),
        ],
    )
    return pl.pallas_call(
        project_kernel,
        grid_spec=grid_spec,
        out_shape=shapes,
        compiler_params=params(),
        cost_estimate=cost(9e9, 1.2e7),
        name="project",
    )(idx, *xs, *aos, meta, w_out, gain, w_router)


HALF = LOCAL // 2
HROWS = HALF * SLOTS
XROWS = D // 4 + FE // 4
QROWS = XROWS // 4


def cut_gate_down(idx, whole, whole_down, xp, e):
    quarter = D // 4
    down_q = FE // 4
    for k in range(4):
        at = (idx[11] + k) % 4
        start = pl.multiple_of(at * quarter, quarter)
        xp[k][e, :quarter, :] = whole[pl.ds(start, quarter), :]
        start = pl.multiple_of(at * down_q, down_q)
        xp[k][e, quarter:, :] = whole_down[pl.ds(start, down_q), :FE]


def cut_up_down(whole, whole_down, z_all, e):
    quarter = D // 4
    down_q = FE // 4
    small = quarter // 4
    small_down = down_q // 4
    for z in range(4):
        for x in range(4):
            start = x * quarter + z * small
            z_all[z, x, e, :small, :] = whole[start : start + small, :]
            start = x * down_q + z * small_down
            z_all[z, x, e, small:, :] = whole_down[start : start + small_down, FE:]


def weight_grads(idx, rows, act, d_out, d_gh, d_up, xp, z_all, whole, whole_down, e):
    whole_down[...] = mm_tn(act, d_out).astype(BF)
    whole[...] = mm_tn(rows, d_gh).astype(BF)
    cut_gate_down(idx, whole, whole_down, xp, e)
    whole[...] = mm_tn(rows, d_up).astype(BF)
    cut_up_down(whole, whole_down, z_all, e)


def experts_kernel(first, idx, *refs):
    mlp_in = refs[0]
    dys = refs[1:9]
    slot_t, gate_t, w_gate, w_up, w_down = refs[9:14]
    refs = refs[14:]
    if first == 0:
        hot, hot_gated, outs, dslots = refs[:4]
        xp = refs[4:8]
        z_all = refs[8]
        dy_all, rows_all, dy_rows, gate_col, whole, whole_down = refs[9:15]
    else:
        hot_before, dslots_before = refs[:2]
        rows_out, act_out, dout_out, dg_out, du_out, hot_gated, outs, dm_same, dm_other = refs[2:11]
        dy_all, rows_all, dy_rows, gate_col, hot, dslots, merged = refs[11:18]
    e = pl.program_id(0)

    @pl.when(e == 0)
    def _():
        for r in range(BLOCKS):
            rows = pl.ds(pl.multiple_of(idx[r] * ROWS, ROWS), ROWS)
            dy_all[rows, :] = dys[r][...]
        for p in range(PAIRS):
            cols = slice(p * 2 * ROWS, (p + 1) * 2 * ROWS)
            part = slice(p * SLOTS, (p + 1) * SLOTS)
            lane = lax.broadcasted_iota(jnp.int32, (1, 2 * ROWS), 1)
            lift = jnp.where(lane >= ROWS, float(CAP), 0.0)
            row_id = lax.broadcasted_iota(jnp.int32, (SLOTS, 2 * ROWS), 0).astype(F32)
            hots = []
            gated = []
            for n in range(HALF):
                slot = slot_t[pl.ds(idx[15] + first + n, 1), cols]
                gate = gate_t[pl.ds(idx[15] + first + n, 1), cols]
                place = jnp.where(slot > -0.5, slot + lift, -1.0)
                one = jnp.where(row_id == place, 1.0, 0.0)
                gated_one = one * gate
                gate_col[n, part, :] = jnp.sum(gated_one, axis=1, keepdims=True)
                hots.append(one.astype(BF))
                gated.append(gated_one.astype(BF))
            hot_pair = jnp.concatenate(hots, axis=0)
            hot[p] = hot_pair
            hot_gated[p] = jnp.concatenate(gated, axis=0)
            taken = mm(hot_pair, mlp_in[cols, :]).astype(BF)
            taken_dy = mm(hot_pair, dy_all[cols, :]).astype(BF)
            for n in range(HALF):
                rows_all[n, part, :] = taken[n * SLOTS : (n + 1) * SLOTS]
                dy_rows[n, part, :] = taken_dy[n * SLOTS : (n + 1) * SLOTS]

    rows = rows_all[e]
    wg = w_gate[0]
    wu = w_up[0]
    wd = w_down[0]
    gate_h = mm(rows, wg)
    up_h = mm(rows, wu)
    sig = 1.0 / (1.0 + jnp.exp(-gate_h))
    silu = gate_h * sig
    act = (silu * up_h).astype(BF)
    out = mm(act, wd).astype(BF)
    outs[e] = out
    dy = dy_rows[e].astype(F32)
    d_gate = jnp.sum(dy * out.astype(F32), axis=1, keepdims=True)
    d_out = (gate_col[e].astype(BF).astype(F32) * dy).astype(BF)
    d_act = mm_nt(d_out, wd)
    d_up = (d_act * silu).astype(BF)
    d_gh = (d_act * up_h * sig * (1.0 + gate_h * (1.0 - sig))).astype(BF)
    dslots[e, :, :D] = (mm_nt(d_gh, wg) + mm_nt(d_up, wu)).astype(BF)
    lane = lax.broadcasted_iota(jnp.int32, (EROWS, 128), 1)
    d_high = d_gate.astype(BF).astype(F32)
    mine = idx[15] + first + e
    extra = jnp.where(lane == mine, d_high, 0.0)
    extra = jnp.where(lane == mine + EXPERTS, d_gate - d_high, extra)
    dslots[e, :, D:] = extra.astype(BF)
    if first == 0:
        weight_grads(idx, rows, act, d_out, d_gh, d_up, xp, z_all, whole, whole_down, e)
        return
    rows_out[e] = rows
    act_out[e] = act
    dout_out[e] = d_out
    dg_out[e] = d_gh
    du_out[e] = d_up

    @pl.when(e == HALF - 1)
    def _():
        my_c = idx[14]
        here = pl.ds(pl.multiple_of(my_c * ROWS, ROWS), ROWS)
        there = pl.ds(pl.multiple_of((1 - my_c) * ROWS, ROWS), ROWS)
        for p in range(PAIRS):
            y_at = (p % 2) * 2 + p // 2
            off = (y_at - idx[13] + 4) % 4
            part = slice(p * SLOTS, (p + 1) * SLOTS)
            picks = jnp.concatenate([hot_before[p], hot[p]], axis=0)
            grads = [dslots_before[n, part, :] for n in range(HALF)]
            grads += [dslots[n, part, :] for n in range(HALF)]
            merged[...] = mm_tn(picks, jnp.concatenate(grads, axis=0)).astype(BF)
            dm_same[pl.ds(off, 1)] = merged[here, :][None]
            dm_other[pl.ds(off, 1)] = merged[there, :][None]


def experts(first, idx, mlp_in, dys, slot_t, gate_t, w_gate, w_up, w_down, before=()):
    hot_shape = jax.ShapeDtypeStruct((PAIRS, HROWS, 2 * ROWS), BF)
    wide = jax.ShapeDtypeStruct((HALF, EROWS, D), BF)
    narrow = jax.ShapeDtypeStruct((HALF, EROWS, FE), BF)
    augmented = jax.ShapeDtypeStruct((HALF, EROWS, AUG), BF)
    scratch = [
        pltpu.VMEM((LEN, D), BF),
        pltpu.VMEM((HALF, EROWS, D), BF),
        pltpu.VMEM((HALF, EROWS, D), BF),
        pltpu.VMEM((HALF, EROWS, 1), F32),
    ]
    if first == 0:
        shapes = [hot_shape, hot_shape, wide, augmented]
        shapes += [jax.ShapeDtypeStruct((HALF, XROWS, FE), BF)] * 4
        shapes += [jax.ShapeDtypeStruct((4, 4, HALF, QROWS, FE), BF)]
        scratch += [pltpu.VMEM((D, FE), BF), pltpu.VMEM((FE, D), BF)]
    else:
        exchanged = jax.ShapeDtypeStruct((4, ROWS, AUG), BF)
        shapes = [wide, narrow, wide, narrow, narrow, hot_shape, wide, exchanged, exchanged]
        scratch += [
            pltpu.VMEM(hot_shape.shape, BF),
            pltpu.VMEM(augmented.shape, BF),
            pltpu.VMEM((2 * ROWS, AUG), BF),
        ]

    def weight(*shape):
        return pl.BlockSpec((1,) + shape, lambda e, s: (s[9] * LOCAL + first + e, 0, 0))

    grid_spec = pltpu.PrefetchScalarGridSpec(
        num_scalar_prefetch=1,
        grid=(HALF,),
        in_specs=[full((LEN, D))]
        + [full((ROWS, D))] * 8
        + [full((EXPERTS, LEN))] * 2
        + [weight(D, FE), weight(D, FE), weight(FE, D)]
        + [full(item.shape) for item in before],
        out_specs=[full(item.shape) for item in shapes],
        scratch_shapes=scratch,
    )
    return pl.pallas_call(
        functools.partial(experts_kernel, first),
        grid_spec=grid_spec,
        out_shape=shapes,
        compiler_params=params(),
        cost_estimate=cost(1.5e10, 1e7),
        name="experts",
    )(idx, mlp_in, *dys, slot_t, gate_t, w_gate, w_up, w_down, *before)


def expert_grads_kernel(idx, rows_ref, act_ref, dout_ref, dg_ref, du_ref, *refs):
    xp = refs[:4]
    z_all, whole, whole_down = refs[4:7]
    weight_grads(
        idx, rows_ref[0], act_ref[0], dout_ref[0], dg_ref[0], du_ref[0], xp, z_all, whole, whole_down, 0
    )


def expert_grads(idx, rows, act, d_out, d_gh, d_up):
    shapes = [jax.ShapeDtypeStruct((HALF, XROWS, FE), BF)] * 4
    shapes += [jax.ShapeDtypeStruct((4, 4, HALF, QROWS, FE), BF)]

    def mine(*shape):
        return pl.BlockSpec((1,) + shape, lambda e, s: (e, 0, 0))

    grid_spec = pltpu.PrefetchScalarGridSpec(
        num_scalar_prefetch=1,
        grid=(HALF,),
        in_specs=[mine(EROWS, D), mine(EROWS, FE), mine(EROWS, D), mine(EROWS, FE), mine(EROWS, FE)],
        out_specs=[mine(XROWS, FE)] * 4
        + [pl.BlockSpec((4, 4, 1, QROWS, FE), lambda e, s: (0, 0, e, 0, 0))],
        scratch_shapes=[pltpu.VMEM((D, FE), BF), pltpu.VMEM((FE, D), BF)],
    )
    return pl.pallas_call(
        expert_grads_kernel,
        grid_spec=grid_spec,
        out_shape=shapes,
        compiler_params=params(),
        cost_estimate=cost(7e9, 1e7),
        name="expert_grads",
    )(idx, rows, act, d_out, d_gh, d_up)


def mixed_kernel(idx, hot_a, hot_b, out_a, out_b, same, other, merged):
    my_c = idx[14]
    here = pl.ds(pl.multiple_of(my_c * ROWS, ROWS), ROWS)
    there = pl.ds(pl.multiple_of((1 - my_c) * ROWS, ROWS), ROWS)
    for p in range(PAIRS):
        y_at = (p % 2) * 2 + p // 2
        off = (y_at - idx[13] + 4) % 4
        part = slice(p * SLOTS, (p + 1) * SLOTS)
        picks = jnp.concatenate([hot_a[p], hot_b[p]], axis=0)
        values = [ref[n, part, :] for ref in (out_a, out_b) for n in range(HALF)]
        merged[...] = mm_tn(picks, jnp.concatenate(values, axis=0)).astype(BF)
        same[pl.ds(off, 1)] = merged[here, :][None]
        other[pl.ds(off, 1)] = merged[there, :][None]


def mixed_sum(idx, hot_a, hot_b, out_a, out_b):
    shapes = [jax.ShapeDtypeStruct((4, ROWS, D), BF)] * 2
    grid_spec = pltpu.PrefetchScalarGridSpec(
        num_scalar_prefetch=1,
        grid=(1,),
        in_specs=[full(hot_a.shape)] * 2 + [full(out_a.shape)] * 2,
        out_specs=[full(item.shape) for item in shapes],
        scratch_shapes=[pltpu.VMEM((2 * ROWS, D), BF)],
    )
    return pl.pallas_call(
        mixed_kernel,
        grid_spec=grid_spec,
        out_shape=shapes,
        compiler_params=params(),
        cost_estimate=cost(4e9, 1e7),
        name="mixed_sum",
    )(idx, hot_a, hot_b, out_a, out_b)


def add_pairs_kernel(same, other, *outs):
    for off in range(4):
        outs[off][...] = (same[off].astype(F32) + other[off].astype(F32)).astype(BF)


def add_pairs(same, other):
    return pl.pallas_call(
        add_pairs_kernel,
        out_shape=[jax.ShapeDtypeStruct(same.shape[1:], BF)] * 4,
        in_specs=[vmem()] * 2,
        out_specs=[vmem()] * 4,
        compiler_params=params(),
        cost_estimate=cost(2e9, 4e6),
        name="add_pairs",
    )(same, other)


def stage_sum_kernel(idx, *refs):
    outs = refs[8:12]
    (total,) = refs[12:13]
    gate_rows = D // 16
    down_rows = FE // 16
    for n in range(LOCAL):
        parts = refs[:4] if n < HALF else refs[4:8]
        acc = parts[0][n % HALF].astype(F32)
        for part in parts[1:]:
            acc = acc + part[n % HALF].astype(F32)
        total[...] = acc.astype(BF)
        for k in range(4):
            at = (idx[12] + k) % 4
            start = pl.multiple_of(at * gate_rows, gate_rows)
            outs[k][n, :gate_rows, :] = total[pl.ds(start, gate_rows), :]
            start = pl.multiple_of(D // 4 + at * down_rows, down_rows)
            outs[k][n, gate_rows:, :] = total[pl.ds(start, down_rows), :]


def stage_sum(idx, parts):
    shapes = [jax.ShapeDtypeStruct((LOCAL, QROWS, FE), BF)] * 4
    grid_spec = pltpu.PrefetchScalarGridSpec(
        num_scalar_prefetch=1,
        grid=(1,),
        in_specs=[full(item.shape) for item in parts],
        out_specs=[full(item.shape) for item in shapes],
        scratch_shapes=[pltpu.VMEM((XROWS, FE), BF)],
    )
    return pl.pallas_call(
        stage_sum_kernel,
        grid_spec=grid_spec,
        out_shape=shapes,
        compiler_params=params(),
        cost_estimate=cost(5e9, 4e6),
        name="stage_sum",
    )(idx, *parts)


def finish_kernel(idx, *refs):
    xs = refs[0:4]
    z_parts = refs[4]
    keep_gate, keep_up, keep_down, send = refs[5:9]
    x_sum, z_sum = refs[9:11]
    big = D // 16
    small = big // 2
    tiny = FE // 32
    for n in range(LOCAL):
        acc = xs[0][n].astype(F32)
        for part in xs[1:]:
            acc = acc + part[n].astype(F32)
        x_sum[n] = acc
        z_sum[n] = z_parts[n].astype(F32)
    mine = idx[9]
    theirs = 1 - mine
    for n in range(LOCAL):
        here = pl.ds(pl.multiple_of(mine * small, small), small)
        there = pl.ds(pl.multiple_of(theirs * small, small), small)
        keep_gate[n] = x_sum[n, here, :]
        keep_up[n] = z_sum[n, here, :]
        send[n, :small, :] = x_sum[n, there, :].astype(BF)
        send[n, small:big, :] = z_sum[n, there, :].astype(BF)
        here = pl.ds(pl.multiple_of(big + mine * tiny, tiny), tiny)
        there = pl.ds(pl.multiple_of(big + theirs * tiny, tiny), tiny)
        keep_down[n, :, :FE] = x_sum[n, here, :]
        keep_down[n, :, FE:] = z_sum[n, here, :]
        send[n, big : big + tiny, :] = x_sum[n, there, :].astype(BF)
        send[n, big + tiny :, :] = z_sum[n, there, :].astype(BF)


def finish(idx, parts):
    shapes = [
        jax.ShapeDtypeStruct((LOCAL, D // 32, FE), F32),
        jax.ShapeDtypeStruct((LOCAL, D // 32, FE), F32),
        jax.ShapeDtypeStruct((LOCAL, FE // 32, D), F32),
        jax.ShapeDtypeStruct((LOCAL, QROWS, FE), BF),
    ]
    grid_spec = pltpu.PrefetchScalarGridSpec(
        num_scalar_prefetch=1,
        grid=(1,),
        in_specs=[full(item.shape) for item in parts],
        out_specs=[full(item.shape) for item in shapes],
        scratch_shapes=[pltpu.VMEM((LOCAL, QROWS, FE), F32)] * 2,
    )
    return pl.pallas_call(
        finish_kernel,
        grid_spec=grid_spec,
        out_shape=shapes,
        compiler_params=params(),
        cost_estimate=cost(3e9, 4e6),
        name="finish",
    )(idx, *parts)


def assemble_kernel(idx, keep_gate, keep_up, keep_down, got, out_gate, out_up, out_down):
    mine = pl.ds(idx[9] * LOCAL, LOCAL)
    theirs = pl.ds((1 - idx[9]) * LOCAL, LOCAL)
    small = D // 32
    tiny = FE // 32
    out_gate[mine] = keep_gate[...]
    out_up[mine] = keep_up[...]
    out_down[mine] = keep_down[...]
    out_gate[theirs] = got[:, :small, :].astype(F32)
    out_up[theirs] = got[:, small : 2 * small, :].astype(F32)
    out_down[theirs, :, :FE] = got[:, 2 * small : 2 * small + tiny, :].astype(F32)
    out_down[theirs, :, FE:] = got[:, 2 * small + tiny :, :].astype(F32)


def assemble(idx, keep_gate, keep_up, keep_down, got):
    shapes = [
        jax.ShapeDtypeStruct((2 * LOCAL, D // 32, FE), F32),
        jax.ShapeDtypeStruct((2 * LOCAL, D // 32, FE), F32),
        jax.ShapeDtypeStruct((2 * LOCAL, FE // 32, D), F32),
    ]
    parts = (keep_gate, keep_up, keep_down, got)
    grid_spec = pltpu.PrefetchScalarGridSpec(
        num_scalar_prefetch=1,
        grid=(1,),
        in_specs=[full(item.shape) for item in parts],
        out_specs=[full(item.shape) for item in shapes],
    )
    return pl.pallas_call(
        assemble_kernel,
        grid_spec=grid_spec,
        out_shape=shapes,
        compiler_params=params(),
        cost_estimate=cost(2e9, 4e6),
        name="assemble",
    )(idx, *parts)


def middle_kernel(*refs):
    parts = refs[:4]
    h_ref, gate_ref, dy_ref, gain_ref, w_router = refs[4:9]
    dh_ref, db_ref, side_ref = refs[9:12]
    total = parts[0][...].astype(F32)
    for part in parts[1:]:
        total = total + part[...].astype(F32)
    extra = total[:, D:]
    d_gate = extra + pltpu.roll(extra, 128 - EXPERTS, 1)
    gate = gate_ref[...]
    d_chosen = gate * (d_gate - jnp.sum(gate * d_gate, axis=1, keepdims=True))
    d_logits = d_chosen.astype(BF)
    d_mlp = total[:, :D] + mm_nt(d_logits, w_router[...])
    h = h_ref[...]
    gain = gain_ref[...].astype(F32)
    scale = lax.rsqrt(jnp.mean(h * h, axis=1, keepdims=True) + EPS)
    normed = h * scale
    mlp_in = (normed * gain).astype(BF)
    scaled = d_mlp * gain
    d_h = (
        dy_ref[...].astype(F32)
        + scale * scaled
        - h * (scale * scale * scale) * jnp.mean(scaled * h, axis=1, keepdims=True)
    )
    dh_ref[...] = d_h
    db_ref[...] = d_h.astype(BF)
    router = mm_tn(mlp_in, d_logits)
    d_gain = jnp.sum(d_mlp * normed, axis=0, keepdims=True)
    column = jnp.transpose(jnp.broadcast_to(d_gain, (128, D)))
    lane = lax.broadcasted_iota(jnp.int32, (D, 128), 1)
    side_ref[...] = jnp.where(lane == GAIN_LANE, column, router).astype(BF)


def middle(parts, h_own, gate_own, dy, gain, w_router):
    return pl.pallas_call(
        middle_kernel,
        out_shape=[
            jax.ShapeDtypeStruct((ROWS, D), F32),
            jax.ShapeDtypeStruct((ROWS, D), BF),
            jax.ShapeDtypeStruct((D, 128), BF),
        ],
        in_specs=[vmem()] * 9,
        out_specs=[vmem()] * 3,
        compiler_params=params(),
        cost_estimate=cost(1e8, 4e6),
        name="middle",
    )(*parts, h_own, gate_own, dy, gain, w_router)


def attend_back_kernel(idx, *refs):
    dbs = refs[:8]
    w_out, p_ref, q_ref, k_ref, v_ref, attn_in, ao_all, side, cos_ref, sin_ref = refs[8:18]
    dqkv_ref = refs[18]
    xp = refs[19:23]
    zp = refs[23:27]
    db_all, d_attn, dk_acc, dv_acc, whole = refs[27:32]
    for r in range(BLOCKS):
        rows = pl.ds(pl.multiple_of(idx[r] * ROWS, ROWS), ROWS)
        db_all[rows, :] = dbs[r][...]
    d_attn[...] = mm_nt(db_all[...], w_out[...]).astype(BF)
    dk_acc[...] = jnp.zeros((LEN, HD), F32)
    dv_acc[...] = jnp.zeros((LEN, HD), F32)
    quarter = D // 4
    small = quarter // 4
    own = pl.ds(pl.multiple_of(idx[8] * 128, 128), 128)
    whole[:, :128] = mm_tn(ao_all[...], db_all[:, own]).astype(BF)
    whole[:, 128:] = side[...]
    for k in range(4):
        at = (idx[12] + k) % 4
        for x in range(4):
            start = pl.multiple_of(x * quarter + at * small, small)
            zp[k][x * small : (x + 1) * small, :] = whole[pl.ds(start, small), :]
    for i in range(BLOCKS):
        lo = max(0, i - WIN // ROWS) * ROWS
        hi = (i + 1) * ROWS
        span = hi - lo
        rows = slice(i * ROWS, hi)
        do2 = jnp.concatenate([d_attn[rows, :HD], d_attn[rows, HD:]], axis=0)
        q2 = jnp.concatenate([q_ref[rows, :HD], q_ref[rows, HD:]], axis=0)
        probs_low = p_ref[i, :, :span]
        probs = probs_low.astype(F32)
        d_probs = mm_nt(do2, v_ref[lo:hi, :])
        weighted = probs * d_probs
        d_scores = (
            weighted - probs * jnp.sum(weighted, axis=1, keepdims=True)
        ).astype(BF)
        dq = mm(d_scores, k_ref[lo:hi, :]) * HD**-0.5
        dk_acc[lo:hi, :] += mm_tn(d_scores, q2)
        dv_acc[lo:hi, :] += mm_tn(probs_low, do2)
        dq = jnp.concatenate([dq[:ROWS], dq[ROWS:]], axis=1).astype(BF).astype(F32)
        dq = dq * cos_ref[rows, :] - swap_halves(dq) * sin_ref[rows, :]
        dqkv_ref[rows, : 2 * HD] = dq.astype(BF)
    pair = jnp.concatenate([dk_acc[...], dv_acc[...]], axis=1).astype(BF).astype(F32)
    turned = pair * cos_ref[...] - swap_halves(pair) * sin_ref[...]
    lane = lax.broadcasted_iota(jnp.int32, pair.shape, 1)
    dqkv_ref[:, 2 * HD :] = jnp.where(lane < HD, turned, pair).astype(BF)
    whole[...] = mm_tn(attn_in[...], dqkv_ref[...]).astype(BF)
    for k in range(4):
        at = (idx[11] + k) % 4
        xp[k][...] = whole[pl.ds(pl.multiple_of(at * quarter, quarter), quarter), :]


def attend_back(idx, dbs, w_out, p, q, k, v, attn_in, ao_all, side, cos_tab, sin_tab):
    span = WIN + ROWS
    shapes = [jax.ShapeDtypeStruct((LEN, 256), BF)] + [jax.ShapeDtypeStruct((D // 4, 256), BF)] * 8
    grid_spec = pltpu.PrefetchScalarGridSpec(
        num_scalar_prefetch=1,
        grid=(1,),
        in_specs=[full((ROWS, D))] * 8
        + [
            pl.BlockSpec((128, D), lambda i, s: (s[8], 0)),
            full((BLOCKS, 2 * ROWS, span)),
            full((LEN, 2 * HD)),
            full((LEN, HD)),
            full((LEN, HD)),
            full((LEN, D)),
            full((LEN, D)),
            full((D, 128)),
            full((LEN, 128)),
            full((LEN, 128)),
        ],
        out_specs=[full(s.shape) for s in shapes],
        scratch_shapes=[
            pltpu.VMEM((LEN, D), BF),
            pltpu.VMEM((LEN, 2 * HD), BF),
            pltpu.VMEM((LEN, HD), F32),
            pltpu.VMEM((LEN, HD), F32),
            pltpu.VMEM((D, 256), BF),
        ],
    )
    return pl.pallas_call(
        attend_back_kernel,
        grid_spec=grid_spec,
        out_shape=shapes,
        compiler_params=params(),
        cost_estimate=cost(1.3e10, 1.5e7),
        name="attend_back",
    )(idx, *dbs, w_out, p, q, k, v, attn_in, ao_all, side, cos_tab, sin_tab)


def input_grad_kernel(dqkv, x_ref, dh_ref, gain_ref, w_query, w_key, w_value, out_ref, dq, dk, dv):
    for b in range(BLOCKS):
        dq[:, b * 128 : (b + 1) * 128] = dqkv[b, :, :128]
    for b in range(0, BLOCKS, 2):
        first = dqkv[b, :, 128:].astype(F32)
        second = dqkv[b + 1, :, 128:].astype(F32)
        cols = slice(b * HD, (b + 2) * HD)
        dk[:, cols] = jnp.concatenate([first[:, :HD], second[:, :HD]], axis=1).astype(BF)
        dv[:, cols] = jnp.concatenate([first[:, HD:], second[:, HD:]], axis=1).astype(BF)
    d_in = mm_nt(dq[...], w_query[...]) + mm_nt(dk[...], w_key[...]) + mm_nt(dv[...], w_value[...])
    x = x_ref[...].astype(F32)
    scale = lax.rsqrt(jnp.mean(x * x, axis=1, keepdims=True) + EPS)
    scaled = d_in * gain_ref[...].astype(F32)
    out_ref[...] = (
        dh_ref[...]
        + scale * scaled
        - x * (scale * scale * scale) * jnp.mean(scaled * x, axis=1, keepdims=True)
    ).astype(BF)


def input_grad(dqkv, x, d_h, gain, w_query, w_key, w_value):
    return pl.pallas_call(
        input_grad_kernel,
        out_shape=jax.ShapeDtypeStruct((ROWS, D), BF),
        in_specs=[vmem()] * 7,
        out_specs=vmem(),
        scratch_shapes=[
            pltpu.VMEM((ROWS, H * HD), BF),
            pltpu.VMEM((ROWS, KVH * HD), BF),
            pltpu.VMEM((ROWS, KVH * HD), BF),
        ],
        compiler_params=params(),
        cost_estimate=cost(6e8, 6e6),
        name="input_grad",
    )(dqkv, x, d_h, gain, w_query, w_key, w_value)


def dense_sum_kernel(axis_slot, idx, *refs):
    parts = refs[:4]
    outs = refs[4:8]
    (total,) = refs[8:9]
    acc = parts[0][...].astype(F32)
    for part in parts[1:]:
        acc = acc + part[...].astype(F32)
    total[...] = acc.astype(BF)
    rows = D // 16
    for k in range(4):
        at = (idx[axis_slot] + k) % 4
        outs[k][...] = total[pl.ds(pl.multiple_of(at * rows, rows), rows), :]


def dense_sum(axis_slot, idx, parts):
    shapes = [jax.ShapeDtypeStruct((D // 16, 256), BF)] * 4
    grid_spec = pltpu.PrefetchScalarGridSpec(
        num_scalar_prefetch=1,
        grid=(1,),
        in_specs=[full(item.shape) for item in parts],
        out_specs=[full(item.shape) for item in shapes],
        scratch_shapes=[pltpu.VMEM((D // 4, 256), BF)],
    )
    return pl.pallas_call(
        functools.partial(dense_sum_kernel, axis_slot),
        grid_spec=grid_spec,
        out_shape=shapes,
        compiler_params=params(),
        cost_estimate=cost(1e9, 1e6),
        name="dense_sum",
    )(idx, *parts)


def dense_total_kernel(*refs):
    out = refs[8]
    for half in range(2):
        parts = refs[half * 4 : half * 4 + 4]
        acc = parts[0][...].astype(F32)
        for part in parts[1:]:
            acc = acc + part[...].astype(F32)
        out[:, half * 256 : (half + 1) * 256] = acc


def dense_total(parts):
    return pl.pallas_call(
        dense_total_kernel,
        out_shape=jax.ShapeDtypeStruct((D // 16, 512), F32),
        in_specs=[vmem()] * 8,
        out_specs=vmem(),
        compiler_params=params(),
        cost_estimate=cost(1e9, 1e6),
        name="dense_total",
    )(*parts)


def dense_out_kernel(idx, dense, w_query, w_key, w_value, gain, dq, dk, dv, do, router, gains):
    for b in range(BLOCKS):
        dq[:, b * 128 : (b + 1) * 128] = dense[b, :, :128]
        do[:, b * 128 : (b + 1) * 128] = dense[b, :, 256:384]
    for b in range(0, BLOCKS, 2):
        first = dense[b, :, 128:256]
        second = dense[b + 1, :, 128:256]
        cols = slice(b * HD, (b + 2) * HD)
        dk[:, cols] = jnp.concatenate([first[:, :HD], second[:, :HD]], axis=1)
        dv[:, cols] = jnp.concatenate([first[:, HD:], second[:, HD:]], axis=1)
    side = dense[0, :, 384:]
    for b in range(1, BLOCKS):
        side = side + dense[b, :, 384:]
    router[...] = side
    odd = idx[8] % 2 == 1
    total = jnp.zeros((8, 1), F32)
    for weight, grad in ((w_query, dq), (w_key, dk), (w_value, dv)):
        wide = weight[...].astype(F32)
        rows = jnp.where(odd, wide[8:], wide[:8])
        total = total + jnp.sum(rows * grad[...], axis=1, keepdims=True)
    gains[...] = jnp.broadcast_to(total / gain[...], (8, 128))


def dense_out(idx, dense, w_query, w_key, w_value, gain_col):
    shapes = [
        jax.ShapeDtypeStruct((8, H * HD), F32),
        jax.ShapeDtypeStruct((8, KVH * HD), F32),
        jax.ShapeDtypeStruct((8, KVH * HD), F32),
        jax.ShapeDtypeStruct((8, D), F32),
        jax.ShapeDtypeStruct((8, 128), F32),
        jax.ShapeDtypeStruct((8, 128), F32),
    ]

    def pair_rows(width):
        return pl.BlockSpec((16, width), lambda i, s: ((s[11] * 4 + s[12]) * 4 + s[8] // 2, 0))

    grid_spec = pltpu.PrefetchScalarGridSpec(
        num_scalar_prefetch=1,
        grid=(1,),
        in_specs=[
            full(dense.shape),
            pair_rows(H * HD),
            pair_rows(KVH * HD),
            pair_rows(KVH * HD),
            pl.BlockSpec((8, 1), lambda i, s: ((s[11] * 4 + s[12]) * 8 + s[8], 0)),
        ],
        out_specs=[full(item.shape) for item in shapes],
    )
    return pl.pallas_call(
        dense_out_kernel,
        grid_spec=grid_spec,
        out_shape=shapes,
        compiler_params=params(),
        cost_estimate=cost(1e9, 1e6),
        name="dense_out",
    )(idx, dense, w_query, w_key, w_value, gain_col)


def from_x(value, off):
    size = lax.axis_size("x")
    return lax.ppermute(value, "x", [(i, (i + off) % size) for i in range(size)])


def from_z(value, off):
    size = lax.axis_size("z")
    return lax.ppermute(value, "z", [(i, (i + off) % size) for i in range(size)])


def along_y(value, off):
    route = []
    for y in range(4):
        to = (y + off) % 4
        route.append(((y % 2) * 2 + y // 2, (to % 2) * 2 + to // 2))
    return lax.ppermute(value, ("yl", "yh"), route)


def other_core(value):
    return lax.ppermute(value, "c", [(0, 1), (1, 0)])


def near_ring(value):
    return [value] + [along_y(value, -off) for off in (1, 2, 3)]


def both_cores(near):
    far = [other_core(item) for item in near]
    return [item for pair in zip(near, far) for item in pair]


def gather_ring(value):
    return both_cores(near_ring(value))


def reduce_ring(pieces):
    return [pieces[0]] + [along_y(pieces[off], off) for off in (1, 2, 3)]


def scatter_parts(parts, send):
    return [parts[0]] + [send(parts[k], k) for k in (1, 2, 3)]


def after(values, *earlier):
    return lax.optimization_barrier((values, earlier))[0]


def local(
    tokens,
    segments,
    routes,
    drop_order,
    gain_attn,
    w_query,
    w_key,
    w_value,
    w_out,
    gain_mlp,
    w_router,
    w_gate,
    w_up,
    w_down,
    cotangent,
):
    x_at = lax.axis_index("x")
    z_at = lax.axis_index("z")
    yl = lax.axis_index("yl")
    yh = lax.axis_index("yh")
    core = lax.axis_index("c")
    y_at = yh * 2 + yl
    own = yl * 4 + yh * 2 + core
    expert_at = yh * 2 + core

    entries = []
    for off in range(4):
        y = (y_at + off) % 4
        for dc in range(2):
            entries.append((y % 2) * 4 + (y // 2) * 2 + (core + dc) % 2)
    entries += [own, yl, expert_at, x_at, z_at, y_at, core, expert_at * 8 + yl * LOCAL]
    idx = jnp.stack([jnp.asarray(entry, jnp.int32) for entry in entries])

    cos_np, sin_np = rotary_tables()
    cos_tab = jnp.asarray(cos_np)
    sin_tab = jnp.asarray(sin_np)
    gain_one = gain_attn.astype(F32).reshape(1, D)
    gain_two = gain_mlp.astype(F32).reshape(1, D)
    gain_col = gain_attn.astype(F32).reshape(D, 1)
    router_pad = jnp.pad(w_router, ((0, 0), (0, 128 - EXPERTS)))

    xs = gather_ring(tokens)
    meta = slots(routes.T, drop_order, segments.reshape(1, ROWS))
    meta_all = lax.all_gather(meta, GROUP, axis=0, tiled=True)
    dy_near = near_ring(after(cotangent, *xs, meta_all))

    attn_in, q, k, v, p, ao = attend(
        idx, xs, meta_all, gain_one, w_query, w_key, w_value, cos_tab, sin_tab
    )
    dys = both_cores(dy_near)
    aos = gather_ring(after(ao, *dy_near))
    mlp_in, slot_t, gate_t, h_own, gate_own, ao_all = project(
        idx, xs, aos, meta_all, w_out, gain_two, router_pad
    )
    expert_args = (idx, mlp_in, dys, slot_t, gate_t, w_gate, w_up, w_down)
    call_a = experts(0, *expert_args)
    hot_a, gated_a, outs_a, dslots_a = call_a[:4]
    pieces_a = call_a[4:8]
    z_half_a = lax.psum_scatter(call_a[8], "z", scatter_dimension=0, tiled=True)
    x_near_a = [from_x(pieces_a[1], 1), from_x(pieces_a[3], 3)]
    call_b = experts(HALF, *expert_args, before=(hot_a, dslots_a))
    rows, act, d_out, d_gh, d_up, gated_b, outs_b, dm_same, dm_other = call_b

    dm_pieces = add_pairs(dm_same, other_core(dm_other))
    dm_parts = reduce_ring(dm_pieces)
    x_far_a = from_x(after(pieces_a[2], *x_near_a, *dm_pieces), 2)
    call_grads = expert_grads(idx, after(rows, *dm_pieces), act, d_out, d_gh, d_up)
    pieces_b = call_grads[:4]
    z_half_b = lax.psum_scatter(call_grads[4], "z", scatter_dimension=0, tiled=True)
    d_h, d_branch, side = middle(
        after(dm_parts, pieces_b[0]), h_own, gate_own, cotangent, gain_two, router_pad
    )
    db_near = near_ring(d_branch)
    x_near_b = [from_x(after(pieces_b[k], x_far_a, d_branch), k) for k in (1, 3)]
    dbs = both_cores(db_near)

    mx_same, mx_other = mixed_sum(idx, gated_a, gated_b, after(outs_a, d_branch), outs_b)
    mx_pieces = add_pairs(mx_same, other_core(mx_other))
    mx_parts = reduce_ring(after(mx_pieces, *db_near))

    back = attend_back(
        idx, after(dbs, *mx_pieces), w_out, p, q, k, v, attn_in, ao_all, side, cos_tab, sin_tab
    )
    x_far_b = from_x(after(pieces_b[2], *x_near_b), 2)
    x_dense = scatter_parts(back[1:5], from_x)
    z_dense = scatter_parts(back[5:9], from_z)
    dqkv = lax.all_to_all(
        back[0].reshape(BLOCKS, ROWS, 256), GROUP, split_axis=0, concat_axis=0, tiled=True
    )
    d_tokens = input_grad(dqkv, tokens, d_h, gain_one, w_query, w_key, w_value)
    total = h_own
    for part in mx_parts:
        total = total + part.astype(F32)
    block_out = total.astype(BF)

    x_first = [pieces_a[0], x_near_a[0], x_far_a, x_near_a[1]]
    x_first += [pieces_b[0], x_near_b[0], x_far_b, x_near_b[1]]
    x_second = scatter_parts(stage_sum(idx, after(x_first, back[0])), from_z)
    z_half = jnp.concatenate([z_half_a[0], z_half_b[0]], axis=1)
    z_second = lax.psum_scatter(z_half, "x", scatter_dimension=0, tiled=True)[0]
    keep_gate, keep_up, keep_down, sent = finish(idx, x_second + [z_second])
    got = lax.ppermute(sent, "yl", [(0, 1), (1, 0)])
    d_w_gate, d_w_up, d_w_down = assemble(idx, keep_gate, keep_up, keep_down, got)

    x_dense = scatter_parts(dense_sum(12, idx, x_dense), from_z)
    z_dense = scatter_parts(dense_sum(11, idx, z_dense), from_x)
    dense = dense_total(x_dense + z_dense).reshape(BLOCKS, 8, 512)
    dense = lax.all_to_all(dense, GROUP, split_axis=0, concat_axis=0, tiled=True)
    d_w_query, d_w_key, d_w_value, d_w_out, routed, gains = dense_out(
        idx, dense, w_query, w_key, w_value, gain_col
    )
    d_w_router = routed[:, :EXPERTS]
    d_gain_mlp = routed[:, GAIN_LANE]
    d_gain_attn = gains[:, 0]

    return (
        block_out,
        d_tokens,
        d_gain_attn,
        d_w_query,
        d_w_key,
        d_w_value,
        d_w_out,
        d_gain_mlp,
        d_w_router,
        d_w_gate,
        d_w_up,
        d_w_down,
    )


def solution(mesh):
    side = 4 if mesh.shape["dp"] == 32 else 1
    names = ("x", "z", "yl", "yh", "c")
    grid = Mesh(mesh.devices.reshape(side, side, 2, 2, 2), names)
    tokens = names
    experts_axes = ("yh", "c")
    dp = ("x", "z", "yl")
    in_specs = (
        P(tokens, None),
        P(tokens),
        P(tokens, None),
        P(tokens, None),
        P(),
        P(),
        P(),
        P(),
        P(),
        P(),
        P(),
        P(experts_axes, None, None),
        P(experts_axes, None, None),
        P(experts_axes, None, None),
        P(tokens, None),
    )
    out_specs = (
        P(tokens, None),
        P(tokens, None),
        P(tokens),
        P(tokens, None),
        P(tokens, None),
        P(tokens, None),
        P(tokens, None),
        P(tokens),
        P(tokens, None),
        P(experts_axes, dp, None),
        P(experts_axes, dp, None),
        P(experts_axes, dp, None),
    )
    return jax.shard_map(local, mesh=grid, in_specs=in_specs, out_specs=out_specs, check_vma=False)
```

```python
import functools

import jax
import jax.numpy as jnp
import numpy as np
from jax import lax
from jax.experimental import pallas as pl
from jax.experimental.pallas import tpu as pltpu
from jax.sharding import Mesh, PartitionSpec as P

H = 16
KVH = 8
HD = 64
D = 1024
FE = 512
TOPK = 8
EXPERTS = 32
CAP = 36
ROWS = 128
LEN = 1024
BLOCKS = LEN // ROWS
WIN = 512
LOCAL = 4
PAIRS = BLOCKS // 2
SLOTS = 80
EROWS = PAIRS * SLOTS
AUG = D + 128
GAIN_LANE = 32
FAR_LIMIT = 56
SHARE = 0.1
EPS = 1e-06
THETA = 10000.0
NEG = -1e30
BF = jnp.bfloat16
F32 = jnp.float32
GROUP = ("yl", "yh", "c")


def mm(left, right):
    return jnp.dot(left, right, preferred_element_type=F32)


def mm_nt(left, right):
    return lax.dot_general(left, right, (((1,), (1,)), ((), ())), preferred_element_type=F32)


def mm_tn(left, right):
    return lax.dot_general(left, right, (((0,), (0,)), ((), ())), preferred_element_type=F32)


def rotary_tables():
    half = HD // 2
    frequency = THETA ** (-np.arange(half, dtype=np.float64) * 2.0 / HD)
    angles = np.arange(LEN, dtype=np.float64)[:, None] * frequency[None, :]
    cosine = np.cos(angles)
    sine = np.sin(angles)
    cos_full = np.concatenate([cosine] * 4, axis=1).astype(np.float32)
    sin_full = np.concatenate([-sine, sine, -sine, sine], axis=1).astype(np.float32)
    return cos_full, sin_full


def swap_halves(array_in):
    half = HD // 2
    lane = lax.broadcasted_iota(jnp.int32, array_in.shape, 1)
    ahead = pltpu.roll(array_in, array_in.shape[1] - half, 1)
    behind = pltpu.roll(array_in, half, 1)
    return jnp.where(lane % HD < half, ahead, behind)


def vmem(*shape, dtype=BF):
    return pltpu.VMEM(shape, dtype)


def hbm(*shape, dtype=BF):
    return pltpu.HBM(shape, dtype)


def auto(*shape, dtype=BF):
    return jax.ShapeDtypeStruct(shape, dtype)


def cost(micros):
    return pl.CostEstimate(
        flops=int(micros * 1.15e9 * SHARE), bytes_accessed=int(micros * 1e6), transcendentals=0
    )


def run(
    kernel,
    name,
    micros,
    ins,
    outs,
    scratch=(),
    far_in=0,
    far_out=0,
    limit=24,
    idx=None,
):
    inside = pl.BlockSpec(memory_space=pltpu.VMEM)
    outside = pl.BlockSpec(memory_space=pltpu.HBM)
    in_specs = [inside] * (len(ins) - far_in) + [outside] * far_in
    operands = list(ins)
    if idx is not None:
        in_specs = [pl.BlockSpec(memory_space=pltpu.SMEM)] + in_specs
        operands = [idx] + operands
    return pl.pallas_call(
        kernel,
        out_shape=list(outs),
        in_specs=in_specs,
        out_specs=[inside] * (len(outs) - far_out) + [outside] * far_out,
        scratch_shapes=list(scratch),
        compiler_params=pltpu.CompilerParams(vmem_limit_bytes=limit * 1024 * 1024),
        cost_estimate=cost(micros),
        name=name,
    )(*operands)


def run_far(kernel, name, micros, ins, outs, scratch=(), idx=None):
    count = len(ins)
    given = 0 if idx is None else 1

    def body(*refs):
        lead = refs[:given]
        sources = refs[given : given + count]
        targets = refs[given + count : given + count + len(outs)]
        rest = refs[given + count + len(outs) :]
        in_bufs = rest[:count]
        out_bufs = rest[count : count + len(outs)]
        in_sems, out_sems = rest[count + len(outs) : count + len(outs) + 2]
        for copy in fetch(sources, in_bufs, in_sems):
            copy.wait()
        kernel(*lead, *in_bufs, *out_bufs, *rest[count + len(outs) + 2 :])
        for copy in fetch(out_bufs, targets, out_sems):
            copy.wait()

    bufs = [pltpu.VMEM(item.shape, item.dtype) for item in ins]
    bufs += [pltpu.VMEM(item.shape, item.dtype) for item in outs]
    bufs += [pltpu.SemaphoreType.DMA((count,)), pltpu.SemaphoreType.DMA((len(outs),))]
    return run(
        body,
        name,
        micros,
        ins,
        outs,
        bufs + list(scratch),
        far_in=count,
        far_out=len(outs),
        limit=FAR_LIMIT,
        idx=idx,
    )


def fetch(sources, targets, sems):
    copies = [
        pltpu.make_async_copy(source, target, sems.at[n])
        for n, (source, target) in enumerate(zip(sources, targets))
    ]
    for copy in copies:
        copy.start()
    return copies


def slots_kernel(routes_ref, order_ref, meta_ref, place_ref):
    order = order_ref[...]
    index = lax.broadcasted_iota(jnp.int32, (1, ROWS * TOPK), 1)
    token_of = order // TOPK
    choice_of = order - token_of * TOPK
    at_token = (token_of == lax.broadcasted_iota(jnp.int32, (ROWS, ROWS * TOPK), 0)).astype(F32)
    choice = lax.broadcasted_iota(jnp.int32, (2 * TOPK, ROWS * TOPK), 0)
    high = index // 32
    low = index - high * 32
    part = jnp.where(choice < TOPK, high, low).astype(F32)
    choice_mod = jnp.where(choice < TOPK, choice, choice - TOPK)
    table = jnp.where(choice_mod == choice_of, part, 0.0)
    found = mm_nt(at_token.astype(BF), table.astype(BF))
    place = found[:, :TOPK] * 32.0 + found[:, TOPK:]
    lane = lax.broadcasted_iota(jnp.int32, (ROWS, 128), 1)
    wide = jnp.concatenate(
        [
            routes_ref[...].astype(F32),
            jnp.zeros((ROWS - TOPK, ROWS), F32),
        ],
        axis=0,
    )
    turned = jnp.transpose(wide)
    lane_f = lane.astype(F32)
    placed = jnp.full((ROWS, 128), 4096.0, F32)
    for k in range(TOPK):
        placed = jnp.where(turned[:, k : k + 1] == lane_f, place[:, k : k + 1], placed)
    place_ref[...] = placed

    def count(step, total):
        for inner in range(8):
            row = place_ref[pl.ds(step * 8 + inner, 1), :]
            total = total + jnp.where(row < placed, 1.0, 0.0)
        return total

    rank = lax.fori_loop(0, ROWS // 8, count, jnp.zeros((ROWS, 128), F32))
    slot = jnp.where(placed < 4000.0, jnp.where(rank < CAP, rank, -1.0), -2.0)
    meta_ref[...] = slot.astype(BF)


def slots(routes_t, drop_order):
    return run(
        slots_kernel,
        "slots",
        3,
        [routes_t, drop_order],
        [auto(ROWS, 128)],
        [pltpu.VMEM((ROWS, 128), F32)],
        limit=8,
    )[0]


def attend_kernel(idx, *refs):
    xs = refs[:8]
    slots_ref, gain, wq, wk, wv, cos_ref, sin_ref = refs[8:15]
    out_ref = refs[15]
    far = refs[16:21]
    attn_in, q_ref, k_ref, v_ref, p_ref, seg_row, seg_col, sems = refs[21:29]
    near = (attn_in, q_ref, k_ref, v_ref)
    copies = [pltpu.make_async_copy(near[n], far[n], sems.at[n]) for n in range(4)]
    gain_full = gain[...]
    for r in range(BLOCKS):
        rows = pl.ds(pl.multiple_of(idx[r] * ROWS, ROWS), ROWS)
        x = xs[r][:, :D].astype(F32)
        scale = lax.rsqrt(jnp.mean(x * x, axis=1, keepdims=True) + EPS)
        attn_in[rows, :] = (x * scale * gain_full).astype(BF)
        segs = xs[r][:, D:].astype(F32)
        seg_col[rows, :] = segs
        seg_row[:, rows] = jnp.transpose(segs)[:8, :]
    copies[0].start()
    out_ref[LEN:, :] = slots_ref[...]
    odd = (idx[8] % 2) == 1
    half = LEN // 2
    for part in range(2):
        rows = slice(part * half, (part + 1) * half)
        block = attn_in[rows, :]
        cosine = cos_ref[rows, :]
        sine = sin_ref[rows, :]
        q = mm(block, wq[...])
        q = q * cosine + swap_halves(q) * sine
        q_ref[rows, :] = (q.astype(BF).astype(F32) * HD**-0.5).astype(BF)
        k = mm(block, wk[...])
        k = jnp.where(odd, pltpu.roll(k, HD, 1), k)
        k = k * cosine + swap_halves(k) * sine
        k_ref[rows, :] = k[:, :HD].astype(BF)
        v = mm(block, wv[...])
        v = jnp.where(odd, pltpu.roll(v, HD, 1), v)
        v_ref[rows, :] = v[:, :HD].astype(BF)
    for copy in copies[1:]:
        copy.start()
    for i in range(BLOCKS):
        lo = max(0, i - WIN // ROWS) * ROWS
        hi = (i + 1) * ROWS
        span = hi - lo
        rows = slice(i * ROWS, hi)
        q2 = jnp.concatenate([q_ref[rows, :HD], q_ref[rows, HD:]], axis=0)
        scores = mm_nt(q2, k_ref[lo:hi, :])
        q_pos = i * ROWS + lax.broadcasted_iota(jnp.int32, (ROWS, span), 0)
        k_pos = lo + lax.broadcasted_iota(jnp.int32, (ROWS, span), 1)
        allowed = (k_pos <= q_pos) & (k_pos > q_pos - WIN)
        allowed = allowed & (seg_row[0:1, lo:hi] == seg_col[rows, 0:1])
        bias = jnp.where(allowed, 0.0, NEG)
        scores = scores + jnp.concatenate([bias, bias], axis=0)
        top = jnp.max(scores, axis=1, keepdims=True)
        expo = jnp.exp(scores - top)
        total = jnp.sum(expo, axis=1, keepdims=True)
        probs = (expo * (1.0 / total)).astype(BF)
        p_ref[i, :, :span] = probs
        if span < WIN + ROWS:
            p_ref[i, :, span:] = jnp.zeros((2 * ROWS, WIN + ROWS - span), BF)
        copy = pltpu.make_async_copy(p_ref.at[i], far[4].at[i], sems.at[4 + i])
        copy.start()
        copies.append(copy)
        out = mm(probs, v_ref[lo:hi, :])
        out_ref[rows, :] = jnp.concatenate([out[:ROWS], out[ROWS:]], axis=1).astype(BF)
    for copy in copies:
        copy.wait()


def attend(idx, xs, slot_own, gain, wq, wk, wv, cos_tab, sin_tab):
    shapes = [(LEN, D), (LEN, 2 * HD), (LEN, HD), (LEN, HD), (BLOCKS, 2 * ROWS, WIN + ROWS)]
    outs = [vmem(LEN + ROWS, 2 * HD)] + [hbm(*shape) for shape in shapes]
    scratch = [pltpu.VMEM(shape, BF) for shape in shapes]
    scratch += [pltpu.VMEM((8, LEN), F32), pltpu.VMEM((LEN, 128), F32)]
    scratch += [pltpu.SemaphoreType.DMA((4 + BLOCKS,))]
    ins = [*xs, slot_own, gain, wq, wk, wv, cos_tab, sin_tab]
    return run(attend_kernel, "attend", 7, ins, outs, scratch, far_out=5, limit=16, idx=idx)


def project_kernel(idx, *refs):
    xs = refs[:8]
    aos = refs[8:16]
    w_out, gain, router_t = refs[16:19]
    mlp_in, slot_t, gate_t, h_far, gate_far, ao_far = refs[19:25]
    ao_all, h_own, gate_own, sems = refs[25:29]
    for r in range(BLOCKS):
        cols = pl.ds(pl.multiple_of(idx[r] * ROWS, ROWS), ROWS)
        ao_all[:, cols] = aos[r][:LEN, :]
    ao_copy = pltpu.make_async_copy(ao_all, ao_far, sems.at[0])
    ao_copy.start()
    gain_full = gain[...]
    for p in range(PAIRS):
        rows = slice(p * 2 * ROWS, (p + 1) * 2 * ROWS)
        places = [pl.ds(pl.multiple_of(idx[2 * p + n] * ROWS, ROWS), ROWS) for n in range(2)]
        attended = jnp.concatenate([ao_all[place, :] for place in places], axis=0)
        x = jnp.concatenate([xs[2 * p + n][:, :D] for n in range(2)], axis=0).astype(F32)
        h = x + mm(attended, w_out[...])
        scale = lax.rsqrt(jnp.mean(h * h, axis=1, keepdims=True) + EPS)
        normed = (h * scale * gain_full).astype(BF)
        mlp_in[rows, :] = normed
        logits = mm_nt(normed, router_t[...])
        slot = jnp.concatenate([aos[2 * p + n][LEN:, :] for n in range(2)], axis=0).astype(F32)
        lane = lax.broadcasted_iota(jnp.int32, slot.shape, 1)
        routed = (slot > -1.5) & (lane < EXPERTS)
        logits = jnp.where(routed, logits, NEG)
        top = jnp.max(logits, axis=1, keepdims=True)
        expo = jnp.where(routed, jnp.exp(logits - top), 0.0)
        gate = expo / jnp.sum(expo, axis=1, keepdims=True)
        slot_t[:, rows] = jnp.transpose(slot)[:EXPERTS, :]
        gate_t[:, rows] = jnp.transpose(gate)[:EXPERTS, :]
        if p == 0:
            h_own[...] = h[:ROWS]
            gate_own[...] = gate[:ROWS]
            own_copies = [
                pltpu.make_async_copy(h_own, h_far, sems.at[1]),
                pltpu.make_async_copy(gate_own, gate_far, sems.at[2]),
            ]
            for copy in own_copies:
                copy.start()
    ao_copy.wait()
    for copy in own_copies:
        copy.wait()


def project(idx, xs, aos, w_out, gain, router_t):
    outs = [
        vmem(LEN, D),
        vmem(EXPERTS, LEN, dtype=F32),
        vmem(EXPERTS, LEN, dtype=F32),
        hbm(ROWS, D, dtype=F32),
        hbm(ROWS, 128, dtype=F32),
        hbm(LEN, D),
    ]
    scratch = [
        pltpu.VMEM((LEN, D), BF),
        pltpu.VMEM((ROWS, D), F32),
        pltpu.VMEM((ROWS, 128), F32),
        pltpu.SemaphoreType.DMA((3,)),
    ]
    ins = [*xs, *aos, w_out, gain, router_t]
    return run(project_kernel, "project", 5, ins, outs, scratch, far_out=3, limit=14, idx=idx)


PROWS = LOCAL * SLOTS
HALF = LOCAL // 2
LEFT = FE
XROWS = D // 4 + FE // 4 * (LEFT // FE)
QROWS = XROWS // 4
ZROWS = D // 16 + FE // 16 * ((D - LEFT) // FE)


def experts_kernel(idx, *refs):
    mlp_in = refs[0]
    dys = refs[1:9]
    slot_t, gate_t, w_gate, w_up, w_down = refs[9:14]
    rows_out, act_out, dout_out, du_out, dm_same, dm_other = refs[14:20]
    far = refs[20:26]
    wg_buf, wu_buf, wd_buf, sems, dy_rows, gate_col, hot, dslots = refs[26:34]
    dg_out, hot_gated, outs, far_sems = refs[34:38]
    kept = (rows_out, act_out, dout_out, dg_out, outs)
    stores = []

    def load(e):
        at = idx[9] * LOCAL + e
        group = []
        for n, (weight, buf) in enumerate(((w_gate, wg_buf), (w_up, wu_buf), (w_down, wd_buf))):
            copy = pltpu.make_async_copy(weight.at[at], buf.at[e % 2], sems.at[e % 2, n])
            copy.start()
            group.append(copy)
        return group

    loads = [load(0), load(1)]
    for p in range(PAIRS):
        cols = slice(p * 2 * ROWS, (p + 1) * 2 * ROWS)
        part = slice(p * SLOTS, (p + 1) * SLOTS)
        lane = lax.broadcasted_iota(jnp.int32, (1, 2 * ROWS), 1)
        lift = jnp.where(lane >= ROWS, float(CAP), 0.0)
        row_id = lax.broadcasted_iota(jnp.int32, (SLOTS, 2 * ROWS), 0).astype(F32)
        hots = []
        for n in range(LOCAL):
            slot = slot_t[pl.ds(idx[15] + n, 1), cols]
            gate = gate_t[pl.ds(idx[15] + n, 1), cols]
            place = jnp.where(slot > -0.5, slot + lift, -1.0)
            one = jnp.where(row_id == place, 1.0, 0.0)
            gated_one = one * gate
            gate_col[n, part, :] = jnp.sum(gated_one, axis=1, keepdims=True)
            hots.append(one.astype(BF))
            hot_gated[p, n * SLOTS : (n + 1) * SLOTS, :] = gated_one.astype(BF)
        hot_pair = jnp.concatenate(hots, axis=0)
        hot[p] = hot_pair
        taken = mm(hot_pair, mlp_in[cols, :]).astype(BF)
        dy = jnp.concatenate([dys[2 * p][...], dys[2 * p + 1][...]], axis=0)
        taken_dy = mm(hot_pair, dy).astype(BF)
        for n in range(LOCAL):
            rows_out[n, part, :] = taken[n * SLOTS : (n + 1) * SLOTS]
            dy_rows[n, part, :] = taken_dy[n * SLOTS : (n + 1) * SLOTS]
    hot_copy = pltpu.make_async_copy(hot_gated, far[5], far_sems.at[LOCAL, 0])
    hot_copy.start()
    stores.append(hot_copy)

    for e in range(LOCAL):
        for copy in loads[e]:
            copy.wait()
        rows = rows_out[e]
        wg = wg_buf[e % 2]
        wu = wu_buf[e % 2]
        wd = wd_buf[e % 2]
        gate_h = mm(rows, wg)
        up_h = mm(rows, wu)
        sig = 1.0 / (1.0 + jnp.exp(-gate_h))
        silu = gate_h * sig
        act = (silu * up_h).astype(BF)
        act_out[e] = act
        out = mm(act, wd).astype(BF)
        outs[e] = out
        dy = dy_rows[e].astype(F32)
        d_gate = jnp.sum(dy * out.astype(F32), axis=1, keepdims=True)
        d_out = (gate_col[e].astype(BF).astype(F32) * dy).astype(BF)
        dout_out[e] = d_out
        d_act = mm_nt(d_out, wd)
        d_up = (d_act * silu).astype(BF)
        d_gh = (d_act * up_h * sig * (1.0 + gate_h * (1.0 - sig))).astype(BF)
        dg_out[e] = d_gh
        du_out[e] = d_up
        dslots[e, :, :D] = (mm_nt(d_gh, wg) + mm_nt(d_up, wu)).astype(BF)
        lane = lax.broadcasted_iota(jnp.int32, (EROWS, 128), 1)
        d_high = d_gate.astype(BF).astype(F32)
        mine = idx[15] + e
        extra = jnp.where(lane == mine, d_high, 0.0)
        extra = jnp.where(lane == mine + EXPERTS, d_gate - d_high, extra)
        dslots[e, :, D:] = extra.astype(BF)
        for n, (buf, target) in enumerate(zip(kept, far)):
            copy = pltpu.make_async_copy(buf.at[e], target.at[e], far_sems.at[e, n])
            copy.start()
            stores.append(copy)
        if e + 2 < LOCAL:
            loads.append(load(e + 2))

    for p in range(PAIRS):
        part = slice(p * SLOTS, (p + 1) * SLOTS)
        grads = jnp.concatenate([dslots[n, part, :] for n in range(LOCAL)], axis=0)
        merged = mm_tn(hot[p], grads).astype(BF)
        dm_same[p] = merged[:ROWS]
        dm_other[p] = merged[ROWS:]
    for copy in stores:
        copy.wait()


def experts(idx, mlp_in, dys, slot_t, gate_t, w_gate, w_up, w_down):
    wide = (LOCAL, EROWS, D)
    narrow = (LOCAL, EROWS, FE)
    hot_shape = (PAIRS, PROWS, 2 * ROWS)
    outs = [vmem(*shape) for shape in (wide, narrow, wide, narrow)]
    outs += [vmem(4, ROWS, AUG)] * 2
    outs += [hbm(*shape) for shape in (wide, narrow, wide, narrow, wide, hot_shape)]
    scratch = [
        pltpu.VMEM((2, D, FE), BF),
        pltpu.VMEM((2, D, FE), BF),
        pltpu.VMEM((2, FE, D), BF),
        pltpu.SemaphoreType.DMA((2, 3)),
        pltpu.VMEM(wide, BF),
        pltpu.VMEM((LOCAL, EROWS, 1), F32),
        pltpu.VMEM(hot_shape, BF),
        pltpu.VMEM((LOCAL, EROWS, AUG), BF),
        pltpu.VMEM(narrow, BF),
        pltpu.VMEM(hot_shape, BF),
        pltpu.VMEM(wide, BF),
        pltpu.SemaphoreType.DMA((LOCAL + 1, 5)),
    ]
    ins = [mlp_in, *dys, slot_t, gate_t, w_gate, w_up, w_down]
    return run(
        experts_kernel,
        "experts",
        16,
        ins,
        outs,
        scratch,
        far_in=3,
        far_out=6,
        limit=32,
        idx=idx,
    )


def send_out(bufs, targets, sems):
    copies = [
        pltpu.make_async_copy(buf, target, sems.at[n])
        for n, (buf, target) in enumerate(zip(bufs, targets))
    ]
    for copy in copies:
        copy.start()
    for copy in copies:
        copy.wait()


def x_grads_kernel(idx, rows_far, act_far, dout_far, dg_far, *refs):
    far = refs[:5]
    bufs = refs[5:10]
    up, down, own, up_late, down_late = bufs
    rows, act, d_out, d_gh, whole, whole_down, in_sems, sems = refs[10:18]
    quarter = D // 4
    down_q = FE // 4
    loads = [
        fetch(
            [rows_far.at[e], act_far.at[e], dout_far.at[e], dg_far.at[e]],
            [rows.at[e], act.at[e], d_out.at[e], d_gh.at[e]],
            in_sems.at[e],
        )
        for e in range(LOCAL)
    ]

    def piece(k, target, e):
        at = (idx[11] + k) % 4
        start = pl.multiple_of(at * quarter, quarter)
        target[e, :quarter, :] = whole[pl.ds(start, quarter), :]
        start = pl.multiple_of(at * down_q, down_q)
        for n in range(LEFT // FE):
            to = quarter + n * down_q
            target[e, to : to + down_q, :] = whole_down[pl.ds(start, down_q), n * FE : (n + 1) * FE]

    for e in range(LOCAL):
        for copy in loads[e]:
            copy.wait()
        whole[...] = mm_tn(rows[e], d_gh[e]).astype(BF)
        whole_down[...] = mm_tn(act[e], d_out[e, :, :LEFT]).astype(BF)
        piece(0, own, e)
        if e < HALF:
            piece(2, up, e)
            piece(1, up_late, e)
            piece(3, down, e + HALF)
        else:
            piece(1, up, e)
            piece(2, down, e - HALF)
            piece(3, down_late, e - HALF)
    send_out(bufs, far, sems)


def x_grads(idx, rows, act, d_out, d_gh):
    whole = (LOCAL, XROWS, FE)
    half = (HALF, XROWS, FE)
    shapes = (whole, whole, whole, half, half)
    ins = [rows, act, d_out, d_gh]
    outs = [hbm(*shape) for shape in shapes]
    scratch = [pltpu.VMEM(shape, BF) for shape in shapes]
    scratch += [pltpu.VMEM(item.shape, BF) for item in ins]
    scratch += [
        pltpu.VMEM((D, FE), BF),
        pltpu.VMEM((FE, LEFT), BF),
        pltpu.SemaphoreType.DMA((LOCAL, 4)),
        pltpu.SemaphoreType.DMA((5,)),
    ]
    return run(
        x_grads_kernel,
        "x_grads",
        3,
        ins,
        outs,
        scratch,
        far_in=4,
        far_out=5,
        limit=FAR_LIMIT,
        idx=idx,
    )


def z_grads_kernel(rows, act, d_out, d_up, z_all, z_buf, sems):
    quarter = D // 4
    down_q = FE // 4
    small = quarter // 4
    small_down = down_q // 4
    copies = []
    for e in range(LOCAL):
        whole = mm_tn(rows[e], d_up[e]).astype(BF)
        if LEFT < D:
            whole_down = mm_tn(act[e], d_out[e, :, LEFT:]).astype(BF)
        for z in range(4):
            for x in range(4):
                start = x * quarter + z * small
                z_buf[e, z, x, :small, :] = whole[start : start + small]
                if LEFT < D:
                    start = x * down_q + z * small_down
                    z_buf[e, z, x, small:, :] = whole_down[start : start + small_down]
        copy = pltpu.make_async_copy(z_buf.at[e], z_all.at[:, :, e], sems.at[e])
        copy.start()
        copies.append(copy)
    for copy in copies:
        copy.wait()


def z_grads(rows, act, d_out, d_up):
    scratch = [pltpu.VMEM((LOCAL, 4, 4, ZROWS, FE), BF), pltpu.SemaphoreType.DMA((LOCAL,))]
    outs = [hbm(4, 4, LOCAL, ZROWS, FE)]
    return run(
        z_grads_kernel, "z_grads", 3, [rows, act, d_out, d_up], outs, scratch, far_out=1, limit=14
    )[0]


def relay_kernel(up_late, from_below, down_late, from_above, up, down):
    for e in range(HALF):
        up[e] = (up_late[e].astype(F32) + from_below[e].astype(F32)).astype(BF)
        down[e] = (down_late[e].astype(F32) + from_above[e].astype(F32)).astype(BF)


def relay(up_late, from_below, down_late, from_above):
    ins = [up_late, from_below, down_late, from_above]
    return run_far(relay_kernel, "relay", 0.3, ins, [hbm(*up_late.shape)] * 2)


def mixed_kernel(hot_gated, outs, same, other):
    for p in range(PAIRS):
        part = slice(p * SLOTS, (p + 1) * SLOTS)
        values = jnp.concatenate([outs[n, part, :] for n in range(LOCAL)], axis=0)
        merged = mm_tn(hot_gated[p], values).astype(BF)
        same[p] = merged[:ROWS]
        other[p] = merged[ROWS:]


def mixed_sum(hot_gated, outs):
    return run_far(mixed_kernel, "mixed_sum", 0.6, [hot_gated, outs], [hbm(4, ROWS, D)] * 2)


def add_pairs_kernel(same, other, *outs):
    for off in range(4):
        outs[off][...] = (same[off].astype(F32) + other[off].astype(F32)).astype(BF)


def add_pairs(same, other):
    return run(
        add_pairs_kernel, "add_pairs", 0.3, [same, other], [vmem(*same.shape[1:])] * 4, limit=4
    )


def add_pairs_out(same, other):
    def kernel(same_ref, other_ref, *refs):
        add_pairs_kernel(same_ref, other_ref, *refs[4:8])
        for copy in fetch(refs[4:8], refs[:4], refs[8]):
            copy.wait()

    shape = same.shape[1:]
    scratch = [pltpu.VMEM(shape, BF)] * 4 + [pltpu.SemaphoreType.DMA((4,))]
    outs = [hbm(*shape)] * 4
    return run(kernel, "add_pairs", 0.3, [same, other], outs, scratch, far_out=4, limit=6)


def add_pairs_far(same, other):
    return run_far(add_pairs_kernel, "add_pairs", 0.3, [same, other], [hbm(*same.shape[1:])] * 4)


def stage_sum_kernel(idx, *refs):
    far = refs[:5]
    outs_far = refs[5:9]
    bufs = refs[9:14]
    outs = refs[14:18]
    total, in_sems, out_sems = refs[18:21]
    own, from_below, from_above, late_below, late_above = range(5)
    gate_rows = D // 16
    down_rows = FE // 16
    loads = []
    for n in range(LOCAL):
        if n < HALF:
            needed = ((own, n), (late_below, n), (from_above, n + HALF))
        else:
            needed = ((own, n), (from_below, n), (late_above, n - HALF))
        sources = [far[item].at[at] for item, at in needed]
        targets = [bufs[item].at[at] for item, at in needed]
        loads.append((needed, fetch(sources, targets, in_sems.at[n])))
    stores = []
    for n in range(LOCAL):
        needed, copies = loads[n]
        for copy in copies:
            copy.wait()
        acc = sum(bufs[item][at].astype(F32) for item, at in needed)
        total[...] = acc.astype(BF)
        for k in range(4):
            at = (idx[12] + k) % 4
            start = pl.multiple_of(at * gate_rows, gate_rows)
            outs[k][n, :gate_rows, :] = total[pl.ds(start, gate_rows), :]
            for m in range(LEFT // FE):
                start = pl.multiple_of(D // 4 + m * (FE // 4) + at * down_rows, down_rows)
                to = gate_rows + m * down_rows
                outs[k][n, to : to + down_rows, :] = total[pl.ds(start, down_rows), :]
        stores += fetch([out.at[n] for out in outs], [out.at[n] for out in outs_far], out_sems.at[n])
    for copy in stores:
        copy.wait()


def stage_sum(idx, parts):
    outs = [hbm(LOCAL, QROWS, FE)] * 4
    scratch = [pltpu.VMEM(part.shape, BF) for part in parts]
    scratch += [pltpu.VMEM((LOCAL, QROWS, FE), BF)] * 4
    scratch += [pltpu.VMEM((XROWS, FE), BF)]
    scratch += [pltpu.SemaphoreType.DMA((LOCAL, 3)), pltpu.SemaphoreType.DMA((LOCAL, 4))]
    return run(
        stage_sum_kernel,
        "stage_sum",
        1,
        parts,
        outs,
        scratch,
        far_in=5,
        far_out=4,
        limit=FAR_LIMIT,
        idx=idx,
    )


SEND_ROWS = (QROWS + ZROWS) // 2


def finish_kernel(idx, *refs):
    bufs = refs[:5]
    keep_gate, keep_up, keep_down, send = refs[5:9]
    x_sum, z_sum = refs[9:11]
    big = D // 16
    small = big // 2
    tiny = FE // 32
    mine = idx[9]
    theirs = 1 - mine
    for n in range(LOCAL):
        acc = bufs[0][n].astype(F32)
        for part in bufs[1:4]:
            acc = acc + part[n].astype(F32)
        x_sum[n] = acc
        z_sum[n] = bufs[4][n].astype(F32)
        here = pl.ds(pl.multiple_of(mine * small, small), small)
        there = pl.ds(pl.multiple_of(theirs * small, small), small)
        keep_gate[n] = x_sum[n, here, :]
        keep_up[n] = z_sum[n, here, :]
        send[n, :small, :] = x_sum[n, there, :].astype(BF)
        send[n, small:big, :] = z_sum[n, there, :].astype(BF)
        for m in range(D // FE):
            source, at = (x_sum, m) if m < LEFT // FE else (z_sum, m - LEFT // FE)
            first = big + at * 2 * tiny
            here = pl.ds(pl.multiple_of(first + mine * tiny, tiny), tiny)
            there = pl.ds(pl.multiple_of(first + theirs * tiny, tiny), tiny)
            keep_down[n, :, m * FE : (m + 1) * FE] = source[n, here, :]
            send[n, big + m * tiny : big + (m + 1) * tiny, :] = source[n, there, :].astype(BF)


def finish(idx, parts):
    outs = [
        hbm(LOCAL, D // 32, FE, dtype=F32),
        hbm(LOCAL, D // 32, FE, dtype=F32),
        hbm(LOCAL, FE // 32, D, dtype=F32),
        hbm(LOCAL, SEND_ROWS, FE),
    ]
    scratch = [pltpu.VMEM((LOCAL, QROWS, FE), F32), pltpu.VMEM((LOCAL, ZROWS, FE), F32)]
    return run_far(finish_kernel, "finish", 1, parts, outs, scratch, idx=idx)


def assemble_kernel(idx, keep_gate, keep_up, keep_down, got, out_gate, out_up, out_down):
    mine = pl.ds(idx[9] * LOCAL, LOCAL)
    theirs = pl.ds((1 - idx[9]) * LOCAL, LOCAL)
    small = D // 32
    tiny = FE // 32
    out_gate[mine] = keep_gate[...]
    out_up[mine] = keep_up[...]
    out_down[mine] = keep_down[...]
    out_gate[theirs] = got[:, :small, :].astype(F32)
    out_up[theirs] = got[:, small : 2 * small, :].astype(F32)
    out_down[theirs, :, :FE] = got[:, 2 * small : 2 * small + tiny, :].astype(F32)
    out_down[theirs, :, FE:] = got[:, 2 * small + tiny :, :].astype(F32)


def assemble(idx, keep_gate, keep_up, keep_down, got):
    outs = [
        hbm(2 * LOCAL, D // 32, FE, dtype=F32),
        hbm(2 * LOCAL, D // 32, FE, dtype=F32),
        hbm(2 * LOCAL, FE // 32, D, dtype=F32),
    ]
    ins = [keep_gate, keep_up, keep_down, got]
    return run_far(assemble_kernel, "assemble", 2, ins, outs, idx=idx)


def middle_kernel(*refs):
    parts = refs[:4]
    h_ref, gate_ref, dy_ref, gain_ref, router_t, w_out = refs[4:10]
    dh_ref, send_ref, side_ref = refs[10:13]
    total = parts[0][...].astype(F32)
    for part in parts[1:]:
        total = total + part[...].astype(F32)
    extra = total[:, D:]
    d_gate = extra + pltpu.roll(extra, 128 - EXPERTS, 1)
    gate = gate_ref[...]
    d_chosen = gate * (d_gate - jnp.sum(gate * d_gate, axis=1, keepdims=True))
    d_logits = d_chosen.astype(BF)
    d_mlp = total[:, :D] + mm(d_logits, router_t[...])
    h = h_ref[...]
    gain = gain_ref[...].astype(F32)
    scale = lax.rsqrt(jnp.mean(h * h, axis=1, keepdims=True) + EPS)
    normed = h * scale
    mlp_in = (normed * gain).astype(BF)
    scaled = d_mlp * gain
    d_h = (
        dy_ref[...].astype(F32)
        + scale * scaled
        - h * (scale * scale * scale) * jnp.mean(scaled * h, axis=1, keepdims=True)
    )
    dh_ref[...] = d_h
    d_branch = d_h.astype(BF)
    d_attn = mm_nt(d_branch, w_out[...]).astype(BF)
    for b in range(BLOCKS):
        cols = slice(b * 128, (b + 1) * 128)
        send_ref[b, :, :128] = d_attn[:, cols]
        send_ref[b, :, 128:] = d_branch[:, cols]
    router = mm_tn(mlp_in, d_logits)
    d_gain = jnp.sum(d_mlp * normed, axis=0, keepdims=True)
    column = jnp.transpose(jnp.broadcast_to(d_gain, (128, D)))
    lane = lax.broadcasted_iota(jnp.int32, (D, 128), 1)
    side_ref[...] = jnp.where(lane == GAIN_LANE, column, router).astype(BF)


def middle(parts, h_own, gate_own, dy, gain, router_t, w_out):
    shapes = [((ROWS, D), F32), ((BLOCKS, ROWS, 256), BF), ((D, 128), BF)]

    def kernel(*refs):
        inputs = refs[:10]
        far = refs[10:13]
        bufs = refs[13:16]
        middle_kernel(*inputs, *bufs)
        for copy in fetch(bufs, far, refs[16]):
            copy.wait()

    outs = [hbm(*shape, dtype=kind) for shape, kind in shapes]
    scratch = [pltpu.VMEM(shape, kind) for shape, kind in shapes] + [pltpu.SemaphoreType.DMA((3,))]
    ins = [*parts, h_own, gate_own, dy, gain, router_t, w_out]
    return run(kernel, "middle", 0.5, ins, outs, scratch, far_out=3, limit=10)


def attend_back_kernel(idx, *refs):
    early_far = refs[:6]
    far = refs[6:10]
    dqkv_far = refs[10:14]
    dense_far = refs[14]
    early = refs[15:21]
    p_ref, attn_in, ao_all, side_ref, dk_acc, dv_acc, dqkv_ref, dense, sems, early_sems = refs[21:31]
    grads, q_ref, k_ref, v_ref, cos_ref, sin_ref = early
    early_copies = fetch(early_far, early, early_sems)
    p_copies = [
        pltpu.make_async_copy(far[0].at[i], p_ref.at[i], sems.at[i]) for i in range(BLOCKS)
    ]
    ao_copy = pltpu.make_async_copy(far[2], ao_all, sems.at[BLOCKS])
    in_copy = pltpu.make_async_copy(far[1], attn_in, sems.at[BLOCKS + 1])
    for copy in p_copies:
        copy.start()
    side_copy = pltpu.make_async_copy(far[3], side_ref, sems.at[2 * BLOCKS + 3])
    ao_copy.start()
    in_copy.start()
    side_copy.start()
    dk_acc[...] = jnp.zeros((LEN, HD), F32)
    dv_acc[...] = jnp.zeros((LEN, HD), F32)
    for copy in early_copies:
        copy.wait()
    for i in range(BLOCKS):
        lo = max(0, i - WIN // ROWS) * ROWS
        hi = (i + 1) * ROWS
        span = hi - lo
        rows = slice(i * ROWS, hi)
        do2 = jnp.concatenate([grads[i, :, :HD], grads[i, :, HD : 2 * HD]], axis=0)
        q2 = jnp.concatenate([q_ref[rows, :HD], q_ref[rows, HD:]], axis=0)
        p_copies[i].wait()
        probs_low = p_ref[i, :, :span]
        probs = probs_low.astype(F32)
        d_probs = mm_nt(do2, v_ref[lo:hi, :])
        weighted = probs * d_probs
        d_scores = (weighted - probs * jnp.sum(weighted, axis=1, keepdims=True)).astype(BF)
        dq = mm(d_scores, k_ref[lo:hi, :]) * HD**-0.5
        dk_acc[lo:hi, :] += mm_tn(d_scores, q2)
        dv_acc[lo:hi, :] += mm_tn(probs_low, do2)
        dq = jnp.concatenate([dq[:ROWS], dq[ROWS:]], axis=1).astype(BF).astype(F32)
        dq = dq * cos_ref[rows, :] - swap_halves(dq) * sin_ref[rows, :]
        dqkv_ref[rows, : 2 * HD] = dq.astype(BF)
    pair = jnp.concatenate([dk_acc[...], dv_acc[...]], axis=1).astype(BF).astype(F32)
    turned = pair * cos_ref[...] - swap_halves(pair) * sin_ref[...]
    lane = lax.broadcasted_iota(jnp.int32, pair.shape, 1)
    dqkv_ref[:, 2 * HD :] = jnp.where(lane < HD, turned, pair).astype(BF)
    dqkv_copies = []
    for r in range(BLOCKS):
        rows = pl.ds(pl.multiple_of(idx[r] * ROWS, ROWS), ROWS)
        copy = pltpu.make_async_copy(
            dqkv_ref.at[rows, :], dqkv_far[r // 2].at[r % 2], sems.at[BLOCKS + 3 + r]
        )
        copy.start()
        dqkv_copies.append(copy)
    in_copy.wait()
    ao_copy.wait()
    half = D // 2
    side_copy.wait()
    d_branch = jnp.concatenate([grads[b, :, 128:] for b in range(BLOCKS)], axis=0)
    for part in range(2):
        rows = slice(part * half, (part + 1) * half)
        left = mm_tn(attn_in[:, rows], dqkv_ref[...])
        right = jnp.concatenate(
            [mm_tn(ao_all[:, rows], d_branch), side_ref[rows, :].astype(F32)], axis=1
        )
        both = jnp.concatenate([left.reshape(-1, 8, 256), right.reshape(-1, 8, 256)], axis=1)
        dense[part * (half // 8) : (part + 1) * (half // 8)] = both.astype(BF)
    dense_copy = pltpu.make_async_copy(dense, dense_far, sems.at[BLOCKS + 2])
    dense_copy.start()
    for copy in dqkv_copies:
        copy.wait()
    dense_copy.wait()


def attend_back(idx, grads, p, q, k, v, attn_in, ao_all, side, cos_tab, sin_tab):
    early = [grads, q, k, v, cos_tab, sin_tab]
    outs = [hbm(2, ROWS, 256)] * 4 + [hbm(D // 8, 16, 256)]
    scratch = [pltpu.VMEM(item.shape, item.dtype) for item in early]
    scratch += [
        pltpu.VMEM(p.shape, BF),
        pltpu.VMEM((LEN, D), BF),
        pltpu.VMEM((LEN, D), BF),
        pltpu.VMEM((D, 128), BF),
        pltpu.VMEM((LEN, HD), F32),
        pltpu.VMEM((LEN, HD), F32),
        pltpu.VMEM((LEN, 256), BF),
        pltpu.VMEM((D // 8, 16, 256), BF),
        pltpu.SemaphoreType.DMA((2 * BLOCKS + 4,)),
        pltpu.SemaphoreType.DMA((6,)),
    ]
    ins = [*early, p, attn_in, ao_all, side]
    return run(
        attend_back_kernel,
        "attend_back",
        8,
        ins,
        outs,
        scratch,
        far_in=10,
        far_out=5,
        limit=FAR_LIMIT,
        idx=idx,
    )


def input_grad_kernel(idx, *refs):
    near = refs[:4]
    far = refs[4:8]
    x_ref, dh_ref, gain_ref, w_query, w_key, w_value, out_ref, dq, dk, dv = refs[8:18]
    odd = idx[14] == 1
    for dy in range(4):
        mine = near[dy][0].astype(F32)
        other = far[dy][1].astype(F32)
        first = jnp.where(odd, other, mine)
        second = jnp.where(odd, mine, other)
        pair = idx[2 * dy] // 2
        cols = pl.ds(pl.multiple_of(pair * 256, 256), 256)
        dq[:, cols] = jnp.concatenate([first[:, :128], second[:, :128]], axis=1).astype(BF)
        cols = pl.ds(pl.multiple_of(pair * 128, 128), 128)
        dk[:, cols] = jnp.concatenate([first[:, 128:192], second[:, 128:192]], axis=1).astype(BF)
        dv[:, cols] = jnp.concatenate([first[:, 192:], second[:, 192:]], axis=1).astype(BF)
    d_in = mm_nt(dq[...], w_query[...]) + mm_nt(dk[...], w_key[...]) + mm_nt(dv[...], w_value[...])
    x = x_ref[...].astype(F32)
    scale = lax.rsqrt(jnp.mean(x * x, axis=1, keepdims=True) + EPS)
    scaled = d_in * gain_ref[...]
    out_ref[...] = (
        dh_ref[...]
        + scale * scaled
        - x * (scale * scale * scale) * jnp.mean(scaled * x, axis=1, keepdims=True)
    ).astype(BF)


def input_grad(idx, near, far, x, d_h, gain, w_query, w_key, w_value):
    scratch = [
        pltpu.VMEM((ROWS, H * HD), BF),
        pltpu.VMEM((ROWS, KVH * HD), BF),
        pltpu.VMEM((ROWS, KVH * HD), BF),
    ]
    ins = [*near, *far, x, d_h, gain, w_query, w_key, w_value]
    return run_far(
        input_grad_kernel, "input_grad", 1, ins, [hbm(ROWS, D)], scratch, idx=idx
    )[0]


def dense_out_kernel(idx, dense, w_query, w_key, w_value, gain, *refs):
    dq, dk, dv, do, router, gains, turned = refs
    total = jnp.sum(dense[...].astype(F32).reshape(-1, BLOCKS, 16, 256), axis=0)
    for b in range(BLOCKS):
        dq[:, b * 128 : (b + 1) * 128] = total[b, :8, :128]
        do[:, b * 128 : (b + 1) * 128] = total[b, 8:, :128]
    for b in range(0, BLOCKS, 2):
        first = total[b, :8, 128:]
        second = total[b + 1, :8, 128:]
        cols = slice(b * HD, (b + 2) * HD)
        dk[:, cols] = jnp.concatenate([first[:, :HD], second[:, :HD]], axis=1)
        dv[:, cols] = jnp.concatenate([first[:, HD:], second[:, HD:]], axis=1)
    side = jnp.sum(total[:, 8:, 128:], axis=0)
    router[...] = side[:, :EXPERTS]
    dot = jnp.zeros((8, 1), F32)
    for weight, grad in ((w_query, dq), (w_key, dk), (w_value, dv)):
        dot = dot + jnp.sum(weight[...] * grad[...], axis=1, keepdims=True)
    chunk = pl.ds(pl.multiple_of(idx[16] * 128, 128), 128)
    turned[...] = jnp.transpose(jnp.broadcast_to(gain[:, chunk], (128, 128)))
    gain_rows = turned[pl.ds(pl.multiple_of(idx[17] * 8, 8), 8), 0:1]
    lane = lax.broadcasted_iota(jnp.int32, (8, 128), 1)
    both = jnp.where(lane == GAIN_LANE, side, dot / gain_rows)
    turned[:8, :] = both
    flat = jnp.transpose(turned[...])
    gains[...] = flat[GAIN_LANE - 8 : GAIN_LANE + 8, :]


def dense_out(idx, dense, w_query, w_key, w_value, gain):
    outs = [
        hbm(8, H * HD, dtype=F32),
        hbm(8, KVH * HD, dtype=F32),
        hbm(8, KVH * HD, dtype=F32),
        hbm(8, D, dtype=F32),
        hbm(8, EXPERTS, dtype=F32),
        hbm(16, 128, dtype=F32),
    ]
    ins = [dense, w_query, w_key, w_value, gain]
    scratch = [pltpu.VMEM((128, 128), F32)]
    return run_far(dense_out_kernel, "dense_out", 1, ins, outs, scratch, idx=idx)


def from_x(value, off):
    size = lax.axis_size("x")
    return lax.ppermute(value, "x", [(i, (i + off) % size) for i in range(size)])


def from_z(value, off):
    size = lax.axis_size("z")
    return lax.ppermute(value, "z", [(i, (i + off) % size) for i in range(size)])


def along_y(value, off):
    route = []
    for y in range(4):
        to = (y + off) % 4
        route.append(((y % 2) * 2 + y // 2, (to % 2) * 2 + to // 2))
    return lax.ppermute(value, ("yl", "yh"), route)


def other_core(value):
    return lax.ppermute(value, "c", [(0, 1), (1, 0)])


def near_ring(value):
    return [value] + [along_y(value, -off) for off in (1, 2, 3)]


def both_cores(near):
    far = [other_core(item) for item in near]
    return [item for pair in zip(near, far) for item in pair]


def gather_ring(value):
    return both_cores(near_ring(value))


def reduce_ring(pieces):
    return [pieces[0]] + [along_y(pieces[off], off) for off in (1, 2, 3)]


def scatter_parts(parts, send):
    return [parts[0]] + [send(parts[k], k) for k in (1, 2, 3)]


def together(*values):
    return lax.optimization_barrier(values)


def after(values, *earlier):
    return lax.optimization_barrier((values, earlier))[0]


def local(
    tokens,
    segments,
    routes,
    drop_order,
    gain_attn,
    w_query,
    w_key,
    w_value,
    w_out,
    gain_mlp,
    w_router,
    w_gate,
    w_up,
    w_down,
    cotangent,
):
    x_at = lax.axis_index("x")
    z_at = lax.axis_index("z")
    yl = lax.axis_index("yl")
    yh = lax.axis_index("yh")
    core = lax.axis_index("c")
    y_at = yh * 2 + yl
    own = yl * 4 + yh * 2 + core
    expert_at = yh * 2 + core

    entries = []
    for off in range(4):
        y = (y_at + off) % 4
        for dc in range(2):
            entries.append((y % 2) * 4 + (y // 2) * 2 + (core + dc) % 2)
    entries += [own, yl, expert_at, x_at, z_at, y_at, core, expert_at * 8 + yl * LOCAL]
    first_row = ((x_at * 4 + z_at) * 8 + own) * 8
    entries += [first_row // 128, first_row % 128 // 8]
    idx = jnp.stack([jnp.asarray(entry, jnp.int32) for entry in entries])

    cos_np, sin_np = rotary_tables()
    cos_tab = jnp.asarray(cos_np)
    sin_tab = jnp.asarray(sin_np)
    gain_one = gain_attn.astype(F32).reshape(1, D)
    gain_two = gain_mlp.astype(F32).reshape(1, D)
    router_t = jnp.pad(w_router.T, ((0, 128 - EXPERTS), (0, 0)))

    def columns(weight, block):
        return lax.dynamic_slice_in_dim(weight, block * 128, 128, 1)

    def out_rows(weight):
        return lax.dynamic_slice_in_dim(weight, first_row, 8, 0).astype(F32)

    wq_cols = columns(w_query, own)
    wk_cols = columns(w_key, own // 2)
    wv_cols = columns(w_value, own // 2)
    finals = [out_rows(w_query), out_rows(w_key), out_rows(w_value)]
    early = [idx, gain_one, gain_two, router_t, wq_cols, wk_cols, wv_cols, finals]

    seg_cols = jnp.broadcast_to(segments.astype(BF)[:, None], (ROWS, AUG - D))
    x_near = near_ring(jnp.concatenate([tokens, seg_cols], axis=1))
    slot_own = slots(routes.T, drop_order)
    x_near, slot_own, early = together(x_near, slot_own, early)
    idx, gain_one, gain_two, router_t, wq_cols, wk_cols, wv_cols, finals = early
    xs = both_cores(x_near)
    dy_near = near_ring(after(cotangent, *xs))

    ao, attn_in, q, k, v, p = attend(
        idx, xs, slot_own, gain_one, wq_cols, wk_cols, wv_cols, cos_tab, sin_tab
    )
    dys = both_cores(dy_near)
    aos = gather_ring(after(ao, *dy_near))
    mlp_in, slot_t, gate_t, h_own, gate_own, ao_all = project(
        idx, xs, aos, w_out, gain_two, router_t
    )
    expert_results = experts(idx, mlp_in, dys, slot_t, gate_t, w_gate, w_up, w_down)
    rows, act, d_out, d_up, dm_same, dm_other = expert_results[:6]
    x_args = expert_results[6:10]
    outs, hot_gated = expert_results[10:]

    got = other_core(dm_other)
    z_all = z_grads(rows, act, d_out, d_up)
    z_all, got = together(z_all, got)
    dm_pieces = add_pairs_out(dm_same, got)
    dm_parts = reduce_ring(dm_pieces)
    z_half = lax.psum_scatter(after(z_all, *dm_pieces), "z", scatter_dimension=0, tiled=True)
    x_up, x_down, *x_keep = x_grads(idx, after(x_args[0], *dm_pieces), *x_args[1:])
    mx = mixed_sum(after(hot_gated, x_up), outs)
    mx, dm_parts, x_up, x_down = together(mx, dm_parts, x_up, x_down)
    x_below = from_x(x_up, 1)
    x_above = from_x(x_down, 3)
    d_h, to_heads, side = middle(
        dm_parts, h_own, gate_own, cotangent, gain_two, router_t, w_out
    )
    grads = lax.all_to_all(to_heads, GROUP, split_axis=0, concat_axis=0, tiled=True)
    back = attend_back(
        idx, grads, p, q, k, v, attn_in, ao_all, side, cos_tab, sin_tab
    )
    back, x_below, x_above = together(back, x_below, x_above)

    dqkv_near = [reduce_ring(back[:4])[off] for off in (0, 3, 2, 1)]
    x_relay = relay(x_keep[1], x_below, x_keep[2], x_above)
    late_below = from_x(x_relay[0], 1)
    late_above = from_x(x_relay[1], 3)
    dqkv_near, x_relay = together(dqkv_near, x_relay)
    dqkv_far = [other_core(item) for item in dqkv_near]
    d_tokens = input_grad(
        idx, dqkv_near, dqkv_far, tokens, d_h, gain_one, w_query, w_key, w_value
    )
    dense = lax.all_to_all(
        back[4],
        ("x", "z", "yl", "yh", "c"),
        split_axis=0,
        concat_axis=0,
        tiled=True,
    )
    d_tokens, dense, late_below, late_above, z_half = together(
        d_tokens, dense, late_below, late_above, z_half
    )
    z_second = lax.psum_scatter(z_half[0], "x", scatter_dimension=0, tiled=True)[0]
    second = stage_sum(idx, [x_keep[0], x_below, x_above, late_below, late_above])
    x_second = scatter_parts(second, from_z)
    mx_pieces = add_pairs_far(mx[0], other_core(after(mx[1], *second)))
    mx_parts = reduce_ring(mx_pieces)
    dense_rows = dense_out(idx, after(dense, *mx_pieces), *finals, gain_one)
    mx_parts, dense_rows, x_second = together(mx_parts, dense_rows, x_second)
    total = h_own
    for part in mx_parts:
        total = total + part.astype(F32)
    block_out = total.astype(BF)

    keep_gate, keep_up, keep_down, sent = finish(idx, [*x_second, z_second])
    got = lax.ppermute(sent, "yl", [(0, 1), (1, 0)])
    d_w_gate, d_w_up, d_w_down = assemble(idx, keep_gate, keep_up, keep_down, got)

    d_w_query, d_w_key, d_w_value, d_w_out, d_w_router, gains = dense_rows
    d_gain_attn = gains[0, :8]
    d_gain_mlp = gains[8, :8]

    return (
        block_out,
        d_tokens,
        d_gain_attn,
        d_w_query,
        d_w_key,
        d_w_value,
        d_w_out,
        d_gain_mlp,
        d_w_router,
        d_w_gate,
        d_w_up,
        d_w_down,
    )


def solution(mesh):
    side = 4 if mesh.shape["dp"] == 32 else 1
    names = ("x", "z", "yl", "yh", "c")
    grid = Mesh(mesh.devices.reshape(side, side, 2, 2, 2), names)
    tokens = names
    experts_axes = ("yh", "c")
    dp = ("x", "z", "yl")
    in_specs = (
        P(tokens, None),
        P(tokens),
        P(tokens, None),
        P(tokens, None),
        P(),
        P(),
        P(),
        P(),
        P(),
        P(),
        P(),
        P(experts_axes, None, None),
        P(experts_axes, None, None),
        P(experts_axes, None, None),
        P(tokens, None),
    )
    out_specs = (
        P(tokens, None),
        P(tokens, None),
        P(tokens),
        P(tokens, None),
        P(tokens, None),
        P(tokens, None),
        P(tokens, None),
        P(tokens),
        P(tokens, None),
        P(experts_axes, dp, None),
        P(experts_axes, dp, None),
        P(experts_axes, dp, None),
    )
    return jax.shard_map(local, mesh=grid, in_specs=in_specs, out_specs=out_specs, check_vma=False)
```

```python
import functools

import jax
import jax.numpy as jnp
import numpy as np
from jax import lax
from jax.experimental import pallas as pl
from jax.experimental.pallas import tpu as pltpu
from jax.sharding import Mesh, PartitionSpec as P

H = 16
KVH = 8
HD = 64
D = 1024
FE = 512
TOPK = 8
EXPERTS = 32
CAP = 36
ROWS = 128
LEN = 1024
BLOCKS = LEN // ROWS
WIN = 512
LOCAL = 4
PAIRS = BLOCKS // 2
SLOTS = 80
EROWS = PAIRS * SLOTS
AUG = D + 128
GAIN_LANE = 32
FAR_LIMIT = 56
SHARE = 0.1
EPS = 1e-06
THETA = 10000.0
NEG = -1e30
BF = jnp.bfloat16
F32 = jnp.float32
GROUP = ("yl", "yh", "c")


def mm(left, right):
    return jnp.dot(left, right, preferred_element_type=F32)


def mm_nt(left, right):
    return lax.dot_general(left, right, (((1,), (1,)), ((), ())), preferred_element_type=F32)


def mm_tn(left, right):
    return lax.dot_general(left, right, (((0,), (0,)), ((), ())), preferred_element_type=F32)


def rotary_tables():
    half = HD // 2
    frequency = THETA ** (-np.arange(half, dtype=np.float64) * 2.0 / HD)
    angles = np.arange(LEN, dtype=np.float64)[:, None] * frequency[None, :]
    cosine = np.cos(angles)
    sine = np.sin(angles)
    cos_full = np.concatenate([cosine] * 4, axis=1).astype(np.float32)
    sin_full = np.concatenate([-sine, sine, -sine, sine], axis=1).astype(np.float32)
    return cos_full, sin_full


def swap_halves(array_in):
    half = HD // 2
    lane = lax.broadcasted_iota(jnp.int32, array_in.shape, 1)
    ahead = pltpu.roll(array_in, array_in.shape[1] - half, 1)
    behind = pltpu.roll(array_in, half, 1)
    return jnp.where(lane % HD < half, ahead, behind)


def vmem(*shape, dtype=BF):
    return pltpu.VMEM(shape, dtype)


def hbm(*shape, dtype=BF):
    return pltpu.HBM(shape, dtype)


def auto(*shape, dtype=BF):
    return jax.ShapeDtypeStruct(shape, dtype)


def cost(micros):
    return pl.CostEstimate(
        flops=int(micros * 1.15e9 * SHARE), bytes_accessed=int(micros * 1e6), transcendentals=0
    )


def run(
    kernel,
    name,
    micros,
    ins,
    outs,
    scratch=(),
    far_in=0,
    far_out=0,
    limit=24,
    idx=None,
    aliases=None,
):
    inside = pl.BlockSpec(memory_space=pltpu.VMEM)
    outside = pl.BlockSpec(memory_space=pltpu.HBM)
    in_specs = [inside] * (len(ins) - far_in) + [outside] * far_in
    operands = list(ins)
    if idx is not None:
        in_specs = [pl.BlockSpec(memory_space=pltpu.SMEM)] + in_specs
        operands = [idx] + operands
    return pl.pallas_call(
        kernel,
        out_shape=list(outs),
        in_specs=in_specs,
        out_specs=[inside] * (len(outs) - far_out) + [outside] * far_out,
        scratch_shapes=list(scratch),
        input_output_aliases=aliases or {},
        compiler_params=pltpu.CompilerParams(vmem_limit_bytes=limit * 1024 * 1024),
        cost_estimate=cost(micros),
        name=name,
    )(*operands)


def run_far(kernel, name, micros, ins, outs, scratch=(), idx=None):
    count = len(ins)
    given = 0 if idx is None else 1

    def body(*refs):
        lead = refs[:given]
        sources = refs[given : given + count]
        targets = refs[given + count : given + count + len(outs)]
        rest = refs[given + count + len(outs) :]
        in_bufs = rest[:count]
        out_bufs = rest[count : count + len(outs)]
        in_sems, out_sems = rest[count + len(outs) : count + len(outs) + 2]
        for copy in fetch(sources, in_bufs, in_sems):
            copy.wait()
        kernel(*lead, *in_bufs, *out_bufs, *rest[count + len(outs) + 2 :])
        for copy in fetch(out_bufs, targets, out_sems):
            copy.wait()

    bufs = [pltpu.VMEM(item.shape, item.dtype) for item in ins]
    bufs += [pltpu.VMEM(item.shape, item.dtype) for item in outs]
    bufs += [pltpu.SemaphoreType.DMA((count,)), pltpu.SemaphoreType.DMA((len(outs),))]
    return run(
        body,
        name,
        micros,
        ins,
        outs,
        bufs + list(scratch),
        far_in=count,
        far_out=len(outs),
        limit=FAR_LIMIT,
        idx=idx,
    )


def fetch(sources, targets, sems):
    copies = [
        pltpu.make_async_copy(source, target, sems.at[n])
        for n, (source, target) in enumerate(zip(sources, targets))
    ]
    for copy in copies:
        copy.start()
    return copies


def slots_kernel(routes_ref, order_ref, meta_ref, place_ref):
    order = order_ref[...]
    index = lax.broadcasted_iota(jnp.int32, (1, ROWS * TOPK), 1)
    token_of = order // TOPK
    choice_of = order - token_of * TOPK
    at_token = (token_of == lax.broadcasted_iota(jnp.int32, (ROWS, ROWS * TOPK), 0)).astype(F32)
    choice = lax.broadcasted_iota(jnp.int32, (2 * TOPK, ROWS * TOPK), 0)
    high = index // 32
    low = index - high * 32
    part = jnp.where(choice < TOPK, high, low).astype(F32)
    choice_mod = jnp.where(choice < TOPK, choice, choice - TOPK)
    table = jnp.where(choice_mod == choice_of, part, 0.0)
    found = mm_nt(at_token.astype(BF), table.astype(BF))
    place = found[:, :TOPK] * 32.0 + found[:, TOPK:]
    lane = lax.broadcasted_iota(jnp.int32, (ROWS, 128), 1)
    wide = jnp.concatenate(
        [
            routes_ref[...].astype(F32),
            jnp.zeros((ROWS - TOPK, ROWS), F32),
        ],
        axis=0,
    )
    turned = jnp.transpose(wide)
    lane_f = lane.astype(F32)
    placed = jnp.full((ROWS, 128), 4096.0, F32)
    for k in range(TOPK):
        placed = jnp.where(turned[:, k : k + 1] == lane_f, place[:, k : k + 1], placed)
    place_ref[...] = placed

    def count(step, total):
        for inner in range(8):
            row = place_ref[pl.ds(step * 8 + inner, 1), :]
            total = total + jnp.where(row < placed, 1.0, 0.0)
        return total

    rank = lax.fori_loop(0, ROWS // 8, count, jnp.zeros((ROWS, 128), F32))
    slot = jnp.where(placed < 4000.0, jnp.where(rank < CAP, rank, -1.0), -2.0)
    meta_ref[...] = slot.astype(BF)


def slots(routes_t, drop_order):
    return run(
        slots_kernel,
        "slots",
        3,
        [routes_t, drop_order],
        [auto(ROWS, 128)],
        [pltpu.VMEM((ROWS, 128), F32)],
        limit=8,
    )[0]


def attend_kernel(idx, *refs):
    xs = refs[:8]
    slots_ref, gain, wq, wk, wv, cos_ref, sin_ref = refs[8:15]
    out_ref = refs[15]
    far = refs[16:21]
    attn_in, q_ref, k_ref, v_ref, p_ref, seg_row, seg_col, sems = refs[21:29]
    near = (attn_in, q_ref, k_ref, v_ref)
    copies = [pltpu.make_async_copy(near[n], far[n], sems.at[n]) for n in range(4)]
    gain_full = gain[...]
    for r in range(BLOCKS):
        rows = pl.ds(pl.multiple_of(idx[r] * ROWS, ROWS), ROWS)
        x = xs[r][:, :D].astype(F32)
        scale = lax.rsqrt(jnp.mean(x * x, axis=1, keepdims=True) + EPS)
        attn_in[rows, :] = (x * scale * gain_full).astype(BF)
        segs = xs[r][:, D:].astype(F32)
        seg_col[rows, :] = segs
        seg_row[:, rows] = jnp.transpose(segs)[:8, :]
    copies[0].start()
    out_ref[LEN:, :] = slots_ref[...]
    odd = (idx[8] % 2) == 1
    half = LEN // 2
    for part in range(2):
        rows = slice(part * half, (part + 1) * half)
        block = attn_in[rows, :]
        cosine = cos_ref[rows, :]
        sine = sin_ref[rows, :]
        q = mm(block, wq[...])
        q = q * cosine + swap_halves(q) * sine
        q_ref[rows, :] = (q.astype(BF).astype(F32) * HD**-0.5).astype(BF)
        k = mm(block, wk[...])
        k = jnp.where(odd, pltpu.roll(k, HD, 1), k)
        k = k * cosine + swap_halves(k) * sine
        k_ref[rows, :] = k[:, :HD].astype(BF)
        v = mm(block, wv[...])
        v = jnp.where(odd, pltpu.roll(v, HD, 1), v)
        v_ref[rows, :] = v[:, :HD].astype(BF)
    for copy in copies[1:]:
        copy.start()
    for i in range(BLOCKS):
        lo = max(0, i - WIN // ROWS) * ROWS
        hi = (i + 1) * ROWS
        span = hi - lo
        rows = slice(i * ROWS, hi)
        q2 = jnp.concatenate([q_ref[rows, :HD], q_ref[rows, HD:]], axis=0)
        scores = mm_nt(q2, k_ref[lo:hi, :])
        q_pos = i * ROWS + lax.broadcasted_iota(jnp.int32, (ROWS, span), 0)
        k_pos = lo + lax.broadcasted_iota(jnp.int32, (ROWS, span), 1)
        allowed = (k_pos <= q_pos) & (k_pos > q_pos - WIN)
        allowed = allowed & (seg_row[0:1, lo:hi] == seg_col[rows, 0:1])
        bias = jnp.where(allowed, 0.0, NEG)
        scores = scores + jnp.concatenate([bias, bias], axis=0)
        top = jnp.max(scores, axis=1, keepdims=True)
        expo = jnp.exp(scores - top)
        total = jnp.sum(expo, axis=1, keepdims=True)
        probs = (expo * (1.0 / total)).astype(BF)
        p_ref[i, :, :span] = probs
        if span < WIN + ROWS:
            p_ref[i, :, span:] = jnp.zeros((2 * ROWS, WIN + ROWS - span), BF)
        copy = pltpu.make_async_copy(p_ref.at[i], far[4].at[i], sems.at[4 + i])
        copy.start()
        copies.append(copy)
        out = mm(probs, v_ref[lo:hi, :])
        out_ref[rows, :] = jnp.concatenate([out[:ROWS], out[ROWS:]], axis=1).astype(BF)
    for copy in copies:
        copy.wait()


def attend(idx, xs, slot_own, gain, wq, wk, wv, cos_tab, sin_tab):
    shapes = [(LEN, D), (LEN, 2 * HD), (LEN, HD), (LEN, HD), (BLOCKS, 2 * ROWS, WIN + ROWS)]
    outs = [vmem(LEN + ROWS, 2 * HD)] + [hbm(*shape) for shape in shapes]
    scratch = [pltpu.VMEM(shape, BF) for shape in shapes]
    scratch += [pltpu.VMEM((8, LEN), F32), pltpu.VMEM((LEN, 128), F32)]
    scratch += [pltpu.SemaphoreType.DMA((4 + BLOCKS,))]
    ins = [*xs, slot_own, gain, wq, wk, wv, cos_tab, sin_tab]
    return run(attend_kernel, "attend", 7, ins, outs, scratch, far_out=5, limit=16, idx=idx)


def project_kernel(idx, *refs):
    xs = refs[:8]
    aos = refs[8:16]
    w_out, gain, router_t = refs[16:19]
    mlp_in, slot_t, gate_t, h_far, gate_far, ao_far = refs[19:25]
    ao_all, h_own, gate_own, sems = refs[25:29]
    for r in range(BLOCKS):
        cols = pl.ds(pl.multiple_of(idx[r] * ROWS, ROWS), ROWS)
        ao_all[:, cols] = aos[r][:LEN, :]
    ao_copy = pltpu.make_async_copy(ao_all, ao_far, sems.at[0])
    ao_copy.start()
    gain_full = gain[...]
    for p in range(PAIRS):
        rows = slice(p * 2 * ROWS, (p + 1) * 2 * ROWS)
        places = [pl.ds(pl.multiple_of(idx[2 * p + n] * ROWS, ROWS), ROWS) for n in range(2)]
        attended = jnp.concatenate([ao_all[place, :] for place in places], axis=0)
        x = jnp.concatenate([xs[2 * p + n][:, :D] for n in range(2)], axis=0).astype(F32)
        h = x + mm(attended, w_out[...])
        scale = lax.rsqrt(jnp.mean(h * h, axis=1, keepdims=True) + EPS)
        normed = (h * scale * gain_full).astype(BF)
        mlp_in[rows, :] = normed
        logits = mm_nt(normed, router_t[...])
        slot = jnp.concatenate([aos[2 * p + n][LEN:, :] for n in range(2)], axis=0).astype(F32)
        lane = lax.broadcasted_iota(jnp.int32, slot.shape, 1)
        routed = (slot > -1.5) & (lane < EXPERTS)
        logits = jnp.where(routed, logits, NEG)
        top = jnp.max(logits, axis=1, keepdims=True)
        expo = jnp.where(routed, jnp.exp(logits - top), 0.0)
        gate = expo / jnp.sum(expo, axis=1, keepdims=True)
        slot_t[:, rows] = jnp.transpose(slot)[:EXPERTS, :]
        gate_t[:, rows] = jnp.transpose(gate)[:EXPERTS, :]
        if p == 0:
            h_own[...] = h[:ROWS]
            gate_own[...] = gate[:ROWS]
            own_copies = [
                pltpu.make_async_copy(h_own, h_far, sems.at[1]),
                pltpu.make_async_copy(gate_own, gate_far, sems.at[2]),
            ]
            for copy in own_copies:
                copy.start()
    ao_copy.wait()
    for copy in own_copies:
        copy.wait()


def project(idx, xs, aos, w_out, gain, router_t):
    outs = [
        vmem(LEN, D),
        vmem(EXPERTS, LEN, dtype=F32),
        vmem(EXPERTS, LEN, dtype=F32),
        hbm(ROWS, D, dtype=F32),
        hbm(ROWS, 128, dtype=F32),
        hbm(LEN, D),
    ]
    scratch = [
        pltpu.VMEM((LEN, D), BF),
        pltpu.VMEM((ROWS, D), F32),
        pltpu.VMEM((ROWS, 128), F32),
        pltpu.SemaphoreType.DMA((3,)),
    ]
    ins = [*xs, *aos, w_out, gain, router_t]
    return run(project_kernel, "project", 5, ins, outs, scratch, far_out=3, limit=14, idx=idx)


PROWS = LOCAL * SLOTS
HALF = LOCAL // 2
LEFT = FE
XROWS = D // 4 + FE // 4 * (LEFT // FE)
QROWS = XROWS // 4
ZROWS = D // 16 + FE // 16 * ((D - LEFT) // FE)


def experts_kernel(idx, *refs):
    mlp_in = refs[0]
    dys = refs[1:9]
    slot_t, gate_t, w_gate, w_up, w_down = refs[9:14]
    rows_out, act_out, dout_out, dg_out, du_out, hot_gated, outs, dm_same, dm_other = refs[14:23]
    wg_buf, wu_buf, wd_buf, sems, dy_rows, gate_col, hot, dslots = refs[23:31]

    def load(e):
        at = idx[9] * LOCAL + e
        slot = lax.rem(e, 2)
        return [
            pltpu.make_async_copy(weight.at[at], buf.at[slot], sems.at[slot, n])
            for n, (weight, buf) in enumerate(((w_gate, wg_buf), (w_up, wu_buf), (w_down, wd_buf)))
        ]

    for e in range(2):
        for copy in load(jnp.int32(e)):
            copy.start()
    for p in range(PAIRS):
        cols = slice(p * 2 * ROWS, (p + 1) * 2 * ROWS)
        part = slice(p * SLOTS, (p + 1) * SLOTS)
        lane = lax.broadcasted_iota(jnp.int32, (1, 2 * ROWS), 1)
        lift = jnp.where(lane >= ROWS, float(CAP), 0.0)
        row_id = lax.broadcasted_iota(jnp.int32, (SLOTS, 2 * ROWS), 0).astype(F32)
        hots = []
        for n in range(LOCAL):
            slot = slot_t[pl.ds(idx[15] + n, 1), cols]
            gate = gate_t[pl.ds(idx[15] + n, 1), cols]
            place = jnp.where(slot > -0.5, slot + lift, -1.0)
            one = jnp.where(row_id == place, 1.0, 0.0)
            gated_one = one * gate
            gate_col[n, part, :] = jnp.sum(gated_one, axis=1, keepdims=True)
            hots.append(one.astype(BF))
            hot_gated[p, n * SLOTS : (n + 1) * SLOTS, :] = gated_one.astype(BF)
        hot_pair = jnp.concatenate(hots, axis=0)
        hot[p] = hot_pair
        taken = mm(hot_pair, mlp_in[cols, :]).astype(BF)
        dy = jnp.concatenate([dys[2 * p][...], dys[2 * p + 1][...]], axis=0)
        taken_dy = mm(hot_pair, dy).astype(BF)
        for n in range(LOCAL):
            rows_out[n, part, :] = taken[n * SLOTS : (n + 1) * SLOTS]
            dy_rows[n, part, :] = taken_dy[n * SLOTS : (n + 1) * SLOTS]

    def one_expert(e, carry):
        for copy in load(e):
            copy.wait()
        at = lax.rem(e, 2)
        rows = rows_out[e]
        wg = wg_buf[at]
        wu = wu_buf[at]
        wd = wd_buf[at]
        gate_h = mm(rows, wg)
        up_h = mm(rows, wu)
        sig = 1.0 / (1.0 + jnp.exp(-gate_h))
        silu = gate_h * sig
        act = (silu * up_h).astype(BF)
        act_out[e] = act
        out = mm(act, wd).astype(BF)
        outs[e] = out
        dy = dy_rows[e].astype(F32)
        d_gate = jnp.sum(dy * out.astype(F32), axis=1, keepdims=True)
        d_out = (gate_col[e].astype(BF).astype(F32) * dy).astype(BF)
        dout_out[e] = d_out
        d_act = mm_nt(d_out, wd)
        d_up = (d_act * silu).astype(BF)
        d_gh = (d_act * up_h * sig * (1.0 + gate_h * (1.0 - sig))).astype(BF)
        dg_out[e] = d_gh
        du_out[e] = d_up
        dslots[e, :, :D] = (mm_nt(d_gh, wg) + mm_nt(d_up, wu)).astype(BF)
        lane = lax.broadcasted_iota(jnp.int32, (EROWS, 128), 1)
        d_high = d_gate.astype(BF).astype(F32)
        mine = idx[15] + e
        extra = jnp.where(lane == mine, d_high, 0.0)
        extra = jnp.where(lane == mine + EXPERTS, d_gate - d_high, extra)
        dslots[e, :, D:] = extra.astype(BF)

        @pl.when(e + 2 < LOCAL)
        def _():
            for copy in load(e + 2):
                copy.start()

        return carry

    lax.fori_loop(0, LOCAL, one_expert, 0)

    for p in range(PAIRS):
        part = slice(p * SLOTS, (p + 1) * SLOTS)
        grads = jnp.concatenate([dslots[n, part, :] for n in range(LOCAL)], axis=0)
        merged = mm_tn(hot[p], grads).astype(BF)
        dm_same[p] = merged[:ROWS]
        dm_other[p] = merged[ROWS:]


def experts(idx, mlp_in, dys, slot_t, gate_t, w_gate, w_up, w_down):
    wide = (LOCAL, EROWS, D)
    narrow = (LOCAL, EROWS, FE)
    hot_shape = (PAIRS, PROWS, 2 * ROWS)
    outs = [vmem(*shape) for shape in (wide, narrow, wide, narrow, narrow, hot_shape, wide)]
    outs += [vmem(4, ROWS, AUG)] * 2
    scratch = [
        pltpu.VMEM((2, D, FE), BF),
        pltpu.VMEM((2, D, FE), BF),
        pltpu.VMEM((2, FE, D), BF),
        pltpu.SemaphoreType.DMA((2, 3)),
        pltpu.VMEM(wide, BF),
        pltpu.VMEM((LOCAL, EROWS, 1), F32),
        pltpu.VMEM(hot_shape, BF),
        pltpu.VMEM((LOCAL, EROWS, AUG), BF),
    ]
    ins = [mlp_in, *dys, slot_t, gate_t, w_gate, w_up, w_down]
    return run(experts_kernel, "experts", 16, ins, outs, scratch, far_in=3, limit=26, idx=idx)


def ring_places(e):
    if e < HALF:
        return ((0, 2, e), (2, 0, e), (1, 3, e), (3, 1, e + HALF))
    return ((0, 2, e), (1, 0, e), (2, 1, e - HALF), (3, 4, e - HALF))


def weight_grads_kernel(idx, rows, act, d_out, d_gh, d_up, *refs):
    x_far = refs[:5]
    z_far = refs[5:10]
    x_bufs = refs[10:15]
    z_bufs = refs[15:20]
    whole, whole_down, x_sems, z_sems = refs[20:24]
    quarter = D // 4
    down_q = FE // 4
    small = quarter // 4
    small_down = down_q // 4
    copies = []
    for e in range(LOCAL):
        both = jnp.concatenate([d_gh[e], d_up[e]], axis=1)
        whole[...] = mm_tn(rows[e], both).astype(BF)
        whole_down[...] = mm_tn(act[e], d_out[e]).astype(BF)
        for k, item, place in ring_places(e):
            target = x_bufs[item].at[place]
            at = (idx[11] + k) % 4
            start = pl.multiple_of(at * quarter, quarter)
            target[:quarter, :] = whole[pl.ds(start, quarter), :FE]
            start = pl.multiple_of(at * down_q, down_q)
            target[quarter:, :] = whole_down[pl.ds(start, down_q), :FE]
            copy = pltpu.make_async_copy(target, x_far[item].at[place], x_sems.at[e, k])
            copy.start()
            copies.append(copy)
        for k, item, place in ring_places(e):
            target = z_bufs[item].at[place]
            at = (idx[12] + k) % 4
            for x in range(4):
                start = pl.multiple_of(x * quarter + at * small, small)
                target[x, :small, :] = whole[pl.ds(start, small), FE:]
                start = pl.multiple_of(x * down_q + at * small_down, small_down)
                target[x, small:, :] = whole_down[pl.ds(start, small_down), FE:]
            copy = pltpu.make_async_copy(target, z_far[item].at[place], z_sems.at[e, k])
            copy.start()
            copies.append(copy)
    for copy in copies:
        copy.wait()


def weight_grads(idx, rows, act, d_out, d_gh, d_up):
    x_piece = (XROWS, FE)
    z_piece = (4, ZROWS, FE)
    shapes = [(LOCAL, *x_piece)] * 3 + [(HALF, *x_piece)] * 2
    shapes += [(LOCAL, *z_piece)] * 3 + [(HALF, *z_piece)] * 2
    outs = [hbm(*shape) for shape in shapes]
    scratch = [pltpu.VMEM(shape, BF) for shape in shapes]
    scratch += [pltpu.VMEM((D, 2 * FE), BF), pltpu.VMEM((FE, D), BF)]
    scratch += [pltpu.SemaphoreType.DMA((LOCAL, 4))] * 2
    ins = [rows, act, d_out, d_gh, d_up]
    results = run(
        weight_grads_kernel, "weight_grads", 6, ins, outs, scratch, far_out=10, limit=24, idx=idx
    )
    return results[:5], results[5:]


def relay_kernel(*refs):
    far = refs[:8]
    outs_far = refs[8:12]
    bufs = refs[12:20]
    outs = refs[20:24]
    in_sems, out_sems = refs[24:26]
    loads = [
        [
            fetch(
                [item.at[e] for item in far[pair : pair + 2]],
                [item.at[e] for item in bufs[pair : pair + 2]],
                in_sems.at[pair // 2, e],
            )
            for e in range(HALF)
        ]
        for pair in range(0, 8, 2)
    ]
    stores = []
    for n in range(4):
        for e in range(HALF):
            for copy in loads[n][e]:
                copy.wait()
            outs[n][e] = (bufs[2 * n][e].astype(F32) + bufs[2 * n + 1][e].astype(F32)).astype(BF)
            copy = pltpu.make_async_copy(outs[n].at[e], outs_far[n].at[e], out_sems.at[n, e])
            copy.start()
            stores.append(copy)
    for copy in stores:
        copy.wait()


def relay(x_parts, z_parts):
    ins = [*x_parts, *z_parts]
    x_shape, z_shape = x_parts[0].shape, z_parts[0].shape
    shapes = [x_shape, x_shape, z_shape, z_shape]
    scratch = [pltpu.VMEM(shape, BF) for shape in (x_shape,) * 4 + (z_shape,) * 4]
    scratch += [pltpu.VMEM(shape, BF) for shape in shapes]
    scratch += [pltpu.SemaphoreType.DMA((4, HALF, 2)), pltpu.SemaphoreType.DMA((4, HALF))]
    outs = [hbm(*shape) for shape in shapes]
    return run(
        relay_kernel, "relay", 300, ins, outs, scratch, far_in=8, far_out=4, limit=FAR_LIMIT
    )


def mixed_kernel(idx, hot_gated, outs, far, blocks, sems):
    copies = []
    for p in range(PAIRS):
        part = slice(p * SLOTS, (p + 1) * SLOTS)
        values = jnp.concatenate([outs[n, part, :] for n in range(LOCAL)], axis=0)
        merged = mm_tn(hot_gated[p], values).astype(BF)
        for n in range(2):
            r = 2 * p + n
            blocks[r] = merged[n * ROWS : (n + 1) * ROWS]
            copy = pltpu.make_async_copy(
                blocks.at[r], far.at[idx[r], :, pl.ds(256, D)], sems.at[r]
            )
            copy.start()
            copies.append(copy)
    for copy in copies:
        copy.wait()


def mixed_sum(idx, hot_gated, outs):
    scratch = [pltpu.VMEM((BLOCKS, ROWS, D), BF), pltpu.SemaphoreType.DMA((BLOCKS,))]
    far = [hbm(BLOCKS, ROWS, 256 + D)]
    ins = [hot_gated, outs]
    return run(mixed_kernel, "mixed_sum", 0.6, ins, far, scratch, far_out=1, limit=10, idx=idx)[0]


def add_pairs_kernel(same, other, *outs):
    for off in range(4):
        outs[off][...] = (same[off].astype(F32) + other[off].astype(F32)).astype(BF)


def add_pairs(same, other):
    return run(
        add_pairs_kernel, "add_pairs", 0.3, [same, other], [vmem(*same.shape[1:])] * 4, limit=4
    )


def stage_kernel(idx, *refs):
    far = (refs[:5], refs[5:10])
    outs_far = (refs[10:14], refs[14:18])
    bufs = (refs[18:23], refs[23:28])
    outs = (refs[28:32], refs[32:36])
    totals = refs[36:38]
    in_sems, out_sems = refs[38:40]
    own, from_below, from_above, late_below, late_above = range(5)
    needed = []
    loads = []
    for n in range(LOCAL):
        if n < HALF:
            places = ((own, n), (late_below, n), (from_above, n + HALF))
        else:
            places = ((own, n), (from_below, n), (late_above, n - HALF))
        needed.append(places)
        loads.append(
            [
                fetch(
                    [far[path][item].at[at] for item, at in places],
                    [bufs[path][item].at[at] for item, at in places],
                    in_sems.at[path, n],
                )
                for path in range(2)
            ]
        )
    stores = []
    for n in range(LOCAL):
        for path in range(2):
            for copy in loads[n][path]:
                copy.wait()
            parts = [bufs[path][item][at].astype(F32) for item, at in needed[n]]
            totals[path][...] = (parts[0] + parts[1] + parts[2]).astype(BF)
            (cut_along_z, cut_along_x)[path](idx, totals[path], outs[path], n)
            stores += fetch(
                [item.at[n] for item in outs[path]],
                [item.at[n] for item in outs_far[path]],
                out_sems.at[path, n],
            )
    for copy in stores:
        copy.wait()


def stage_sums(idx, x_parts, z_parts):
    parts = [*x_parts, *z_parts]
    shapes = [(LOCAL, QROWS, FE)] * 4 + [(LOCAL, ZROWS, FE)] * 4
    scratch = [pltpu.VMEM(part.shape, BF) for part in parts]
    scratch += [pltpu.VMEM(shape, BF) for shape in shapes]
    scratch += [pltpu.VMEM(x_parts[0].shape[1:], BF), pltpu.VMEM(z_parts[0].shape[1:], BF)]
    scratch += [pltpu.SemaphoreType.DMA((2, LOCAL, 3)), pltpu.SemaphoreType.DMA((2, LOCAL, 4))]
    results = run(
        stage_kernel,
        "stage_sums",
        400,
        parts,
        [hbm(*shape) for shape in shapes],
        scratch,
        far_in=10,
        far_out=8,
        limit=FAR_LIMIT,
        idx=idx,
    )
    return results[:4], results[4:]


def cut_along_z(idx, total, outs, n):
    gate_rows = D // 16
    down_rows = FE // 16
    for k in range(4):
        at = (idx[12] + k) % 4
        start = pl.multiple_of(at * gate_rows, gate_rows)
        outs[k][n, :gate_rows, :] = total[pl.ds(start, gate_rows), :]
        for m in range(LEFT // FE):
            start = pl.multiple_of(D // 4 + m * (FE // 4) + at * down_rows, down_rows)
            to = gate_rows + m * down_rows
            outs[k][n, to : to + down_rows, :] = total[pl.ds(start, down_rows), :]


def cut_along_x(idx, total, outs, n):
    for k in range(4):
        outs[k][n] = total[pl.ds((idx[11] + k) % 4, 1)][0]


SEND_ROWS = (QROWS + ZROWS) // 2


def finish_kernel(idx, *refs):
    far = refs[:8]
    outs_far = refs[8:11]
    send_far = refs[11]
    bufs = refs[12:20]
    keep_gate, keep_up, keep_down, send = keeps = refs[20:24]
    x_sum, z_sum, in_sems, out_sems = refs[24:28]
    loads = [
        fetch([item.at[n] for item in far], [item.at[n] for item in bufs], in_sems.at[n])
        for n in range(LOCAL)
    ]
    big = D // 16
    small = big // 2
    tiny = FE // 32
    mine = idx[9]
    theirs = 1 - mine
    stores = []
    for n in range(LOCAL):
        for copy in loads[n]:
            copy.wait()
        acc = bufs[0][n].astype(F32)
        for part in bufs[1:4]:
            acc = acc + part[n].astype(F32)
        x_sum[...] = acc
        acc = bufs[4][n].astype(F32)
        for part in bufs[5:8]:
            acc = acc + part[n].astype(F32)
        z_sum[...] = acc
        here = pl.ds(pl.multiple_of(mine * small, small), small)
        there = pl.ds(pl.multiple_of(theirs * small, small), small)
        keep_gate[n] = x_sum[here, :]
        keep_up[n] = z_sum[here, :]
        send[n, :small, :] = x_sum[there, :].astype(BF)
        send[n, small:big, :] = z_sum[there, :].astype(BF)
        for m in range(D // FE):
            source, at = (x_sum, m) if m < LEFT // FE else (z_sum, m - LEFT // FE)
            first = big + at * 2 * tiny
            here = pl.ds(pl.multiple_of(first + mine * tiny, tiny), tiny)
            there = pl.ds(pl.multiple_of(first + theirs * tiny, tiny), tiny)
            keep_down[n, :, m * FE : (m + 1) * FE] = source[here, :]
            send[n, big + m * tiny : big + (m + 1) * tiny, :] = source[there, :].astype(BF)
        targets = [item.at[mine * LOCAL + n] for item in outs_far] + [send_far.at[n]]
        stores += fetch([item.at[n] for item in keeps], targets, out_sems.at[n])
    for copy in stores:
        copy.wait()


def finish(idx, parts):
    outs = [
        hbm(2 * LOCAL, D // 32, FE, dtype=F32),
        hbm(2 * LOCAL, D // 32, FE, dtype=F32),
        hbm(2 * LOCAL, FE // 32, D, dtype=F32),
        hbm(LOCAL, SEND_ROWS, FE),
    ]
    scratch = [pltpu.VMEM(part.shape, BF) for part in parts]
    scratch += [
        pltpu.VMEM((LOCAL, D // 32, FE), F32),
        pltpu.VMEM((LOCAL, D // 32, FE), F32),
        pltpu.VMEM((LOCAL, FE // 32, D), F32),
        pltpu.VMEM((LOCAL, SEND_ROWS, FE), BF),
        pltpu.VMEM((QROWS, FE), F32),
        pltpu.VMEM((ZROWS, FE), F32),
        pltpu.SemaphoreType.DMA((LOCAL, 8)),
        pltpu.SemaphoreType.DMA((LOCAL, 4)),
    ]
    return run(
        finish_kernel,
        "finish",
        1,
        parts,
        outs,
        scratch,
        far_in=8,
        far_out=4,
        limit=FAR_LIMIT,
        idx=idx,
    )


def assemble_kernel(idx, got, gate_in, up_in, down_in, *refs):
    outs_far = refs[:3]
    gate, up, down, out_sems = refs[3:7]
    small = D // 32
    tiny = FE // 32
    stores = []
    for n in range(LOCAL):
        gate[n] = got[n, :small, :].astype(F32)
        up[n] = got[n, small : 2 * small, :].astype(F32)
        down[n, :, :FE] = got[n, 2 * small : 2 * small + tiny, :].astype(F32)
        down[n, :, FE:] = got[n, 2 * small + tiny :, :].astype(F32)
        targets = [item.at[(1 - idx[9]) * LOCAL + n] for item in outs_far]
        stores += fetch([gate.at[n], up.at[n], down.at[n]], targets, out_sems.at[n])
    for copy in stores:
        copy.wait()


def assemble(idx, got, results):
    outs = [hbm(*item.shape, dtype=F32) for item in results]
    scratch = [
        pltpu.VMEM((LOCAL, D // 32, FE), F32),
        pltpu.VMEM((LOCAL, D // 32, FE), F32),
        pltpu.VMEM((LOCAL, FE // 32, D), F32),
        pltpu.SemaphoreType.DMA((LOCAL, 3)),
    ]
    return run(
        assemble_kernel,
        "assemble",
        1,
        [got, *results],
        outs,
        scratch,
        far_in=3,
        far_out=3,
        limit=8,
        idx=idx,
        aliases={2: 0, 3: 1, 4: 2},
    )


def middle_kernel(*refs):
    parts = refs[:4]
    h_ref, gate_ref, dy_ref, gain_ref, router_t, w_out = refs[4:10]
    dh_ref, send_ref, side_ref = refs[10:13]
    total = parts[0][...].astype(F32)
    for part in parts[1:]:
        total = total + part[...].astype(F32)
    extra = total[:, D:]
    d_gate = extra + pltpu.roll(extra, 128 - EXPERTS, 1)
    gate = gate_ref[...]
    d_chosen = gate * (d_gate - jnp.sum(gate * d_gate, axis=1, keepdims=True))
    d_logits = d_chosen.astype(BF)
    d_mlp = total[:, :D] + mm(d_logits, router_t[...])
    h = h_ref[...]
    gain = gain_ref[...].astype(F32)
    scale = lax.rsqrt(jnp.mean(h * h, axis=1, keepdims=True) + EPS)
    normed = h * scale
    mlp_in = (normed * gain).astype(BF)
    scaled = d_mlp * gain
    d_h = (
        dy_ref[...].astype(F32)
        + scale * scaled
        - h * (scale * scale * scale) * jnp.mean(scaled * h, axis=1, keepdims=True)
    )
    dh_ref[...] = d_h
    d_branch = d_h.astype(BF)
    d_attn = mm_nt(d_branch, w_out[...]).astype(BF)
    for b in range(BLOCKS):
        cols = slice(b * 128, (b + 1) * 128)
        send_ref[b, :, :128] = d_attn[:, cols]
        send_ref[b, :, 128:] = d_branch[:, cols]
    router = mm_tn(mlp_in, d_logits)
    d_gain = jnp.sum(d_mlp * normed, axis=0, keepdims=True)
    column = jnp.transpose(jnp.broadcast_to(d_gain, (128, D)))
    lane = lax.broadcasted_iota(jnp.int32, (D, 128), 1)
    side_ref[...] = jnp.where(lane == GAIN_LANE, column, router).astype(BF)


def middle(parts, h_own, gate_own, dy, gain, router_t, w_out):
    shapes = [((ROWS, D), F32), ((BLOCKS, ROWS, 256), BF), ((D, 128), BF)]

    def kernel(*refs):
        inputs = refs[:10]
        far = refs[10:13]
        bufs = refs[13:16]
        middle_kernel(*inputs, *bufs)
        for copy in fetch(bufs, far, refs[16]):
            copy.wait()

    outs = [hbm(*shape, dtype=kind) for shape, kind in shapes]
    scratch = [pltpu.VMEM(shape, kind) for shape, kind in shapes] + [pltpu.SemaphoreType.DMA((3,))]
    ins = [*parts, h_own, gate_own, dy, gain, router_t, w_out]
    return run(kernel, "middle", 100, ins, outs, scratch, far_out=3, limit=10)


def attend_back_kernel(idx, *refs):
    early_far = refs[:6]
    far = refs[6:10]
    pack, dense_far = refs[11:13]
    early = refs[13:19]
    p_ref, attn_in, ao_all, side_ref, dk_acc, dv_acc, dqkv_ref, dense = refs[19:27]
    sems, early_sems, tables_sems = refs[27:30]
    grads, q_ref, k_ref, v_ref, cos_ref, sin_ref = early
    early_copies = fetch(early_far[:4], early[:4], early_sems)
    table_copies = fetch(early_far[4:], early[4:], tables_sems)
    p_copies = [
        pltpu.make_async_copy(far[0].at[i], p_ref.at[i], sems.at[i]) for i in range(BLOCKS)
    ]
    ao_copy = pltpu.make_async_copy(far[2], ao_all, sems.at[BLOCKS])
    in_copy = pltpu.make_async_copy(far[1], attn_in, sems.at[BLOCKS + 1])
    for copy in p_copies:
        copy.start()
    side_copy = pltpu.make_async_copy(far[3], side_ref, sems.at[2 * BLOCKS + 3])
    ao_copy.start()
    in_copy.start()
    side_copy.start()
    dk_acc[...] = jnp.zeros((LEN, HD), F32)
    dv_acc[...] = jnp.zeros((LEN, HD), F32)
    for copy in early_copies:
        copy.wait()
    for i in range(BLOCKS):
        lo = max(0, i - WIN // ROWS) * ROWS
        hi = (i + 1) * ROWS
        span = hi - lo
        rows = slice(i * ROWS, hi)
        do2 = jnp.concatenate([grads[i, :, :HD], grads[i, :, HD : 2 * HD]], axis=0)
        q2 = jnp.concatenate([q_ref[rows, :HD], q_ref[rows, HD:]], axis=0)
        p_copies[i].wait()
        probs_low = p_ref[i, :, :span]
        probs = probs_low.astype(F32)
        d_probs = mm_nt(do2, v_ref[lo:hi, :])
        weighted = probs * d_probs
        d_scores = (weighted - probs * jnp.sum(weighted, axis=1, keepdims=True)).astype(BF)
        dq = mm(d_scores, k_ref[lo:hi, :]) * HD**-0.5
        dk_acc[lo:hi, :] += mm_tn(d_scores, q2)
        dv_acc[lo:hi, :] += mm_tn(probs_low, do2)
        dq = jnp.concatenate([dq[:ROWS], dq[ROWS:]], axis=1).astype(BF).astype(F32)
        if i == 0:
            for copy in table_copies:
                copy.wait()
        dq = dq * cos_ref[rows, :] - swap_halves(dq) * sin_ref[rows, :]
        dqkv_ref[rows, : 2 * HD] = dq.astype(BF)
    pair = jnp.concatenate([dk_acc[...], dv_acc[...]], axis=1).astype(BF).astype(F32)
    turned = pair * cos_ref[...] - swap_halves(pair) * sin_ref[...]
    lane = lax.broadcasted_iota(jnp.int32, pair.shape, 1)
    dqkv_ref[:, 2 * HD :] = jnp.where(lane < HD, turned, pair).astype(BF)
    dqkv_copies = []
    for r in range(BLOCKS):
        copy = pltpu.make_async_copy(
            dqkv_ref.at[pl.ds(r * ROWS, ROWS), :],
            pack.at[r, :, pl.ds(0, 256)],
            sems.at[BLOCKS + 3 + r],
        )
        copy.start()
        dqkv_copies.append(copy)
    in_copy.wait()
    ao_copy.wait()
    half = D // 2
    side_copy.wait()
    d_branch = jnp.concatenate([grads[b, :, 128:] for b in range(BLOCKS)], axis=0)
    for part in range(2):
        rows = slice(part * half, (part + 1) * half)
        left = mm_tn(attn_in[:, rows], dqkv_ref[...])
        right = jnp.concatenate(
            [mm_tn(ao_all[:, rows], d_branch), side_ref[rows, :].astype(F32)], axis=1
        )
        both = jnp.concatenate([left.reshape(-1, 8, 256), right.reshape(-1, 8, 256)], axis=1)
        dense[part * (half // 8) : (part + 1) * (half // 8)] = both.astype(BF)
    dense_copy = pltpu.make_async_copy(dense, dense_far, sems.at[BLOCKS + 2])
    dense_copy.start()
    for copy in dqkv_copies:
        copy.wait()
    dense_copy.wait()


def attend_back(idx, grads, p, q, k, v, attn_in, ao_all, side, cos_tab, sin_tab, pack):
    early = [grads, q, k, v, cos_tab, sin_tab]
    outs = [hbm(*pack.shape), hbm(D // 8, 16, 256)]
    scratch = [pltpu.VMEM(item.shape, item.dtype) for item in early]
    scratch += [
        pltpu.VMEM(p.shape, BF),
        pltpu.VMEM((LEN, D), BF),
        pltpu.VMEM((LEN, D), BF),
        pltpu.VMEM((D, 128), BF),
        pltpu.VMEM((LEN, HD), F32),
        pltpu.VMEM((LEN, HD), F32),
        pltpu.VMEM((LEN, 256), BF),
        pltpu.VMEM((D // 8, 16, 256), BF),
        pltpu.SemaphoreType.DMA((2 * BLOCKS + 4,)),
        pltpu.SemaphoreType.DMA((4,)),
        pltpu.SemaphoreType.DMA((2,)),
    ]
    ins = [*early, p, attn_in, ao_all, side, pack]
    return run(
        attend_back_kernel,
        "attend_back",
        8,
        ins,
        outs,
        scratch,
        far_in=11,
        far_out=2,
        limit=FAR_LIMIT,
        idx=idx,
        aliases={11: 0},
    )


def input_grad_kernel(pack, *refs):
    far = refs[:7]
    outs_far = refs[7:9]
    bufs = refs[9:16]
    out, block, dq, dk, dv, early_sems, late_sems, out_sems = refs[16:24]
    early = fetch(far[:4], bufs[:4], early_sems)
    late = fetch(far[4:], bufs[4:], late_sems)
    x_ref, dh_ref, gain_ref, h_own, w_query, w_key, w_value = bufs
    for b in range(BLOCKS):
        dq[:, b * 128 : (b + 1) * 128] = pack[b, :, :128]
    for b in range(0, BLOCKS, 2):
        first = pack[b, :, 128:256].astype(F32)
        second = pack[b + 1, :, 128:256].astype(F32)
        cols = slice(b * HD, (b + 2) * HD)
        dk[:, cols] = jnp.concatenate([first[:, :HD], second[:, :HD]], axis=1).astype(BF)
        dv[:, cols] = jnp.concatenate([first[:, HD:], second[:, HD:]], axis=1).astype(BF)
    for copy in early:
        copy.wait()
    total = h_own[...]
    for b in range(BLOCKS):
        total = total + pack[b, :, 256:].astype(F32)
    block[...] = total.astype(BF)
    for copy in late:
        copy.wait()
    d_in = mm_nt(dq[...], w_query[...]) + mm_nt(dk[...], w_key[...]) + mm_nt(dv[...], w_value[...])
    x = x_ref[...].astype(F32)
    scale = lax.rsqrt(jnp.mean(x * x, axis=1, keepdims=True) + EPS)
    scaled = d_in * gain_ref[...]
    out[...] = (
        dh_ref[...]
        + scale * scaled
        - x * (scale * scale * scale) * jnp.mean(scaled * x, axis=1, keepdims=True)
    ).astype(BF)
    for copy in fetch((out, block), outs_far, out_sems):
        copy.wait()


def input_grad(pack, x, d_h, gain, h_own, w_query, w_key, w_value):
    ins = [pack, x, d_h, gain, h_own, w_query, w_key, w_value]
    scratch = [pltpu.VMEM(item.shape, item.dtype) for item in ins[1:]]
    scratch += [
        pltpu.VMEM((ROWS, D), BF),
        pltpu.VMEM((ROWS, D), BF),
        pltpu.VMEM((ROWS, H * HD), BF),
        pltpu.VMEM((ROWS, KVH * HD), BF),
        pltpu.VMEM((ROWS, KVH * HD), BF),
        pltpu.SemaphoreType.DMA((4,)),
        pltpu.SemaphoreType.DMA((3,)),
        pltpu.SemaphoreType.DMA((2,)),
    ]
    return run(
        input_grad_kernel,
        "input_grad",
        1,
        ins,
        [hbm(ROWS, D)] * 2,
        scratch,
        far_in=len(ins) - 1,
        far_out=2,
        limit=40,
    )


def dense_out_kernel(idx, dense, w_query, w_key, w_value, gain, *refs):
    dq, dk, dv, do, router, gains, turned = refs
    total = jnp.sum(dense[...].astype(F32).reshape(-1, BLOCKS, 16, 256), axis=0)
    for b in range(BLOCKS):
        dq[:, b * 128 : (b + 1) * 128] = total[b, :8, :128]
        do[:, b * 128 : (b + 1) * 128] = total[b, 8:, :128]
    for b in range(0, BLOCKS, 2):
        first = total[b, :8, 128:]
        second = total[b + 1, :8, 128:]
        cols = slice(b * HD, (b + 2) * HD)
        dk[:, cols] = jnp.concatenate([first[:, :HD], second[:, :HD]], axis=1)
        dv[:, cols] = jnp.concatenate([first[:, HD:], second[:, HD:]], axis=1)
    side = jnp.sum(total[:, 8:, 128:], axis=0)
    router[...] = side[:, :EXPERTS]
    dot = jnp.zeros((8, 1), F32)
    for weight, grad in ((w_query, dq), (w_key, dk), (w_value, dv)):
        dot = dot + jnp.sum(weight[...] * grad[...], axis=1, keepdims=True)
    chunk = pl.ds(pl.multiple_of(idx[16] * 128, 128), 128)
    turned[...] = jnp.transpose(jnp.broadcast_to(gain[:, chunk], (128, 128)))
    gain_rows = turned[pl.ds(pl.multiple_of(idx[17] * 8, 8), 8), 0:1]
    lane = lax.broadcasted_iota(jnp.int32, (8, 128), 1)
    both = jnp.where(lane == GAIN_LANE, side, dot / gain_rows)
    turned[:8, :] = both
    flat = jnp.transpose(turned[...])
    gains[...] = flat[GAIN_LANE - 8 : GAIN_LANE + 8, :]


def dense_out(idx, dense, w_query, w_key, w_value, gain):
    outs = [
        auto(8, H * HD, dtype=F32),
        auto(8, KVH * HD, dtype=F32),
        auto(8, KVH * HD, dtype=F32),
        auto(8, D, dtype=F32),
        auto(8, EXPERTS, dtype=F32),
        auto(16, 128, dtype=F32),
    ]
    ins = [dense, w_query, w_key, w_value, gain]
    scratch = [pltpu.VMEM((128, 128), F32)]
    return run(dense_out_kernel, "dense_out", 1, ins, outs, scratch, limit=8, idx=idx)


def from_x(value, off):
    size = lax.axis_size("x")
    return lax.ppermute(value, "x", [(i, (i + off) % size) for i in range(size)])


def from_z(value, off):
    size = lax.axis_size("z")
    return lax.ppermute(value, "z", [(i, (i + off) % size) for i in range(size)])


def along_y(value, off):
    route = []
    for y in range(4):
        to = (y + off) % 4
        route.append(((y % 2) * 2 + y // 2, (to % 2) * 2 + to // 2))
    return lax.ppermute(value, ("yl", "yh"), route)


def other_core(value):
    return lax.ppermute(value, "c", [(0, 1), (1, 0)])


def near_ring(value):
    return [value] + [along_y(value, -off) for off in (1, 2, 3)]


def both_cores(near):
    far = [other_core(item) for item in near]
    return [item for pair in zip(near, far) for item in pair]


def gather_ring(value):
    return both_cores(near_ring(value))


def reduce_ring(pieces):
    return [pieces[0]] + [along_y(pieces[off], off) for off in (1, 2, 3)]


def scatter_parts(parts, send):
    return [parts[0]] + [send(parts[k], k) for k in (1, 2, 3)]


def together(*values):
    return lax.optimization_barrier(values)


def after(values, *earlier):
    return lax.optimization_barrier((values, earlier))[0]


def local(
    tokens,
    segments,
    routes,
    drop_order,
    gain_attn,
    w_query,
    w_key,
    w_value,
    w_out,
    gain_mlp,
    w_router,
    w_gate,
    w_up,
    w_down,
    cotangent,
):
    x_at = lax.axis_index("x")
    z_at = lax.axis_index("z")
    yl = lax.axis_index("yl")
    yh = lax.axis_index("yh")
    core = lax.axis_index("c")
    y_at = yh * 2 + yl
    own = yl * 4 + yh * 2 + core
    expert_at = yh * 2 + core

    entries = []
    for off in range(4):
        y = (y_at + off) % 4
        for dc in range(2):
            entries.append((y % 2) * 4 + (y // 2) * 2 + (core + dc) % 2)
    entries += [own, yl, expert_at, x_at, z_at, y_at, core, expert_at * 8 + yl * LOCAL]
    first_row = ((x_at * 4 + z_at) * 8 + own) * 8
    entries += [first_row // 128, first_row % 128 // 8]
    idx = jnp.stack([jnp.asarray(entry, jnp.int32) for entry in entries])

    cos_np, sin_np = rotary_tables()
    cos_tab = jnp.asarray(cos_np)
    sin_tab = jnp.asarray(sin_np)
    gain_one = gain_attn.astype(F32).reshape(1, D)
    gain_two = gain_mlp.astype(F32).reshape(1, D)
    router_t = jnp.pad(w_router.T, ((0, 128 - EXPERTS), (0, 0)))

    def columns(weight, block):
        return lax.dynamic_slice_in_dim(weight, block * 128, 128, 1)

    def out_rows(weight):
        return lax.dynamic_slice_in_dim(weight, first_row, 8, 0).astype(F32)

    wq_cols = columns(w_query, own)
    wk_cols = columns(w_key, own // 2)
    wv_cols = columns(w_value, own // 2)
    finals = [out_rows(w_query), out_rows(w_key), out_rows(w_value)]
    early = [idx, gain_one, gain_two, router_t, wq_cols, wk_cols, wv_cols, finals]

    seg_cols = jnp.broadcast_to(segments.astype(BF)[:, None], (ROWS, AUG - D))
    x_near = near_ring(jnp.concatenate([tokens, seg_cols], axis=1))
    slot_own = slots(routes.T, drop_order)
    x_near, slot_own, early = together(x_near, slot_own, early)
    idx, gain_one, gain_two, router_t, wq_cols, wk_cols, wv_cols, finals = early
    xs = both_cores(x_near)
    dy_near = near_ring(after(cotangent, *xs))

    ao, attn_in, q, k, v, p = attend(
        idx, xs, slot_own, gain_one, wq_cols, wk_cols, wv_cols, cos_tab, sin_tab
    )
    dys = both_cores(dy_near)
    aos = gather_ring(after(ao, *dy_near))
    mlp_in, slot_t, gate_t, h_own, gate_own, ao_all = project(
        idx, xs, aos, w_out, gain_two, router_t
    )
    rows, act, d_out, d_gh, d_up, hot_gated, outs, dm_same, dm_other = experts(
        idx, mlp_in, dys, slot_t, gate_t, w_gate, w_up, w_down
    )

    got = other_core(dm_other)
    pack = mixed_sum(idx, hot_gated, outs)
    pack, got = together(pack, got)
    dm_pieces = add_pairs(dm_same, got)
    dm_parts = reduce_ring(dm_pieces)
    (x_up, x_down, *x_keep), (z_up, z_down, *z_keep) = weight_grads(
        idx, after(rows, *dm_pieces), act, d_out, d_gh, d_up
    )
    x_below = from_x(x_up, 1)
    x_above = from_x(x_down, 3)
    z_keep, dm_parts = together(z_keep, dm_parts)
    d_h, to_heads, side = middle(
        dm_parts, h_own, gate_own, cotangent, gain_two, router_t, w_out
    )
    z_below = from_z(after(z_up, to_heads), 1)
    z_above = from_z(after(z_down, to_heads), 3)
    grads = lax.all_to_all(to_heads, GROUP, split_axis=0, concat_axis=0, tiled=True)
    pack, dense = attend_back(
        idx, grads, p, q, k, v, attn_in, ao_all, side, cos_tab, sin_tab, pack
    )
    x_below, x_above, z_below, z_above = after([x_below, x_above, z_below, z_above], pack)
    dense = lax.all_to_all(
        dense, ("x", "z", "yl", "yh", "c"), split_axis=0, concat_axis=0, tiled=True
    )

    relayed = relay(
        [x_keep[1], x_below, x_keep[2], x_above], [z_keep[1], z_below, z_keep[2], z_above]
    )
    x_late = [from_x(relayed[0], 1), from_x(relayed[1], 3)]
    z_late = [from_z(relayed[2], 1), from_z(relayed[3], 3)]
    pack = lax.all_to_all(
        after(pack, dense, *relayed), GROUP, split_axis=0, concat_axis=0, tiled=True
    )
    dense_rows = dense_out(idx, dense, *finals, gain_one)
    x_late, z_late = together(x_late, z_late)
    x_pieces, z_pieces = stage_sums(
        idx, [x_keep[0], x_below, x_above, *x_late], [z_keep[0], z_below, z_above, *z_late]
    )
    x_second = scatter_parts(x_pieces, from_z)
    z_second = scatter_parts(z_pieces, from_x)
    d_tokens, block_out = input_grad(
        after(pack, *x_pieces), tokens, d_h, gain_one, h_own, w_query, w_key, w_value
    )
    d_tokens, x_second, z_second, dense_rows = together(d_tokens, x_second, z_second, dense_rows)

    *results, sent = finish(idx, [*x_second, *z_second])
    got = lax.ppermute(sent, "yl", [(0, 1), (1, 0)])
    d_w_gate, d_w_up, d_w_down = assemble(idx, got, results)
    d_w_query, d_w_key, d_w_value, d_w_out, d_w_router, gains = dense_rows
    d_gain_attn = gains[0, :8]
    d_gain_mlp = gains[8, :8]

    return (
        block_out,
        d_tokens,
        d_gain_attn,
        d_w_query,
        d_w_key,
        d_w_value,
        d_w_out,
        d_gain_mlp,
        d_w_router,
        d_w_gate,
        d_w_up,
        d_w_down,
    )


def solution(mesh):
    side = 4 if mesh.shape["dp"] == 32 else 1
    names = ("x", "z", "yl", "yh", "c")
    grid = Mesh(mesh.devices.reshape(side, side, 2, 2, 2), names)
    tokens = names
    experts_axes = ("yh", "c")
    dp = ("x", "z", "yl")
    in_specs = (
        P(tokens, None),
        P(tokens),
        P(tokens, None),
        P(tokens, None),
        P(),
        P(),
        P(),
        P(),
        P(),
        P(),
        P(),
        P(experts_axes, None, None),
        P(experts_axes, None, None),
        P(experts_axes, None, None),
        P(tokens, None),
    )
    out_specs = (
        P(tokens, None),
        P(tokens, None),
        P(tokens),
        P(tokens, None),
        P(tokens, None),
        P(tokens, None),
        P(tokens, None),
        P(tokens),
        P(tokens, None),
        P(experts_axes, dp, None),
        P(experts_axes, dp, None),
        P(experts_axes, dp, None),
    )
    return jax.shard_map(local, mesh=grid, in_specs=in_specs, out_specs=out_specs, check_vma=False)
```

```python
import functools

import jax
import jax.numpy as jnp
import numpy as np
from jax import lax
from jax.experimental import pallas as pl
from jax.experimental.pallas import tpu as pltpu
from jax.sharding import Mesh, PartitionSpec as P

H = 16
KVH = 8
HD = 64
D = 1024
FE = 512
TOPK = 8
EXPERTS = 32
CAP = 36
ROWS = 128
LEN = 1024
BLOCKS = LEN // ROWS
WIN = 512
LOCAL = 4
PAIRS = BLOCKS // 2
SLOTS = 80
EROWS = PAIRS * SLOTS
AUG = D + 128
GAIN_LANE = 32
FAR_LIMIT = 56
SHARE = 0.1
EPS = 1e-06
THETA = 10000.0
NEG = -1e30
BF = jnp.bfloat16
F32 = jnp.float32
GROUP = ("yl", "yh", "c")


def mm(left, right):
    return jnp.dot(left, right, preferred_element_type=F32)


def mm_nt(left, right):
    return lax.dot_general(left, right, (((1,), (1,)), ((), ())), preferred_element_type=F32)


def mm_tn(left, right):
    return lax.dot_general(left, right, (((0,), (0,)), ((), ())), preferred_element_type=F32)


def rotary_tables():
    half = HD // 2
    frequency = THETA ** (-np.arange(half, dtype=np.float64) * 2.0 / HD)
    angles = np.arange(LEN, dtype=np.float64)[:, None] * frequency[None, :]
    cosine = np.cos(angles)
    sine = np.sin(angles)
    cos_full = np.concatenate([cosine] * 4, axis=1).astype(np.float32)
    sin_full = np.concatenate([-sine, sine, -sine, sine], axis=1).astype(np.float32)
    return cos_full, sin_full


def swap_halves(array_in):
    half = HD // 2
    lane = lax.broadcasted_iota(jnp.int32, array_in.shape, 1)
    ahead = pltpu.roll(array_in, array_in.shape[1] - half, 1)
    behind = pltpu.roll(array_in, half, 1)
    return jnp.where(lane % HD < half, ahead, behind)


def vmem(*shape, dtype=BF):
    return pltpu.VMEM(shape, dtype)


def hbm(*shape, dtype=BF):
    return pltpu.HBM(shape, dtype)


def auto(*shape, dtype=BF):
    return jax.ShapeDtypeStruct(shape, dtype)


def cost(micros):
    return pl.CostEstimate(
        flops=int(micros * 1.15e9 * SHARE), bytes_accessed=int(micros * 1e6), transcendentals=0
    )


def run(
    kernel,
    name,
    micros,
    ins,
    outs,
    scratch=(),
    far_in=0,
    far_out=0,
    limit=24,
    idx=None,
    aliases=None,
):
    inside = pl.BlockSpec(memory_space=pltpu.VMEM)
    outside = pl.BlockSpec(memory_space=pltpu.HBM)
    in_specs = [inside] * (len(ins) - far_in) + [outside] * far_in
    operands = list(ins)
    if idx is not None:
        in_specs = [pl.BlockSpec(memory_space=pltpu.SMEM)] + in_specs
        operands = [idx] + operands
    return pl.pallas_call(
        kernel,
        out_shape=list(outs),
        in_specs=in_specs,
        out_specs=[inside] * (len(outs) - far_out) + [outside] * far_out,
        scratch_shapes=list(scratch),
        input_output_aliases=aliases or {},
        compiler_params=pltpu.CompilerParams(vmem_limit_bytes=limit * 1024 * 1024),
        cost_estimate=cost(micros),
        name=name,
    )(*operands)


def run_far(kernel, name, micros, ins, outs, scratch=(), idx=None):
    count = len(ins)
    given = 0 if idx is None else 1

    def body(*refs):
        lead = refs[:given]
        sources = refs[given : given + count]
        targets = refs[given + count : given + count + len(outs)]
        rest = refs[given + count + len(outs) :]
        in_bufs = rest[:count]
        out_bufs = rest[count : count + len(outs)]
        in_sems, out_sems = rest[count + len(outs) : count + len(outs) + 2]
        for copy in fetch(sources, in_bufs, in_sems):
            copy.wait()
        kernel(*lead, *in_bufs, *out_bufs, *rest[count + len(outs) + 2 :])
        for copy in fetch(out_bufs, targets, out_sems):
            copy.wait()

    bufs = [pltpu.VMEM(item.shape, item.dtype) for item in ins]
    bufs += [pltpu.VMEM(item.shape, item.dtype) for item in outs]
    bufs += [pltpu.SemaphoreType.DMA((count,)), pltpu.SemaphoreType.DMA((len(outs),))]
    return run(
        body,
        name,
        micros,
        ins,
        outs,
        bufs + list(scratch),
        far_in=count,
        far_out=len(outs),
        limit=FAR_LIMIT,
        idx=idx,
    )


def fetch(sources, targets, sems):
    copies = [
        pltpu.make_async_copy(source, target, sems.at[n])
        for n, (source, target) in enumerate(zip(sources, targets))
    ]
    for copy in copies:
        copy.start()
    return copies


def slots_kernel(routes_ref, order_ref, meta_ref, place_ref):
    order = order_ref[...]
    index = lax.broadcasted_iota(jnp.int32, (1, ROWS * TOPK), 1)
    token_of = order // TOPK
    choice_of = order - token_of * TOPK
    at_token = (token_of == lax.broadcasted_iota(jnp.int32, (ROWS, ROWS * TOPK), 0)).astype(F32)
    choice = lax.broadcasted_iota(jnp.int32, (2 * TOPK, ROWS * TOPK), 0)
    high = index // 32
    low = index - high * 32
    part = jnp.where(choice < TOPK, high, low).astype(F32)
    choice_mod = jnp.where(choice < TOPK, choice, choice - TOPK)
    table = jnp.where(choice_mod == choice_of, part, 0.0)
    found = mm_nt(at_token.astype(BF), table.astype(BF))
    place = found[:, :TOPK] * 32.0 + found[:, TOPK:]
    lane = lax.broadcasted_iota(jnp.int32, (ROWS, 128), 1)
    wide = jnp.concatenate(
        [
            routes_ref[...].astype(F32),
            jnp.zeros((ROWS - TOPK, ROWS), F32),
        ],
        axis=0,
    )
    turned = jnp.transpose(wide)
    lane_f = lane.astype(F32)
    placed = jnp.full((ROWS, 128), 4096.0, F32)
    for k in range(TOPK):
        placed = jnp.where(turned[:, k : k + 1] == lane_f, place[:, k : k + 1], placed)
    place_ref[...] = placed

    def count(step, total):
        for inner in range(8):
            row = place_ref[pl.ds(step * 8 + inner, 1), :]
            total = total + jnp.where(row < placed, 1.0, 0.0)
        return total

    rank = lax.fori_loop(0, ROWS // 8, count, jnp.zeros((ROWS, 128), F32))
    slot = jnp.where(placed < 4000.0, jnp.where(rank < CAP, rank, -1.0), -2.0)
    meta_ref[...] = jnp.transpose(slot)[:EXPERTS, :].astype(BF)


def slots(routes_t, drop_order):
    return run(
        slots_kernel,
        "slots",
        3,
        [routes_t, drop_order],
        [auto(EXPERTS, ROWS)],
        [pltpu.VMEM((ROWS, 128), F32)],
        limit=8,
    )[0]


def attend_kernel(idx, *refs):
    xs = refs[:8]
    slots_ref, gain, wq, wk, wv, cos_ref, sin_ref = refs[8:15]
    out_ref = refs[15]
    far = refs[16:21]
    attn_in, q_ref, k_ref, v_ref, p_ref, seg_row, seg_col, v_turned, sems = refs[21:30]
    near = (attn_in, q_ref, k_ref, v_ref)
    copies = [pltpu.make_async_copy(near[n], far[n], sems.at[n]) for n in range(4)]
    gain_full = gain[...]
    for r in range(BLOCKS):
        rows = pl.ds(pl.multiple_of(idx[r] * ROWS, ROWS), ROWS)
        x = xs[r][:, :D].astype(F32)
        scale = lax.rsqrt(jnp.mean(x * x, axis=1, keepdims=True) + EPS)
        attn_in[rows, :] = (x * scale * gain_full).astype(BF)
        segs = xs[r][:, D:].astype(F32)
        seg_col[rows, :] = segs
        seg_row[:, rows] = jnp.transpose(segs)[:8, :]
    copies[0].start()
    out_ref[LEN:, :] = slots_ref[...]
    odd = (idx[8] % 2) == 1
    half = LEN // 2
    for part in range(2):
        rows = slice(part * half, (part + 1) * half)
        block = attn_in[rows, :]
        cosine = cos_ref[rows, :]
        sine = sin_ref[rows, :]
        q = mm(block, wq[...])
        q = q * cosine + swap_halves(q) * sine
        q_ref[rows, :] = (q.astype(BF).astype(F32) * HD**-0.5).astype(BF)
        k = mm(block, wk[...])
        k = jnp.where(odd, pltpu.roll(k, HD, 1), k)
        k = k * cosine + swap_halves(k) * sine
        k_ref[rows, :] = k[:, :HD].astype(BF)
        v = mm(block, wv[...])
        v = jnp.where(odd, pltpu.roll(v, HD, 1), v)
        v_ref[rows, :] = v[:, :HD].astype(BF)
        v_turned[:, rows] = jnp.transpose(v)[:HD, :].astype(BF)
    for copy in copies[1:]:
        copy.start()
    k_at = lax.broadcasted_iota(jnp.int32, (ROWS, ROWS), 0)
    q_at = lax.broadcasted_iota(jnp.int32, (ROWS, ROWS), 1)
    causal = jnp.where(k_at <= q_at, 0.0, NEG)
    inside = jnp.where(k_at > q_at, 0.0, NEG)
    for i in range(BLOCKS):
        lo = max(0, i - WIN // ROWS) * ROWS
        hi = (i + 1) * ROWS
        span = hi - lo
        rows = slice(i * ROWS, hi)
        q2 = jnp.concatenate([q_ref[rows, :HD], q_ref[rows, HD:]], axis=0)
        scores = mm_nt(k_ref[lo:hi, :], q2)
        same = jnp.where(seg_col[lo:hi, 0:1] == seg_row[0:1, rows], 0.0, NEG)
        pieces = [same[n * ROWS : (n + 1) * ROWS] for n in range(span // ROWS)]
        pieces[-1] = pieces[-1] + causal
        if i >= WIN // ROWS:
            pieces[0] = pieces[0] + inside
        bias = jnp.concatenate(pieces, axis=0)
        scores = scores + jnp.concatenate([bias, bias], axis=1)
        top = jnp.max(scores, axis=0, keepdims=True)
        expo = jnp.exp(scores - top)
        total = jnp.sum(expo, axis=0, keepdims=True)
        probs = (expo * (1.0 / total)).astype(BF)
        p_ref[i, :span, :] = probs
        if span < WIN + ROWS:
            p_ref[i, span:, :] = jnp.zeros((WIN + ROWS - span, 2 * ROWS), BF)
        copy = pltpu.make_async_copy(p_ref.at[i], far[4].at[i], sems.at[4 + i])
        copy.start()
        copies.append(copy)
        out = mm(v_turned[:, lo:hi], probs)
        out = jnp.concatenate([out[:, :ROWS], out[:, ROWS:]], axis=0)
        out_ref[rows, :] = jnp.transpose(out).astype(BF)
    for copy in copies:
        copy.wait()


def attend(idx, xs, slot_own, gain, wq, wk, wv, cos_tab, sin_tab):
    shapes = [(LEN, D), (LEN, 2 * HD), (LEN, HD), (LEN, HD), (BLOCKS, WIN + ROWS, 2 * ROWS)]
    outs = [vmem(LEN + EXPERTS, 2 * HD)] + [hbm(*shape) for shape in shapes]
    scratch = [pltpu.VMEM(shape, BF) for shape in shapes]
    scratch += [pltpu.VMEM((8, LEN), F32), pltpu.VMEM((LEN, 128), F32)]
    scratch += [pltpu.VMEM((HD, LEN), BF), pltpu.SemaphoreType.DMA((4 + BLOCKS,))]
    ins = [*xs, slot_own, gain, wq, wk, wv, cos_tab, sin_tab]
    return run(attend_kernel, "attend", 7, ins, outs, scratch, far_out=5, limit=16, idx=idx)


def project_kernel(idx, *refs):
    xs = refs[:8]
    aos = refs[8:16]
    w_out, gain, router_t = refs[16:19]
    mlp_in, slot_t, gate_t, h_far, gate_far, ao_far = refs[19:25]
    ao_all, h_own, gate_own, sems = refs[25:29]
    for r in range(BLOCKS):
        cols = pl.ds(pl.multiple_of(idx[r] * ROWS, ROWS), ROWS)
        ao_all[:, cols] = aos[r][:LEN, :]
    ao_copy = pltpu.make_async_copy(ao_all, ao_far, sems.at[0])
    ao_copy.start()
    gain_full = gain[...]
    for p in range(PAIRS):
        rows = slice(p * 2 * ROWS, (p + 1) * 2 * ROWS)
        places = [pl.ds(pl.multiple_of(idx[2 * p + n] * ROWS, ROWS), ROWS) for n in range(2)]
        attended = jnp.concatenate([ao_all[place, :] for place in places], axis=0)
        x = jnp.concatenate([xs[2 * p + n][:, :D] for n in range(2)], axis=0).astype(F32)
        h = x + mm(attended, w_out[...])
        scale = lax.rsqrt(jnp.mean(h * h, axis=1, keepdims=True) + EPS)
        normed = (h * scale * gain_full).astype(BF)
        mlp_in[rows, :] = normed
        logits = mm_nt(router_t[:EXPERTS, :], normed)
        slot = jnp.concatenate([aos[2 * p + n][LEN:, :] for n in range(2)], axis=1).astype(F32)
        routed = slot > -1.5
        logits = jnp.where(routed, logits, NEG)
        top = jnp.max(logits, axis=0, keepdims=True)
        expo = jnp.where(routed, jnp.exp(logits - top), 0.0)
        gate = expo / jnp.sum(expo, axis=0, keepdims=True)
        slot_t[:, rows] = slot
        gate_t[:, rows] = gate
        if p == 0:
            h_own[...] = h[:ROWS]
            wide = jnp.concatenate(
                [gate[:, :ROWS], jnp.zeros((128 - EXPERTS, ROWS), F32)], axis=0
            )
            gate_own[...] = jnp.transpose(wide)
            own_copies = [
                pltpu.make_async_copy(h_own, h_far, sems.at[1]),
                pltpu.make_async_copy(gate_own, gate_far, sems.at[2]),
            ]
            for copy in own_copies:
                copy.start()
    ao_copy.wait()
    for copy in own_copies:
        copy.wait()


def project(idx, xs, aos, w_out, gain, router_t):
    outs = [
        vmem(LEN, D),
        vmem(EXPERTS, LEN, dtype=F32),
        vmem(EXPERTS, LEN, dtype=F32),
        hbm(ROWS, D, dtype=F32),
        hbm(ROWS, 128, dtype=F32),
        hbm(LEN, D),
    ]
    scratch = [
        pltpu.VMEM((LEN, D), BF),
        pltpu.VMEM((ROWS, D), F32),
        pltpu.VMEM((ROWS, 128), F32),
        pltpu.SemaphoreType.DMA((3,)),
    ]
    ins = [*xs, *aos, w_out, gain, router_t]
    return run(project_kernel, "project", 5, ins, outs, scratch, far_out=3, limit=14, idx=idx)


PROWS = LOCAL * SLOTS
HALF = LOCAL // 2
LEFT = FE
XROWS = D // 4 + FE // 4 * (LEFT // FE)
QROWS = XROWS // 4
ZROWS = D // 16 + FE // 16 * ((D - LEFT) // FE)


def experts_kernel(idx, *refs):
    mlp_in = refs[0]
    dys = refs[1:9]
    slot_t, gate_t, w_gate, w_up, w_down = refs[9:14]
    rows_out, act_out, dout_out, dg_out, du_out, hot_gated, outs, dm_same, dm_other = refs[14:23]
    wg_buf, wu_buf, wd_buf, sems, dy_rows, gate_col, hot, dslots = refs[23:31]

    def load(e):
        at = idx[9] * LOCAL + e
        slot = lax.rem(e, 2)
        return [
            pltpu.make_async_copy(weight.at[at], buf.at[slot], sems.at[slot, n])
            for n, (weight, buf) in enumerate(((w_gate, wg_buf), (w_up, wu_buf), (w_down, wd_buf)))
        ]

    for e in range(2):
        for copy in load(jnp.int32(e)):
            copy.start()
    for p in range(PAIRS):
        cols = slice(p * 2 * ROWS, (p + 1) * 2 * ROWS)
        part = slice(p * SLOTS, (p + 1) * SLOTS)
        lane = lax.broadcasted_iota(jnp.int32, (1, 2 * ROWS), 1)
        lift = jnp.where(lane >= ROWS, float(CAP), 0.0)
        row_id = lax.broadcasted_iota(jnp.int32, (SLOTS, 2 * ROWS), 0).astype(F32)
        hots = []
        for n in range(LOCAL):
            slot = slot_t[pl.ds(idx[15] + n, 1), cols]
            gate = gate_t[pl.ds(idx[15] + n, 1), cols]
            place = jnp.where(slot > -0.5, slot + lift, -1.0)
            one = jnp.where(row_id == place, 1.0, 0.0)
            gated_one = one * gate
            gate_col[n, part, :] = jnp.sum(gated_one, axis=1, keepdims=True)
            hots.append(one.astype(BF))
            hot_gated[p, n * SLOTS : (n + 1) * SLOTS, :] = gated_one.astype(BF)
        hot_pair = jnp.concatenate(hots, axis=0)
        hot[p] = hot_pair
        taken = mm(hot_pair, mlp_in[cols, :]).astype(BF)
        dy = jnp.concatenate([dys[2 * p][...], dys[2 * p + 1][...]], axis=0)
        taken_dy = mm(hot_pair, dy).astype(BF)
        for n in range(LOCAL):
            rows_out[n, part, :] = taken[n * SLOTS : (n + 1) * SLOTS]
            dy_rows[n, part, :] = taken_dy[n * SLOTS : (n + 1) * SLOTS]

    def one_expert(e, carry):
        for copy in load(e):
            copy.wait()
        at = lax.rem(e, 2)
        rows = rows_out[e]
        wg = wg_buf[at]
        wu = wu_buf[at]
        wd = wd_buf[at]
        gate_h = mm(rows, wg)
        up_h = mm(rows, wu)
        sig = 1.0 / (1.0 + jnp.exp(-gate_h))
        silu = gate_h * sig
        act = (silu * up_h).astype(BF)
        act_out[e] = act
        out = mm(act, wd).astype(BF)
        outs[e] = out
        dy = dy_rows[e].astype(F32)
        d_gate = jnp.sum(dy * out.astype(F32), axis=1, keepdims=True)
        d_out = (gate_col[e].astype(BF).astype(F32) * dy).astype(BF)
        dout_out[e] = d_out
        d_act = mm_nt(d_out, wd)
        d_up = (d_act * silu).astype(BF)
        d_gh = (d_act * up_h * sig * (1.0 + gate_h * (1.0 - sig))).astype(BF)
        dg_out[e] = d_gh
        du_out[e] = d_up
        dslots[e, :, :D] = (mm_nt(d_gh, wg) + mm_nt(d_up, wu)).astype(BF)
        lane = lax.broadcasted_iota(jnp.int32, (EROWS, 128), 1)
        d_high = d_gate.astype(BF).astype(F32)
        mine = idx[15] + e
        extra = jnp.where(lane == mine, d_high, 0.0)
        extra = jnp.where(lane == mine + EXPERTS, d_gate - d_high, extra)
        dslots[e, :, D:] = extra.astype(BF)

        @pl.when(e + 2 < LOCAL)
        def _():
            for copy in load(e + 2):
                copy.start()

        return carry

    lax.fori_loop(0, LOCAL, one_expert, 0)

    for p in range(PAIRS):
        part = slice(p * SLOTS, (p + 1) * SLOTS)
        grads = jnp.concatenate([dslots[n, part, :] for n in range(LOCAL)], axis=0)
        merged = mm_tn(hot[p], grads).astype(BF)
        dm_same[p] = merged[:ROWS]
        dm_other[p] = merged[ROWS:]


def experts(idx, mlp_in, dys, slot_t, gate_t, w_gate, w_up, w_down):
    wide = (LOCAL, EROWS, D)
    narrow = (LOCAL, EROWS, FE)
    hot_shape = (PAIRS, PROWS, 2 * ROWS)
    outs = [vmem(*shape) for shape in (wide, narrow, wide, narrow, narrow, hot_shape, wide)]
    outs += [vmem(4, ROWS, AUG)] * 2
    scratch = [
        pltpu.VMEM((2, D, FE), BF),
        pltpu.VMEM((2, D, FE), BF),
        pltpu.VMEM((2, FE, D), BF),
        pltpu.SemaphoreType.DMA((2, 3)),
        pltpu.VMEM(wide, BF),
        pltpu.VMEM((LOCAL, EROWS, 1), F32),
        pltpu.VMEM(hot_shape, BF),
        pltpu.VMEM((LOCAL, EROWS, AUG), BF),
    ]
    ins = [mlp_in, *dys, slot_t, gate_t, w_gate, w_up, w_down]
    return run(experts_kernel, "experts", 16, ins, outs, scratch, far_in=3, limit=26, idx=idx)


def ring_places(e):
    if e < HALF:
        return ((0, 2, e), (2, 0, e), (1, 3, e), (3, 1, e + HALF))
    return ((0, 2, e), (1, 0, e), (2, 1, e - HALF), (3, 4, e - HALF))


def weight_grads_kernel(idx, rows, act, d_out, d_gh, d_up, *refs):
    x_far = refs[:5]
    z_far = refs[5:10]
    x_bufs = refs[10:15]
    z_bufs = refs[15:20]
    whole, whole_down, x_sems, z_sems = refs[20:24]
    quarter = D // 4
    down_q = FE // 4
    small = quarter // 4
    small_down = down_q // 4
    copies = []
    for e in range(LOCAL):
        both = jnp.concatenate([d_gh[e], d_up[e]], axis=1)
        whole[...] = mm_tn(rows[e], both).astype(BF)
        whole_down[...] = mm_tn(act[e], d_out[e]).astype(BF)
        for k, item, place in ring_places(e):
            target = x_bufs[item].at[place]
            at = (idx[11] + k) % 4
            start = pl.multiple_of(at * quarter, quarter)
            target[:quarter, :] = whole[pl.ds(start, quarter), :FE]
            start = pl.multiple_of(at * down_q, down_q)
            target[quarter:, :] = whole_down[pl.ds(start, down_q), :FE]
            copy = pltpu.make_async_copy(target, x_far[item].at[place], x_sems.at[e, k])
            copy.start()
            copies.append(copy)
        for k, item, place in ring_places(e):
            target = z_bufs[item].at[place]
            at = (idx[12] + k) % 4
            for x in range(4):
                start = pl.multiple_of(x * quarter + at * small, small)
                target[x, :small, :] = whole[pl.ds(start, small), FE:]
                start = pl.multiple_of(x * down_q + at * small_down, small_down)
                target[x, small:, :] = whole_down[pl.ds(start, small_down), FE:]
            copy = pltpu.make_async_copy(target, z_far[item].at[place], z_sems.at[e, k])
            copy.start()
            copies.append(copy)
    for copy in copies:
        copy.wait()


def weight_grads(idx, rows, act, d_out, d_gh, d_up):
    x_piece = (XROWS, FE)
    z_piece = (4, ZROWS, FE)
    shapes = [(LOCAL, *x_piece)] * 3 + [(HALF, *x_piece)] * 2
    shapes += [(LOCAL, *z_piece)] * 3 + [(HALF, *z_piece)] * 2
    outs = [hbm(*shape) for shape in shapes]
    scratch = [pltpu.VMEM(shape, BF) for shape in shapes]
    scratch += [pltpu.VMEM((D, 2 * FE), BF), pltpu.VMEM((FE, D), BF)]
    scratch += [pltpu.SemaphoreType.DMA((LOCAL, 4))] * 2
    ins = [rows, act, d_out, d_gh, d_up]
    results = run(
        weight_grads_kernel, "weight_grads", 6, ins, outs, scratch, far_out=10, limit=24, idx=idx
    )
    return results[:5], results[5:]


def relay_kernel(*refs):
    far = refs[:8]
    outs_far = refs[8:12]
    bufs = refs[12:20]
    outs = refs[20:24]
    in_sems, out_sems = refs[24:26]
    loads = [
        [
            fetch(
                [item.at[e] for item in far[pair : pair + 2]],
                [item.at[e] for item in bufs[pair : pair + 2]],
                in_sems.at[pair // 2, e],
            )
            for e in range(HALF)
        ]
        for pair in range(0, 8, 2)
    ]
    stores = []
    for n in range(4):
        for e in range(HALF):
            for copy in loads[n][e]:
                copy.wait()
            outs[n][e] = (bufs[2 * n][e].astype(F32) + bufs[2 * n + 1][e].astype(F32)).astype(BF)
            copy = pltpu.make_async_copy(outs[n].at[e], outs_far[n].at[e], out_sems.at[n, e])
            copy.start()
            stores.append(copy)
    for copy in stores:
        copy.wait()


def relay(x_parts, z_parts):
    ins = [*x_parts, *z_parts]
    x_shape, z_shape = x_parts[0].shape, z_parts[0].shape
    shapes = [x_shape, x_shape, z_shape, z_shape]
    scratch = [pltpu.VMEM(shape, BF) for shape in (x_shape,) * 4 + (z_shape,) * 4]
    scratch += [pltpu.VMEM(shape, BF) for shape in shapes]
    scratch += [pltpu.SemaphoreType.DMA((4, HALF, 2)), pltpu.SemaphoreType.DMA((4, HALF))]
    outs = [hbm(*shape) for shape in shapes]
    return run(
        relay_kernel, "relay", 300, ins, outs, scratch, far_in=8, far_out=4, limit=FAR_LIMIT
    )


def mixed_kernel(idx, hot_gated, outs, far, blocks, sems):
    copies = []
    for p in range(PAIRS):
        part = slice(p * SLOTS, (p + 1) * SLOTS)
        values = jnp.concatenate([outs[n, part, :] for n in range(LOCAL)], axis=0)
        merged = mm_tn(hot_gated[p], values).astype(BF)
        for n in range(2):
            r = 2 * p + n
            blocks[r] = merged[n * ROWS : (n + 1) * ROWS]
            copy = pltpu.make_async_copy(
                blocks.at[r], far.at[idx[r], :, pl.ds(256, D)], sems.at[r]
            )
            copy.start()
            copies.append(copy)
    for copy in copies:
        copy.wait()


def mixed_sum(idx, hot_gated, outs):
    scratch = [pltpu.VMEM((BLOCKS, ROWS, D), BF), pltpu.SemaphoreType.DMA((BLOCKS,))]
    far = [hbm(BLOCKS, ROWS, 256 + D)]
    ins = [hot_gated, outs]
    return run(mixed_kernel, "mixed_sum", 0.6, ins, far, scratch, far_out=1, limit=10, idx=idx)[0]


def add_pairs_kernel(same, other, *outs):
    for off in range(4):
        outs[off][...] = (same[off].astype(F32) + other[off].astype(F32)).astype(BF)


def add_pairs(same, other):
    return run(
        add_pairs_kernel, "add_pairs", 0.3, [same, other], [vmem(*same.shape[1:])] * 4, limit=4
    )


def stage_kernel(idx, *refs):
    far = (refs[:5], refs[5:10])
    outs_far = (refs[10:14], refs[14:18])
    bufs = (refs[18:23], refs[23:28])
    outs = (refs[28:32], refs[32:36])
    totals = refs[36:38]
    in_sems, out_sems = refs[38:40]
    own, from_below, from_above, late_below, late_above = range(5)
    needed = []
    loads = []
    for n in range(LOCAL):
        if n < HALF:
            places = ((own, n), (late_below, n), (from_above, n + HALF))
        else:
            places = ((own, n), (from_below, n), (late_above, n - HALF))
        needed.append(places)
        loads.append(
            [
                fetch(
                    [far[path][item].at[at] for item, at in places],
                    [bufs[path][item].at[at] for item, at in places],
                    in_sems.at[path, n],
                )
                for path in range(2)
            ]
        )
    stores = []
    for n in range(LOCAL):
        for path in range(2):
            for copy in loads[n][path]:
                copy.wait()
            parts = [bufs[path][item][at].astype(F32) for item, at in needed[n]]
            totals[path][...] = (parts[0] + parts[1] + parts[2]).astype(BF)
            (cut_along_z, cut_along_x)[path](idx, totals[path], outs[path], n)
            stores += fetch(
                [item.at[n] for item in outs[path]],
                [item.at[n] for item in outs_far[path]],
                out_sems.at[path, n],
            )
    for copy in stores:
        copy.wait()


def stage_sums(idx, x_parts, z_parts):
    parts = [*x_parts, *z_parts]
    shapes = [(LOCAL, QROWS, FE)] * 4 + [(LOCAL, ZROWS, FE)] * 4
    scratch = [pltpu.VMEM(part.shape, BF) for part in parts]
    scratch += [pltpu.VMEM(shape, BF) for shape in shapes]
    scratch += [pltpu.VMEM(x_parts[0].shape[1:], BF), pltpu.VMEM(z_parts[0].shape[1:], BF)]
    scratch += [pltpu.SemaphoreType.DMA((2, LOCAL, 3)), pltpu.SemaphoreType.DMA((2, LOCAL, 4))]
    results = run(
        stage_kernel,
        "stage_sums",
        400,
        parts,
        [hbm(*shape) for shape in shapes],
        scratch,
        far_in=10,
        far_out=8,
        limit=FAR_LIMIT,
        idx=idx,
    )
    return results[:4], results[4:]


def cut_along_z(idx, total, outs, n):
    gate_rows = D // 16
    down_rows = FE // 16
    for k in range(4):
        at = (idx[12] + k) % 4
        start = pl.multiple_of(at * gate_rows, gate_rows)
        outs[k][n, :gate_rows, :] = total[pl.ds(start, gate_rows), :]
        for m in range(LEFT // FE):
            start = pl.multiple_of(D // 4 + m * (FE // 4) + at * down_rows, down_rows)
            to = gate_rows + m * down_rows
            outs[k][n, to : to + down_rows, :] = total[pl.ds(start, down_rows), :]


def cut_along_x(idx, total, outs, n):
    for k in range(4):
        outs[k][n] = total[pl.ds((idx[11] + k) % 4, 1)][0]


SEND_ROWS = (QROWS + ZROWS) // 2


def finish_kernel(idx, *refs):
    far = refs[:8]
    outs_far = refs[8:11]
    send_far = refs[11]
    bufs = refs[12:20]
    keep_gate, keep_up, keep_down, send = keeps = refs[20:24]
    x_sum, z_sum, in_sems, out_sems = refs[24:28]
    loads = [
        fetch([item.at[n] for item in far], [item.at[n] for item in bufs], in_sems.at[n])
        for n in range(LOCAL)
    ]
    big = D // 16
    small = big // 2
    tiny = FE // 32
    mine = idx[9]
    theirs = 1 - mine
    stores = []
    for n in range(LOCAL):
        for copy in loads[n]:
            copy.wait()
        acc = bufs[0][n].astype(F32)
        for part in bufs[1:4]:
            acc = acc + part[n].astype(F32)
        x_sum[...] = acc
        acc = bufs[4][n].astype(F32)
        for part in bufs[5:8]:
            acc = acc + part[n].astype(F32)
        z_sum[...] = acc
        here = pl.ds(pl.multiple_of(mine * small, small), small)
        there = pl.ds(pl.multiple_of(theirs * small, small), small)
        keep_gate[n] = x_sum[here, :]
        keep_up[n] = z_sum[here, :]
        send[n, :small, :] = x_sum[there, :].astype(BF)
        send[n, small:big, :] = z_sum[there, :].astype(BF)
        for m in range(D // FE):
            source, at = (x_sum, m) if m < LEFT // FE else (z_sum, m - LEFT // FE)
            first = big + at * 2 * tiny
            here = pl.ds(pl.multiple_of(first + mine * tiny, tiny), tiny)
            there = pl.ds(pl.multiple_of(first + theirs * tiny, tiny), tiny)
            keep_down[n, :, m * FE : (m + 1) * FE] = source[here, :]
            send[n, big + m * tiny : big + (m + 1) * tiny, :] = source[there, :].astype(BF)
        targets = [item.at[mine * LOCAL + n] for item in outs_far] + [send_far.at[n]]
        stores += fetch([item.at[n] for item in keeps], targets, out_sems.at[n])
    for copy in stores:
        copy.wait()


def finish(idx, parts):
    outs = [
        hbm(2 * LOCAL, D // 32, FE, dtype=F32),
        hbm(2 * LOCAL, D // 32, FE, dtype=F32),
        hbm(2 * LOCAL, FE // 32, D, dtype=F32),
        hbm(LOCAL, SEND_ROWS, FE),
    ]
    scratch = [pltpu.VMEM(part.shape, BF) for part in parts]
    scratch += [
        pltpu.VMEM((LOCAL, D // 32, FE), F32),
        pltpu.VMEM((LOCAL, D // 32, FE), F32),
        pltpu.VMEM((LOCAL, FE // 32, D), F32),
        pltpu.VMEM((LOCAL, SEND_ROWS, FE), BF),
        pltpu.VMEM((QROWS, FE), F32),
        pltpu.VMEM((ZROWS, FE), F32),
        pltpu.SemaphoreType.DMA((LOCAL, 8)),
        pltpu.SemaphoreType.DMA((LOCAL, 4)),
    ]
    return run(
        finish_kernel,
        "finish",
        1,
        parts,
        outs,
        scratch,
        far_in=8,
        far_out=4,
        limit=FAR_LIMIT,
        idx=idx,
    )


def assemble_kernel(idx, got, gate_in, up_in, down_in, *refs):
    outs_far = refs[:3]
    gate, up, down, out_sems = refs[3:7]
    small = D // 32
    tiny = FE // 32
    stores = []
    for n in range(LOCAL):
        gate[n] = got[n, :small, :].astype(F32)
        up[n] = got[n, small : 2 * small, :].astype(F32)
        down[n, :, :FE] = got[n, 2 * small : 2 * small + tiny, :].astype(F32)
        down[n, :, FE:] = got[n, 2 * small + tiny :, :].astype(F32)
        targets = [item.at[(1 - idx[9]) * LOCAL + n] for item in outs_far]
        stores += fetch([gate.at[n], up.at[n], down.at[n]], targets, out_sems.at[n])
    for copy in stores:
        copy.wait()


def assemble(idx, got, results):
    outs = [hbm(*item.shape, dtype=F32) for item in results]
    scratch = [
        pltpu.VMEM((LOCAL, D // 32, FE), F32),
        pltpu.VMEM((LOCAL, D // 32, FE), F32),
        pltpu.VMEM((LOCAL, FE // 32, D), F32),
        pltpu.SemaphoreType.DMA((LOCAL, 3)),
    ]
    return run(
        assemble_kernel,
        "assemble",
        1,
        [got, *results],
        outs,
        scratch,
        far_in=3,
        far_out=3,
        limit=8,
        idx=idx,
        aliases={2: 0, 3: 1, 4: 2},
    )


def middle_kernel(*refs):
    parts = refs[:4]
    h_ref, gate_ref, dy_ref, gain_ref, router_t, w_out = refs[4:10]
    dh_ref, send_ref, side_ref = refs[10:13]
    total = parts[0][...].astype(F32)
    for part in parts[1:]:
        total = total + part[...].astype(F32)
    extra = total[:, D:]
    d_gate = extra + pltpu.roll(extra, 128 - EXPERTS, 1)
    gate = gate_ref[...]
    d_chosen = gate * (d_gate - jnp.sum(gate * d_gate, axis=1, keepdims=True))
    d_logits = d_chosen.astype(BF)
    d_mlp = total[:, :D] + mm(d_logits, router_t[...])
    h = h_ref[...]
    gain = gain_ref[...].astype(F32)
    scale = lax.rsqrt(jnp.mean(h * h, axis=1, keepdims=True) + EPS)
    normed = h * scale
    mlp_in = (normed * gain).astype(BF)
    scaled = d_mlp * gain
    d_h = (
        dy_ref[...].astype(F32)
        + scale * scaled
        - h * (scale * scale * scale) * jnp.mean(scaled * h, axis=1, keepdims=True)
    )
    dh_ref[...] = d_h
    d_branch = d_h.astype(BF)
    d_attn = mm_nt(d_branch, w_out[...]).astype(BF)
    for b in range(BLOCKS):
        cols = slice(b * 128, (b + 1) * 128)
        send_ref[b, :, :128] = d_attn[:, cols]
        send_ref[b, :, 128:] = d_branch[:, cols]
    router = mm_tn(mlp_in, d_logits)
    d_gain = jnp.sum(d_mlp * normed, axis=0, keepdims=True)
    column = jnp.transpose(jnp.broadcast_to(d_gain, (128, D)))
    lane = lax.broadcasted_iota(jnp.int32, (D, 128), 1)
    side_ref[...] = jnp.where(lane == GAIN_LANE, column, router).astype(BF)


def middle(parts, h_own, gate_own, dy, gain, router_t, w_out):
    shapes = [((ROWS, D), F32), ((BLOCKS, ROWS, 256), BF), ((D, 128), BF)]

    def kernel(*refs):
        inputs = refs[:10]
        far = refs[10:13]
        bufs = refs[13:16]
        middle_kernel(*inputs, *bufs)
        for copy in fetch(bufs, far, refs[16]):
            copy.wait()

    outs = [hbm(*shape, dtype=kind) for shape, kind in shapes]
    scratch = [pltpu.VMEM(shape, kind) for shape, kind in shapes] + [pltpu.SemaphoreType.DMA((3,))]
    ins = [*parts, h_own, gate_own, dy, gain, router_t, w_out]
    return run(kernel, "middle", 100, ins, outs, scratch, far_out=3, limit=10)


def attend_back_kernel(idx, *refs):
    early_far = refs[:6]
    far = refs[6:10]
    pack, dense_far = refs[11:13]
    early = refs[13:19]
    p_ref, attn_in, ao_all, side_ref, dk_acc, dv_acc, dqkv_ref, dense, k_turned = refs[19:28]
    sems, early_sems, tables_sems = refs[28:31]
    grads, q_ref, k_ref, v_ref, cos_ref, sin_ref = early
    early_copies = fetch(early_far[:4], early[:4], early_sems)
    p_copies = [
        pltpu.make_async_copy(far[0].at[i], p_ref.at[i], sems.at[i]) for i in range(BLOCKS)
    ]
    ao_copy = pltpu.make_async_copy(far[2], ao_all, sems.at[BLOCKS])
    in_copy = pltpu.make_async_copy(far[1], attn_in, sems.at[BLOCKS + 1])
    p_copies[0].start()
    table_copies = fetch(early_far[4:], early[4:], tables_sems)
    p_copies[1].start()
    p_copies[2].start()
    side_copy = pltpu.make_async_copy(far[3], side_ref, sems.at[2 * BLOCKS + 3])
    dk_acc[...] = jnp.zeros((LEN, HD), F32)
    dv_acc[...] = jnp.zeros((LEN, HD), F32)
    for copy in early_copies:
        copy.wait()
    k_wide = jnp.concatenate([k_ref[...], k_ref[...]], axis=1).astype(F32)
    k_turned[...] = jnp.transpose(k_wide)[:HD, :].astype(BF)
    for i in range(BLOCKS):
        lo = max(0, i - WIN // ROWS) * ROWS
        hi = (i + 1) * ROWS
        span = hi - lo
        rows = slice(i * ROWS, hi)
        do2 = jnp.concatenate([grads[i, :, :HD], grads[i, :, HD : 2 * HD]], axis=0)
        q2 = jnp.concatenate([q_ref[rows, :HD], q_ref[rows, HD:]], axis=0)
        p_copies[i].wait()
        if i + 3 < BLOCKS:
            p_copies[i + 3].start()
        if i == 2:
            in_copy.start()
            side_copy.start()
            ao_copy.start()
        probs_low = p_ref[i, :span, :]
        probs = probs_low.astype(F32)
        d_probs = mm_nt(v_ref[lo:hi, :], do2)
        weighted = probs * d_probs
        d_scores = (weighted - probs * jnp.sum(weighted, axis=0, keepdims=True)).astype(BF)
        dk_acc[lo:hi, :] += mm(d_scores, q2)
        dv_acc[lo:hi, :] += mm(probs_low, do2)
        dq = mm(k_turned[:, lo:hi], d_scores) * HD**-0.5
        dq = jnp.transpose(jnp.concatenate([dq[:, :ROWS], dq[:, ROWS:]], axis=0))
        dq = dq.astype(BF).astype(F32)
        if i == 0:
            for copy in table_copies:
                copy.wait()
        dq = dq * cos_ref[rows, :] - swap_halves(dq) * sin_ref[rows, :]
        dqkv_ref[rows, : 2 * HD] = dq.astype(BF)
    pair = jnp.concatenate([dk_acc[...], dv_acc[...]], axis=1).astype(BF).astype(F32)
    turned = pair * cos_ref[...] - swap_halves(pair) * sin_ref[...]
    lane = lax.broadcasted_iota(jnp.int32, pair.shape, 1)
    dqkv_ref[:, 2 * HD :] = jnp.where(lane < HD, turned, pair).astype(BF)
    dqkv_copies = []
    for r in range(BLOCKS):
        copy = pltpu.make_async_copy(
            dqkv_ref.at[pl.ds(r * ROWS, ROWS), :],
            pack.at[r, :, pl.ds(0, 256)],
            sems.at[BLOCKS + 3 + r],
        )
        copy.start()
        dqkv_copies.append(copy)
    in_copy.wait()
    ao_copy.wait()
    half = D // 2
    side_copy.wait()
    d_branch = jnp.concatenate([grads[b, :, 128:] for b in range(BLOCKS)], axis=0)
    left_turned = mm_tn(dqkv_ref[...], attn_in[...])
    right_turned = mm_tn(d_branch, ao_all[...])
    for part in range(2):
        rows = slice(part * half, (part + 1) * half)
        left = jnp.transpose(left_turned[:, rows])
        right = jnp.concatenate(
            [jnp.transpose(right_turned[:, rows]), side_ref[rows, :].astype(F32)], axis=1
        )
        both = jnp.concatenate([left.reshape(-1, 8, 256), right.reshape(-1, 8, 256)], axis=1)
        places = pl.ds(part * (half // 8), half // 8)
        dense[places] = both.astype(BF)
        copy = pltpu.make_async_copy(
            dense.at[places], dense_far.at[places], sems.at[(BLOCKS + 2, 2 * BLOCKS + 4)[part]]
        )
        copy.start()
        dqkv_copies.append(copy)
    for copy in dqkv_copies:
        copy.wait()


def attend_back(idx, grads, p, q, k, v, attn_in, ao_all, side, cos_tab, sin_tab, pack):
    early = [grads, q, k, v, cos_tab, sin_tab]
    outs = [hbm(*pack.shape), hbm(D // 8, 16, 256)]
    scratch = [pltpu.VMEM(item.shape, item.dtype) for item in early]
    scratch += [
        pltpu.VMEM(p.shape, BF),
        pltpu.VMEM((LEN, D), BF),
        pltpu.VMEM((LEN, D), BF),
        pltpu.VMEM((D, 128), BF),
        pltpu.VMEM((LEN, HD), F32),
        pltpu.VMEM((LEN, HD), F32),
        pltpu.VMEM((LEN, 256), BF),
        pltpu.VMEM((D // 8, 16, 256), BF),
        pltpu.VMEM((HD, LEN), BF),
        pltpu.SemaphoreType.DMA((2 * BLOCKS + 5,)),
        pltpu.SemaphoreType.DMA((4,)),
        pltpu.SemaphoreType.DMA((2,)),
    ]
    ins = [*early, p, attn_in, ao_all, side, pack]
    return run(
        attend_back_kernel,
        "attend_back",
        8,
        ins,
        outs,
        scratch,
        far_in=11,
        far_out=2,
        limit=FAR_LIMIT,
        idx=idx,
        aliases={11: 0},
    )


def input_grad_kernel(pack, *refs):
    far = refs[:7]
    outs_far = refs[7:9]
    bufs = refs[9:16]
    out, block, dq, dk, dv, early_sems, late_sems, out_sems = refs[16:24]
    early = fetch(far[:4], bufs[:4], early_sems)
    late = fetch(far[4:], bufs[4:], late_sems)
    x_ref, dh_ref, gain_ref, h_own, w_query, w_key, w_value = bufs
    for b in range(BLOCKS):
        dq[:, b * 128 : (b + 1) * 128] = pack[b, :, :128]
    for b in range(0, BLOCKS, 2):
        first = pack[b, :, 128:256].astype(F32)
        second = pack[b + 1, :, 128:256].astype(F32)
        cols = slice(b * HD, (b + 2) * HD)
        dk[:, cols] = jnp.concatenate([first[:, :HD], second[:, :HD]], axis=1).astype(BF)
        dv[:, cols] = jnp.concatenate([first[:, HD:], second[:, HD:]], axis=1).astype(BF)
    for copy in early:
        copy.wait()
    total = h_own[...]
    for b in range(BLOCKS):
        total = total + pack[b, :, 256:].astype(F32)
    block[...] = total.astype(BF)
    for copy in late:
        copy.wait()
    d_in = mm_nt(dq[...], w_query[...]) + mm_nt(dk[...], w_key[...]) + mm_nt(dv[...], w_value[...])
    x = x_ref[...].astype(F32)
    scale = lax.rsqrt(jnp.mean(x * x, axis=1, keepdims=True) + EPS)
    scaled = d_in * gain_ref[...]
    out[...] = (
        dh_ref[...]
        + scale * scaled
        - x * (scale * scale * scale) * jnp.mean(scaled * x, axis=1, keepdims=True)
    ).astype(BF)
    for copy in fetch((out, block), outs_far, out_sems):
        copy.wait()


def input_grad(pack, x, d_h, gain, h_own, w_query, w_key, w_value):
    ins = [pack, x, d_h, gain, h_own, w_query, w_key, w_value]
    scratch = [pltpu.VMEM(item.shape, item.dtype) for item in ins[1:]]
    scratch += [
        pltpu.VMEM((ROWS, D), BF),
        pltpu.VMEM((ROWS, D), BF),
        pltpu.VMEM((ROWS, H * HD), BF),
        pltpu.VMEM((ROWS, KVH * HD), BF),
        pltpu.VMEM((ROWS, KVH * HD), BF),
        pltpu.SemaphoreType.DMA((4,)),
        pltpu.SemaphoreType.DMA((3,)),
        pltpu.SemaphoreType.DMA((2,)),
    ]
    return run(
        input_grad_kernel,
        "input_grad",
        1,
        ins,
        [hbm(ROWS, D)] * 2,
        scratch,
        far_in=len(ins) - 1,
        far_out=2,
        limit=FAR_LIMIT,
    )


def dense_out_kernel(idx, dense, w_query, w_key, w_value, gain, *refs):
    dq, dk, dv, do, router, gains, turned = refs
    total = jnp.sum(dense[...].astype(F32).reshape(-1, BLOCKS, 16, 256), axis=0)
    for b in range(BLOCKS):
        dq[:, b * 128 : (b + 1) * 128] = total[b, :8, :128]
        do[:, b * 128 : (b + 1) * 128] = total[b, 8:, :128]
    for b in range(0, BLOCKS, 2):
        first = total[b, :8, 128:]
        second = total[b + 1, :8, 128:]
        cols = slice(b * HD, (b + 2) * HD)
        dk[:, cols] = jnp.concatenate([first[:, :HD], second[:, :HD]], axis=1)
        dv[:, cols] = jnp.concatenate([first[:, HD:], second[:, HD:]], axis=1)
    side = jnp.sum(total[:, 8:, 128:], axis=0)
    router[...] = side[:, :EXPERTS]
    dot = jnp.zeros((8, 1), F32)
    for weight, grad in ((w_query, dq), (w_key, dk), (w_value, dv)):
        dot = dot + jnp.sum(weight[...] * grad[...], axis=1, keepdims=True)
    chunk = pl.ds(pl.multiple_of(idx[16] * 128, 128), 128)
    turned[...] = jnp.transpose(jnp.broadcast_to(gain[:, chunk], (128, 128)))
    gain_rows = turned[pl.ds(pl.multiple_of(idx[17] * 8, 8), 8), 0:1]
    lane = lax.broadcasted_iota(jnp.int32, (8, 128), 1)
    both = jnp.where(lane == GAIN_LANE, side, dot / gain_rows)
    turned[:8, :] = both
    flat = jnp.transpose(turned[...])
    gains[...] = flat[GAIN_LANE - 8 : GAIN_LANE + 8, :]


def dense_out(idx, dense, w_query, w_key, w_value, gain):
    outs = [
        auto(8, H * HD, dtype=F32),
        auto(8, KVH * HD, dtype=F32),
        auto(8, KVH * HD, dtype=F32),
        auto(8, D, dtype=F32),
        auto(8, EXPERTS, dtype=F32),
        auto(16, 128, dtype=F32),
    ]
    ins = [dense, w_query, w_key, w_value, gain]
    scratch = [pltpu.VMEM((128, 128), F32)]
    return run(dense_out_kernel, "dense_out", 1, ins, outs, scratch, limit=8, idx=idx)


def from_x(value, off):
    size = lax.axis_size("x")
    return lax.ppermute(value, "x", [(i, (i + off) % size) for i in range(size)])


def from_z(value, off):
    size = lax.axis_size("z")
    return lax.ppermute(value, "z", [(i, (i + off) % size) for i in range(size)])


def along_y(value, off):
    route = []
    for y in range(4):
        to = (y + off) % 4
        route.append(((y % 2) * 2 + y // 2, (to % 2) * 2 + to // 2))
    return lax.ppermute(value, ("yl", "yh"), route)


def other_core(value):
    return lax.ppermute(value, "c", [(0, 1), (1, 0)])


def near_ring(value):
    return [value] + [along_y(value, -off) for off in (1, 2, 3)]


def both_cores(near):
    far = [other_core(item) for item in near]
    return [item for pair in zip(near, far) for item in pair]


def gather_ring(value):
    return both_cores(near_ring(value))


def reduce_ring(pieces):
    return [pieces[0]] + [along_y(pieces[off], off) for off in (1, 2, 3)]


def scatter_parts(parts, send):
    return [parts[0]] + [send(parts[k], k) for k in (1, 2, 3)]


def together(*values):
    return lax.optimization_barrier(values)


def after(values, *earlier):
    return lax.optimization_barrier((values, earlier))[0]


def local(
    tokens,
    segments,
    routes,
    drop_order,
    gain_attn,
    w_query,
    w_key,
    w_value,
    w_out,
    gain_mlp,
    w_router,
    w_gate,
    w_up,
    w_down,
    cotangent,
):
    x_at = lax.axis_index("x")
    z_at = lax.axis_index("z")
    yl = lax.axis_index("yl")
    yh = lax.axis_index("yh")
    core = lax.axis_index("c")
    y_at = yh * 2 + yl
    own = yl * 4 + yh * 2 + core
    expert_at = yh * 2 + core

    entries = []
    for off in range(4):
        y = (y_at + off) % 4
        for dc in range(2):
            entries.append((y % 2) * 4 + (y // 2) * 2 + (core + dc) % 2)
    entries += [own, yl, expert_at, x_at, z_at, y_at, core, expert_at * 8 + yl * LOCAL]
    first_row = ((x_at * 4 + z_at) * 8 + own) * 8
    entries += [first_row // 128, first_row % 128 // 8]
    idx = jnp.stack([jnp.asarray(entry, jnp.int32) for entry in entries])

    cos_np, sin_np = rotary_tables()
    cos_tab = jnp.asarray(cos_np)
    sin_tab = jnp.asarray(sin_np)
    gain_one = gain_attn.astype(F32).reshape(1, D)
    gain_two = gain_mlp.astype(F32).reshape(1, D)
    router_t = jnp.pad(w_router.T, ((0, 128 - EXPERTS), (0, 0)))

    def columns(weight, block):
        return lax.dynamic_slice_in_dim(weight, block * 128, 128, 1)

    def out_rows(weight):
        return lax.dynamic_slice_in_dim(weight, first_row, 8, 0).astype(F32)

    wq_cols = columns(w_query, own)
    wk_cols = columns(w_key, own // 2)
    wv_cols = columns(w_value, own // 2)
    finals = [out_rows(w_query), out_rows(w_key), out_rows(w_value)]
    early = [idx, gain_one, gain_two, router_t, wq_cols, wk_cols, wv_cols, finals]

    seg_cols = jnp.broadcast_to(segments.astype(BF)[:, None], (ROWS, AUG - D))
    x_near = near_ring(jnp.concatenate([tokens, seg_cols], axis=1))
    slot_own = slots(routes.T, drop_order)
    x_near, slot_own, early = together(x_near, slot_own, early)
    idx, gain_one, gain_two, router_t, wq_cols, wk_cols, wv_cols, finals = early
    xs = both_cores(x_near)
    dy_near = near_ring(after(cotangent, slot_own))

    ao, attn_in, q, k, v, p = attend(
        idx, xs, slot_own, gain_one, wq_cols, wk_cols, wv_cols, cos_tab, sin_tab
    )
    dys = both_cores(dy_near)
    aos = gather_ring(after(ao, *dy_near))
    mlp_in, slot_t, gate_t, h_own, gate_own, ao_all = project(
        idx, xs, aos, w_out, gain_two, router_t
    )
    rows, act, d_out, d_gh, d_up, hot_gated, outs, dm_same, dm_other = experts(
        idx, mlp_in, dys, slot_t, gate_t, w_gate, w_up, w_down
    )

    got = other_core(dm_other)
    pack = mixed_sum(idx, hot_gated, outs)
    pack, got = together(pack, got)
    dm_pieces = add_pairs(dm_same, got)
    dm_parts = reduce_ring(dm_pieces)
    (x_up, x_down, *x_keep), (z_up, z_down, *z_keep) = weight_grads(
        idx, after(rows, *dm_pieces), act, d_out, d_gh, d_up
    )
    x_below = from_x(x_up, 1)
    x_above = from_x(x_down, 3)
    z_keep, z_up, z_down, dm_parts = together(z_keep, z_up, z_down, dm_parts)
    z_below = from_z(z_up, 1)
    z_above = from_z(z_down, 3)
    d_h, to_heads, side = middle(
        dm_parts, h_own, gate_own, cotangent, gain_two, router_t, w_out
    )
    grads = lax.all_to_all(to_heads, GROUP, split_axis=0, concat_axis=0, tiled=True)
    pack, dense = attend_back(
        idx, grads, p, q, k, v, attn_in, ao_all, side, cos_tab, sin_tab, pack
    )
    x_below, x_above, z_below, z_above = after([x_below, x_above, z_below, z_above], pack)
    dense = lax.all_to_all(
        dense, ("x", "z", "yl", "yh", "c"), split_axis=0, concat_axis=0, tiled=True
    )

    relayed = relay(
        [x_keep[1], x_below, x_keep[2], x_above], [z_keep[1], z_below, z_keep[2], z_above]
    )
    x_late = [from_x(relayed[0], 1), from_x(relayed[1], 3)]
    z_late = [from_z(relayed[2], 1), from_z(relayed[3], 3)]
    pack = lax.all_to_all(
        after(pack, dense, *relayed), GROUP, split_axis=0, concat_axis=0, tiled=True
    )
    dense_rows = dense_out(idx, dense, *finals, gain_one)
    x_late, z_late = together(x_late, z_late)
    x_pieces, z_pieces = stage_sums(
        idx, [x_keep[0], x_below, x_above, *x_late], [z_keep[0], z_below, z_above, *z_late]
    )
    x_second = scatter_parts(x_pieces, from_z)
    z_second = scatter_parts(z_pieces, from_x)
    d_tokens, block_out = input_grad(
        after(pack, *x_pieces), tokens, d_h, gain_one, h_own, w_query, w_key, w_value
    )
    d_tokens, x_second, z_second, dense_rows = together(d_tokens, x_second, z_second, dense_rows)

    *results, sent = finish(idx, [*x_second, *z_second])
    got = lax.ppermute(sent, "yl", [(0, 1), (1, 0)])
    d_w_gate, d_w_up, d_w_down = assemble(idx, got, results)
    d_w_query, d_w_key, d_w_value, d_w_out, d_w_router, gains = dense_rows
    d_gain_attn = gains[0, :8]
    d_gain_mlp = gains[8, :8]

    return (
        block_out,
        d_tokens,
        d_gain_attn,
        d_w_query,
        d_w_key,
        d_w_value,
        d_w_out,
        d_gain_mlp,
        d_w_router,
        d_w_gate,
        d_w_up,
        d_w_down,
    )


def solution(mesh):
    side = 4 if mesh.shape["dp"] == 32 else 1
    names = ("x", "z", "yl", "yh", "c")
    grid = Mesh(mesh.devices.reshape(side, side, 2, 2, 2), names)
    tokens = names
    experts_axes = ("yh", "c")
    dp = ("x", "z", "yl")
    in_specs = (
        P(tokens, None),
        P(tokens),
        P(tokens, None),
        P(tokens, None),
        P(),
        P(),
        P(),
        P(),
        P(),
        P(),
        P(),
        P(experts_axes, None, None),
        P(experts_axes, None, None),
        P(experts_axes, None, None),
        P(tokens, None),
    )
    out_specs = (
        P(tokens, None),
        P(tokens, None),
        P(tokens),
        P(tokens, None),
        P(tokens, None),
        P(tokens, None),
        P(tokens, None),
        P(tokens),
        P(tokens, None),
        P(experts_axes, dp, None),
        P(experts_axes, dp, None),
        P(experts_axes, dp, None),
    )
    return jax.shard_map(local, mesh=grid, in_specs=in_specs, out_specs=out_specs, check_vma=False)
```

```python
import functools

import jax
import jax.numpy as jnp
import numpy as np
from jax import lax
from jax.experimental import pallas as pl
from jax.experimental.pallas import tpu as pltpu
from jax.sharding import Mesh, PartitionSpec as P

H = 16
KVH = 8
HD = 64
D = 1024
FE = 512
TOPK = 8
EXPERTS = 32
CAP = 36
ROWS = 128
LEN = 1024
BLOCKS = LEN // ROWS
WIN = 512
LOCAL = 4
PAIRS = BLOCKS // 2
SLOTS = 80
EROWS = PAIRS * SLOTS
AUG = D + 128
GAIN_LANE = 32
FAR_LIMIT = 56
SHARE = 0.1
EPS = 1e-06
THETA = 10000.0
NEG = -1e30
BF = jnp.bfloat16
F32 = jnp.float32
GROUP = ("yl", "yh", "c")


def mm(left, right):
    return jnp.dot(left, right, preferred_element_type=F32)


def mm_nt(left, right):
    return lax.dot_general(left, right, (((1,), (1,)), ((), ())), preferred_element_type=F32)


def mm_tn(left, right):
    return lax.dot_general(left, right, (((0,), (0,)), ((), ())), preferred_element_type=F32)


def rotary_tables():
    half = HD // 2
    frequency = THETA ** (-np.arange(half, dtype=np.float64) * 2.0 / HD)
    angles = np.arange(LEN, dtype=np.float64)[:, None] * frequency[None, :]
    cosine = np.cos(angles)
    sine = np.sin(angles)
    cos_full = np.concatenate([cosine] * 4, axis=1).astype(np.float32)
    sin_full = np.concatenate([-sine, sine, -sine, sine], axis=1).astype(np.float32)
    return cos_full, sin_full


def swap_halves(array_in):
    half = HD // 2
    lane = lax.broadcasted_iota(jnp.int32, array_in.shape, 1)
    ahead = pltpu.roll(array_in, array_in.shape[1] - half, 1)
    behind = pltpu.roll(array_in, half, 1)
    return jnp.where(lane % HD < half, ahead, behind)


def vmem(*shape, dtype=BF):
    return pltpu.VMEM(shape, dtype)


def hbm(*shape, dtype=BF):
    return pltpu.HBM(shape, dtype)


def auto(*shape, dtype=BF):
    return jax.ShapeDtypeStruct(shape, dtype)


def cost(micros):
    return pl.CostEstimate(
        flops=int(micros * 1.15e9 * SHARE), bytes_accessed=int(micros * 1e6), transcendentals=0
    )


def run(
    kernel,
    name,
    micros,
    ins,
    outs,
    scratch=(),
    far_in=0,
    far_out=0,
    limit=24,
    idx=None,
    aliases=None,
):
    inside = pl.BlockSpec(memory_space=pltpu.VMEM)
    outside = pl.BlockSpec(memory_space=pltpu.HBM)
    in_specs = [inside] * (len(ins) - far_in) + [outside] * far_in
    operands = list(ins)
    if idx is not None:
        in_specs = [pl.BlockSpec(memory_space=pltpu.SMEM)] + in_specs
        operands = [idx] + operands
    return pl.pallas_call(
        kernel,
        out_shape=list(outs),
        in_specs=in_specs,
        out_specs=[inside] * (len(outs) - far_out) + [outside] * far_out,
        scratch_shapes=list(scratch),
        input_output_aliases=aliases or {},
        compiler_params=pltpu.CompilerParams(vmem_limit_bytes=limit * 1024 * 1024),
        cost_estimate=cost(micros),
        name=name,
    )(*operands)


def run_far(kernel, name, micros, ins, outs, scratch=(), idx=None):
    count = len(ins)
    given = 0 if idx is None else 1

    def body(*refs):
        lead = refs[:given]
        sources = refs[given : given + count]
        targets = refs[given + count : given + count + len(outs)]
        rest = refs[given + count + len(outs) :]
        in_bufs = rest[:count]
        out_bufs = rest[count : count + len(outs)]
        in_sems, out_sems = rest[count + len(outs) : count + len(outs) + 2]
        for copy in fetch(sources, in_bufs, in_sems):
            copy.wait()
        kernel(*lead, *in_bufs, *out_bufs, *rest[count + len(outs) + 2 :])
        for copy in fetch(out_bufs, targets, out_sems):
            copy.wait()

    bufs = [pltpu.VMEM(item.shape, item.dtype) for item in ins]
    bufs += [pltpu.VMEM(item.shape, item.dtype) for item in outs]
    bufs += [pltpu.SemaphoreType.DMA((count,)), pltpu.SemaphoreType.DMA((len(outs),))]
    return run(
        body,
        name,
        micros,
        ins,
        outs,
        bufs + list(scratch),
        far_in=count,
        far_out=len(outs),
        limit=FAR_LIMIT,
        idx=idx,
    )


def fetch(sources, targets, sems):
    copies = [
        pltpu.make_async_copy(source, target, sems.at[n])
        for n, (source, target) in enumerate(zip(sources, targets))
    ]
    for copy in copies:
        copy.start()
    return copies


def slots_kernel(routes_ref, order_ref, meta_ref, place_ref):
    order = order_ref[...]
    index = lax.broadcasted_iota(jnp.int32, (1, ROWS * TOPK), 1)
    token_of = order // TOPK
    choice_of = order - token_of * TOPK
    at_token = (token_of == lax.broadcasted_iota(jnp.int32, (ROWS, ROWS * TOPK), 0)).astype(F32)
    choice = lax.broadcasted_iota(jnp.int32, (2 * TOPK, ROWS * TOPK), 0)
    high = index // 32
    low = index - high * 32
    part = jnp.where(choice < TOPK, high, low).astype(F32)
    choice_mod = jnp.where(choice < TOPK, choice, choice - TOPK)
    table = jnp.where(choice_mod == choice_of, part, 0.0)
    found = mm_nt(at_token.astype(BF), table.astype(BF))
    place = found[:, :TOPK] * 32.0 + found[:, TOPK:]
    lane = lax.broadcasted_iota(jnp.int32, (ROWS, 128), 1)
    wide = jnp.concatenate(
        [
            routes_ref[...].astype(F32),
            jnp.zeros((ROWS - TOPK, ROWS), F32),
        ],
        axis=0,
    )
    turned = jnp.transpose(wide)
    lane_f = lane.astype(F32)
    placed = jnp.full((ROWS, 128), 4096.0, F32)
    for k in range(TOPK):
        placed = jnp.where(turned[:, k : k + 1] == lane_f, place[:, k : k + 1], placed)
    place_ref[...] = placed

    def count(step, total):
        for inner in range(8):
            row = place_ref[pl.ds(step * 8 + inner, 1), :]
            total = total + jnp.where(row < placed, 1.0, 0.0)
        return total

    rank = lax.fori_loop(0, ROWS // 8, count, jnp.zeros((ROWS, 128), F32))
    slot = jnp.where(placed < 4000.0, jnp.where(rank < CAP, rank, -1.0), -2.0)
    meta_ref[...] = jnp.transpose(slot)[:EXPERTS, :].astype(BF)


def slots(routes_t, drop_order):
    return run(
        slots_kernel,
        "slots",
        3,
        [routes_t, drop_order],
        [auto(EXPERTS, ROWS)],
        [pltpu.VMEM((ROWS, 128), F32)],
        limit=8,
    )[0]


def attend_kernel(idx, *refs):
    xs = refs[:8]
    slots_ref, gain, wq, wk, wv, cos_ref, sin_ref = refs[8:15]
    out_ref = refs[15]
    far = refs[16:21]
    attn_in, q_ref, k_ref, v_ref, p_ref, seg_row, seg_col, v_turned, sems = refs[21:30]
    near = (attn_in, q_ref, k_ref, v_ref)
    copies = [pltpu.make_async_copy(near[n], far[n], sems.at[n]) for n in range(4)]
    gain_full = gain[...]
    for r in range(BLOCKS):
        rows = pl.ds(pl.multiple_of(idx[r] * ROWS, ROWS), ROWS)
        x = xs[r][:, :D].astype(F32)
        scale = lax.rsqrt(jnp.mean(x * x, axis=1, keepdims=True) + EPS)
        attn_in[rows, :] = (x * scale * gain_full).astype(BF)
        segs = xs[r][:, D:].astype(F32)
        seg_col[rows, :] = segs
        seg_row[:, rows] = jnp.transpose(segs)[:8, :]
    copies[0].start()
    out_ref[LEN:, :] = slots_ref[...]
    odd = (idx[8] % 2) == 1
    half = LEN // 2
    for part in range(2):
        rows = slice(part * half, (part + 1) * half)
        block = attn_in[rows, :]
        cosine = cos_ref[rows, :]
        sine = sin_ref[rows, :]
        q = mm(block, wq[...])
        q = q * cosine + swap_halves(q) * sine
        q_ref[rows, :] = (q.astype(BF).astype(F32) * HD**-0.5).astype(BF)
        k = mm(block, wk[...])
        k = jnp.where(odd, pltpu.roll(k, HD, 1), k)
        k = k * cosine + swap_halves(k) * sine
        k_ref[rows, :] = k[:, :HD].astype(BF)
        v = mm(block, wv[...])
        v = jnp.where(odd, pltpu.roll(v, HD, 1), v)
        v_ref[rows, :] = v[:, :HD].astype(BF)
        v_turned[:, rows] = jnp.transpose(v)[:HD, :].astype(BF)
    for copy in copies[1:]:
        copy.start()
    k_at = lax.broadcasted_iota(jnp.int32, (ROWS, ROWS), 0)
    q_at = lax.broadcasted_iota(jnp.int32, (ROWS, ROWS), 1)
    causal = jnp.where(k_at <= q_at, 0.0, NEG)
    inside = jnp.where(k_at > q_at, 0.0, NEG)
    for i in range(BLOCKS):
        lo = max(0, i - WIN // ROWS) * ROWS
        hi = (i + 1) * ROWS
        span = hi - lo
        rows = slice(i * ROWS, hi)
        q2 = jnp.concatenate([q_ref[rows, :HD], q_ref[rows, HD:]], axis=0)
        scores = mm_nt(k_ref[lo:hi, :], q2)
        same = jnp.where(seg_col[lo:hi, 0:1] == seg_row[0:1, rows], 0.0, NEG)
        pieces = [same[n * ROWS : (n + 1) * ROWS] for n in range(span // ROWS)]
        pieces[-1] = pieces[-1] + causal
        if i >= WIN // ROWS:
            pieces[0] = pieces[0] + inside
        bias = jnp.concatenate(pieces, axis=0)
        scores = scores + jnp.concatenate([bias, bias], axis=1)
        top = jnp.max(scores, axis=0, keepdims=True)
        expo = jnp.exp(scores - top)
        total = jnp.sum(expo, axis=0, keepdims=True)
        probs = (expo * (1.0 / total)).astype(BF)
        p_ref[i, :span, :] = probs
        if span < WIN + ROWS:
            p_ref[i, span:, :] = jnp.zeros((WIN + ROWS - span, 2 * ROWS), BF)
        copy = pltpu.make_async_copy(p_ref.at[i], far[4].at[i], sems.at[4 + i])
        copy.start()
        copies.append(copy)
        out = mm(v_turned[:, lo:hi], probs)
        out = jnp.concatenate([out[:, :ROWS], out[:, ROWS:]], axis=0)
        out_ref[rows, :] = jnp.transpose(out).astype(BF)
    for copy in copies:
        copy.wait()


def attend(idx, xs, slot_own, gain, wq, wk, wv, cos_tab, sin_tab):
    shapes = [(LEN, D), (LEN, 2 * HD), (LEN, HD), (LEN, HD), (BLOCKS, WIN + ROWS, 2 * ROWS)]
    outs = [vmem(LEN + EXPERTS, 2 * HD)] + [hbm(*shape) for shape in shapes]
    scratch = [pltpu.VMEM(shape, BF) for shape in shapes]
    scratch += [pltpu.VMEM((8, LEN), F32), pltpu.VMEM((LEN, 128), F32)]
    scratch += [pltpu.VMEM((HD, LEN), BF), pltpu.SemaphoreType.DMA((4 + BLOCKS,))]
    ins = [*xs, slot_own, gain, wq, wk, wv, cos_tab, sin_tab]
    return run(attend_kernel, "attend", 7, ins, outs, scratch, far_out=5, limit=16, idx=idx)


def project_kernel(idx, *refs):
    xs = refs[:8]
    aos = refs[8:16]
    w_out, gain, router_t = refs[16:19]
    mlp_in, slot_t, gate_t, h_far, gate_far, ao_far = refs[19:25]
    ao_all, h_own, gate_own, sems = refs[25:29]
    for r in range(BLOCKS):
        cols = pl.ds(pl.multiple_of(idx[r] * ROWS, ROWS), ROWS)
        ao_all[:, cols] = aos[r][:LEN, :]
    ao_copy = pltpu.make_async_copy(ao_all, ao_far, sems.at[0])
    ao_copy.start()
    gain_full = gain[...]
    for p in range(PAIRS):
        rows = slice(p * 2 * ROWS, (p + 1) * 2 * ROWS)
        places = [pl.ds(pl.multiple_of(idx[2 * p + n] * ROWS, ROWS), ROWS) for n in range(2)]
        attended = jnp.concatenate([ao_all[place, :] for place in places], axis=0)
        x = jnp.concatenate([xs[2 * p + n][:, :D] for n in range(2)], axis=0).astype(F32)
        h = x + mm(attended, w_out[...])
        scale = lax.rsqrt(jnp.mean(h * h, axis=1, keepdims=True) + EPS)
        normed = (h * scale * gain_full).astype(BF)
        mlp_in[rows, :] = normed
        logits = mm_nt(router_t[:EXPERTS, :], normed)
        slot = jnp.concatenate([aos[2 * p + n][LEN:, :] for n in range(2)], axis=1).astype(F32)
        routed = slot > -1.5
        logits = jnp.where(routed, logits, NEG)
        top = jnp.max(logits, axis=0, keepdims=True)
        expo = jnp.where(routed, jnp.exp(logits - top), 0.0)
        gate = expo / jnp.sum(expo, axis=0, keepdims=True)
        slot_t[:, rows] = slot
        gate_t[:, rows] = gate
        if p == 0:
            h_own[...] = h[:ROWS]
            wide = jnp.concatenate(
                [gate[:, :ROWS], jnp.zeros((128 - EXPERTS, ROWS), F32)], axis=0
            )
            gate_own[...] = jnp.transpose(wide)
            own_copies = [
                pltpu.make_async_copy(h_own, h_far, sems.at[1]),
                pltpu.make_async_copy(gate_own, gate_far, sems.at[2]),
            ]
            for copy in own_copies:
                copy.start()
    ao_copy.wait()
    for copy in own_copies:
        copy.wait()


def project(idx, xs, aos, w_out, gain, router_t):
    outs = [
        vmem(LEN, D),
        vmem(EXPERTS, LEN, dtype=F32),
        vmem(EXPERTS, LEN, dtype=F32),
        hbm(ROWS, D, dtype=F32),
        hbm(ROWS, 128, dtype=F32),
        hbm(LEN, D),
    ]
    scratch = [
        pltpu.VMEM((LEN, D), BF),
        pltpu.VMEM((ROWS, D), F32),
        pltpu.VMEM((ROWS, 128), F32),
        pltpu.SemaphoreType.DMA((3,)),
    ]
    ins = [*xs, *aos, w_out, gain, router_t]
    return run(project_kernel, "project", 5, ins, outs, scratch, far_out=3, limit=14, idx=idx)


PROWS = LOCAL * SLOTS
HALF = LOCAL // 2
LEFT = FE
XROWS = D // 4 + FE // 4 * (LEFT // FE)
QROWS = XROWS // 4
ZROWS = D // 16 + FE // 16 * ((D - LEFT) // FE)


def experts_kernel(idx, *refs):
    mlp_in = refs[0]
    dys = refs[1:9]
    slot_t, gate_t, w_gate, w_up, w_down = refs[9:14]
    rows_out, act_out, dout_out, dg_out, du_out, hot_gated, outs, dm_same, dm_other = refs[14:23]
    wg_buf, wu_buf, wd_buf, sems, dy_rows, gate_col, hot, dslots = refs[23:31]

    def load(e):
        at = idx[9] * LOCAL + e
        slot = lax.rem(e, 2)
        return [
            pltpu.make_async_copy(weight.at[at], buf.at[slot], sems.at[slot, n])
            for n, (weight, buf) in enumerate(((w_gate, wg_buf), (w_up, wu_buf), (w_down, wd_buf)))
        ]

    for e in range(2):
        for copy in load(jnp.int32(e)):
            copy.start()
    for p in range(PAIRS):
        cols = slice(p * 2 * ROWS, (p + 1) * 2 * ROWS)
        part = slice(p * SLOTS, (p + 1) * SLOTS)
        lane = lax.broadcasted_iota(jnp.int32, (1, 2 * ROWS), 1)
        lift = jnp.where(lane >= ROWS, float(CAP), 0.0)
        row_id = lax.broadcasted_iota(jnp.int32, (SLOTS, 2 * ROWS), 0).astype(F32)
        hots = []
        for n in range(LOCAL):
            slot = slot_t[pl.ds(idx[15] + n, 1), cols]
            gate = gate_t[pl.ds(idx[15] + n, 1), cols]
            place = jnp.where(slot > -0.5, slot + lift, -1.0)
            one = jnp.where(row_id == place, 1.0, 0.0)
            gated_one = one * gate
            gate_col[n, part, :] = jnp.sum(gated_one, axis=1, keepdims=True)
            hots.append(one.astype(BF))
            hot_gated[p, n * SLOTS : (n + 1) * SLOTS, :] = gated_one.astype(BF)
        hot_pair = jnp.concatenate(hots, axis=0)
        hot[p] = hot_pair
        taken = mm(hot_pair, mlp_in[cols, :]).astype(BF)
        dy = jnp.concatenate([dys[2 * p][...], dys[2 * p + 1][...]], axis=0)
        taken_dy = mm(hot_pair, dy).astype(BF)
        for n in range(LOCAL):
            rows_out[n, part, :] = taken[n * SLOTS : (n + 1) * SLOTS]
            dy_rows[n, part, :] = taken_dy[n * SLOTS : (n + 1) * SLOTS]

    def one_expert(e, carry):
        for copy in load(e):
            copy.wait()
        at = lax.rem(e, 2)
        rows = rows_out[e]
        wg = wg_buf[at]
        wu = wu_buf[at]
        wd = wd_buf[at]
        gate_h = mm(rows, wg)
        up_h = mm(rows, wu)
        sig = 1.0 / (1.0 + jnp.exp(-gate_h))
        silu = gate_h * sig
        act = (silu * up_h).astype(BF)
        act_out[e] = act
        out = mm(act, wd).astype(BF)
        outs[e] = out
        dy = dy_rows[e].astype(F32)
        d_gate = jnp.sum(dy * out.astype(F32), axis=1, keepdims=True)
        d_out = (gate_col[e].astype(BF).astype(F32) * dy).astype(BF)
        dout_out[e] = d_out
        d_act = mm_nt(d_out, wd)
        d_up = (d_act * silu).astype(BF)
        d_gh = (d_act * up_h * sig * (1.0 + gate_h * (1.0 - sig))).astype(BF)
        dg_out[e] = d_gh
        du_out[e] = d_up
        dslots[e, :, :D] = (mm_nt(d_gh, wg) + mm_nt(d_up, wu)).astype(BF)
        lane = lax.broadcasted_iota(jnp.int32, (EROWS, 128), 1)
        d_high = d_gate.astype(BF).astype(F32)
        mine = idx[15] + e
        extra = jnp.where(lane == mine, d_high, 0.0)
        extra = jnp.where(lane == mine + EXPERTS, d_gate - d_high, extra)
        dslots[e, :, D:] = extra.astype(BF)

        @pl.when(e + 2 < LOCAL)
        def _():
            for copy in load(e + 2):
                copy.start()

        return carry

    lax.fori_loop(0, LOCAL, one_expert, 0)

    for p in range(PAIRS):
        part = slice(p * SLOTS, (p + 1) * SLOTS)
        grads = jnp.concatenate([dslots[n, part, :] for n in range(LOCAL)], axis=0)
        merged = mm_tn(hot[p], grads).astype(BF)
        dm_same[p] = merged[:ROWS]
        dm_other[p] = merged[ROWS:]


def experts(idx, mlp_in, dys, slot_t, gate_t, w_gate, w_up, w_down):
    wide = (LOCAL, EROWS, D)
    narrow = (LOCAL, EROWS, FE)
    hot_shape = (PAIRS, PROWS, 2 * ROWS)
    outs = [vmem(*shape) for shape in (wide, narrow, wide, narrow, narrow, hot_shape, wide)]
    outs += [vmem(4, ROWS, AUG)] * 2
    scratch = [
        pltpu.VMEM((2, D, FE), BF),
        pltpu.VMEM((2, D, FE), BF),
        pltpu.VMEM((2, FE, D), BF),
        pltpu.SemaphoreType.DMA((2, 3)),
        pltpu.VMEM(wide, BF),
        pltpu.VMEM((LOCAL, EROWS, 1), F32),
        pltpu.VMEM(hot_shape, BF),
        pltpu.VMEM((LOCAL, EROWS, AUG), BF),
    ]
    ins = [mlp_in, *dys, slot_t, gate_t, w_gate, w_up, w_down]
    return run(experts_kernel, "experts", 16, ins, outs, scratch, far_in=3, limit=26, idx=idx)


def ring_places(e):
    if e < HALF:
        return ((0, 2, e), (2, 0, e), (1, 3, e), (3, 1, e + HALF))
    return ((0, 2, e), (1, 0, e), (2, 1, e - HALF), (3, 4, e - HALF))


def weight_grads_kernel(idx, rows, act, d_out, d_gh, d_up, *refs):
    x_far = refs[:5]
    z_far = refs[5:10]
    x_bufs = refs[10:15]
    z_bufs = refs[15:20]
    whole, whole_down, x_sems, z_sems = refs[20:24]
    quarter = D // 4
    down_q = FE // 4
    small = quarter // 4
    small_down = down_q // 4
    copies = []
    for e in range(LOCAL):
        both = jnp.concatenate([d_gh[e], d_up[e]], axis=1)
        whole[...] = mm_tn(rows[e], both).astype(BF)
        whole_down[...] = mm_tn(act[e], d_out[e]).astype(BF)
        for k, item, place in ring_places(e):
            target = x_bufs[item].at[place]
            at = (idx[11] + k) % 4
            start = pl.multiple_of(at * quarter, quarter)
            target[:quarter, :] = whole[pl.ds(start, quarter), :FE]
            start = pl.multiple_of(at * down_q, down_q)
            target[quarter:, :] = whole_down[pl.ds(start, down_q), :FE]
            copy = pltpu.make_async_copy(target, x_far[item].at[place], x_sems.at[e, k])
            copy.start()
            copies.append(copy)
        for k, item, place in ring_places(e):
            target = z_bufs[item].at[place]
            at = (idx[12] + k) % 4
            for x in range(4):
                start = pl.multiple_of(x * quarter + at * small, small)
                target[x, :small, :] = whole[pl.ds(start, small), FE:]
                start = pl.multiple_of(x * down_q + at * small_down, small_down)
                target[x, small:, :] = whole_down[pl.ds(start, small_down), FE:]
            copy = pltpu.make_async_copy(target, z_far[item].at[place], z_sems.at[e, k])
            copy.start()
            copies.append(copy)
    for copy in copies:
        copy.wait()


def weight_grads(idx, rows, act, d_out, d_gh, d_up):
    x_piece = (XROWS, FE)
    z_piece = (4, ZROWS, FE)
    shapes = [(LOCAL, *x_piece)] * 3 + [(HALF, *x_piece)] * 2
    shapes += [(LOCAL, *z_piece)] * 3 + [(HALF, *z_piece)] * 2
    outs = [hbm(*shape) for shape in shapes]
    scratch = [pltpu.VMEM(shape, BF) for shape in shapes]
    scratch += [pltpu.VMEM((D, 2 * FE), BF), pltpu.VMEM((FE, D), BF)]
    scratch += [pltpu.SemaphoreType.DMA((LOCAL, 4))] * 2
    ins = [rows, act, d_out, d_gh, d_up]
    results = run(
        weight_grads_kernel, "weight_grads", 6, ins, outs, scratch, far_out=10, limit=24, idx=idx
    )
    return results[:5], results[5:]


def relay_kernel(*refs):
    far = refs[:8]
    outs_far = refs[8:12]
    bufs = refs[12:20]
    outs = refs[20:24]
    in_sems, out_sems = refs[24:26]
    loads = [
        [
            fetch(
                [item.at[e] for item in far[pair : pair + 2]],
                [item.at[e] for item in bufs[pair : pair + 2]],
                in_sems.at[pair // 2, e],
            )
            for e in range(HALF)
        ]
        for pair in range(0, 8, 2)
    ]
    stores = []
    for n in range(4):
        for e in range(HALF):
            for copy in loads[n][e]:
                copy.wait()
            outs[n][e] = (bufs[2 * n][e].astype(F32) + bufs[2 * n + 1][e].astype(F32)).astype(BF)
            copy = pltpu.make_async_copy(outs[n].at[e], outs_far[n].at[e], out_sems.at[n, e])
            copy.start()
            stores.append(copy)
    for copy in stores:
        copy.wait()


def relay(x_parts, z_parts):
    ins = [*x_parts, *z_parts]
    x_shape, z_shape = x_parts[0].shape, z_parts[0].shape
    shapes = [x_shape, x_shape, z_shape, z_shape]
    scratch = [pltpu.VMEM(shape, BF) for shape in (x_shape,) * 4 + (z_shape,) * 4]
    scratch += [pltpu.VMEM(shape, BF) for shape in shapes]
    scratch += [pltpu.SemaphoreType.DMA((4, HALF, 2)), pltpu.SemaphoreType.DMA((4, HALF))]
    outs = [hbm(*shape) for shape in shapes]
    return run(
        relay_kernel, "relay", 300, ins, outs, scratch, far_in=8, far_out=4, limit=FAR_LIMIT
    )


def mixed_kernel(idx, hot_gated, outs, far, blocks, sems):
    copies = []
    for p in range(PAIRS):
        part = slice(p * SLOTS, (p + 1) * SLOTS)
        values = jnp.concatenate([outs[n, part, :] for n in range(LOCAL)], axis=0)
        merged = mm_tn(hot_gated[p], values).astype(BF)
        for n in range(2):
            r = 2 * p + n
            blocks[r] = merged[n * ROWS : (n + 1) * ROWS]
            copy = pltpu.make_async_copy(
                blocks.at[r], far.at[idx[r], :, pl.ds(256, D)], sems.at[r]
            )
            copy.start()
            copies.append(copy)
    for copy in copies:
        copy.wait()


def mixed_sum(idx, hot_gated, outs):
    scratch = [pltpu.VMEM((BLOCKS, ROWS, D), BF), pltpu.SemaphoreType.DMA((BLOCKS,))]
    far = [hbm(BLOCKS, ROWS, 256 + D)]
    ins = [hot_gated, outs]
    return run(mixed_kernel, "mixed_sum", 0.6, ins, far, scratch, far_out=1, limit=10, idx=idx)[0]


def add_pairs_kernel(same, other, *outs):
    for off in range(4):
        outs[off][...] = (same[off].astype(F32) + other[off].astype(F32)).astype(BF)


def add_pairs(same, other):
    return run(
        add_pairs_kernel, "add_pairs", 0.3, [same, other], [vmem(*same.shape[1:])] * 4, limit=4
    )


def stage_kernel(cut, idx, *refs):
    far = refs[:5]
    outs_far = refs[5:9]
    bufs = refs[9:14]
    outs = refs[14:18]
    total, in_sems, out_sems = refs[18:21]
    own, from_below, from_above, late_below, late_above = range(5)
    needed = []
    loads = []
    for n in range(LOCAL):
        if n < HALF:
            places = ((own, n), (late_below, n), (from_above, n + HALF))
        else:
            places = ((own, n), (from_below, n), (late_above, n - HALF))
        needed.append(places)
        loads.append(
            fetch(
                [far[item].at[at] for item, at in places],
                [bufs[item].at[at] for item, at in places],
                in_sems.at[n],
            )
        )
    stores = []
    for n in range(LOCAL):
        for copy in loads[n]:
            copy.wait()
        parts = [bufs[item][at].astype(F32) for item, at in needed[n]]
        total[...] = (parts[0] + parts[1] + parts[2]).astype(BF)
        cut(idx, total, outs, n)
        stores += fetch(
            [item.at[n] for item in outs], [item.at[n] for item in outs_far], out_sems.at[n]
        )
    for copy in stores:
        copy.wait()


def stage_sums(idx, name, micros, cut, rows, parts):
    shapes = [(LOCAL, rows, FE)] * 4
    scratch = [pltpu.VMEM(part.shape, BF) for part in parts]
    scratch += [pltpu.VMEM(shape, BF) for shape in shapes]
    scratch += [pltpu.VMEM(parts[0].shape[1:], BF)]
    scratch += [pltpu.SemaphoreType.DMA((LOCAL, 3)), pltpu.SemaphoreType.DMA((LOCAL, 4))]
    return run(
        functools.partial(stage_kernel, cut),
        name,
        micros,
        parts,
        [hbm(*shape) for shape in shapes],
        scratch,
        far_in=5,
        far_out=4,
        limit=FAR_LIMIT,
        idx=idx,
    )


def cut_along_z(idx, total, outs, n):
    gate_rows = D // 16
    down_rows = FE // 16
    for k in range(4):
        at = (idx[12] + k) % 4
        start = pl.multiple_of(at * gate_rows, gate_rows)
        outs[k][n, :gate_rows, :] = total[pl.ds(start, gate_rows), :]
        for m in range(LEFT // FE):
            start = pl.multiple_of(D // 4 + m * (FE // 4) + at * down_rows, down_rows)
            to = gate_rows + m * down_rows
            outs[k][n, to : to + down_rows, :] = total[pl.ds(start, down_rows), :]


def cut_along_x(idx, total, outs, n):
    for k in range(4):
        outs[k][n] = total[pl.ds((idx[11] + k) % 4, 1)][0]


SEND_ROWS = (QROWS + ZROWS) // 2


def finish_kernel(idx, *refs):
    far = refs[:8]
    outs_far = refs[8:11]
    send_far = refs[11]
    bufs = refs[12:20]
    keep_gate, keep_up, keep_down, send = keeps = refs[20:24]
    x_sum, z_sum, in_sems, out_sems = refs[24:28]
    loads = [
        fetch([item.at[n] for item in far], [item.at[n] for item in bufs], in_sems.at[n])
        for n in range(LOCAL)
    ]
    big = D // 16
    small = big // 2
    tiny = FE // 32
    mine = idx[9]
    theirs = 1 - mine
    stores = []
    for n in range(LOCAL):
        for copy in loads[n]:
            copy.wait()
        acc = bufs[0][n].astype(F32)
        for part in bufs[1:4]:
            acc = acc + part[n].astype(F32)
        x_sum[...] = acc
        acc = bufs[4][n].astype(F32)
        for part in bufs[5:8]:
            acc = acc + part[n].astype(F32)
        z_sum[...] = acc
        here = pl.ds(pl.multiple_of(mine * small, small), small)
        there = pl.ds(pl.multiple_of(theirs * small, small), small)
        keep_gate[n] = x_sum[here, :]
        keep_up[n] = z_sum[here, :]
        send[n, :small, :] = x_sum[there, :].astype(BF)
        send[n, small:big, :] = z_sum[there, :].astype(BF)
        for m in range(D // FE):
            source, at = (x_sum, m) if m < LEFT // FE else (z_sum, m - LEFT // FE)
            first = big + at * 2 * tiny
            here = pl.ds(pl.multiple_of(first + mine * tiny, tiny), tiny)
            there = pl.ds(pl.multiple_of(first + theirs * tiny, tiny), tiny)
            keep_down[n, :, m * FE : (m + 1) * FE] = source[here, :]
            send[n, big + m * tiny : big + (m + 1) * tiny, :] = source[there, :].astype(BF)
        targets = [item.at[mine * LOCAL + n] for item in outs_far] + [send_far.at[n]]
        stores += fetch([item.at[n] for item in keeps], targets, out_sems.at[n])
    for copy in stores:
        copy.wait()


def finish(idx, parts):
    outs = [
        hbm(2 * LOCAL, D // 32, FE, dtype=F32),
        hbm(2 * LOCAL, D // 32, FE, dtype=F32),
        hbm(2 * LOCAL, FE // 32, D, dtype=F32),
        hbm(LOCAL, SEND_ROWS, FE),
    ]
    scratch = [pltpu.VMEM(part.shape, BF) for part in parts]
    scratch += [
        pltpu.VMEM((LOCAL, D // 32, FE), F32),
        pltpu.VMEM((LOCAL, D // 32, FE), F32),
        pltpu.VMEM((LOCAL, FE // 32, D), F32),
        pltpu.VMEM((LOCAL, SEND_ROWS, FE), BF),
        pltpu.VMEM((QROWS, FE), F32),
        pltpu.VMEM((ZROWS, FE), F32),
        pltpu.SemaphoreType.DMA((LOCAL, 8)),
        pltpu.SemaphoreType.DMA((LOCAL, 4)),
    ]
    return run(
        finish_kernel,
        "finish",
        1,
        parts,
        outs,
        scratch,
        far_in=8,
        far_out=4,
        limit=FAR_LIMIT,
        idx=idx,
    )


def assemble_kernel(idx, got, gate_in, up_in, down_in, *refs):
    outs_far = refs[:3]
    gate, up, down, out_sems = refs[3:7]
    small = D // 32
    tiny = FE // 32
    stores = []
    for n in range(LOCAL):
        gate[n] = got[n, :small, :].astype(F32)
        up[n] = got[n, small : 2 * small, :].astype(F32)
        down[n, :, :FE] = got[n, 2 * small : 2 * small + tiny, :].astype(F32)
        down[n, :, FE:] = got[n, 2 * small + tiny :, :].astype(F32)
        targets = [item.at[(1 - idx[9]) * LOCAL + n] for item in outs_far]
        stores += fetch([gate.at[n], up.at[n], down.at[n]], targets, out_sems.at[n])
    for copy in stores:
        copy.wait()


def assemble(idx, got, results):
    outs = [hbm(*item.shape, dtype=F32) for item in results]
    scratch = [
        pltpu.VMEM((LOCAL, D // 32, FE), F32),
        pltpu.VMEM((LOCAL, D // 32, FE), F32),
        pltpu.VMEM((LOCAL, FE // 32, D), F32),
        pltpu.SemaphoreType.DMA((LOCAL, 3)),
    ]
    return run(
        assemble_kernel,
        "assemble",
        1,
        [got, *results],
        outs,
        scratch,
        far_in=3,
        far_out=3,
        limit=8,
        idx=idx,
        aliases={2: 0, 3: 1, 4: 2},
    )


def middle_kernel(*refs):
    parts = refs[:4]
    h_ref, gate_ref, dy_ref, gain_ref, router_t, w_out = refs[4:10]
    dh_ref, send_ref, side_ref = refs[10:13]
    total = parts[0][...].astype(F32)
    for part in parts[1:]:
        total = total + part[...].astype(F32)
    extra = total[:, D:]
    d_gate = extra + pltpu.roll(extra, 128 - EXPERTS, 1)
    gate = gate_ref[...]
    d_chosen = gate * (d_gate - jnp.sum(gate * d_gate, axis=1, keepdims=True))
    d_logits = d_chosen.astype(BF)
    d_mlp = total[:, :D] + mm(d_logits, router_t[...])
    h = h_ref[...]
    gain = gain_ref[...].astype(F32)
    scale = lax.rsqrt(jnp.mean(h * h, axis=1, keepdims=True) + EPS)
    normed = h * scale
    mlp_in = (normed * gain).astype(BF)
    scaled = d_mlp * gain
    d_h = (
        dy_ref[...].astype(F32)
        + scale * scaled
        - h * (scale * scale * scale) * jnp.mean(scaled * h, axis=1, keepdims=True)
    )
    dh_ref[...] = d_h
    d_branch = d_h.astype(BF)
    d_attn = mm_nt(d_branch, w_out[...]).astype(BF)
    for b in range(BLOCKS):
        cols = slice(b * 128, (b + 1) * 128)
        send_ref[b, :, :128] = d_attn[:, cols]
        send_ref[b, :, 128:] = d_branch[:, cols]
    router = mm_tn(mlp_in, d_logits)
    d_gain = jnp.sum(d_mlp * normed, axis=0, keepdims=True)
    column = jnp.transpose(jnp.broadcast_to(d_gain, (128, D)))
    lane = lax.broadcasted_iota(jnp.int32, (D, 128), 1)
    side_ref[...] = jnp.where(lane == GAIN_LANE, column, router).astype(BF)


def middle(parts, h_own, gate_own, dy, gain, router_t, w_out):
    shapes = [((ROWS, D), F32), ((BLOCKS, ROWS, 256), BF), ((D, 128), BF)]

    def kernel(*refs):
        inputs = refs[:10]
        far = refs[10:13]
        bufs = refs[13:16]
        middle_kernel(*inputs, *bufs)
        for copy in fetch(bufs, far, refs[16]):
            copy.wait()

    outs = [hbm(*shape, dtype=kind) for shape, kind in shapes]
    scratch = [pltpu.VMEM(shape, kind) for shape, kind in shapes] + [pltpu.SemaphoreType.DMA((3,))]
    ins = [*parts, h_own, gate_own, dy, gain, router_t, w_out]
    return run(kernel, "middle", 100, ins, outs, scratch, far_out=3, limit=10)


def attend_back_kernel(idx, *refs):
    early_far = refs[:6]
    far = refs[6:10]
    pack, dense_far = refs[11:13]
    early = refs[13:19]
    p_ref, attn_in, ao_all, side_ref, dk_acc, dv_acc, dqkv_ref, dense, k_turned = refs[19:28]
    sems, early_sems, tables_sems = refs[28:31]
    grads, q_ref, k_ref, v_ref, cos_ref, sin_ref = early
    early_copies = fetch(early_far[:4], early[:4], early_sems)
    p_copies = [
        pltpu.make_async_copy(far[0].at[i], p_ref.at[i], sems.at[i]) for i in range(BLOCKS)
    ]
    ao_copy = pltpu.make_async_copy(far[2], ao_all, sems.at[BLOCKS])
    in_copy = pltpu.make_async_copy(far[1], attn_in, sems.at[BLOCKS + 1])
    p_copies[0].start()
    table_copies = fetch(early_far[4:], early[4:], tables_sems)
    p_copies[1].start()
    p_copies[2].start()
    side_copy = pltpu.make_async_copy(far[3], side_ref, sems.at[2 * BLOCKS + 3])
    dk_acc[...] = jnp.zeros((LEN, HD), F32)
    dv_acc[...] = jnp.zeros((LEN, HD), F32)
    for copy in early_copies:
        copy.wait()
    k_wide = jnp.concatenate([k_ref[...], k_ref[...]], axis=1).astype(F32)
    k_turned[...] = jnp.transpose(k_wide)[:HD, :].astype(BF)
    for i in range(BLOCKS):
        lo = max(0, i - WIN // ROWS) * ROWS
        hi = (i + 1) * ROWS
        span = hi - lo
        rows = slice(i * ROWS, hi)
        do2 = jnp.concatenate([grads[i, :, :HD], grads[i, :, HD : 2 * HD]], axis=0)
        q2 = jnp.concatenate([q_ref[rows, :HD], q_ref[rows, HD:]], axis=0)
        p_copies[i].wait()
        if i + 3 < BLOCKS:
            p_copies[i + 3].start()
        if i == 2:
            in_copy.start()
            side_copy.start()
            ao_copy.start()
        probs_low = p_ref[i, :span, :]
        probs = probs_low.astype(F32)
        d_probs = mm_nt(v_ref[lo:hi, :], do2)
        weighted = probs * d_probs
        d_scores = (weighted - probs * jnp.sum(weighted, axis=0, keepdims=True)).astype(BF)
        dk_acc[lo:hi, :] += mm(d_scores, q2)
        dv_acc[lo:hi, :] += mm(probs_low, do2)
        dq = mm(k_turned[:, lo:hi], d_scores) * HD**-0.5
        dq = jnp.transpose(jnp.concatenate([dq[:, :ROWS], dq[:, ROWS:]], axis=0))
        dq = dq.astype(BF).astype(F32)
        if i == 0:
            for copy in table_copies:
                copy.wait()
        dq = dq * cos_ref[rows, :] - swap_halves(dq) * sin_ref[rows, :]
        dqkv_ref[rows, : 2 * HD] = dq.astype(BF)
    pair = jnp.concatenate([dk_acc[...], dv_acc[...]], axis=1).astype(BF).astype(F32)
    turned = pair * cos_ref[...] - swap_halves(pair) * sin_ref[...]
    lane = lax.broadcasted_iota(jnp.int32, pair.shape, 1)
    dqkv_ref[:, 2 * HD :] = jnp.where(lane < HD, turned, pair).astype(BF)
    dqkv_copies = []
    for r in range(BLOCKS):
        copy = pltpu.make_async_copy(
            dqkv_ref.at[pl.ds(r * ROWS, ROWS), :],
            pack.at[r, :, pl.ds(0, 256)],
            sems.at[BLOCKS + 3 + r],
        )
        copy.start()
        dqkv_copies.append(copy)
    in_copy.wait()
    ao_copy.wait()
    half = D // 2
    side_copy.wait()
    d_branch = jnp.concatenate([grads[b, :, 128:] for b in range(BLOCKS)], axis=0)
    left_turned = mm_tn(dqkv_ref[...], attn_in[...])
    right_turned = mm_tn(d_branch, ao_all[...])
    for part in range(2):
        rows = slice(part * half, (part + 1) * half)
        left = jnp.transpose(left_turned[:, rows])
        right = jnp.concatenate(
            [jnp.transpose(right_turned[:, rows]), side_ref[rows, :].astype(F32)], axis=1
        )
        both = jnp.concatenate([left.reshape(-1, 8, 256), right.reshape(-1, 8, 256)], axis=1)
        places = pl.ds(part * (half // 8), half // 8)
        dense[places] = both.astype(BF)
        copy = pltpu.make_async_copy(
            dense.at[places], dense_far.at[places], sems.at[(BLOCKS + 2, 2 * BLOCKS + 4)[part]]
        )
        copy.start()
        dqkv_copies.append(copy)
    for copy in dqkv_copies:
        copy.wait()


def attend_back(idx, grads, p, q, k, v, attn_in, ao_all, side, cos_tab, sin_tab, pack):
    early = [grads, q, k, v, cos_tab, sin_tab]
    outs = [hbm(*pack.shape), hbm(D // 8, 16, 256)]
    scratch = [pltpu.VMEM(item.shape, item.dtype) for item in early]
    scratch += [
        pltpu.VMEM(p.shape, BF),
        pltpu.VMEM((LEN, D), BF),
        pltpu.VMEM((LEN, D), BF),
        pltpu.VMEM((D, 128), BF),
        pltpu.VMEM((LEN, HD), F32),
        pltpu.VMEM((LEN, HD), F32),
        pltpu.VMEM((LEN, 256), BF),
        pltpu.VMEM((D // 8, 16, 256), BF),
        pltpu.VMEM((HD, LEN), BF),
        pltpu.SemaphoreType.DMA((2 * BLOCKS + 5,)),
        pltpu.SemaphoreType.DMA((4,)),
        pltpu.SemaphoreType.DMA((2,)),
    ]
    ins = [*early, p, attn_in, ao_all, side, pack]
    return run(
        attend_back_kernel,
        "attend_back",
        8,
        ins,
        outs,
        scratch,
        far_in=11,
        far_out=2,
        limit=FAR_LIMIT,
        idx=idx,
        aliases={11: 0},
    )


def input_grad_kernel(pack, *refs):
    far = refs[:7]
    outs_far = refs[7:9]
    bufs = refs[9:16]
    out, block, dq, dk, dv, early_sems, late_sems, out_sems = refs[16:24]
    early = fetch(far[:4], bufs[:4], early_sems)
    late = fetch(far[4:], bufs[4:], late_sems)
    x_ref, dh_ref, gain_ref, h_own, w_query, w_key, w_value = bufs
    for b in range(BLOCKS):
        dq[:, b * 128 : (b + 1) * 128] = pack[b, :, :128]
    for b in range(0, BLOCKS, 2):
        first = pack[b, :, 128:256].astype(F32)
        second = pack[b + 1, :, 128:256].astype(F32)
        cols = slice(b * HD, (b + 2) * HD)
        dk[:, cols] = jnp.concatenate([first[:, :HD], second[:, :HD]], axis=1).astype(BF)
        dv[:, cols] = jnp.concatenate([first[:, HD:], second[:, HD:]], axis=1).astype(BF)
    for copy in early:
        copy.wait()
    total = h_own[...]
    for b in range(BLOCKS):
        total = total + pack[b, :, 256:].astype(F32)
    block[...] = total.astype(BF)
    for copy in late:
        copy.wait()
    d_in = mm_nt(dq[...], w_query[...]) + mm_nt(dk[...], w_key[...]) + mm_nt(dv[...], w_value[...])
    x = x_ref[...].astype(F32)
    scale = lax.rsqrt(jnp.mean(x * x, axis=1, keepdims=True) + EPS)
    scaled = d_in * gain_ref[...]
    out[...] = (
        dh_ref[...]
        + scale * scaled
        - x * (scale * scale * scale) * jnp.mean(scaled * x, axis=1, keepdims=True)
    ).astype(BF)
    for copy in fetch((out, block), outs_far, out_sems):
        copy.wait()


def input_grad(pack, x, d_h, gain, h_own, w_query, w_key, w_value):
    ins = [pack, x, d_h, gain, h_own, w_query, w_key, w_value]
    scratch = [pltpu.VMEM(item.shape, item.dtype) for item in ins[1:]]
    scratch += [
        pltpu.VMEM((ROWS, D), BF),
        pltpu.VMEM((ROWS, D), BF),
        pltpu.VMEM((ROWS, H * HD), BF),
        pltpu.VMEM((ROWS, KVH * HD), BF),
        pltpu.VMEM((ROWS, KVH * HD), BF),
        pltpu.SemaphoreType.DMA((4,)),
        pltpu.SemaphoreType.DMA((3,)),
        pltpu.SemaphoreType.DMA((2,)),
    ]
    return run(
        input_grad_kernel,
        "input_grad",
        1,
        ins,
        [hbm(ROWS, D)] * 2,
        scratch,
        far_in=len(ins) - 1,
        far_out=2,
        limit=FAR_LIMIT,
    )


def dense_out_kernel(idx, dense, w_query, w_key, w_value, gain, *refs):
    dq, dk, dv, do, router, gains, turned = refs
    total = jnp.sum(dense[...].astype(F32).reshape(-1, BLOCKS, 16, 256), axis=0)
    for b in range(BLOCKS):
        dq[:, b * 128 : (b + 1) * 128] = total[b, :8, :128]
        do[:, b * 128 : (b + 1) * 128] = total[b, 8:, :128]
    for b in range(0, BLOCKS, 2):
        first = total[b, :8, 128:]
        second = total[b + 1, :8, 128:]
        cols = slice(b * HD, (b + 2) * HD)
        dk[:, cols] = jnp.concatenate([first[:, :HD], second[:, :HD]], axis=1)
        dv[:, cols] = jnp.concatenate([first[:, HD:], second[:, HD:]], axis=1)
    side = jnp.sum(total[:, 8:, 128:], axis=0)
    router[...] = side[:, :EXPERTS]
    dot = jnp.zeros((8, 1), F32)
    for weight, grad in ((w_query, dq), (w_key, dk), (w_value, dv)):
        dot = dot + jnp.sum(weight[...] * grad[...], axis=1, keepdims=True)
    chunk = pl.ds(pl.multiple_of(idx[16] * 128, 128), 128)
    turned[...] = jnp.transpose(jnp.broadcast_to(gain[:, chunk], (128, 128)))
    gain_rows = turned[pl.ds(pl.multiple_of(idx[17] * 8, 8), 8), 0:1]
    lane = lax.broadcasted_iota(jnp.int32, (8, 128), 1)
    both = jnp.where(lane == GAIN_LANE, side, dot / gain_rows)
    turned[:8, :] = both
    flat = jnp.transpose(turned[...])
    gains[...] = flat[GAIN_LANE - 8 : GAIN_LANE + 8, :]


def dense_out(idx, dense, w_query, w_key, w_value, gain):
    outs = [
        auto(8, H * HD, dtype=F32),
        auto(8, KVH * HD, dtype=F32),
        auto(8, KVH * HD, dtype=F32),
        auto(8, D, dtype=F32),
        auto(8, EXPERTS, dtype=F32),
        auto(16, 128, dtype=F32),
    ]
    ins = [dense, w_query, w_key, w_value, gain]
    scratch = [pltpu.VMEM((128, 128), F32)]
    return run(dense_out_kernel, "dense_out", 1, ins, outs, scratch, limit=8, idx=idx)


def from_x(value, off):
    size = lax.axis_size("x")
    return lax.ppermute(value, "x", [(i, (i + off) % size) for i in range(size)])


def from_z(value, off):
    size = lax.axis_size("z")
    return lax.ppermute(value, "z", [(i, (i + off) % size) for i in range(size)])


def along_y(value, off):
    route = []
    for y in range(4):
        to = (y + off) % 4
        route.append(((y % 2) * 2 + y // 2, (to % 2) * 2 + to // 2))
    return lax.ppermute(value, ("yl", "yh"), route)


def other_core(value):
    return lax.ppermute(value, "c", [(0, 1), (1, 0)])


def near_ring(value):
    return [value] + [along_y(value, -off) for off in (1, 2, 3)]


def both_cores(near):
    far = [other_core(item) for item in near]
    return [item for pair in zip(near, far) for item in pair]


def gather_ring(value):
    return both_cores(near_ring(value))


def reduce_ring(pieces):
    return [pieces[0]] + [along_y(pieces[off], off) for off in (1, 2, 3)]


def scatter_parts(parts, send):
    return [parts[0]] + [send(parts[k], k) for k in (1, 2, 3)]


def together(*values):
    return lax.optimization_barrier(values)


def after(values, *earlier):
    return lax.optimization_barrier((values, earlier))[0]


def local(
    tokens,
    segments,
    routes,
    drop_order,
    gain_attn,
    w_query,
    w_key,
    w_value,
    w_out,
    gain_mlp,
    w_router,
    w_gate,
    w_up,
    w_down,
    cotangent,
):
    x_at = lax.axis_index("x")
    z_at = lax.axis_index("z")
    yl = lax.axis_index("yl")
    yh = lax.axis_index("yh")
    core = lax.axis_index("c")
    y_at = yh * 2 + yl
    own = yl * 4 + yh * 2 + core
    expert_at = yh * 2 + core

    entries = []
    for off in range(4):
        y = (y_at + off) % 4
        for dc in range(2):
            entries.append((y % 2) * 4 + (y // 2) * 2 + (core + dc) % 2)
    entries += [own, yl, expert_at, x_at, z_at, y_at, core, expert_at * 8 + yl * LOCAL]
    first_row = ((x_at * 4 + z_at) * 8 + own) * 8
    entries += [first_row // 128, first_row % 128 // 8]
    idx = jnp.stack([jnp.asarray(entry, jnp.int32) for entry in entries])

    cos_np, sin_np = rotary_tables()
    cos_tab = jnp.asarray(cos_np)
    sin_tab = jnp.asarray(sin_np)
    gain_one = gain_attn.astype(F32).reshape(1, D)
    gain_two = gain_mlp.astype(F32).reshape(1, D)
    router_t = jnp.pad(w_router.T, ((0, 128 - EXPERTS), (0, 0)))

    def columns(weight, block):
        return lax.dynamic_slice_in_dim(weight, block * 128, 128, 1)

    def out_rows(weight):
        return lax.dynamic_slice_in_dim(weight, first_row, 8, 0).astype(F32)

    wq_cols = columns(w_query, own)
    wk_cols = columns(w_key, own // 2)
    wv_cols = columns(w_value, own // 2)
    finals = [out_rows(w_query), out_rows(w_key), out_rows(w_value)]
    early = [idx, gain_one, gain_two, router_t, wq_cols, wk_cols, wv_cols, finals]

    seg_cols = jnp.broadcast_to(segments.astype(BF)[:, None], (ROWS, AUG - D))
    x_near = near_ring(jnp.concatenate([tokens, seg_cols], axis=1))
    slot_own = slots(routes.T, drop_order)
    x_near, slot_own, early = together(x_near, slot_own, early)
    idx, gain_one, gain_two, router_t, wq_cols, wk_cols, wv_cols, finals = early
    xs = both_cores(x_near)
    dy_near = near_ring(after(cotangent, slot_own))

    ao, attn_in, q, k, v, p = attend(
        idx, xs, slot_own, gain_one, wq_cols, wk_cols, wv_cols, cos_tab, sin_tab
    )
    dys = both_cores(dy_near)
    aos = gather_ring(after(ao, *dy_near))
    mlp_in, slot_t, gate_t, h_own, gate_own, ao_all = project(
        idx, xs, aos, w_out, gain_two, router_t
    )
    rows, act, d_out, d_gh, d_up, hot_gated, outs, dm_same, dm_other = experts(
        idx, mlp_in, dys, slot_t, gate_t, w_gate, w_up, w_down
    )

    got = other_core(dm_other)
    pack = mixed_sum(idx, hot_gated, outs)
    pack, got = together(pack, got)
    dm_pieces = add_pairs(dm_same, got)
    dm_parts = reduce_ring(dm_pieces)
    (x_up, x_down, *x_keep), (z_up, z_down, *z_keep) = weight_grads(
        idx, after(rows, *dm_pieces), act, d_out, d_gh, d_up
    )
    x_below = from_x(x_up, 1)
    x_above = from_x(x_down, 3)
    z_keep, z_up, z_down, dm_parts = together(z_keep, z_up, z_down, dm_parts)
    z_below = from_z(z_up, 1)
    z_above = from_z(z_down, 3)
    d_h, to_heads, side = middle(
        dm_parts, h_own, gate_own, cotangent, gain_two, router_t, w_out
    )
    grads = lax.all_to_all(to_heads, GROUP, split_axis=0, concat_axis=0, tiled=True)
    pack, dense = attend_back(
        idx, grads, p, q, k, v, attn_in, ao_all, side, cos_tab, sin_tab, pack
    )
    x_below, x_above, z_below, z_above = after([x_below, x_above, z_below, z_above], pack)
    dense = lax.all_to_all(
        dense, ("x", "z", "yl", "yh", "c"), split_axis=0, concat_axis=0, tiled=True
    )

    relayed = relay(
        [x_keep[1], x_below, x_keep[2], x_above], [z_keep[1], z_below, z_keep[2], z_above]
    )
    x_late = [from_x(relayed[0], 1), from_x(relayed[1], 3)]
    z_late = [from_z(relayed[2], 1), from_z(relayed[3], 3)]
    pack = lax.all_to_all(
        after(pack, dense, *relayed), GROUP, split_axis=0, concat_axis=0, tiled=True
    )
    dense_rows = dense_out(idx, dense, *finals, gain_one)
    x_pieces = stage_sums(
        idx, "x_sums", 200, cut_along_z, QROWS, [x_keep[0], x_below, x_above, *x_late]
    )
    z_pieces = stage_sums(
        idx, "z_sums", 200, cut_along_x, ZROWS, [z_keep[0], z_below, z_above, *z_late]
    )
    x_second = scatter_parts(x_pieces, from_z)
    z_second = scatter_parts(z_pieces, from_x)
    d_tokens, block_out = input_grad(
        after(pack, *x_pieces, *z_pieces), tokens, d_h, gain_one, h_own, w_query, w_key, w_value
    )
    d_tokens, x_second, z_second, dense_rows = together(d_tokens, x_second, z_second, dense_rows)

    *results, sent = finish(idx, [*x_second, *z_second])
    got = lax.ppermute(sent, "yl", [(0, 1), (1, 0)])
    d_w_gate, d_w_up, d_w_down = assemble(idx, got, results)
    d_w_query, d_w_key, d_w_value, d_w_out, d_w_router, gains = dense_rows
    d_gain_attn = gains[0, :8]
    d_gain_mlp = gains[8, :8]

    return (
        block_out,
        d_tokens,
        d_gain_attn,
        d_w_query,
        d_w_key,
        d_w_value,
        d_w_out,
        d_gain_mlp,
        d_w_router,
        d_w_gate,
        d_w_up,
        d_w_down,
    )


def solution(mesh):
    side = 4 if mesh.shape["dp"] == 32 else 1
    names = ("x", "z", "yl", "yh", "c")
    grid = Mesh(mesh.devices.reshape(side, side, 2, 2, 2), names)
    tokens = names
    experts_axes = ("yh", "c")
    dp = ("x", "z", "yl")
    in_specs = (
        P(tokens, None),
        P(tokens),
        P(tokens, None),
        P(tokens, None),
        P(),
        P(),
        P(),
        P(),
        P(),
        P(),
        P(),
        P(experts_axes, None, None),
        P(experts_axes, None, None),
        P(experts_axes, None, None),
        P(tokens, None),
    )
    out_specs = (
        P(tokens, None),
        P(tokens, None),
        P(tokens),
        P(tokens, None),
        P(tokens, None),
        P(tokens, None),
        P(tokens, None),
        P(tokens),
        P(tokens, None),
        P(experts_axes, dp, None),
        P(experts_axes, dp, None),
        P(experts_axes, dp, None),
    )
    return jax.shard_map(local, mesh=grid, in_specs=in_specs, out_specs=out_specs, check_vma=False)
```

```python
import functools

import jax
import jax.numpy as jnp
import numpy as np
from jax import lax
from jax.experimental import pallas as pl
from jax.experimental.pallas import tpu as pltpu
from jax.sharding import Mesh, PartitionSpec as P

H = 16
KVH = 8
HD = 64
D = 1024
FE = 512
TOPK = 8
EXPERTS = 32
CAP = 36
ROWS = 128
LEN = 1024
BLOCKS = LEN // ROWS
WIN = 512
LOCAL = 4
PAIRS = BLOCKS // 2
SLOTS = 80
EROWS = PAIRS * SLOTS
AUG = D + 128
GAIN_LANE = 32
FAR_LIMIT = 63
SHARE = 0.1
EPS = 1e-06
THETA = 10000.0
NEG = -1e30
BF = jnp.bfloat16
F32 = jnp.float32
GROUP = ("yl", "yh", "c")


def mm(left, right):
    return jnp.dot(left, right, preferred_element_type=F32)


def mm_nt(left, right):
    return lax.dot_general(left, right, (((1,), (1,)), ((), ())), preferred_element_type=F32)


def mm_tn(left, right):
    return lax.dot_general(left, right, (((0,), (0,)), ((), ())), preferred_element_type=F32)


def rotary_tables():
    half = HD // 2
    frequency = THETA ** (-np.arange(half, dtype=np.float64) * 2.0 / HD)
    angles = np.arange(LEN, dtype=np.float64)[:, None] * frequency[None, :]
    cosine = np.cos(angles)
    sine = np.sin(angles)
    cos_full = np.concatenate([cosine] * 4, axis=1).astype(np.float32)
    sin_full = np.concatenate([-sine, sine, -sine, sine], axis=1).astype(np.float32)
    return cos_full, sin_full


def swap_halves(array_in):
    half = HD // 2
    lane = lax.broadcasted_iota(jnp.int32, array_in.shape, 1)
    ahead = pltpu.roll(array_in, array_in.shape[1] - half, 1)
    behind = pltpu.roll(array_in, half, 1)
    return jnp.where(lane % HD < half, ahead, behind)


def vmem(*shape, dtype=BF):
    return pltpu.VMEM(shape, dtype)


def hbm(*shape, dtype=BF):
    return pltpu.HBM(shape, dtype)


def auto(*shape, dtype=BF):
    return jax.ShapeDtypeStruct(shape, dtype)


def cost(micros):
    return pl.CostEstimate(
        flops=int(micros * 1.15e9 * SHARE), bytes_accessed=int(micros * 1e6), transcendentals=0
    )


def run(
    kernel,
    name,
    micros,
    ins,
    outs,
    scratch=(),
    far_in=0,
    far_out=0,
    limit=24,
    idx=None,
    aliases=None,
):
    inside = pl.BlockSpec(memory_space=pltpu.VMEM)
    outside = pl.BlockSpec(memory_space=pltpu.HBM)
    in_specs = [inside] * (len(ins) - far_in) + [outside] * far_in
    operands = list(ins)
    if idx is not None:
        in_specs = [pl.BlockSpec(memory_space=pltpu.SMEM)] + in_specs
        operands = [idx] + operands
    return pl.pallas_call(
        kernel,
        out_shape=list(outs),
        in_specs=in_specs,
        out_specs=[inside] * (len(outs) - far_out) + [outside] * far_out,
        scratch_shapes=list(scratch),
        input_output_aliases=aliases or {},
        compiler_params=pltpu.CompilerParams(vmem_limit_bytes=limit * 1024 * 1024),
        cost_estimate=cost(micros),
        name=name,
    )(*operands)


def run_far(kernel, name, micros, ins, outs, scratch=(), idx=None):
    count = len(ins)
    given = 0 if idx is None else 1

    def body(*refs):
        lead = refs[:given]
        sources = refs[given : given + count]
        targets = refs[given + count : given + count + len(outs)]
        rest = refs[given + count + len(outs) :]
        in_bufs = rest[:count]
        out_bufs = rest[count : count + len(outs)]
        in_sems, out_sems = rest[count + len(outs) : count + len(outs) + 2]
        for copy in fetch(sources, in_bufs, in_sems):
            copy.wait()
        kernel(*lead, *in_bufs, *out_bufs, *rest[count + len(outs) + 2 :])
        for copy in fetch(out_bufs, targets, out_sems):
            copy.wait()

    bufs = [pltpu.VMEM(item.shape, item.dtype) for item in ins]
    bufs += [pltpu.VMEM(item.shape, item.dtype) for item in outs]
    bufs += [pltpu.SemaphoreType.DMA((count,)), pltpu.SemaphoreType.DMA((len(outs),))]
    return run(
        body,
        name,
        micros,
        ins,
        outs,
        bufs + list(scratch),
        far_in=count,
        far_out=len(outs),
        limit=FAR_LIMIT,
        idx=idx,
    )


def fetch(sources, targets, sems):
    copies = [
        pltpu.make_async_copy(source, target, sems.at[n])
        for n, (source, target) in enumerate(zip(sources, targets))
    ]
    for copy in copies:
        copy.start()
    return copies


def slots_kernel(routes_ref, order_ref, meta_ref, place_ref):
    order = order_ref[...]
    index = lax.broadcasted_iota(jnp.int32, (1, ROWS * TOPK), 1)
    token_of = order // TOPK
    choice_of = order - token_of * TOPK
    at_token = (token_of == lax.broadcasted_iota(jnp.int32, (ROWS, ROWS * TOPK), 0)).astype(F32)
    choice = lax.broadcasted_iota(jnp.int32, (2 * TOPK, ROWS * TOPK), 0)
    high = index // 32
    low = index - high * 32
    part = jnp.where(choice < TOPK, high, low).astype(F32)
    choice_mod = jnp.where(choice < TOPK, choice, choice - TOPK)
    table = jnp.where(choice_mod == choice_of, part, 0.0)
    found = mm_nt(at_token.astype(BF), table.astype(BF))
    place = found[:, :TOPK] * 32.0 + found[:, TOPK:]
    lane = lax.broadcasted_iota(jnp.int32, (ROWS, 128), 1)
    wide = jnp.concatenate(
        [
            routes_ref[...].astype(F32),
            jnp.zeros((ROWS - TOPK, ROWS), F32),
        ],
        axis=0,
    )
    turned = jnp.transpose(wide)
    lane_f = lane.astype(F32)
    placed = jnp.full((ROWS, 128), 4096.0, F32)
    for k in range(TOPK):
        placed = jnp.where(turned[:, k : k + 1] == lane_f, place[:, k : k + 1], placed)
    place_ref[...] = placed

    def count(step, total):
        for inner in range(8):
            row = place_ref[pl.ds(step * 8 + inner, 1), :]
            total = total + jnp.where(row < placed, 1.0, 0.0)
        return total

    rank = lax.fori_loop(0, ROWS // 8, count, jnp.zeros((ROWS, 128), F32))
    slot = jnp.where(placed < 4000.0, jnp.where(rank < CAP, rank, -1.0), -2.0)
    meta_ref[...] = jnp.transpose(slot)[:EXPERTS, :].astype(BF)


def slots(routes_t, drop_order):
    return run(
        slots_kernel,
        "slots",
        3,
        [routes_t, drop_order],
        [auto(EXPERTS, ROWS)],
        [pltpu.VMEM((ROWS, 128), F32)],
        limit=8,
    )[0]


def attend_kernel(idx, *refs):
    xs = refs[:8]
    slots_ref, gain, wq, wk, wv, cos_ref, sin_ref = refs[8:15]
    out_ref = refs[15]
    far = refs[16:21]
    attn_in, q_ref, k_ref, v_ref, p_ref, seg_row, seg_col, v_turned, sems = refs[21:30]
    near = (attn_in, q_ref, k_ref, v_ref)
    copies = [pltpu.make_async_copy(near[n], far[n], sems.at[n]) for n in range(4)]
    gain_full = gain[...]
    for r in range(BLOCKS):
        rows = pl.ds(pl.multiple_of(idx[r] * ROWS, ROWS), ROWS)
        x = xs[r][:, :D].astype(F32)
        scale = lax.rsqrt(jnp.mean(x * x, axis=1, keepdims=True) + EPS)
        attn_in[rows, :] = (x * scale * gain_full).astype(BF)
        segs = xs[r][:, D:].astype(F32)
        seg_col[rows, :] = segs
        seg_row[:, rows] = jnp.transpose(segs)[:8, :]
    copies[0].start()
    out_ref[LEN:, :] = slots_ref[...]
    odd = (idx[8] % 2) == 1
    half = LEN // 2
    for part in range(2):
        rows = slice(part * half, (part + 1) * half)
        block = attn_in[rows, :]
        cosine = cos_ref[rows, :]
        sine = sin_ref[rows, :]
        q = mm(block, wq[...])
        q = q * cosine + swap_halves(q) * sine
        q_ref[rows, :] = (q.astype(BF).astype(F32) * HD**-0.5).astype(BF)
        k = mm(block, wk[...])
        k = jnp.where(odd, pltpu.roll(k, HD, 1), k)
        k = k * cosine + swap_halves(k) * sine
        k_ref[rows, :] = k[:, :HD].astype(BF)
        v = mm(block, wv[...])
        v = jnp.where(odd, pltpu.roll(v, HD, 1), v)
        v_ref[rows, :] = v[:, :HD].astype(BF)
        v_turned[:, rows] = jnp.transpose(v)[:HD, :].astype(BF)
    for copy in copies[1:]:
        copy.start()
    k_at = lax.broadcasted_iota(jnp.int32, (ROWS, ROWS), 0)
    q_at = lax.broadcasted_iota(jnp.int32, (ROWS, ROWS), 1)
    causal = jnp.where(k_at <= q_at, 0.0, NEG)
    inside = jnp.where(k_at > q_at, 0.0, NEG)
    for i in range(BLOCKS):
        lo = max(0, i - WIN // ROWS) * ROWS
        hi = (i + 1) * ROWS
        span = hi - lo
        rows = slice(i * ROWS, hi)
        q2 = jnp.concatenate([q_ref[rows, :HD], q_ref[rows, HD:]], axis=0)
        scores = mm_nt(k_ref[lo:hi, :], q2)
        same = jnp.where(seg_col[lo:hi, 0:1] == seg_row[0:1, rows], 0.0, NEG)
        pieces = [same[n * ROWS : (n + 1) * ROWS] for n in range(span // ROWS)]
        pieces[-1] = pieces[-1] + causal
        if i >= WIN // ROWS:
            pieces[0] = pieces[0] + inside
        bias = jnp.concatenate(pieces, axis=0)
        scores = scores + jnp.concatenate([bias, bias], axis=1)
        top = jnp.max(scores, axis=0, keepdims=True)
        expo = jnp.exp(scores - top)
        total = jnp.sum(expo, axis=0, keepdims=True)
        probs = (expo * (1.0 / total)).astype(BF)
        p_ref[i, :span, :] = probs
        if span < WIN + ROWS:
            p_ref[i, span:, :] = jnp.zeros((WIN + ROWS - span, 2 * ROWS), BF)
        copy = pltpu.make_async_copy(p_ref.at[i], far[4].at[i], sems.at[4 + i])
        copy.start()
        copies.append(copy)
        out = mm(v_turned[:, lo:hi], probs)
        out = jnp.concatenate([out[:, :ROWS], out[:, ROWS:]], axis=0)
        out_ref[rows, :] = jnp.transpose(out).astype(BF)
    for copy in copies:
        copy.wait()


def attend(idx, xs, slot_own, gain, wq, wk, wv, cos_tab, sin_tab):
    shapes = [(LEN, D), (LEN, 2 * HD), (LEN, HD), (LEN, HD), (BLOCKS, WIN + ROWS, 2 * ROWS)]
    outs = [vmem(LEN + EXPERTS, 2 * HD)] + [hbm(*shape) for shape in shapes]
    scratch = [pltpu.VMEM(shape, BF) for shape in shapes]
    scratch += [pltpu.VMEM((8, LEN), F32), pltpu.VMEM((LEN, 128), F32)]
    scratch += [pltpu.VMEM((HD, LEN), BF), pltpu.SemaphoreType.DMA((4 + BLOCKS,))]
    ins = [*xs, slot_own, gain, wq, wk, wv, cos_tab, sin_tab]
    return run(attend_kernel, "attend", 7, ins, outs, scratch, far_out=5, limit=16, idx=idx)


def project_kernel(idx, *refs):
    xs = refs[:8]
    aos = refs[8:16]
    w_out, gain, router_t = refs[16:19]
    mlp_in, slot_t, gate_t, h_far, gate_far, ao_far = refs[19:25]
    ao_all, h_own, gate_own, sems = refs[25:29]
    for r in range(BLOCKS):
        cols = pl.ds(pl.multiple_of(idx[r] * ROWS, ROWS), ROWS)
        ao_all[:, cols] = aos[r][:LEN, :]
    ao_copy = pltpu.make_async_copy(ao_all, ao_far, sems.at[0])
    ao_copy.start()
    gain_full = gain[...]
    for p in range(PAIRS):
        rows = slice(p * 2 * ROWS, (p + 1) * 2 * ROWS)
        places = [pl.ds(pl.multiple_of(idx[2 * p + n] * ROWS, ROWS), ROWS) for n in range(2)]
        attended = jnp.concatenate([ao_all[place, :] for place in places], axis=0)
        x = jnp.concatenate([xs[2 * p + n][:, :D] for n in range(2)], axis=0).astype(F32)
        h = x + mm(attended, w_out[...])
        scale = lax.rsqrt(jnp.mean(h * h, axis=1, keepdims=True) + EPS)
        normed = (h * scale * gain_full).astype(BF)
        mlp_in[rows, :] = normed
        logits = mm_nt(router_t[:EXPERTS, :], normed)
        slot = jnp.concatenate([aos[2 * p + n][LEN:, :] for n in range(2)], axis=1).astype(F32)
        routed = slot > -1.5
        logits = jnp.where(routed, logits, NEG)
        top = jnp.max(logits, axis=0, keepdims=True)
        expo = jnp.where(routed, jnp.exp(logits - top), 0.0)
        gate = expo / jnp.sum(expo, axis=0, keepdims=True)
        slot_t[:, rows] = slot
        gate_t[:, rows] = gate
        if p == 0:
            h_own[...] = h[:ROWS]
            wide = jnp.concatenate(
                [gate[:, :ROWS], jnp.zeros((128 - EXPERTS, ROWS), F32)], axis=0
            )
            gate_own[...] = jnp.transpose(wide)
            own_copies = [
                pltpu.make_async_copy(h_own, h_far, sems.at[1]),
                pltpu.make_async_copy(gate_own, gate_far, sems.at[2]),
            ]
            for copy in own_copies:
                copy.start()
    ao_copy.wait()
    for copy in own_copies:
        copy.wait()


def project(idx, xs, aos, w_out, gain, router_t):
    outs = [
        vmem(LEN, D),
        vmem(EXPERTS, LEN, dtype=F32),
        vmem(EXPERTS, LEN, dtype=F32),
        hbm(ROWS, D, dtype=F32),
        hbm(ROWS, 128, dtype=F32),
        hbm(LEN, D),
    ]
    scratch = [
        pltpu.VMEM((LEN, D), BF),
        pltpu.VMEM((ROWS, D), F32),
        pltpu.VMEM((ROWS, 128), F32),
        pltpu.SemaphoreType.DMA((3,)),
    ]
    ins = [*xs, *aos, w_out, gain, router_t]
    return run(project_kernel, "project", 5, ins, outs, scratch, far_out=3, limit=14, idx=idx)


PROWS = LOCAL * SLOTS
HALF = LOCAL // 2
LEFT = FE
XROWS = D // 4 + FE // 4 * (LEFT // FE)
QROWS = XROWS // 4
ZROWS = D // 16 + FE // 16 * ((D - LEFT) // FE)


def experts_kernel(idx, *refs):
    mlp_in = refs[0]
    dys = refs[1:9]
    slot_t, gate_t, w_gate, w_up, w_down = refs[9:14]
    rows_out, act_out, dout_out, dg_out, du_out, hot_gated, outs, dm_same, dm_other = refs[14:23]
    wg_buf, wu_buf, wd_buf, sems, dy_rows, gate_col, hot, dslots = refs[23:31]

    def load(e):
        at = idx[9] * LOCAL + e
        slot = lax.rem(e, 2)
        return [
            pltpu.make_async_copy(weight.at[at], buf.at[slot], sems.at[slot, n])
            for n, (weight, buf) in enumerate(((w_gate, wg_buf), (w_up, wu_buf), (w_down, wd_buf)))
        ]

    for e in range(2):
        for copy in load(jnp.int32(e)):
            copy.start()
    for p in range(PAIRS):
        cols = slice(p * 2 * ROWS, (p + 1) * 2 * ROWS)
        part = slice(p * SLOTS, (p + 1) * SLOTS)
        lane = lax.broadcasted_iota(jnp.int32, (1, 2 * ROWS), 1)
        lift = jnp.where(lane >= ROWS, float(CAP), 0.0)
        row_id = lax.broadcasted_iota(jnp.int32, (SLOTS, 2 * ROWS), 0).astype(F32)
        hots = []
        for n in range(LOCAL):
            slot = slot_t[pl.ds(idx[15] + n, 1), cols]
            gate = gate_t[pl.ds(idx[15] + n, 1), cols]
            place = jnp.where(slot > -0.5, slot + lift, -1.0)
            one = jnp.where(row_id == place, 1.0, 0.0)
            gated_one = one * gate
            gate_col[n, part, :] = jnp.sum(gated_one, axis=1, keepdims=True)
            hots.append(one.astype(BF))
            hot_gated[p, n * SLOTS : (n + 1) * SLOTS, :] = gated_one.astype(BF)
        hot_pair = jnp.concatenate(hots, axis=0)
        hot[p] = hot_pair
        taken = mm(hot_pair, mlp_in[cols, :]).astype(BF)
        dy = jnp.concatenate([dys[2 * p][...], dys[2 * p + 1][...]], axis=0)
        taken_dy = mm(hot_pair, dy).astype(BF)
        for n in range(LOCAL):
            rows_out[n, part, :] = taken[n * SLOTS : (n + 1) * SLOTS]
            dy_rows[n, part, :] = taken_dy[n * SLOTS : (n + 1) * SLOTS]

    def one_expert(e, carry):
        for copy in load(e):
            copy.wait()
        at = lax.rem(e, 2)
        rows = rows_out[e]
        wg = wg_buf[at]
        wu = wu_buf[at]
        wd = wd_buf[at]
        gate_h = mm(rows, wg)
        up_h = mm(rows, wu)
        sig = 1.0 / (1.0 + jnp.exp(-gate_h))
        silu = gate_h * sig
        act = (silu * up_h).astype(BF)
        act_out[e] = act
        out = mm(act, wd).astype(BF)
        outs[e] = out
        dy = dy_rows[e].astype(F32)
        d_gate = jnp.sum(dy * out.astype(F32), axis=1, keepdims=True)
        d_out = (gate_col[e].astype(BF).astype(F32) * dy).astype(BF)
        dout_out[e] = d_out
        d_act = mm_nt(d_out, wd)
        d_up = (d_act * silu).astype(BF)
        d_gh = (d_act * up_h * sig * (1.0 + gate_h * (1.0 - sig))).astype(BF)
        dg_out[e] = d_gh
        du_out[e] = d_up
        dslots[e, :, :D] = (mm_nt(d_gh, wg) + mm_nt(d_up, wu)).astype(BF)
        lane = lax.broadcasted_iota(jnp.int32, (EROWS, 128), 1)
        d_high = d_gate.astype(BF).astype(F32)
        mine = idx[15] + e
        extra = jnp.where(lane == mine, d_high, 0.0)
        extra = jnp.where(lane == mine + EXPERTS, d_gate - d_high, extra)
        dslots[e, :, D:] = extra.astype(BF)

        @pl.when(e + 2 < LOCAL)
        def _():
            for copy in load(e + 2):
                copy.start()

        return carry

    lax.fori_loop(0, LOCAL, one_expert, 0)

    for p in range(PAIRS):
        part = slice(p * SLOTS, (p + 1) * SLOTS)
        grads = jnp.concatenate([dslots[n, part, :] for n in range(LOCAL)], axis=0)
        merged = mm_tn(hot[p], grads).astype(BF)
        dm_same[p] = merged[:ROWS]
        dm_other[p] = merged[ROWS:]


def experts(idx, mlp_in, dys, slot_t, gate_t, w_gate, w_up, w_down):
    wide = (LOCAL, EROWS, D)
    narrow = (LOCAL, EROWS, FE)
    hot_shape = (PAIRS, PROWS, 2 * ROWS)
    outs = [vmem(*shape) for shape in (wide, narrow, wide, narrow, narrow, hot_shape, wide)]
    outs += [vmem(4, ROWS, AUG)] * 2
    scratch = [
        pltpu.VMEM((2, D, FE), BF),
        pltpu.VMEM((2, D, FE), BF),
        pltpu.VMEM((2, FE, D), BF),
        pltpu.SemaphoreType.DMA((2, 3)),
        pltpu.VMEM(wide, BF),
        pltpu.VMEM((LOCAL, EROWS, 1), F32),
        pltpu.VMEM(hot_shape, BF),
        pltpu.VMEM((LOCAL, EROWS, AUG), BF),
    ]
    ins = [mlp_in, *dys, slot_t, gate_t, w_gate, w_up, w_down]
    return run(experts_kernel, "experts", 16, ins, outs, scratch, far_in=3, limit=26, idx=idx)


def ring_places(e):
    if e < HALF:
        return ((0, 2, e), (2, 0, e), (1, 3, e), (3, 1, e + HALF))
    return ((0, 2, e), (1, 0, e), (2, 1, e - HALF), (3, 4, e - HALF))


def weight_grads_kernel(idx, rows, act, d_out, d_gh, d_up, *refs):
    x_far = refs[:5]
    z_far = refs[5:10]
    x_bufs = refs[10:15]
    z_bufs = refs[15:20]
    whole, whole_down, x_sems, z_sems = refs[20:24]
    quarter = D // 4
    down_q = FE // 4
    small = quarter // 4
    small_down = down_q // 4
    copies = []
    for e in range(LOCAL):
        both = jnp.concatenate([d_gh[e], d_up[e]], axis=1)
        whole[...] = mm_tn(rows[e], both).astype(BF)
        whole_down[...] = mm_tn(act[e], d_out[e]).astype(BF)
        for k, item, place in ring_places(e):
            target = x_bufs[item].at[place]
            at = (idx[11] + k) % 4
            start = pl.multiple_of(at * quarter, quarter)
            target[:quarter, :] = whole[pl.ds(start, quarter), :FE]
            start = pl.multiple_of(at * down_q, down_q)
            target[quarter:, :] = whole_down[pl.ds(start, down_q), :FE]
            copy = pltpu.make_async_copy(target, x_far[item].at[place], x_sems.at[e, k])
            copy.start()
            copies.append(copy)
        for k, item, place in ring_places(e):
            target = z_bufs[item].at[place]
            at = (idx[12] + k) % 4
            for x in range(4):
                start = pl.multiple_of(x * quarter + at * small, small)
                target[x, :small, :] = whole[pl.ds(start, small), FE:]
                start = pl.multiple_of(x * down_q + at * small_down, small_down)
                target[x, small:, :] = whole_down[pl.ds(start, small_down), FE:]
            copy = pltpu.make_async_copy(target, z_far[item].at[place], z_sems.at[e, k])
            copy.start()
            copies.append(copy)
    for copy in copies:
        copy.wait()


def weight_grads(idx, rows, act, d_out, d_gh, d_up):
    x_piece = (XROWS, FE)
    z_piece = (4, ZROWS, FE)
    shapes = [(LOCAL, *x_piece)] * 3 + [(HALF, *x_piece)] * 2
    shapes += [(LOCAL, *z_piece)] * 3 + [(HALF, *z_piece)] * 2
    outs = [hbm(*shape) for shape in shapes]
    scratch = [pltpu.VMEM(shape, BF) for shape in shapes]
    scratch += [pltpu.VMEM((D, 2 * FE), BF), pltpu.VMEM((FE, D), BF)]
    scratch += [pltpu.SemaphoreType.DMA((LOCAL, 4))] * 2
    ins = [rows, act, d_out, d_gh, d_up]
    results = run(
        weight_grads_kernel, "weight_grads", 6, ins, outs, scratch, far_out=10, limit=24, idx=idx
    )
    return results[:5], results[5:]


def relay_kernel(*refs):
    far = refs[:8]
    outs_far = refs[8:12]
    bufs = refs[12:20]
    outs = refs[20:24]
    in_sems, out_sems = refs[24:26]
    loads = [
        [
            fetch(
                [item.at[e] for item in far[pair : pair + 2]],
                [item.at[e] for item in bufs[pair : pair + 2]],
                in_sems.at[pair // 2, e],
            )
            for e in range(HALF)
        ]
        for pair in range(0, 8, 2)
    ]
    stores = []
    for n in range(4):
        for e in range(HALF):
            for copy in loads[n][e]:
                copy.wait()
            outs[n][e] = (bufs[2 * n][e].astype(F32) + bufs[2 * n + 1][e].astype(F32)).astype(BF)
            copy = pltpu.make_async_copy(outs[n].at[e], outs_far[n].at[e], out_sems.at[n, e])
            copy.start()
            stores.append(copy)
    for copy in stores:
        copy.wait()


def relay(x_parts, z_parts):
    ins = [*x_parts, *z_parts]
    x_shape, z_shape = x_parts[0].shape, z_parts[0].shape
    shapes = [x_shape, x_shape, z_shape, z_shape]
    scratch = [pltpu.VMEM(shape, BF) for shape in (x_shape,) * 4 + (z_shape,) * 4]
    scratch += [pltpu.VMEM(shape, BF) for shape in shapes]
    scratch += [pltpu.SemaphoreType.DMA((4, HALF, 2)), pltpu.SemaphoreType.DMA((4, HALF))]
    outs = [hbm(*shape) for shape in shapes]
    return run(
        relay_kernel, "relay", 300, ins, outs, scratch, far_in=8, far_out=4, limit=FAR_LIMIT
    )


def mixed_kernel(idx, hot_gated, outs, far, blocks, sems):
    copies = []
    for p in range(PAIRS):
        part = slice(p * SLOTS, (p + 1) * SLOTS)
        values = jnp.concatenate([outs[n, part, :] for n in range(LOCAL)], axis=0)
        merged = mm_tn(hot_gated[p], values).astype(BF)
        for n in range(2):
            r = 2 * p + n
            blocks[r] = merged[n * ROWS : (n + 1) * ROWS]
            copy = pltpu.make_async_copy(
                blocks.at[r], far.at[idx[r], :, pl.ds(256, D)], sems.at[r]
            )
            copy.start()
            copies.append(copy)
    for copy in copies:
        copy.wait()


def mixed_sum(idx, hot_gated, outs):
    scratch = [pltpu.VMEM((BLOCKS, ROWS, D), BF), pltpu.SemaphoreType.DMA((BLOCKS,))]
    far = [hbm(BLOCKS, ROWS, 256 + D)]
    ins = [hot_gated, outs]
    return run(mixed_kernel, "mixed_sum", 0.6, ins, far, scratch, far_out=1, limit=10, idx=idx)[0]


def add_pairs_kernel(same, other, *outs):
    for off in range(4):
        outs[off][...] = (same[off].astype(F32) + other[off].astype(F32)).astype(BF)


def add_pairs(same, other):
    return run(
        add_pairs_kernel, "add_pairs", 0.3, [same, other], [vmem(*same.shape[1:])] * 4, limit=4
    )


def stage_kernel(cut, idx, *refs):
    far = refs[:5]
    outs_far = refs[5:9]
    bufs = refs[9:14]
    outs = refs[14:18]
    total, in_sems, out_sems = refs[18:21]
    own, from_below, from_above, late_below, late_above = range(5)
    needed = []
    loads = []
    for n in range(LOCAL):
        if n < HALF:
            places = ((own, n), (late_below, n), (from_above, n + HALF))
        else:
            places = ((own, n), (from_below, n), (late_above, n - HALF))
        needed.append(places)
        loads.append(
            fetch(
                [far[item].at[at] for item, at in places],
                [bufs[item].at[at] for item, at in places],
                in_sems.at[n],
            )
        )
    stores = []
    for n in range(LOCAL):
        for copy in loads[n]:
            copy.wait()
        parts = [bufs[item][at].astype(F32) for item, at in needed[n]]
        total[...] = (parts[0] + parts[1] + parts[2]).astype(BF)
        cut(idx, total, outs, n)
        stores += fetch(
            [item.at[n] for item in outs], [item.at[n] for item in outs_far], out_sems.at[n]
        )
    for copy in stores:
        copy.wait()


def stage_sums(idx, name, micros, cut, rows, parts):
    shapes = [(LOCAL, rows, FE)] * 4
    scratch = [pltpu.VMEM(part.shape, BF) for part in parts]
    scratch += [pltpu.VMEM(shape, BF) for shape in shapes]
    scratch += [pltpu.VMEM(parts[0].shape[1:], BF)]
    scratch += [pltpu.SemaphoreType.DMA((LOCAL, 3)), pltpu.SemaphoreType.DMA((LOCAL, 4))]
    return run(
        functools.partial(stage_kernel, cut),
        name,
        micros,
        parts,
        [hbm(*shape) for shape in shapes],
        scratch,
        far_in=5,
        far_out=4,
        limit=64,
        idx=idx,
    )


def cut_along_z(idx, total, outs, n):
    gate_rows = D // 16
    down_rows = FE // 16
    for k in range(4):
        at = (idx[12] + k) % 4
        start = pl.multiple_of(at * gate_rows, gate_rows)
        outs[k][n, :gate_rows, :] = total[pl.ds(start, gate_rows), :]
        for m in range(LEFT // FE):
            start = pl.multiple_of(D // 4 + m * (FE // 4) + at * down_rows, down_rows)
            to = gate_rows + m * down_rows
            outs[k][n, to : to + down_rows, :] = total[pl.ds(start, down_rows), :]


def cut_along_x(idx, total, outs, n):
    for k in range(4):
        outs[k][n] = total[pl.ds((idx[11] + k) % 4, 1)][0]


SEND_ROWS = (QROWS + ZROWS) // 2


def finish_kernel(idx, *refs):
    far = refs[:8]
    outs_far = refs[8:11]
    send_far = refs[11]
    bufs = refs[12:20]
    keep_gate, keep_up, keep_down, send = keeps = refs[20:24]
    x_sum, z_sum, in_sems, out_sems = refs[24:28]
    loads = [
        fetch([item.at[n] for item in far], [item.at[n] for item in bufs], in_sems.at[n])
        for n in range(LOCAL)
    ]
    big = D // 16
    small = big // 2
    tiny = FE // 32
    mine = idx[9]
    theirs = 1 - mine
    stores = []
    for n in range(LOCAL):
        for copy in loads[n]:
            copy.wait()
        acc = bufs[0][n].astype(F32)
        for part in bufs[1:4]:
            acc = acc + part[n].astype(F32)
        x_sum[...] = acc
        acc = bufs[4][n].astype(F32)
        for part in bufs[5:8]:
            acc = acc + part[n].astype(F32)
        z_sum[...] = acc
        here = pl.ds(pl.multiple_of(mine * small, small), small)
        there = pl.ds(pl.multiple_of(theirs * small, small), small)
        keep_gate[n] = x_sum[here, :]
        keep_up[n] = z_sum[here, :]
        send[n, :small, :] = x_sum[there, :].astype(BF)
        send[n, small:big, :] = z_sum[there, :].astype(BF)
        for m in range(D // FE):
            source, at = (x_sum, m) if m < LEFT // FE else (z_sum, m - LEFT // FE)
            first = big + at * 2 * tiny
            here = pl.ds(pl.multiple_of(first + mine * tiny, tiny), tiny)
            there = pl.ds(pl.multiple_of(first + theirs * tiny, tiny), tiny)
            keep_down[n, :, m * FE : (m + 1) * FE] = source[here, :]
            send[n, big + m * tiny : big + (m + 1) * tiny, :] = source[there, :].astype(BF)
        targets = [item.at[mine * LOCAL + n] for item in outs_far] + [send_far.at[n]]
        stores += fetch([item.at[n] for item in keeps], targets, out_sems.at[n])
    for copy in stores:
        copy.wait()


def finish(idx, parts):
    outs = [
        hbm(2 * LOCAL, D // 32, FE, dtype=F32),
        hbm(2 * LOCAL, D // 32, FE, dtype=F32),
        hbm(2 * LOCAL, FE // 32, D, dtype=F32),
        hbm(LOCAL, SEND_ROWS, FE),
    ]
    scratch = [pltpu.VMEM(part.shape, BF) for part in parts]
    scratch += [
        pltpu.VMEM((LOCAL, D // 32, FE), F32),
        pltpu.VMEM((LOCAL, D // 32, FE), F32),
        pltpu.VMEM((LOCAL, FE // 32, D), F32),
        pltpu.VMEM((LOCAL, SEND_ROWS, FE), BF),
        pltpu.VMEM((QROWS, FE), F32),
        pltpu.VMEM((ZROWS, FE), F32),
        pltpu.SemaphoreType.DMA((LOCAL, 8)),
        pltpu.SemaphoreType.DMA((LOCAL, 4)),
    ]
    return run(
        finish_kernel,
        "finish",
        1,
        parts,
        outs,
        scratch,
        far_in=8,
        far_out=4,
        limit=FAR_LIMIT,
        idx=idx,
    )


def assemble_kernel(idx, got, gate_in, up_in, down_in, *refs):
    outs_far = refs[:3]
    gate, up, down, out_sems = refs[3:7]
    small = D // 32
    tiny = FE // 32
    stores = []
    for n in range(LOCAL):
        gate[n] = got[n, :small, :].astype(F32)
        up[n] = got[n, small : 2 * small, :].astype(F32)
        down[n, :, :FE] = got[n, 2 * small : 2 * small + tiny, :].astype(F32)
        down[n, :, FE:] = got[n, 2 * small + tiny :, :].astype(F32)
        targets = [item.at[(1 - idx[9]) * LOCAL + n] for item in outs_far]
        stores += fetch([gate.at[n], up.at[n], down.at[n]], targets, out_sems.at[n])
    for copy in stores:
        copy.wait()


def assemble(idx, got, results):
    outs = [hbm(*item.shape, dtype=F32) for item in results]
    scratch = [
        pltpu.VMEM((LOCAL, D // 32, FE), F32),
        pltpu.VMEM((LOCAL, D // 32, FE), F32),
        pltpu.VMEM((LOCAL, FE // 32, D), F32),
        pltpu.SemaphoreType.DMA((LOCAL, 3)),
    ]
    return run(
        assemble_kernel,
        "assemble",
        1,
        [got, *results],
        outs,
        scratch,
        far_in=3,
        far_out=3,
        limit=8,
        idx=idx,
        aliases={2: 0, 3: 1, 4: 2},
    )


def middle_kernel(*refs):
    parts = refs[:4]
    h_ref, gate_ref, dy_ref, gain_ref, router_t, w_out = refs[4:10]
    dh_ref, send_ref, side_ref = refs[10:13]
    total = parts[0][...].astype(F32)
    for part in parts[1:]:
        total = total + part[...].astype(F32)
    extra = total[:, D:]
    d_gate = extra + pltpu.roll(extra, 128 - EXPERTS, 1)
    gate = gate_ref[...]
    d_chosen = gate * (d_gate - jnp.sum(gate * d_gate, axis=1, keepdims=True))
    d_logits = d_chosen.astype(BF)
    d_mlp = total[:, :D] + mm(d_logits, router_t[...])
    h = h_ref[...]
    gain = gain_ref[...].astype(F32)
    scale = lax.rsqrt(jnp.mean(h * h, axis=1, keepdims=True) + EPS)
    normed = h * scale
    mlp_in = (normed * gain).astype(BF)
    scaled = d_mlp * gain
    d_h = (
        dy_ref[...].astype(F32)
        + scale * scaled
        - h * (scale * scale * scale) * jnp.mean(scaled * h, axis=1, keepdims=True)
    )
    dh_ref[...] = d_h
    d_branch = d_h.astype(BF)
    d_attn = mm_nt(d_branch, w_out[...]).astype(BF)
    for b in range(BLOCKS):
        cols = slice(b * 128, (b + 1) * 128)
        send_ref[b, :, :128] = d_attn[:, cols]
        send_ref[b, :, 128:] = d_branch[:, cols]
    router = mm_tn(mlp_in, d_logits)
    d_gain = jnp.sum(d_mlp * normed, axis=0, keepdims=True)
    column = jnp.transpose(jnp.broadcast_to(d_gain, (128, D)))
    lane = lax.broadcasted_iota(jnp.int32, (D, 128), 1)
    side_ref[...] = jnp.where(lane == GAIN_LANE, column, router).astype(BF)


def middle(parts, h_own, gate_own, dy, gain, router_t, w_out):
    shapes = [((ROWS, D), F32), ((BLOCKS, ROWS, 256), BF), ((D, 128), BF)]

    def kernel(*refs):
        inputs = refs[:10]
        far = refs[10:13]
        bufs = refs[13:16]
        middle_kernel(*inputs, *bufs)
        for copy in fetch(bufs, far, refs[16]):
            copy.wait()

    outs = [hbm(*shape, dtype=kind) for shape, kind in shapes]
    scratch = [pltpu.VMEM(shape, kind) for shape, kind in shapes] + [pltpu.SemaphoreType.DMA((3,))]
    ins = [*parts, h_own, gate_own, dy, gain, router_t, w_out]
    return run(kernel, "middle", 100, ins, outs, scratch, far_out=3, limit=10)


def attend_back_kernel(idx, *refs):
    early_far = refs[:6]
    far = refs[6:10]
    pack, dense_far = refs[11:13]
    early = refs[13:19]
    p_ref, attn_in, ao_all, side_ref, dk_acc, dv_acc, dqkv_ref, dense, k_turned = refs[19:28]
    sems, early_sems, tables_sems = refs[28:31]
    grads, q_ref, k_ref, v_ref, cos_ref, sin_ref = early
    early_copies = fetch(early_far[:4], early[:4], early_sems)
    p_copies = [
        pltpu.make_async_copy(far[0].at[i], p_ref.at[i], sems.at[i]) for i in range(BLOCKS)
    ]
    ao_copy = pltpu.make_async_copy(far[2], ao_all, sems.at[BLOCKS])
    in_copy = pltpu.make_async_copy(far[1], attn_in, sems.at[BLOCKS + 1])
    p_copies[0].start()
    table_copies = fetch(early_far[4:], early[4:], tables_sems)
    p_copies[1].start()
    p_copies[2].start()
    side_copy = pltpu.make_async_copy(far[3], side_ref, sems.at[2 * BLOCKS + 3])
    dk_acc[...] = jnp.zeros((LEN, HD), F32)
    dv_acc[...] = jnp.zeros((LEN, HD), F32)
    for copy in early_copies:
        copy.wait()
    k_wide = jnp.concatenate([k_ref[...], k_ref[...]], axis=1).astype(F32)
    k_turned[...] = jnp.transpose(k_wide)[:HD, :].astype(BF)
    for i in range(BLOCKS):
        lo = max(0, i - WIN // ROWS) * ROWS
        hi = (i + 1) * ROWS
        span = hi - lo
        rows = slice(i * ROWS, hi)
        do2 = jnp.concatenate([grads[i, :, :HD], grads[i, :, HD : 2 * HD]], axis=0)
        q2 = jnp.concatenate([q_ref[rows, :HD], q_ref[rows, HD:]], axis=0)
        p_copies[i].wait()
        if i + 3 < BLOCKS:
            p_copies[i + 3].start()
        if i == 2:
            in_copy.start()
            side_copy.start()
            ao_copy.start()
        probs_low = p_ref[i, :span, :]
        probs = probs_low.astype(F32)
        d_probs = mm_nt(v_ref[lo:hi, :], do2)
        weighted = probs * d_probs
        d_scores = (weighted - probs * jnp.sum(weighted, axis=0, keepdims=True)).astype(BF)
        dk_acc[lo:hi, :] += mm(d_scores, q2)
        dv_acc[lo:hi, :] += mm(probs_low, do2)
        dq = mm(k_turned[:, lo:hi], d_scores) * HD**-0.5
        dq = jnp.transpose(jnp.concatenate([dq[:, :ROWS], dq[:, ROWS:]], axis=0))
        dq = dq.astype(BF).astype(F32)
        if i == 0:
            for copy in table_copies:
                copy.wait()
        dq = dq * cos_ref[rows, :] - swap_halves(dq) * sin_ref[rows, :]
        dqkv_ref[rows, : 2 * HD] = dq.astype(BF)
    pair = jnp.concatenate([dk_acc[...], dv_acc[...]], axis=1).astype(BF).astype(F32)
    turned = pair * cos_ref[...] - swap_halves(pair) * sin_ref[...]
    lane = lax.broadcasted_iota(jnp.int32, pair.shape, 1)
    dqkv_ref[:, 2 * HD :] = jnp.where(lane < HD, turned, pair).astype(BF)
    dqkv_copies = []
    for r in range(BLOCKS):
        copy = pltpu.make_async_copy(
            dqkv_ref.at[pl.ds(r * ROWS, ROWS), :],
            pack.at[r, :, pl.ds(0, 256)],
            sems.at[BLOCKS + 3 + r],
        )
        copy.start()
        dqkv_copies.append(copy)
    in_copy.wait()
    ao_copy.wait()
    half = D // 2
    side_copy.wait()
    d_branch = jnp.concatenate([grads[b, :, 128:] for b in range(BLOCKS)], axis=0)
    left_turned = mm_tn(dqkv_ref[...], attn_in[...])
    right_turned = mm_tn(d_branch, ao_all[...])
    for part in range(2):
        rows = slice(part * half, (part + 1) * half)
        left = jnp.transpose(left_turned[:, rows])
        right = jnp.concatenate(
            [jnp.transpose(right_turned[:, rows]), side_ref[rows, :].astype(F32)], axis=1
        )
        both = jnp.concatenate([left.reshape(-1, 8, 256), right.reshape(-1, 8, 256)], axis=1)
        places = pl.ds(part * (half // 8), half // 8)
        dense[places] = both.astype(BF)
        copy = pltpu.make_async_copy(
            dense.at[places], dense_far.at[places], sems.at[(BLOCKS + 2, 2 * BLOCKS + 4)[part]]
        )
        copy.start()
        dqkv_copies.append(copy)
    for copy in dqkv_copies:
        copy.wait()


def attend_back(idx, grads, p, q, k, v, attn_in, ao_all, side, cos_tab, sin_tab, pack):
    early = [grads, q, k, v, cos_tab, sin_tab]
    outs = [hbm(*pack.shape), hbm(D // 8, 16, 256)]
    scratch = [pltpu.VMEM(item.shape, item.dtype) for item in early]
    scratch += [
        pltpu.VMEM(p.shape, BF),
        pltpu.VMEM((LEN, D), BF),
        pltpu.VMEM((LEN, D), BF),
        pltpu.VMEM((D, 128), BF),
        pltpu.VMEM((LEN, HD), F32),
        pltpu.VMEM((LEN, HD), F32),
        pltpu.VMEM((LEN, 256), BF),
        pltpu.VMEM((D // 8, 16, 256), BF),
        pltpu.VMEM((HD, LEN), BF),
        pltpu.SemaphoreType.DMA((2 * BLOCKS + 5,)),
        pltpu.SemaphoreType.DMA((4,)),
        pltpu.SemaphoreType.DMA((2,)),
    ]
    ins = [*early, p, attn_in, ao_all, side, pack]
    return run(
        attend_back_kernel,
        "attend_back",
        8,
        ins,
        outs,
        scratch,
        far_in=11,
        far_out=2,
        limit=FAR_LIMIT,
        idx=idx,
        aliases={11: 0},
    )


def input_grad_kernel(pack, *refs):
    far = refs[:7]
    outs_far = refs[7:9]
    bufs = refs[9:16]
    out, block, dq, dk, dv, early_sems, late_sems, out_sems = refs[16:24]
    early = fetch(far[:4], bufs[:4], early_sems)
    late = fetch(far[4:], bufs[4:], late_sems)
    x_ref, dh_ref, gain_ref, h_own, w_query, w_key, w_value = bufs
    for b in range(BLOCKS):
        dq[:, b * 128 : (b + 1) * 128] = pack[b, :, :128]
    for b in range(0, BLOCKS, 2):
        first = pack[b, :, 128:256].astype(F32)
        second = pack[b + 1, :, 128:256].astype(F32)
        cols = slice(b * HD, (b + 2) * HD)
        dk[:, cols] = jnp.concatenate([first[:, :HD], second[:, :HD]], axis=1).astype(BF)
        dv[:, cols] = jnp.concatenate([first[:, HD:], second[:, HD:]], axis=1).astype(BF)
    for copy in early:
        copy.wait()
    total = h_own[...]
    for b in range(BLOCKS):
        total = total + pack[b, :, 256:].astype(F32)
    block[...] = total.astype(BF)
    for copy in late:
        copy.wait()
    d_in = mm_nt(dq[...], w_query[...]) + mm_nt(dk[...], w_key[...]) + mm_nt(dv[...], w_value[...])
    x = x_ref[...].astype(F32)
    scale = lax.rsqrt(jnp.mean(x * x, axis=1, keepdims=True) + EPS)
    scaled = d_in * gain_ref[...]
    out[...] = (
        dh_ref[...]
        + scale * scaled
        - x * (scale * scale * scale) * jnp.mean(scaled * x, axis=1, keepdims=True)
    ).astype(BF)
    for copy in fetch((out, block), outs_far, out_sems):
        copy.wait()


def input_grad(pack, x, d_h, gain, h_own, w_query, w_key, w_value):
    ins = [pack, x, d_h, gain, h_own, w_query, w_key, w_value]
    scratch = [pltpu.VMEM(item.shape, item.dtype) for item in ins[1:]]
    scratch += [
        pltpu.VMEM((ROWS, D), BF),
        pltpu.VMEM((ROWS, D), BF),
        pltpu.VMEM((ROWS, H * HD), BF),
        pltpu.VMEM((ROWS, KVH * HD), BF),
        pltpu.VMEM((ROWS, KVH * HD), BF),
        pltpu.SemaphoreType.DMA((4,)),
        pltpu.SemaphoreType.DMA((3,)),
        pltpu.SemaphoreType.DMA((2,)),
    ]
    return run(
        input_grad_kernel,
        "input_grad",
        1,
        ins,
        [hbm(ROWS, D)] * 2,
        scratch,
        far_in=len(ins) - 1,
        far_out=2,
        limit=FAR_LIMIT,
    )


def dense_out_kernel(idx, dense, w_query, w_key, w_value, gain, *refs):
    dq, dk, dv, do, router, gains, turned = refs
    total = jnp.sum(dense[...].astype(F32).reshape(-1, BLOCKS, 16, 256), axis=0)
    for b in range(BLOCKS):
        dq[:, b * 128 : (b + 1) * 128] = total[b, :8, :128]
        do[:, b * 128 : (b + 1) * 128] = total[b, 8:, :128]
    for b in range(0, BLOCKS, 2):
        first = total[b, :8, 128:]
        second = total[b + 1, :8, 128:]
        cols = slice(b * HD, (b + 2) * HD)
        dk[:, cols] = jnp.concatenate([first[:, :HD], second[:, :HD]], axis=1)
        dv[:, cols] = jnp.concatenate([first[:, HD:], second[:, HD:]], axis=1)
    side = jnp.sum(total[:, 8:, 128:], axis=0)
    router[...] = side[:, :EXPERTS]
    dot = jnp.zeros((8, 1), F32)
    for weight, grad in ((w_query, dq), (w_key, dk), (w_value, dv)):
        dot = dot + jnp.sum(weight[...] * grad[...], axis=1, keepdims=True)
    chunk = pl.ds(pl.multiple_of(idx[16] * 128, 128), 128)
    turned[...] = jnp.transpose(jnp.broadcast_to(gain[:, chunk], (128, 128)))
    gain_rows = turned[pl.ds(pl.multiple_of(idx[17] * 8, 8), 8), 0:1]
    lane = lax.broadcasted_iota(jnp.int32, (8, 128), 1)
    both = jnp.where(lane == GAIN_LANE, side, dot / gain_rows)
    turned[:8, :] = both
    flat = jnp.transpose(turned[...])
    gains[...] = flat[GAIN_LANE - 8 : GAIN_LANE + 8, :]


def dense_out(idx, dense, w_query, w_key, w_value, gain):
    outs = [
        auto(8, H * HD, dtype=F32),
        auto(8, KVH * HD, dtype=F32),
        auto(8, KVH * HD, dtype=F32),
        auto(8, D, dtype=F32),
        auto(8, EXPERTS, dtype=F32),
        auto(16, 128, dtype=F32),
    ]
    ins = [dense, w_query, w_key, w_value, gain]
    scratch = [pltpu.VMEM((128, 128), F32)]
    return run(dense_out_kernel, "dense_out", 1, ins, outs, scratch, limit=8, idx=idx)


def from_x(value, off):
    size = lax.axis_size("x")
    return lax.ppermute(value, "x", [(i, (i + off) % size) for i in range(size)])


def from_z(value, off):
    size = lax.axis_size("z")
    return lax.ppermute(value, "z", [(i, (i + off) % size) for i in range(size)])


def along_y(value, off):
    route = []
    for y in range(4):
        to = (y + off) % 4
        route.append(((y % 2) * 2 + y // 2, (to % 2) * 2 + to // 2))
    return lax.ppermute(value, ("yl", "yh"), route)


def other_core(value):
    return lax.ppermute(value, "c", [(0, 1), (1, 0)])


def near_ring(value):
    return [value] + [along_y(value, -off) for off in (1, 2, 3)]


def both_cores(near):
    far = [other_core(item) for item in near]
    return [item for pair in zip(near, far) for item in pair]


def gather_ring(value):
    return both_cores(near_ring(value))


def reduce_ring(pieces):
    return [pieces[0]] + [along_y(pieces[off], off) for off in (1, 2, 3)]


def scatter_parts(parts, send):
    return [parts[0]] + [send(parts[k], k) for k in (1, 2, 3)]


def together(*values):
    return lax.optimization_barrier(values)


def after(values, *earlier):
    return lax.optimization_barrier((values, earlier))[0]


def local(
    tokens,
    segments,
    routes,
    drop_order,
    gain_attn,
    w_query,
    w_key,
    w_value,
    w_out,
    gain_mlp,
    w_router,
    w_gate,
    w_up,
    w_down,
    cotangent,
):
    x_at = lax.axis_index("x")
    z_at = lax.axis_index("z")
    yl = lax.axis_index("yl")
    yh = lax.axis_index("yh")
    core = lax.axis_index("c")
    y_at = yh * 2 + yl
    own = yl * 4 + yh * 2 + core
    expert_at = yh * 2 + core

    entries = []
    for off in range(4):
        y = (y_at + off) % 4
        for dc in range(2):
            entries.append((y % 2) * 4 + (y // 2) * 2 + (core + dc) % 2)
    entries += [own, yl, expert_at, x_at, z_at, y_at, core, expert_at * 8 + yl * LOCAL]
    first_row = ((x_at * 4 + z_at) * 8 + own) * 8
    entries += [first_row // 128, first_row % 128 // 8]
    idx = jnp.stack([jnp.asarray(entry, jnp.int32) for entry in entries])

    cos_np, sin_np = rotary_tables()
    cos_tab = jnp.asarray(cos_np)
    sin_tab = jnp.asarray(sin_np)
    gain_one = gain_attn.astype(F32).reshape(1, D)
    gain_two = gain_mlp.astype(F32).reshape(1, D)
    router_t = jnp.pad(w_router.T, ((0, 128 - EXPERTS), (0, 0)))

    def columns(weight, block):
        return lax.dynamic_slice_in_dim(weight, block * 128, 128, 1)

    def out_rows(weight):
        return lax.dynamic_slice_in_dim(weight, first_row, 8, 0).astype(F32)

    wq_cols = columns(w_query, own)
    wk_cols = columns(w_key, own // 2)
    wv_cols = columns(w_value, own // 2)
    finals = [out_rows(w_query), out_rows(w_key), out_rows(w_value)]
    early = [idx, gain_one, gain_two, router_t, wq_cols, wk_cols, wv_cols, finals]

    seg_cols = jnp.broadcast_to(segments.astype(BF)[:, None], (ROWS, AUG - D))
    x_near = near_ring(jnp.concatenate([tokens, seg_cols], axis=1))
    slot_own = slots(routes.T, drop_order)
    x_near, slot_own, early = together(x_near, slot_own, early)
    idx, gain_one, gain_two, router_t, wq_cols, wk_cols, wv_cols, finals = early
    xs = both_cores(x_near)
    dy_near = near_ring(after(cotangent, slot_own))

    ao, attn_in, q, k, v, p = attend(
        idx, xs, slot_own, gain_one, wq_cols, wk_cols, wv_cols, cos_tab, sin_tab
    )
    dys = both_cores(dy_near)
    aos = gather_ring(after(ao, *dy_near))
    mlp_in, slot_t, gate_t, h_own, gate_own, ao_all = project(
        idx, xs, aos, w_out, gain_two, router_t
    )
    rows, act, d_out, d_gh, d_up, hot_gated, outs, dm_same, dm_other = experts(
        idx, mlp_in, dys, slot_t, gate_t, w_gate, w_up, w_down
    )

    got = other_core(dm_other)
    pack = mixed_sum(idx, hot_gated, outs)
    pack, got = together(pack, got)
    dm_pieces = add_pairs(dm_same, got)
    dm_parts = reduce_ring(dm_pieces)
    (x_up, x_down, *x_keep), (z_up, z_down, *z_keep) = weight_grads(
        idx, after(rows, *dm_pieces), act, d_out, d_gh, d_up
    )
    x_below = from_x(x_up, 1)
    x_above = from_x(x_down, 3)
    z_keep, z_up, z_down, dm_parts = together(z_keep, z_up, z_down, dm_parts)
    z_below = from_z(z_up, 1)
    z_above = from_z(z_down, 3)
    d_h, to_heads, side = middle(
        dm_parts, h_own, gate_own, cotangent, gain_two, router_t, w_out
    )
    grads = lax.all_to_all(to_heads, GROUP, split_axis=0, concat_axis=0, tiled=True)
    pack, dense = attend_back(
        idx, grads, p, q, k, v, attn_in, ao_all, side, cos_tab, sin_tab, pack
    )
    x_below, x_above, z_below, z_above = after([x_below, x_above, z_below, z_above], pack)
    dense = lax.all_to_all(
        dense, ("x", "z", "yl", "yh", "c"), split_axis=0, concat_axis=0, tiled=True
    )

    relayed = relay(
        [x_keep[1], x_below, x_keep[2], x_above], [z_keep[1], z_below, z_keep[2], z_above]
    )
    x_late = [from_x(relayed[0], 1), from_x(relayed[1], 3)]
    z_late = [from_z(relayed[2], 1), from_z(relayed[3], 3)]
    pack = lax.all_to_all(
        after(pack, dense, *relayed), GROUP, split_axis=0, concat_axis=0, tiled=True
    )
    dense_rows = dense_out(idx, dense, *finals, gain_one)
    x_pieces = stage_sums(
        idx, "x_sums", 200, cut_along_z, QROWS, [x_keep[0], x_below, x_above, *x_late]
    )
    z_pieces = stage_sums(
        idx, "z_sums", 200, cut_along_x, ZROWS, [z_keep[0], z_below, z_above, *z_late]
    )
    x_second = scatter_parts(x_pieces, from_z)
    z_second = scatter_parts(z_pieces, from_x)
    d_tokens, block_out = input_grad(
        after(pack, *x_pieces, *z_pieces), tokens, d_h, gain_one, h_own, w_query, w_key, w_value
    )
    d_tokens, x_second, z_second, dense_rows = together(d_tokens, x_second, z_second, dense_rows)

    *results, sent = finish(idx, [*x_second, *z_second])
    got = lax.ppermute(sent, "yl", [(0, 1), (1, 0)])
    d_w_gate, d_w_up, d_w_down = assemble(idx, got, results)
    d_w_query, d_w_key, d_w_value, d_w_out, d_w_router, gains = dense_rows
    d_gain_attn = gains[0, :8]
    d_gain_mlp = gains[8, :8]

    return (
        block_out,
        d_tokens,
        d_gain_attn,
        d_w_query,
        d_w_key,
        d_w_value,
        d_w_out,
        d_gain_mlp,
        d_w_router,
        d_w_gate,
        d_w_up,
        d_w_down,
    )


def solution(mesh):
    side = 4 if mesh.shape["dp"] == 32 else 1
    names = ("x", "z", "yl", "yh", "c")
    grid = Mesh(mesh.devices.reshape(side, side, 2, 2, 2), names)
    tokens = names
    experts_axes = ("yh", "c")
    dp = ("x", "z", "yl")
    in_specs = (
        P(tokens, None),
        P(tokens),
        P(tokens, None),
        P(tokens, None),
        P(),
        P(),
        P(),
        P(),
        P(),
        P(),
        P(),
        P(experts_axes, None, None),
        P(experts_axes, None, None),
        P(experts_axes, None, None),
        P(tokens, None),
    )
    out_specs = (
        P(tokens, None),
        P(tokens, None),
        P(tokens),
        P(tokens, None),
        P(tokens, None),
        P(tokens, None),
        P(tokens, None),
        P(tokens),
        P(tokens, None),
        P(experts_axes, dp, None),
        P(experts_axes, dp, None),
        P(experts_axes, dp, None),
    )
    return jax.shard_map(local, mesh=grid, in_specs=in_specs, out_specs=out_specs, check_vma=False)
```

```python
import functools

import jax
import jax.numpy as jnp
import numpy as np
from jax import lax
from jax.experimental import pallas as pl
from jax.experimental.pallas import tpu as pltpu
from jax.sharding import Mesh, PartitionSpec as P

H = 16
KVH = 8
HD = 64
D = 1024
FE = 512
TOPK = 8
EXPERTS = 32
CAP = 36
ROWS = 128
LEN = 1024
BLOCKS = LEN // ROWS
WIN = 512
LOCAL = 4
PAIRS = BLOCKS // 2
SLOTS = 80
EROWS = PAIRS * SLOTS
AUG = D + 128
GAIN_LANE = 32
FAR_LIMIT = 63
SHARE = 0.1
EPS = 1e-06
THETA = 10000.0
NEG = -1e30
BF = jnp.bfloat16
F32 = jnp.float32
GROUP = ("yl", "yh", "c")


def mm(left, right):
    return jnp.dot(left, right, preferred_element_type=F32)


def mm_nt(left, right):
    return lax.dot_general(left, right, (((1,), (1,)), ((), ())), preferred_element_type=F32)


def mm_tn(left, right):
    return lax.dot_general(left, right, (((0,), (0,)), ((), ())), preferred_element_type=F32)


def rotary_tables():
    half = HD // 2
    frequency = THETA ** (-np.arange(half, dtype=np.float64) * 2.0 / HD)
    angles = np.arange(LEN, dtype=np.float64)[:, None] * frequency[None, :]
    cosine = np.cos(angles)
    sine = np.sin(angles)
    cos_full = np.concatenate([cosine] * 4, axis=1).astype(np.float32)
    sin_full = np.concatenate([-sine, sine, -sine, sine], axis=1).astype(np.float32)
    return cos_full, sin_full


def swap_halves(array_in):
    half = HD // 2
    lane = lax.broadcasted_iota(jnp.int32, array_in.shape, 1)
    ahead = pltpu.roll(array_in, array_in.shape[1] - half, 1)
    behind = pltpu.roll(array_in, half, 1)
    return jnp.where(lane % HD < half, ahead, behind)


def vmem(*shape, dtype=BF):
    return pltpu.VMEM(shape, dtype)


def hbm(*shape, dtype=BF):
    return pltpu.HBM(shape, dtype)


def auto(*shape, dtype=BF):
    return jax.ShapeDtypeStruct(shape, dtype)


def cost(micros):
    return pl.CostEstimate(
        flops=int(micros * 1.15e9 * SHARE), bytes_accessed=int(micros * 1e6), transcendentals=0
    )


def run(
    kernel,
    name,
    micros,
    ins,
    outs,
    scratch=(),
    far_in=0,
    far_out=0,
    limit=24,
    idx=None,
    aliases=None,
):
    inside = pl.BlockSpec(memory_space=pltpu.VMEM)
    outside = pl.BlockSpec(memory_space=pltpu.HBM)
    in_specs = [inside] * (len(ins) - far_in) + [outside] * far_in
    operands = list(ins)
    if idx is not None:
        in_specs = [pl.BlockSpec(memory_space=pltpu.SMEM)] + in_specs
        operands = [idx] + operands
    return pl.pallas_call(
        kernel,
        out_shape=list(outs),
        in_specs=in_specs,
        out_specs=[inside] * (len(outs) - far_out) + [outside] * far_out,
        scratch_shapes=list(scratch),
        input_output_aliases=aliases or {},
        compiler_params=pltpu.CompilerParams(vmem_limit_bytes=limit * 1024 * 1024),
        cost_estimate=cost(micros),
        name=name,
    )(*operands)


def run_far(kernel, name, micros, ins, outs, scratch=(), idx=None):
    count = len(ins)
    given = 0 if idx is None else 1

    def body(*refs):
        lead = refs[:given]
        sources = refs[given : given + count]
        targets = refs[given + count : given + count + len(outs)]
        rest = refs[given + count + len(outs) :]
        in_bufs = rest[:count]
        out_bufs = rest[count : count + len(outs)]
        in_sems, out_sems = rest[count + len(outs) : count + len(outs) + 2]
        for copy in fetch(sources, in_bufs, in_sems):
            copy.wait()
        kernel(*lead, *in_bufs, *out_bufs, *rest[count + len(outs) + 2 :])
        for copy in fetch(out_bufs, targets, out_sems):
            copy.wait()

    bufs = [pltpu.VMEM(item.shape, item.dtype) for item in ins]
    bufs += [pltpu.VMEM(item.shape, item.dtype) for item in outs]
    bufs += [pltpu.SemaphoreType.DMA((count,)), pltpu.SemaphoreType.DMA((len(outs),))]
    return run(
        body,
        name,
        micros,
        ins,
        outs,
        bufs + list(scratch),
        far_in=count,
        far_out=len(outs),
        limit=FAR_LIMIT,
        idx=idx,
    )


def fetch(sources, targets, sems):
    copies = [
        pltpu.make_async_copy(source, target, sems.at[n])
        for n, (source, target) in enumerate(zip(sources, targets))
    ]
    for copy in copies:
        copy.start()
    return copies


def slots_kernel(routes_ref, order_ref, meta_ref, place_ref):
    order = order_ref[...]
    index = lax.broadcasted_iota(jnp.int32, (1, ROWS * TOPK), 1)
    token_of = order // TOPK
    choice_of = order - token_of * TOPK
    at_token = (token_of == lax.broadcasted_iota(jnp.int32, (ROWS, ROWS * TOPK), 0)).astype(F32)
    choice = lax.broadcasted_iota(jnp.int32, (2 * TOPK, ROWS * TOPK), 0)
    high = index // 32
    low = index - high * 32
    part = jnp.where(choice < TOPK, high, low).astype(F32)
    choice_mod = jnp.where(choice < TOPK, choice, choice - TOPK)
    table = jnp.where(choice_mod == choice_of, part, 0.0)
    found = mm_nt(at_token.astype(BF), table.astype(BF))
    place = found[:, :TOPK] * 32.0 + found[:, TOPK:]
    lane = lax.broadcasted_iota(jnp.int32, (ROWS, 128), 1)
    wide = jnp.concatenate(
        [
            routes_ref[...].astype(F32),
            jnp.zeros((ROWS - TOPK, ROWS), F32),
        ],
        axis=0,
    )
    turned = jnp.transpose(wide)
    lane_f = lane.astype(F32)
    placed = jnp.full((ROWS, 128), 4096.0, F32)
    for k in range(TOPK):
        placed = jnp.where(turned[:, k : k + 1] == lane_f, place[:, k : k + 1], placed)
    place_ref[...] = placed

    def count(step, total):
        for inner in range(8):
            row = place_ref[pl.ds(step * 8 + inner, 1), :]
            total = total + jnp.where(row < placed, 1.0, 0.0)
        return total

    rank = lax.fori_loop(0, ROWS // 8, count, jnp.zeros((ROWS, 128), F32))
    slot = jnp.where(placed < 4000.0, jnp.where(rank < CAP, rank, -1.0), -2.0)
    meta_ref[...] = jnp.transpose(slot)[:EXPERTS, :].astype(BF)


def slots(routes_t, drop_order):
    return run(
        slots_kernel,
        "slots",
        3,
        [routes_t, drop_order],
        [auto(EXPERTS, ROWS)],
        [pltpu.VMEM((ROWS, 128), F32)],
        limit=8,
    )[0]


def attend_kernel(idx, *refs):
    xs = refs[:8]
    slots_ref, gain, wq, wk, wv, cos_ref, sin_ref = refs[8:15]
    out_ref = refs[15]
    far = refs[16:21]
    attn_in, q_ref, k_ref, v_ref, p_ref, seg_row, seg_col, v_turned, sems = refs[21:30]
    near = (attn_in, q_ref, k_ref, v_ref)
    copies = [pltpu.make_async_copy(near[n], far[n], sems.at[n]) for n in range(4)]
    gain_full = gain[...]
    for r in range(BLOCKS):
        rows = pl.ds(pl.multiple_of(idx[r] * ROWS, ROWS), ROWS)
        x = xs[r][:, :D].astype(F32)
        scale = lax.rsqrt(jnp.mean(x * x, axis=1, keepdims=True) + EPS)
        attn_in[rows, :] = (x * scale * gain_full).astype(BF)
        segs = xs[r][:, D:].astype(F32)
        seg_col[rows, :] = segs
        seg_row[:, rows] = jnp.transpose(segs)[:8, :]
    copies[0].start()
    out_ref[LEN:, :] = slots_ref[...]
    odd = (idx[8] % 2) == 1
    half = LEN // 2
    for part in range(2):
        rows = slice(part * half, (part + 1) * half)
        block = attn_in[rows, :]
        cosine = cos_ref[rows, :]
        sine = sin_ref[rows, :]
        q = mm(block, wq[...])
        q = q * cosine + swap_halves(q) * sine
        q_ref[rows, :] = (q.astype(BF).astype(F32) * HD**-0.5).astype(BF)
        k = mm(block, wk[...])
        k = jnp.where(odd, pltpu.roll(k, HD, 1), k)
        k = k * cosine + swap_halves(k) * sine
        k_ref[rows, :] = k[:, :HD].astype(BF)
        v = mm(block, wv[...])
        v = jnp.where(odd, pltpu.roll(v, HD, 1), v)
        v_ref[rows, :] = v[:, :HD].astype(BF)
        v_turned[:, rows] = jnp.transpose(v)[:HD, :].astype(BF)
    for copy in copies[1:]:
        copy.start()
    k_at = lax.broadcasted_iota(jnp.int32, (ROWS, ROWS), 0)
    q_at = lax.broadcasted_iota(jnp.int32, (ROWS, ROWS), 1)
    causal = jnp.where(k_at <= q_at, 0.0, NEG)
    inside = jnp.where(k_at > q_at, 0.0, NEG)
    for i in range(BLOCKS):
        lo = max(0, i - WIN // ROWS) * ROWS
        hi = (i + 1) * ROWS
        span = hi - lo
        rows = slice(i * ROWS, hi)
        q2 = jnp.concatenate([q_ref[rows, :HD], q_ref[rows, HD:]], axis=0)
        scores = mm_nt(k_ref[lo:hi, :], q2)
        same = jnp.where(seg_col[lo:hi, 0:1] == seg_row[0:1, rows], 0.0, NEG)
        pieces = [same[n * ROWS : (n + 1) * ROWS] for n in range(span // ROWS)]
        pieces[-1] = pieces[-1] + causal
        if i >= WIN // ROWS:
            pieces[0] = pieces[0] + inside
        bias = jnp.concatenate(pieces, axis=0)
        scores = scores + jnp.concatenate([bias, bias], axis=1)
        top = jnp.max(scores, axis=0, keepdims=True)
        expo = jnp.exp(scores - top)
        total = jnp.sum(expo, axis=0, keepdims=True)
        probs = (expo * (1.0 / total)).astype(BF)
        p_ref[i, :span, :] = probs
        if span < WIN + ROWS:
            p_ref[i, span:, :] = jnp.zeros((WIN + ROWS - span, 2 * ROWS), BF)
        copy = pltpu.make_async_copy(p_ref.at[i], far[4].at[i], sems.at[4 + i])
        copy.start()
        copies.append(copy)
        out = mm(v_turned[:, lo:hi], probs)
        out = jnp.concatenate([out[:, :ROWS], out[:, ROWS:]], axis=0)
        out_ref[rows, :] = jnp.transpose(out).astype(BF)
    for copy in copies:
        copy.wait()


def attend(idx, xs, slot_own, gain, wq, wk, wv, cos_tab, sin_tab):
    shapes = [(LEN, D), (LEN, 2 * HD), (LEN, HD), (LEN, HD), (BLOCKS, WIN + ROWS, 2 * ROWS)]
    outs = [vmem(LEN + EXPERTS, 2 * HD)] + [hbm(*shape) for shape in shapes]
    scratch = [pltpu.VMEM(shape, BF) for shape in shapes]
    scratch += [pltpu.VMEM((8, LEN), F32), pltpu.VMEM((LEN, 128), F32)]
    scratch += [pltpu.VMEM((HD, LEN), BF), pltpu.SemaphoreType.DMA((4 + BLOCKS,))]
    ins = [*xs, slot_own, gain, wq, wk, wv, cos_tab, sin_tab]
    return run(attend_kernel, "attend", 7, ins, outs, scratch, far_out=5, limit=16, idx=idx)


def project_kernel(idx, *refs):
    xs = refs[:8]
    aos = refs[8:16]
    w_out, gain, router_t = refs[16:19]
    mlp_in, slot_t, gate_t, h_far, gate_far, ao_far = refs[19:25]
    ao_all, h_own, gate_own, sems = refs[25:29]
    for r in range(BLOCKS):
        cols = pl.ds(pl.multiple_of(idx[r] * ROWS, ROWS), ROWS)
        ao_all[:, cols] = aos[r][:LEN, :]
    ao_copy = pltpu.make_async_copy(ao_all, ao_far, sems.at[0])
    ao_copy.start()
    gain_full = gain[...]
    for p in range(PAIRS):
        rows = slice(p * 2 * ROWS, (p + 1) * 2 * ROWS)
        places = [pl.ds(pl.multiple_of(idx[2 * p + n] * ROWS, ROWS), ROWS) for n in range(2)]
        attended = jnp.concatenate([ao_all[place, :] for place in places], axis=0)
        x = jnp.concatenate([xs[2 * p + n][:, :D] for n in range(2)], axis=0).astype(F32)
        h = x + mm(attended, w_out[...])
        scale = lax.rsqrt(jnp.mean(h * h, axis=1, keepdims=True) + EPS)
        normed = (h * scale * gain_full).astype(BF)
        mlp_in[rows, :] = normed
        logits = mm_nt(router_t[:EXPERTS, :], normed)
        slot = jnp.concatenate([aos[2 * p + n][LEN:, :] for n in range(2)], axis=1).astype(F32)
        routed = slot > -1.5
        logits = jnp.where(routed, logits, NEG)
        top = jnp.max(logits, axis=0, keepdims=True)
        expo = jnp.where(routed, jnp.exp(logits - top), 0.0)
        gate = expo / jnp.sum(expo, axis=0, keepdims=True)
        slot_t[:, rows] = slot
        gate_t[:, rows] = gate
        if p == 0:
            h_own[...] = h[:ROWS]
            wide = jnp.concatenate(
                [gate[:, :ROWS], jnp.zeros((128 - EXPERTS, ROWS), F32)], axis=0
            )
            gate_own[...] = jnp.transpose(wide)
            own_copies = [
                pltpu.make_async_copy(h_own, h_far, sems.at[1]),
                pltpu.make_async_copy(gate_own, gate_far, sems.at[2]),
            ]
            for copy in own_copies:
                copy.start()
    ao_copy.wait()
    for copy in own_copies:
        copy.wait()


def project(idx, xs, aos, w_out, gain, router_t):
    outs = [
        vmem(LEN, D),
        vmem(EXPERTS, LEN, dtype=F32),
        vmem(EXPERTS, LEN, dtype=F32),
        hbm(ROWS, D, dtype=F32),
        hbm(ROWS, 128, dtype=F32),
        hbm(LEN, D),
    ]
    scratch = [
        pltpu.VMEM((LEN, D), BF),
        pltpu.VMEM((ROWS, D), F32),
        pltpu.VMEM((ROWS, 128), F32),
        pltpu.SemaphoreType.DMA((3,)),
    ]
    ins = [*xs, *aos, w_out, gain, router_t]
    return run(project_kernel, "project", 5, ins, outs, scratch, far_out=3, limit=14, idx=idx)


PROWS = LOCAL * SLOTS
HALF = LOCAL // 2
LEFT = FE
XROWS = D // 4 + FE // 4 * (LEFT // FE)
QROWS = XROWS // 4
ZROWS = D // 16 + FE // 16 * ((D - LEFT) // FE)


def experts_kernel(idx, *refs):
    mlp_in = refs[0]
    dys = refs[1:9]
    slot_t, gate_t, w_gate, w_up, w_down = refs[9:14]
    rows_out, act_out, dout_out, dg_out, du_out, hot_gated, outs, dm_same, dm_other = refs[14:23]
    wg_buf, wu_buf, wd_buf, sems, dy_rows, gate_col, hot, dslots = refs[23:31]

    def load(e):
        at = idx[9] * LOCAL + e
        slot = lax.rem(e, 2)
        return [
            pltpu.make_async_copy(weight.at[at], buf.at[slot], sems.at[slot, n])
            for n, (weight, buf) in enumerate(((w_gate, wg_buf), (w_up, wu_buf), (w_down, wd_buf)))
        ]

    for e in range(2):
        for copy in load(jnp.int32(e)):
            copy.start()
    for p in range(PAIRS):
        cols = slice(p * 2 * ROWS, (p + 1) * 2 * ROWS)
        part = slice(p * SLOTS, (p + 1) * SLOTS)
        lane = lax.broadcasted_iota(jnp.int32, (1, 2 * ROWS), 1)
        lift = jnp.where(lane >= ROWS, float(CAP), 0.0)
        row_id = lax.broadcasted_iota(jnp.int32, (SLOTS, 2 * ROWS), 0).astype(F32)
        hots = []
        for n in range(LOCAL):
            slot = slot_t[pl.ds(idx[15] + n, 1), cols]
            gate = gate_t[pl.ds(idx[15] + n, 1), cols]
            place = jnp.where(slot > -0.5, slot + lift, -1.0)
            one = jnp.where(row_id == place, 1.0, 0.0)
            gated_one = one * gate
            gate_col[n, part, :] = jnp.sum(gated_one, axis=1, keepdims=True)
            hots.append(one.astype(BF))
            hot_gated[p, n * SLOTS : (n + 1) * SLOTS, :] = gated_one.astype(BF)
        hot_pair = jnp.concatenate(hots, axis=0)
        hot[p] = hot_pair
        taken = mm(hot_pair, mlp_in[cols, :]).astype(BF)
        dy = jnp.concatenate([dys[2 * p][...], dys[2 * p + 1][...]], axis=0)
        taken_dy = mm(hot_pair, dy).astype(BF)
        for n in range(LOCAL):
            rows_out[n, part, :] = taken[n * SLOTS : (n + 1) * SLOTS]
            dy_rows[n, part, :] = taken_dy[n * SLOTS : (n + 1) * SLOTS]

    def one_expert(e, carry):
        for copy in load(e):
            copy.wait()
        at = lax.rem(e, 2)
        rows = rows_out[e]
        wg = wg_buf[at]
        wu = wu_buf[at]
        wd = wd_buf[at]
        gate_h = mm(rows, wg)
        up_h = mm(rows, wu)
        sig = 1.0 / (1.0 + jnp.exp(-gate_h))
        silu = gate_h * sig
        act = (silu * up_h).astype(BF)
        act_out[e] = act
        out = mm(act, wd).astype(BF)
        outs[e] = out
        dy = dy_rows[e].astype(F32)
        d_gate = jnp.sum(dy * out.astype(F32), axis=1, keepdims=True)
        d_out = (gate_col[e].astype(BF).astype(F32) * dy).astype(BF)
        dout_out[e] = d_out
        d_act = mm_nt(d_out, wd)
        d_up = (d_act * silu).astype(BF)
        d_gh = (d_act * up_h * sig * (1.0 + gate_h * (1.0 - sig))).astype(BF)
        dg_out[e] = d_gh
        du_out[e] = d_up
        dslots[e, :, :D] = (mm_nt(d_gh, wg) + mm_nt(d_up, wu)).astype(BF)
        lane = lax.broadcasted_iota(jnp.int32, (EROWS, 128), 1)
        d_high = d_gate.astype(BF).astype(F32)
        mine = idx[15] + e
        extra = jnp.where(lane == mine, d_high, 0.0)
        extra = jnp.where(lane == mine + EXPERTS, d_gate - d_high, extra)
        dslots[e, :, D:] = extra.astype(BF)

        @pl.when(e + 2 < LOCAL)
        def _():
            for copy in load(e + 2):
                copy.start()

        return carry

    lax.fori_loop(0, LOCAL, one_expert, 0)

    for p in range(PAIRS):
        part = slice(p * SLOTS, (p + 1) * SLOTS)
        grads = jnp.concatenate([dslots[n, part, :] for n in range(LOCAL)], axis=0)
        merged = mm_tn(hot[p], grads).astype(BF)
        dm_same[p] = merged[:ROWS]
        dm_other[p] = merged[ROWS:]


def experts(idx, mlp_in, dys, slot_t, gate_t, w_gate, w_up, w_down):
    wide = (LOCAL, EROWS, D)
    narrow = (LOCAL, EROWS, FE)
    hot_shape = (PAIRS, PROWS, 2 * ROWS)
    outs = [vmem(*shape) for shape in (wide, narrow, wide, narrow, narrow, hot_shape, wide)]
    outs += [vmem(4, ROWS, AUG)] * 2
    scratch = [
        pltpu.VMEM((2, D, FE), BF),
        pltpu.VMEM((2, D, FE), BF),
        pltpu.VMEM((2, FE, D), BF),
        pltpu.SemaphoreType.DMA((2, 3)),
        pltpu.VMEM(wide, BF),
        pltpu.VMEM((LOCAL, EROWS, 1), F32),
        pltpu.VMEM(hot_shape, BF),
        pltpu.VMEM((LOCAL, EROWS, AUG), BF),
    ]
    ins = [mlp_in, *dys, slot_t, gate_t, w_gate, w_up, w_down]
    return run(experts_kernel, "experts", 16, ins, outs, scratch, far_in=3, limit=26, idx=idx)


def ring_places(e):
    if e < HALF:
        return ((0, 2, e), (2, 0, e), (1, 3, e), (3, 1, e + HALF))
    return ((0, 2, e), (1, 0, e), (2, 1, e - HALF), (3, 4, e - HALF))


def weight_grads_kernel(idx, rows, act, d_out, d_gh, d_up, *refs):
    x_far = refs[:5]
    z_far = refs[5:10]
    x_bufs = refs[10:15]
    z_bufs = refs[15:20]
    whole, whole_down, x_sems, z_sems = refs[20:24]
    quarter = D // 4
    down_q = FE // 4
    small = quarter // 4
    small_down = down_q // 4
    copies = []
    for e in range(LOCAL):
        both = jnp.concatenate([d_gh[e], d_up[e]], axis=1)
        whole[...] = mm_tn(rows[e], both).astype(BF)
        whole_down[...] = mm_tn(act[e], d_out[e]).astype(BF)
        for k, item, place in ring_places(e):
            target = x_bufs[item].at[place]
            at = (idx[11] + k) % 4
            start = pl.multiple_of(at * quarter, quarter)
            target[:quarter, :] = whole[pl.ds(start, quarter), :FE]
            start = pl.multiple_of(at * down_q, down_q)
            target[quarter:, :] = whole_down[pl.ds(start, down_q), :FE]
            copy = pltpu.make_async_copy(target, x_far[item].at[place], x_sems.at[e, k])
            copy.start()
            copies.append(copy)
        for k, item, place in ring_places(e):
            target = z_bufs[item].at[place]
            at = (idx[12] + k) % 4
            for x in range(4):
                start = pl.multiple_of(x * quarter + at * small, small)
                target[x, :small, :] = whole[pl.ds(start, small), FE:]
                start = pl.multiple_of(x * down_q + at * small_down, small_down)
                target[x, small:, :] = whole_down[pl.ds(start, small_down), FE:]
            copy = pltpu.make_async_copy(target, z_far[item].at[place], z_sems.at[e, k])
            copy.start()
            copies.append(copy)
    for copy in copies:
        copy.wait()


def weight_grads(idx, rows, act, d_out, d_gh, d_up):
    x_piece = (XROWS, FE)
    z_piece = (4, ZROWS, FE)
    shapes = [(LOCAL, *x_piece)] * 3 + [(HALF, *x_piece)] * 2
    shapes += [(LOCAL, *z_piece)] * 3 + [(HALF, *z_piece)] * 2
    outs = [hbm(*shape) for shape in shapes]
    scratch = [pltpu.VMEM(shape, BF) for shape in shapes]
    scratch += [pltpu.VMEM((D, 2 * FE), BF), pltpu.VMEM((FE, D), BF)]
    scratch += [pltpu.SemaphoreType.DMA((LOCAL, 4))] * 2
    ins = [rows, act, d_out, d_gh, d_up]
    results = run(
        weight_grads_kernel, "weight_grads", 6, ins, outs, scratch, far_out=10, limit=24, idx=idx
    )
    return results[:5], results[5:]


def relay_kernel(*refs):
    far = refs[:8]
    outs_far = refs[8:12]
    bufs = refs[12:20]
    outs = refs[20:24]
    in_sems, out_sems = refs[24:26]
    loads = [
        [
            fetch(
                [item.at[e] for item in far[pair : pair + 2]],
                [item.at[e] for item in bufs[pair : pair + 2]],
                in_sems.at[pair // 2, e],
            )
            for e in range(HALF)
        ]
        for pair in range(0, 8, 2)
    ]
    stores = []
    for n in range(4):
        for e in range(HALF):
            for copy in loads[n][e]:
                copy.wait()
            outs[n][e] = (bufs[2 * n][e].astype(F32) + bufs[2 * n + 1][e].astype(F32)).astype(BF)
            copy = pltpu.make_async_copy(outs[n].at[e], outs_far[n].at[e], out_sems.at[n, e])
            copy.start()
            stores.append(copy)
    for copy in stores:
        copy.wait()


def relay(x_parts, z_parts):
    ins = [*x_parts, *z_parts]
    x_shape, z_shape = x_parts[0].shape, z_parts[0].shape
    shapes = [x_shape, x_shape, z_shape, z_shape]
    scratch = [pltpu.VMEM(shape, BF) for shape in (x_shape,) * 4 + (z_shape,) * 4]
    scratch += [pltpu.VMEM(shape, BF) for shape in shapes]
    scratch += [pltpu.SemaphoreType.DMA((4, HALF, 2)), pltpu.SemaphoreType.DMA((4, HALF))]
    outs = [hbm(*shape) for shape in shapes]
    return run(
        relay_kernel, "relay", 300, ins, outs, scratch, far_in=8, far_out=4, limit=FAR_LIMIT
    )


def mixed_kernel(idx, hot_gated, outs, far, blocks, sems):
    copies = []
    for p in range(PAIRS):
        part = slice(p * SLOTS, (p + 1) * SLOTS)
        values = jnp.concatenate([outs[n, part, :] for n in range(LOCAL)], axis=0)
        merged = mm_tn(hot_gated[p], values).astype(BF)
        for n in range(2):
            r = 2 * p + n
            blocks[r] = merged[n * ROWS : (n + 1) * ROWS]
            copy = pltpu.make_async_copy(
                blocks.at[r], far.at[idx[r], :, pl.ds(256, D)], sems.at[r]
            )
            copy.start()
            copies.append(copy)
    for copy in copies:
        copy.wait()


def mixed_sum(idx, hot_gated, outs):
    scratch = [pltpu.VMEM((BLOCKS, ROWS, D), BF), pltpu.SemaphoreType.DMA((BLOCKS,))]
    far = [hbm(BLOCKS, ROWS, 256 + D)]
    ins = [hot_gated, outs]
    return run(mixed_kernel, "mixed_sum", 0.6, ins, far, scratch, far_out=1, limit=10, idx=idx)[0]


def add_pairs_kernel(same, other, *outs):
    for off in range(4):
        outs[off][...] = (same[off].astype(F32) + other[off].astype(F32)).astype(BF)


def add_pairs(same, other):
    return run(
        add_pairs_kernel, "add_pairs", 0.3, [same, other], [vmem(*same.shape[1:])] * 4, limit=4
    )


def stage_kernel(cut, idx, *refs):
    far = refs[:5]
    outs_far = refs[5:9]
    bufs = refs[9:14]
    outs = refs[14:18]
    total, in_sems, out_sems = refs[18:21]
    own, from_below, from_above, late_below, late_above = range(5)
    needed = []
    loads = []
    for n in range(LOCAL):
        if n < HALF:
            places = ((own, n), (late_below, n), (from_above, n + HALF))
        else:
            places = ((own, n), (from_below, n), (late_above, n - HALF))
        needed.append(places)
        loads.append(
            fetch(
                [far[item].at[at] for item, at in places],
                [bufs[item].at[at] for item, at in places],
                in_sems.at[n],
            )
        )
    stores = []
    for n in range(LOCAL):
        for copy in loads[n]:
            copy.wait()
        parts = [bufs[item][at].astype(F32) for item, at in needed[n]]
        total[...] = (parts[0] + parts[1] + parts[2]).astype(BF)
        cut(idx, total, outs, n)
        stores += fetch(
            [item.at[n] for item in outs], [item.at[n] for item in outs_far], out_sems.at[n]
        )
    for copy in stores:
        copy.wait()


def stage_sums(idx, name, micros, cut, rows, parts):
    shapes = [(LOCAL, rows, FE)] * 4
    scratch = [pltpu.VMEM(part.shape, BF) for part in parts]
    scratch += [pltpu.VMEM(shape, BF) for shape in shapes]
    scratch += [pltpu.VMEM(parts[0].shape[1:], BF)]
    scratch += [pltpu.SemaphoreType.DMA((LOCAL, 3)), pltpu.SemaphoreType.DMA((LOCAL, 4))]
    return run(
        functools.partial(stage_kernel, cut),
        name,
        micros,
        parts,
        [hbm(*shape) for shape in shapes],
        scratch,
        far_in=5,
        far_out=4,
        limit=FAR_LIMIT,
        idx=idx,
    )


def cut_along_z(idx, total, outs, n):
    gate_rows = D // 16
    down_rows = FE // 16
    for k in range(4):
        at = (idx[12] + k) % 4
        start = pl.multiple_of(at * gate_rows, gate_rows)
        outs[k][n, :gate_rows, :] = total[pl.ds(start, gate_rows), :]
        for m in range(LEFT // FE):
            start = pl.multiple_of(D // 4 + m * (FE // 4) + at * down_rows, down_rows)
            to = gate_rows + m * down_rows
            outs[k][n, to : to + down_rows, :] = total[pl.ds(start, down_rows), :]


def cut_along_x(idx, total, outs, n):
    for k in range(4):
        outs[k][n] = total[pl.ds((idx[11] + k) % 4, 1)][0]


SEND_ROWS = (QROWS + ZROWS) // 2


def finish_kernel(idx, *refs):
    far = refs[:8]
    outs_far = refs[8:11]
    send_far = refs[11]
    bufs = refs[12:20]
    keep_gate, keep_up, keep_down, send = keeps = refs[20:24]
    x_sum, z_sum, in_sems, out_sems = refs[24:28]
    loads = [
        fetch([item.at[n] for item in far], [item.at[n] for item in bufs], in_sems.at[n])
        for n in range(LOCAL)
    ]
    big = D // 16
    small = big // 2
    tiny = FE // 32
    mine = idx[9]
    theirs = 1 - mine
    stores = []
    for n in range(LOCAL):
        for copy in loads[n]:
            copy.wait()
        acc = bufs[0][n].astype(F32)
        for part in bufs[1:4]:
            acc = acc + part[n].astype(F32)
        x_sum[...] = acc
        acc = bufs[4][n].astype(F32)
        for part in bufs[5:8]:
            acc = acc + part[n].astype(F32)
        z_sum[...] = acc
        here = pl.ds(pl.multiple_of(mine * small, small), small)
        there = pl.ds(pl.multiple_of(theirs * small, small), small)
        keep_gate[n] = x_sum[here, :]
        keep_up[n] = z_sum[here, :]
        send[n, :small, :] = x_sum[there, :].astype(BF)
        send[n, small:big, :] = z_sum[there, :].astype(BF)
        for m in range(D // FE):
            source, at = (x_sum, m) if m < LEFT // FE else (z_sum, m - LEFT // FE)
            first = big + at * 2 * tiny
            here = pl.ds(pl.multiple_of(first + mine * tiny, tiny), tiny)
            there = pl.ds(pl.multiple_of(first + theirs * tiny, tiny), tiny)
            keep_down[n, :, m * FE : (m + 1) * FE] = source[here, :]
            send[n, big + m * tiny : big + (m + 1) * tiny, :] = source[there, :].astype(BF)
        targets = [item.at[mine * LOCAL + n] for item in outs_far] + [send_far.at[n]]
        stores += fetch([item.at[n] for item in keeps], targets, out_sems.at[n])
    for copy in stores:
        copy.wait()


def finish(idx, parts):
    outs = [
        hbm(2 * LOCAL, D // 32, FE, dtype=F32),
        hbm(2 * LOCAL, D // 32, FE, dtype=F32),
        hbm(2 * LOCAL, FE // 32, D, dtype=F32),
        hbm(LOCAL, SEND_ROWS, FE),
    ]
    scratch = [pltpu.VMEM(part.shape, BF) for part in parts]
    scratch += [
        pltpu.VMEM((LOCAL, D // 32, FE), F32),
        pltpu.VMEM((LOCAL, D // 32, FE), F32),
        pltpu.VMEM((LOCAL, FE // 32, D), F32),
        pltpu.VMEM((LOCAL, SEND_ROWS, FE), BF),
        pltpu.VMEM((QROWS, FE), F32),
        pltpu.VMEM((ZROWS, FE), F32),
        pltpu.SemaphoreType.DMA((LOCAL, 8)),
        pltpu.SemaphoreType.DMA((LOCAL, 4)),
    ]
    return run(
        finish_kernel,
        "finish",
        1,
        parts,
        outs,
        scratch,
        far_in=8,
        far_out=4,
        limit=FAR_LIMIT,
        idx=idx,
    )


def assemble_kernel(idx, got, gate_in, up_in, down_in, *refs):
    outs_far = refs[:3]
    gate, up, down, out_sems = refs[3:7]
    small = D // 32
    tiny = FE // 32
    stores = []
    for n in range(LOCAL):
        gate[n] = got[n, :small, :].astype(F32)
        up[n] = got[n, small : 2 * small, :].astype(F32)
        down[n, :, :FE] = got[n, 2 * small : 2 * small + tiny, :].astype(F32)
        down[n, :, FE:] = got[n, 2 * small + tiny :, :].astype(F32)
        targets = [item.at[(1 - idx[9]) * LOCAL + n] for item in outs_far]
        stores += fetch([gate.at[n], up.at[n], down.at[n]], targets, out_sems.at[n])
    for copy in stores:
        copy.wait()


def assemble(idx, got, results):
    outs = [hbm(*item.shape, dtype=F32) for item in results]
    scratch = [
        pltpu.VMEM((LOCAL, D // 32, FE), F32),
        pltpu.VMEM((LOCAL, D // 32, FE), F32),
        pltpu.VMEM((LOCAL, FE // 32, D), F32),
        pltpu.SemaphoreType.DMA((LOCAL, 3)),
    ]
    return run(
        assemble_kernel,
        "assemble",
        1,
        [got, *results],
        outs,
        scratch,
        far_in=3,
        far_out=3,
        limit=8,
        idx=idx,
        aliases={2: 0, 3: 1, 4: 2},
    )


def middle_kernel(*refs):
    parts = refs[:4]
    h_ref, gate_ref, dy_ref, gain_ref, router_t, w_out = refs[4:10]
    dh_ref, send_ref, side_ref = refs[10:13]
    total = parts[0][...].astype(F32)
    for part in parts[1:]:
        total = total + part[...].astype(F32)
    extra = total[:, D:]
    d_gate = extra + pltpu.roll(extra, 128 - EXPERTS, 1)
    gate = gate_ref[...]
    d_chosen = gate * (d_gate - jnp.sum(gate * d_gate, axis=1, keepdims=True))
    d_logits = d_chosen.astype(BF)
    d_mlp = total[:, :D] + mm(d_logits, router_t[...])
    h = h_ref[...]
    gain = gain_ref[...].astype(F32)
    scale = lax.rsqrt(jnp.mean(h * h, axis=1, keepdims=True) + EPS)
    normed = h * scale
    mlp_in = (normed * gain).astype(BF)
    scaled = d_mlp * gain
    d_h = (
        dy_ref[...].astype(F32)
        + scale * scaled
        - h * (scale * scale * scale) * jnp.mean(scaled * h, axis=1, keepdims=True)
    )
    dh_ref[...] = d_h
    d_branch = d_h.astype(BF)
    d_attn = mm_nt(d_branch, w_out[...]).astype(BF)
    for b in range(BLOCKS):
        cols = slice(b * 128, (b + 1) * 128)
        send_ref[b, :, :128] = d_attn[:, cols]
        send_ref[b, :, 128:] = d_branch[:, cols]
    router = mm_tn(mlp_in, d_logits)
    d_gain = jnp.sum(d_mlp * normed, axis=0, keepdims=True)
    column = jnp.transpose(jnp.broadcast_to(d_gain, (128, D)))
    lane = lax.broadcasted_iota(jnp.int32, (D, 128), 1)
    side_ref[...] = jnp.where(lane == GAIN_LANE, column, router).astype(BF)


def middle(parts, h_own, gate_own, dy, gain, router_t, w_out):
    shapes = [((ROWS, D), F32), ((BLOCKS, ROWS, 256), BF), ((D, 128), BF)]

    def kernel(*refs):
        inputs = refs[:10]
        far = refs[10:13]
        bufs = refs[13:16]
        middle_kernel(*inputs, *bufs)
        for copy in fetch(bufs, far, refs[16]):
            copy.wait()

    outs = [hbm(*shape, dtype=kind) for shape, kind in shapes]
    scratch = [pltpu.VMEM(shape, kind) for shape, kind in shapes] + [pltpu.SemaphoreType.DMA((3,))]
    ins = [*parts, h_own, gate_own, dy, gain, router_t, w_out]
    return run(kernel, "middle", 100, ins, outs, scratch, far_out=3, limit=10)


def attend_back_kernel(idx, *refs):
    early_far = refs[:6]
    far = refs[6:10]
    pack, dense_far = refs[11:13]
    early = refs[13:19]
    p_ref, attn_in, ao_all, side_ref, dk_acc, dv_acc, dqkv_ref, dense, k_turned = refs[19:28]
    sems, early_sems, tables_sems = refs[28:31]
    grads, q_ref, k_ref, v_ref, cos_ref, sin_ref = early
    early_copies = fetch(early_far[:4], early[:4], early_sems)
    p_copies = [
        pltpu.make_async_copy(far[0].at[i], p_ref.at[i], sems.at[i]) for i in range(BLOCKS)
    ]
    ao_copy = pltpu.make_async_copy(far[2], ao_all, sems.at[BLOCKS])
    in_copy = pltpu.make_async_copy(far[1], attn_in, sems.at[BLOCKS + 1])
    p_copies[0].start()
    table_copies = fetch(early_far[4:], early[4:], tables_sems)
    p_copies[1].start()
    p_copies[2].start()
    side_copy = pltpu.make_async_copy(far[3], side_ref, sems.at[2 * BLOCKS + 3])
    dk_acc[...] = jnp.zeros((LEN, HD), F32)
    dv_acc[...] = jnp.zeros((LEN, HD), F32)
    for copy in early_copies:
        copy.wait()
    k_wide = jnp.concatenate([k_ref[...], k_ref[...]], axis=1).astype(F32)
    k_turned[...] = jnp.transpose(k_wide)[:HD, :].astype(BF)
    for i in range(BLOCKS):
        lo = max(0, i - WIN // ROWS) * ROWS
        hi = (i + 1) * ROWS
        span = hi - lo
        rows = slice(i * ROWS, hi)
        do2 = jnp.concatenate([grads[i, :, :HD], grads[i, :, HD : 2 * HD]], axis=0)
        q2 = jnp.concatenate([q_ref[rows, :HD], q_ref[rows, HD:]], axis=0)
        p_copies[i].wait()
        if i + 3 < BLOCKS:
            p_copies[i + 3].start()
        if i == 2:
            in_copy.start()
            side_copy.start()
            ao_copy.start()
        probs_low = p_ref[i, :span, :]
        probs = probs_low.astype(F32)
        d_probs = mm_nt(v_ref[lo:hi, :], do2)
        weighted = probs * d_probs
        d_scores = (weighted - probs * jnp.sum(weighted, axis=0, keepdims=True)).astype(BF)
        dk_acc[lo:hi, :] += mm(d_scores, q2)
        dv_acc[lo:hi, :] += mm(probs_low, do2)
        dq = mm(k_turned[:, lo:hi], d_scores) * HD**-0.5
        dq = jnp.transpose(jnp.concatenate([dq[:, :ROWS], dq[:, ROWS:]], axis=0))
        dq = dq.astype(BF).astype(F32)
        if i == 0:
            for copy in table_copies:
                copy.wait()
        dq = dq * cos_ref[rows, :] - swap_halves(dq) * sin_ref[rows, :]
        dqkv_ref[rows, : 2 * HD] = dq.astype(BF)
    pair = jnp.concatenate([dk_acc[...], dv_acc[...]], axis=1).astype(BF).astype(F32)
    turned = pair * cos_ref[...] - swap_halves(pair) * sin_ref[...]
    lane = lax.broadcasted_iota(jnp.int32, pair.shape, 1)
    dqkv_ref[:, 2 * HD :] = jnp.where(lane < HD, turned, pair).astype(BF)
    dqkv_copies = []
    for r in range(BLOCKS):
        copy = pltpu.make_async_copy(
            dqkv_ref.at[pl.ds(r * ROWS, ROWS), :],
            pack.at[r, :, pl.ds(0, 256)],
            sems.at[BLOCKS + 3 + r],
        )
        copy.start()
        dqkv_copies.append(copy)
    in_copy.wait()
    ao_copy.wait()
    half = D // 2
    side_copy.wait()
    d_branch = jnp.concatenate([grads[b, :, 128:] for b in range(BLOCKS)], axis=0)
    left_turned = mm_tn(dqkv_ref[...], attn_in[...])
    right_turned = mm_tn(d_branch, ao_all[...])
    for part in range(2):
        rows = slice(part * half, (part + 1) * half)
        left = jnp.transpose(left_turned[:, rows])
        right = jnp.concatenate(
            [jnp.transpose(right_turned[:, rows]), side_ref[rows, :].astype(F32)], axis=1
        )
        both = jnp.concatenate([left.reshape(-1, 8, 256), right.reshape(-1, 8, 256)], axis=1)
        places = pl.ds(part * (half // 8), half // 8)
        dense[places] = both.astype(BF)
        copy = pltpu.make_async_copy(
            dense.at[places], dense_far.at[places], sems.at[(BLOCKS + 2, 2 * BLOCKS + 4)[part]]
        )
        copy.start()
        dqkv_copies.append(copy)
    for copy in dqkv_copies:
        copy.wait()


def attend_back(idx, grads, p, q, k, v, attn_in, ao_all, side, cos_tab, sin_tab, pack):
    early = [grads, q, k, v, cos_tab, sin_tab]
    outs = [hbm(*pack.shape), hbm(D // 8, 16, 256)]
    scratch = [pltpu.VMEM(item.shape, item.dtype) for item in early]
    scratch += [
        pltpu.VMEM(p.shape, BF),
        pltpu.VMEM((LEN, D), BF),
        pltpu.VMEM((LEN, D), BF),
        pltpu.VMEM((D, 128), BF),
        pltpu.VMEM((LEN, HD), F32),
        pltpu.VMEM((LEN, HD), F32),
        pltpu.VMEM((LEN, 256), BF),
        pltpu.VMEM((D // 8, 16, 256), BF),
        pltpu.VMEM((HD, LEN), BF),
        pltpu.SemaphoreType.DMA((2 * BLOCKS + 5,)),
        pltpu.SemaphoreType.DMA((4,)),
        pltpu.SemaphoreType.DMA((2,)),
    ]
    ins = [*early, p, attn_in, ao_all, side, pack]
    return run(
        attend_back_kernel,
        "attend_back",
        8,
        ins,
        outs,
        scratch,
        far_in=11,
        far_out=2,
        limit=FAR_LIMIT,
        idx=idx,
        aliases={11: 0},
    )


def input_grad_kernel(pack, *refs):
    far = refs[:7]
    outs_far = refs[7:9]
    bufs = refs[9:16]
    out, block, dq, dk, dv, early_sems, late_sems, out_sems = refs[16:24]
    early = fetch(far[:4], bufs[:4], early_sems)
    late = fetch(far[4:], bufs[4:], late_sems)
    x_ref, dh_ref, gain_ref, h_own, w_query, w_key, w_value = bufs
    for b in range(BLOCKS):
        dq[:, b * 128 : (b + 1) * 128] = pack[b, :, :128]
    for b in range(0, BLOCKS, 2):
        first = pack[b, :, 128:256].astype(F32)
        second = pack[b + 1, :, 128:256].astype(F32)
        cols = slice(b * HD, (b + 2) * HD)
        dk[:, cols] = jnp.concatenate([first[:, :HD], second[:, :HD]], axis=1).astype(BF)
        dv[:, cols] = jnp.concatenate([first[:, HD:], second[:, HD:]], axis=1).astype(BF)
    for copy in early:
        copy.wait()
    total = h_own[...]
    for b in range(BLOCKS):
        total = total + pack[b, :, 256:].astype(F32)
    block[...] = total.astype(BF)
    for copy in late:
        copy.wait()
    d_in = mm_nt(dq[...], w_query[...]) + mm_nt(dk[...], w_key[...]) + mm_nt(dv[...], w_value[...])
    x = x_ref[...].astype(F32)
    scale = lax.rsqrt(jnp.mean(x * x, axis=1, keepdims=True) + EPS)
    scaled = d_in * gain_ref[...]
    out[...] = (
        dh_ref[...]
        + scale * scaled
        - x * (scale * scale * scale) * jnp.mean(scaled * x, axis=1, keepdims=True)
    ).astype(BF)
    for copy in fetch((out, block), outs_far, out_sems):
        copy.wait()


def input_grad(pack, x, d_h, gain, h_own, w_query, w_key, w_value):
    ins = [pack, x, d_h, gain, h_own, w_query, w_key, w_value]
    scratch = [pltpu.VMEM(item.shape, item.dtype) for item in ins[1:]]
    scratch += [
        pltpu.VMEM((ROWS, D), BF),
        pltpu.VMEM((ROWS, D), BF),
        pltpu.VMEM((ROWS, H * HD), BF),
        pltpu.VMEM((ROWS, KVH * HD), BF),
        pltpu.VMEM((ROWS, KVH * HD), BF),
        pltpu.SemaphoreType.DMA((4,)),
        pltpu.SemaphoreType.DMA((3,)),
        pltpu.SemaphoreType.DMA((2,)),
    ]
    return run(
        input_grad_kernel,
        "input_grad",
        1,
        ins,
        [hbm(ROWS, D)] * 2,
        scratch,
        far_in=len(ins) - 1,
        far_out=2,
        limit=FAR_LIMIT,
    )


def dense_out_kernel(idx, dense, w_query, w_key, w_value, gain, *refs):
    dq, dk, dv, do, router, gains, turned = refs
    total = jnp.sum(dense[...].astype(F32).reshape(-1, BLOCKS, 16, 256), axis=0)
    for b in range(BLOCKS):
        dq[:, b * 128 : (b + 1) * 128] = total[b, :8, :128]
        do[:, b * 128 : (b + 1) * 128] = total[b, 8:, :128]
    for b in range(0, BLOCKS, 2):
        first = total[b, :8, 128:]
        second = total[b + 1, :8, 128:]
        cols = slice(b * HD, (b + 2) * HD)
        dk[:, cols] = jnp.concatenate([first[:, :HD], second[:, :HD]], axis=1)
        dv[:, cols] = jnp.concatenate([first[:, HD:], second[:, HD:]], axis=1)
    side = jnp.sum(total[:, 8:, 128:], axis=0)
    router[...] = side[:, :EXPERTS]
    dot = jnp.zeros((8, 1), F32)
    for weight, grad in ((w_query, dq), (w_key, dk), (w_value, dv)):
        dot = dot + jnp.sum(weight[...] * grad[...], axis=1, keepdims=True)
    chunk = pl.ds(pl.multiple_of(idx[16] * 128, 128), 128)
    turned[...] = jnp.transpose(jnp.broadcast_to(gain[:, chunk], (128, 128)))
    gain_rows = turned[pl.ds(pl.multiple_of(idx[17] * 8, 8), 8), 0:1]
    lane = lax.broadcasted_iota(jnp.int32, (8, 128), 1)
    both = jnp.where(lane == GAIN_LANE, side, dot / gain_rows)
    turned[:8, :] = both
    flat = jnp.transpose(turned[...])
    gains[...] = flat[GAIN_LANE - 8 : GAIN_LANE + 8, :]


def dense_out(idx, dense, w_query, w_key, w_value, gain):
    outs = [
        auto(8, H * HD, dtype=F32),
        auto(8, KVH * HD, dtype=F32),
        auto(8, KVH * HD, dtype=F32),
        auto(8, D, dtype=F32),
        auto(8, EXPERTS, dtype=F32),
        auto(16, 128, dtype=F32),
    ]
    ins = [dense, w_query, w_key, w_value, gain]
    scratch = [pltpu.VMEM((128, 128), F32)]
    return run(dense_out_kernel, "dense_out", 1, ins, outs, scratch, limit=8, idx=idx)


def from_x(value, off):
    size = lax.axis_size("x")
    return lax.ppermute(value, "x", [(i, (i + off) % size) for i in range(size)])


def from_z(value, off):
    size = lax.axis_size("z")
    return lax.ppermute(value, "z", [(i, (i + off) % size) for i in range(size)])


def along_y(value, off):
    route = []
    for y in range(4):
        to = (y + off) % 4
        route.append(((y % 2) * 2 + y // 2, (to % 2) * 2 + to // 2))
    return lax.ppermute(value, ("yl", "yh"), route)


def other_core(value):
    return lax.ppermute(value, "c", [(0, 1), (1, 0)])


def near_ring(value):
    return [value] + [along_y(value, -off) for off in (1, 2, 3)]


def both_cores(near):
    far = [other_core(item) for item in near]
    return [item for pair in zip(near, far) for item in pair]


def gather_ring(value):
    return both_cores(near_ring(value))


def reduce_ring(pieces):
    return [pieces[0]] + [along_y(pieces[off], off) for off in (1, 2, 3)]


def scatter_parts(parts, send):
    return [parts[0]] + [send(parts[k], k) for k in (1, 2, 3)]


def together(*values):
    return lax.optimization_barrier(values)


def after(values, *earlier):
    return lax.optimization_barrier((values, earlier))[0]


def local(
    tokens,
    segments,
    routes,
    drop_order,
    gain_attn,
    w_query,
    w_key,
    w_value,
    w_out,
    gain_mlp,
    w_router,
    w_gate,
    w_up,
    w_down,
    cotangent,
):
    x_at = lax.axis_index("x")
    z_at = lax.axis_index("z")
    yl = lax.axis_index("yl")
    yh = lax.axis_index("yh")
    core = lax.axis_index("c")
    y_at = yh * 2 + yl
    own = yl * 4 + yh * 2 + core
    expert_at = yh * 2 + core

    entries = []
    for off in range(4):
        y = (y_at + off) % 4
        for dc in range(2):
            entries.append((y % 2) * 4 + (y // 2) * 2 + (core + dc) % 2)
    entries += [own, yl, expert_at, x_at, z_at, y_at, core, expert_at * 8 + yl * LOCAL]
    first_row = ((x_at * 4 + z_at) * 8 + own) * 8
    entries += [first_row // 128, first_row % 128 // 8]
    idx = jnp.stack([jnp.asarray(entry, jnp.int32) for entry in entries])

    cos_np, sin_np = rotary_tables()
    cos_tab = jnp.asarray(cos_np)
    sin_tab = jnp.asarray(sin_np)
    gain_one = gain_attn.astype(F32).reshape(1, D)
    gain_two = gain_mlp.astype(F32).reshape(1, D)
    router_t = jnp.pad(w_router.T, ((0, 128 - EXPERTS), (0, 0)))

    def columns(weight, block):
        return lax.dynamic_slice_in_dim(weight, block * 128, 128, 1)

    def out_rows(weight):
        return lax.dynamic_slice_in_dim(weight, first_row, 8, 0).astype(F32)

    wq_cols = columns(w_query, own)
    wk_cols = columns(w_key, own // 2)
    wv_cols = columns(w_value, own // 2)
    finals = [out_rows(w_query), out_rows(w_key), out_rows(w_value)]
    early = [idx, gain_one, gain_two, router_t, wq_cols, wk_cols, wv_cols, finals]

    seg_cols = jnp.broadcast_to(segments.astype(BF)[:, None], (ROWS, AUG - D))
    x_near = near_ring(jnp.concatenate([tokens, seg_cols], axis=1))
    slot_own = slots(routes.T, drop_order)
    x_near, slot_own, early = together(x_near, slot_own, early)
    idx, gain_one, gain_two, router_t, wq_cols, wk_cols, wv_cols, finals = early
    xs = both_cores(x_near)
    dy_near = near_ring(after(cotangent, slot_own))

    ao, attn_in, q, k, v, p = attend(
        idx, xs, slot_own, gain_one, wq_cols, wk_cols, wv_cols, cos_tab, sin_tab
    )
    dys = both_cores(dy_near)
    aos = gather_ring(after(ao, *dy_near))
    mlp_in, slot_t, gate_t, h_own, gate_own, ao_all = project(
        idx, xs, aos, w_out, gain_two, router_t
    )
    rows, act, d_out, d_gh, d_up, hot_gated, outs, dm_same, dm_other = experts(
        idx, mlp_in, dys, slot_t, gate_t, w_gate, w_up, w_down
    )

    got = other_core(dm_other)
    pack = mixed_sum(idx, hot_gated, outs)
    pack, got = together(pack, got)
    dm_pieces = add_pairs(dm_same, got)
    dm_parts = reduce_ring(dm_pieces)
    (x_up, x_down, *x_keep), (z_up, z_down, *z_keep) = weight_grads(
        idx, after(rows, *dm_pieces), act, d_out, d_gh, d_up
    )
    x_below = from_x(x_up, 1)
    x_above = from_x(x_down, 3)
    z_keep, z_up, z_down, dm_parts = together(z_keep, z_up, z_down, dm_parts)
    z_below = from_z(z_up, 1)
    z_above = from_z(z_down, 3)
    d_h, to_heads, side = middle(
        dm_parts, h_own, gate_own, cotangent, gain_two, router_t, w_out
    )
    grads = lax.all_to_all(to_heads, GROUP, split_axis=0, concat_axis=0, tiled=True)
    pack, dense = attend_back(
        idx, grads, p, q, k, v, attn_in, ao_all, side, cos_tab, sin_tab, pack
    )
    x_below, x_above, z_below, z_above = after([x_below, x_above, z_below, z_above], pack)
    dense = lax.all_to_all(
        dense, ("x", "z", "yl", "yh", "c"), split_axis=0, concat_axis=0, tiled=True
    )

    relayed = relay(
        [x_keep[1], x_below, x_keep[2], x_above], [z_keep[1], z_below, z_keep[2], z_above]
    )
    x_late = [from_x(relayed[0], 1), from_x(relayed[1], 3)]
    z_late = [from_z(relayed[2], 1), from_z(relayed[3], 3)]
    pack = lax.all_to_all(
        after(pack, dense, *relayed), GROUP, split_axis=0, concat_axis=0, tiled=True
    )
    dense_rows = dense_out(idx, dense, *finals, gain_one)
    x_pieces = stage_sums(
        idx, "x_sums", 200, cut_along_z, QROWS, [x_keep[0], x_below, x_above, *x_late]
    )
    z_pieces = stage_sums(
        idx, "z_sums", 200, cut_along_x, ZROWS, [z_keep[0], z_below, z_above, *z_late]
    )
    x_second = scatter_parts(x_pieces, from_z)
    z_second = scatter_parts(z_pieces, from_x)
    d_tokens, block_out = input_grad(
        after(pack, *x_pieces, *z_pieces), tokens, d_h, gain_one, h_own, w_query, w_key, w_value
    )
    d_tokens, x_second, z_second, dense_rows = together(d_tokens, x_second, z_second, dense_rows)

    *results, sent = finish(idx, [*x_second, *z_second])
    got = lax.ppermute(sent, "yl", [(0, 1), (1, 0)])
    d_w_gate, d_w_up, d_w_down = assemble(idx, got, results)
    d_w_query, d_w_key, d_w_value, d_w_out, d_w_router, gains = dense_rows
    d_gain_attn = gains[0, :8]
    d_gain_mlp = gains[8, :8]

    return (
        block_out,
        d_tokens,
        d_gain_attn,
        d_w_query,
        d_w_key,
        d_w_value,
        d_w_out,
        d_gain_mlp,
        d_w_router,
        d_w_gate,
        d_w_up,
        d_w_down,
    )


def solution(mesh):
    side = 4 if mesh.shape["dp"] == 32 else 1
    names = ("x", "z", "yl", "yh", "c")
    grid = Mesh(mesh.devices.reshape(side, side, 2, 2, 2), names)
    tokens = names
    experts_axes = ("yh", "c")
    dp = ("x", "z", "yl")
    in_specs = (
        P(tokens, None),
        P(tokens),
        P(tokens, None),
        P(tokens, None),
        P(),
        P(),
        P(),
        P(),
        P(),
        P(),
        P(),
        P(experts_axes, None, None),
        P(experts_axes, None, None),
        P(experts_axes, None, None),
        P(tokens, None),
    )
    out_specs = (
        P(tokens, None),
        P(tokens, None),
        P(tokens),
        P(tokens, None),
        P(tokens, None),
        P(tokens, None),
        P(tokens, None),
        P(tokens),
        P(tokens, None),
        P(experts_axes, dp, None),
        P(experts_axes, dp, None),
        P(experts_axes, dp, None),
    )
    return jax.shard_map(local, mesh=grid, in_specs=in_specs, out_specs=out_specs, check_vma=False)
```
